32 devices in a mesh: seq: 8 (over z, x), head: 4 (over y, core).
Axes of the slice: x: 2, y: 2, z: 4, core: 2. Of those that a mesh axis runs over, the one named last changes fastest.
Arguments:
- tokens: bfloat16 [1024, 2560], P('seq'), may hold values from -6 to 6
- norm_gain: bfloat16 [2560], replicated, may hold values from 0.5 to 1.5
- x_weight: bfloat16 [2560, 2560], P('seq', 'head'), may hold values from -0.125 to 0.125
- y_weight: bfloat16 [2560, 2560], P('seq', 'head'), may hold values from -0.125 to 0.125
- conv_weight: bfloat16 [4, 2560], P(None, 'head'), may hold values from -3 to 3
- conv_bias: bfloat16 [2560], P('head'), may hold values from -3 to 3
- a_weight: bfloat16 [256, 2560], P(None, 'head'), may hold values from -0.375 to 0.375
- a_bias: bfloat16 [2560], P('head'), may hold values from -4 to 4
- i_weight: bfloat16 [256, 2560], P(None, 'head'), may hold values from -0.375 to 0.375
- i_bias: bfloat16 [2560], P('head'), may hold values from -4 to 4
- decay: float32 [2560], P('head'), may hold values from -14 to -3.5
- out_weight: bfloat16 [2560, 2560], P('seq', 'head'), may hold values from -0.125 to 0.125
- mlp_gain: bfloat16 [2560], replicated, may hold values from 0.5 to 1.5
- gate_weight: bfloat16 [2560, 7680], P('seq', 'head'), may hold values from -0.125 to 0.125
- up_weight: bfloat16 [2560, 7680], P('seq', 'head'), may hold values from -0.125 to 0.125
- down_weight: bfloat16 [2560, 7680], P('seq', 'head'), may hold values from -0.0625 to 0.0625
- cotangent: bfloat16 [1024, 2560], P('seq'), may hold values from -6 to 6
Outputs:
- mixed: bfloat16 [1024, 2560], P('seq', 'head')
- tokens_grad: float32 [1024, 2560], P('seq')
- norm_gain_grad: float32 [2560], replicated
- x_weight_grad: float32 [2560, 2560], P('seq', 'head')
- y_weight_grad: float32 [2560, 2560], P('seq', 'head')
- conv_weight_grad: float32 [4, 2560], P(None, 'head')
- conv_bias_grad: float32 [2560], P('head')
- a_weight_grad: float32 [256, 2560], P(None, 'head')
- a_bias_grad: float32 [2560], P('head')
- i_weight_grad: float32 [256, 2560], P(None, 'head')
- i_bias_grad: float32 [2560], P('head')
- decay_grad: float32 [2560], P('head')
- out_weight_grad: float32 [2560, 2560], P('seq', 'head')
- mlp_gain_grad: float32 [2560], replicated
- gate_weight_grad: float32 [2560, 7680], P('seq', 'head')
- up_weight_grad: float32 [2560, 7680], P('seq', 'head')
- down_weight_grad: float32 [2560, 7680], P('seq', 'head')
The draws below stay inside these ranges and needn't reach their ends.
All inputs are finite; a program needn't handle non-finite values.
Results may differ from the reference program's by a relative error of at most 0.012.
Values may be sent and summed in bfloat16 or wider, within the bound.
A program may use at most 256 MiB of HBM per device.

```python
import jax
import jax.numpy as jnp
from jax import lax

D = 2560
LW = 2560
HEADS = 10
FF = 7680
CONV = 4
HS = 256
SEQ = 1024


def draw_decay(key, part):
    key = jax.random.fold_in(key, 7)
    pick_key, slow_key, fast_key = jax.random.split(key, 3)
    keep_share = 0.5
    slow_rate = jnp.exp(jax.random.uniform(slow_key, (LW,), jnp.float32, jnp.log(0.1 / SEQ), jnp.log(0.5 / SEQ)))
    fast_rate = jnp.exp(jax.random.uniform(fast_key, (LW,), jnp.float32, jnp.log(0.005), jnp.log(0.02)))
    chosen = jnp.where(jax.random.uniform(pick_key, (LW,), jnp.float32) < keep_share, slow_rate, fast_rate)
    return jnp.log(jnp.expm1(chosen))


def block_levels(rng, shape, pieces, low, high):
    def one(dim, shards_of):
        heights = jax.random.uniform(jax.random.fold_in(jax.random.fold_in(rng, 6), dim), (shards_of,), jnp.float32, low / len(pieces), high / len(pieces))
        return jnp.repeat(jnp.exp(heights), shape[dim] // shards_of).reshape((-1,) + (1,) * (len(shape) - dim - 1))

    level = one(*pieces[0])
    for cut in pieces[1:]:
        level = level * one(*cut)
    return level


def noise(rng, extent, deviation, most, cuts=(), kind=jnp.bfloat16):
    entries = jax.random.normal(rng, extent, jnp.float32) * deviation
    if len(cuts) > 0:
        entries = block_levels(rng, extent, cuts, -0.22, 0.18) * entries
    return jnp.clip(entries, min=-most, max=most).astype(kind)


def setup_inputs(seed: int = 0) -> dict:
    streams_of = jax.random.split(jax.random.key(seed), 18)
    tokens = noise(streams_of[0], (SEQ, D), 1.0, 6.0, ((0, 8),))
    norm_gain = jnp.clip(1.0 + 0.1 * jax.random.normal(streams_of[1], (D,), jnp.float32), 0.5, 1.5).astype(jnp.bfloat16)
    x_weight = noise(streams_of[2], (D, LW), D ** -0.5, 0.125, ((0, 8), (1, 4)))
    y_weight = noise(streams_of[3], (D, LW), D ** -0.5, 0.125, ((0, 8), (1, 4)))
    conv_weight = noise(streams_of[4], (CONV, LW), 0.5, 3.0, ((1, 4),))
    conv_bias = noise(streams_of[5], (LW,), 0.5, 3.0, ((0, 4),))
    a_weight = noise(streams_of[6], (HS, LW), HS ** -0.5, 0.375, ((1, 4),))
    a_bias = noise(streams_of[7], (LW,), 1.0, 4.0, ((0, 4),))
    i_weight = noise(streams_of[8], (HS, LW), HS ** -0.5, 0.375, ((1, 4),))
    i_bias = noise(streams_of[9], (LW,), 1.0, 4.0, ((0, 4),))
    decay = draw_decay(jax.random.fold_in(streams_of[17], 71), 0)
    out_weight = noise(streams_of[11], (D, LW), LW ** -0.5, 0.125, ((0, 8), (1, 4)))
    mlp_gain = jnp.clip(1.0 + 0.1 * jax.random.normal(streams_of[12], (D,), jnp.float32), 0.5, 1.5).astype(jnp.bfloat16)
    gate_weight = noise(streams_of[13], (D, FF), D ** -0.5, 0.125, ((0, 8), (1, 4)))
    up_weight = noise(streams_of[14], (D, FF), D ** -0.5, 0.125, ((0, 8), (1, 4)))
    down_weight = noise(streams_of[15], (D, FF), FF ** -0.5, 0.0625, ((0, 8), (1, 4)))
    cotangent = noise(streams_of[16], (SEQ, D), 1.0, 6.0, ((0, 8),))
    return dict(tokens=tokens, norm_gain=norm_gain, x_weight=x_weight, y_weight=y_weight, conv_weight=conv_weight, conv_bias=conv_bias, a_weight=a_weight, a_bias=a_bias, i_weight=i_weight, i_bias=i_bias, decay=decay, out_weight=out_weight, mlp_gain=mlp_gain, gate_weight=gate_weight, up_weight=up_weight, down_weight=down_weight, cotangent=cotangent)


EPSILON = 1e-06
SQUARE_FLOOR = 2.5e-07
HIGHEST_PRECISION = lax.Precision.HIGHEST

@jax.custom_vjp
def low(v):
    return lax.optimization_barrier(v.astype(jnp.bfloat16)).astype(jnp.float32)

@jax.custom_vjp
def low_back(v):
    return v

def low_keep(v):
    return (low(v), None)

def low_pass(kept, grad):
    return (grad,)

def back_keep(v):
    return (v, None)

def back_low(kept, grad):
    return (low(grad),)
low.defvjp(low_keep, low_pass)
low_back.defvjp(back_keep, back_low)

def rms_norm(values, gain):
    return values * lax.rsqrt(lax.optimization_barrier(jnp.mean(values * values, axis=-1, keepdims=True)) + EPSILON) * gain

def linear_pair(earlier, later):
    return (later[0] * earlier[0], later[0] * earlier[1] + later[1])

def block_gate(conv_low, weight, bias, length):
    head_view = conv_low.reshape(length, HS, HEADS)
    product = jnp.einsum('tih,ijh->tjh', head_view, weight.reshape(HS, HS, HEADS), precision=HIGHEST_PRECISION)
    return product.reshape(length, LW) + bias

def forward(tokens, norm_gain, x_weight, y_weight, conv_weight, conv_bias, a_weight, a_bias, i_weight, i_bias, decay, out_weight, mlp_gain, gate_weight, up_weight, down_weight):
    length = tokens.shape[0]
    first_norm = low(rms_norm(tokens, norm_gain))
    x_branch = low_back(low(jnp.dot(first_norm, x_weight, precision=HIGHEST_PRECISION)))
    y_branch = low_back(jnp.dot(first_norm, y_weight, precision=HIGHEST_PRECISION))
    y_gate = jax.nn.gelu(y_branch)
    padded = jnp.pad(x_branch, ((CONV - 1, 0), (0, 0)))
    conv_out = conv_bias + sum((conv_weight[lag_index] * padded[CONV - 1 - lag_index:CONV - 1 - lag_index + length] for lag_index in range(CONV)))
    conv_low = low(conv_out)
    a_pre = low_back(block_gate(conv_low, a_weight, a_bias, length))
    i_pre = low_back(block_gate(conv_low, i_weight, i_bias, length))
    recall = jax.nn.sigmoid(a_pre)
    input_gate = jax.nn.sigmoid(i_pre)
    log_decay = -8.0 * recall * jax.nn.softplus(decay)
    factor = jnp.exp(log_decay)
    root_scale = jnp.sqrt(jnp.maximum(-jnp.expm1(2.0 * log_decay), SQUARE_FLOOR))
    first_row = (jnp.arange(length) == 0)[:, None]
    root_scale = jnp.where(first_row, 1.0, root_scale)
    driven = conv_low * input_gate * root_scale
    state_all = lax.associative_scan(linear_pair, (factor, driven))[1]
    mixed_in = low(state_all * y_gate)
    branch = low_back(jnp.dot(mixed_in, out_weight.T, precision=HIGHEST_PRECISION))
    residual = tokens + branch
    second_norm = low(rms_norm(residual, mlp_gain))
    gate_pre = low_back(jnp.dot(second_norm, gate_weight, precision=HIGHEST_PRECISION))
    up_pre = low_back(jnp.dot(second_norm, up_weight, precision=HIGHEST_PRECISION))
    hidden = low(jax.nn.gelu(gate_pre) * up_pre)
    return residual + jnp.dot(hidden, down_weight.T, precision=HIGHEST_PRECISION)

def reference(tokens, norm_gain, x_weight, y_weight, conv_weight, conv_bias, a_weight, a_bias, i_weight, i_bias, decay, out_weight, mlp_gain, gate_weight, up_weight, down_weight, cotangent):
    inputs = [value.astype(jnp.float32) for value in (tokens, norm_gain, x_weight, y_weight, conv_weight, conv_bias, a_weight, a_bias, i_weight, i_bias, decay, out_weight, mlp_gain, gate_weight, up_weight, down_weight)]
    output, pullback = jax.vjp(forward, *inputs)
    grads = pullback(cotangent.astype(jnp.float32))
    return (output.astype(jnp.bfloat16), grads[0], grads[1], grads[2], grads[3], grads[4], grads[5], grads[6], grads[7], grads[8], grads[9], grads[10], grads[11], grads[12], grads[13], grads[14], grads[15])
```

```python
import functools

import jax
import jax.numpy as jnp
from jax import lax
from jax.experimental import pallas as pl
from jax.experimental.pallas import tpu as pltpu
from jax.sharding import PartitionSpec as P

CONV = 4
EPSILON = 1e-06
SQUARE_FLOOR = 2.5e-07
MESH = pl.DeviceIdType.MESH
F32 = jnp.float32
BF16 = jnp.bfloat16
LANES = 128
EDGE = 16
VM = pltpu.VMEM
ANY = pl.ANY
NN = (((1,), (0,)), ((), ()))
NT = (((1,), (1,)), ((), ()))
TN = (((0,), (0,)), ((), ()))


def mm(left, right, dims=NN):
    return lax.dot_general(left, right, dims, preferred_element_type=F32)


def gelu_pair(values):
    scale = 0.7978845608028654
    square = values * values
    bend = jnp.tanh(scale * values * (1.0 + 0.044715 * square))
    half = 0.5 * (1.0 + bend)
    slope = half + 0.5 * values * (1.0 - bend * bend) * scale * (1.0 + 3.0 * 0.044715 * square)
    return values * half, slope


def minus_expm1(v):
    series = jnp.full_like(v, 1.0 / 40320.0)
    for divisor in (5040.0, 720.0, 120.0, 24.0, 6.0, 2.0, 1.0):
        series = series * v + 1.0 / divisor
    return jnp.where(v > -0.35, -v * series, 1.0 - jnp.exp(v))


def when(condition, action):
    if condition is None:
        action()
    else:
        pl.when(condition)(action)


class Copy:
    def __init__(self, item, goes, comes):
        self.item, self.goes, self.comes = item, goes, comes

    def start(self):
        when(self.goes, lambda: self.item.start())

    def wait_send(self):
        when(self.goes, lambda: self.item.wait_send())

    def wait_recv(self):
        when(self.comes, lambda: self.item.wait_recv())


class Wire:
    def __init__(self, send, recv):
        self.send, self.recv, self.count, self.open = send, recv, 0, []

    def make(self, src, dst, peer, goes=None, comes=None):
        slot = self.count
        self.count += 1
        item = pltpu.make_async_remote_copy(
            src_ref=src,
            dst_ref=dst,
            send_sem=self.send.at[slot],
            recv_sem=self.recv.at[slot],
            device_id=peer,
            device_id_type=MESH,
        )
        copy = Copy(item, goes, comes)
        self.open.append(copy)
        return copy

    def copy(self, src, dst, peer, goes=None, comes=None):
        copy = self.make(src, dst, peer, goes, comes)
        copy.start()
        return copy

    def close(self):
        for item in self.open:
            item.wait_send()


class Chain:
    def __init__(self, wire, count, s, h):
        self.wire, self.count, self.s, self.h, self.zi = wire, count, s, h, s // 2
        self.up = (jnp.minimum(s + 2, 2 * count - 2 + s % 2), h)
        self.down = (jnp.maximum(s - 2, s % 2), h)

    def gather(self, view):
        zi, last = self.zi, self.count - 1

        def hop(step, way):
            index = zi - way * step
            held = jnp.logical_and(index >= 0, index <= last)
            goes = jnp.logical_and(held, zi < last if way > 0 else zi > 0)
            here = index - way
            comes = jnp.logical_and(here >= 0, here <= last)
            block = view(jnp.clip(index, 0, last))
            peer = self.up if way > 0 else self.down
            return self.wire.copy(block, block, peer, goes, comes), comes, jnp.clip(here, 0, last)

        flight = [hop(0, 1), hop(0, -1)]
        yield None, zi
        for step in range(last):
            for side, way in enumerate((1, -1)):
                item, comes, index = flight[side]
                item.wait_recv()
                if step + 1 < last:
                    flight[side] = hop(step + 1, way)
                yield comes, index

    def order(self):
        low, high, out = 0, self.count - 1, []
        while low <= high:
            out.append(high)
            if low < high:
                out.append(low)
            low, high = low + 1, high - 1
        return out

    def passes(self, d, src, up, down):
        zi, last = self.zi, self.count - 1
        first = second = None
        if d > 0:
            comes = jnp.logical_and(zi > 0, zi <= d)
            first = self.wire.make(src, up, self.up, zi < d, comes)
        if d < last:
            comes = jnp.logical_and(zi < last, zi >= d)
            second = self.wire.make(src, down, self.down, zi > d, comes)
        return first, second

    def between(self, d):
        zi, last = self.zi, self.count - 1
        return jnp.logical_and(zi > 0, zi < d), jnp.logical_and(zi < last, zi > d)

    def scatter(self, block, work, out, up, down, own):
        zi, last = self.zi, self.count - 1
        flight = {}

        def take(item, got, into):
            def action():
                item.item.wait_recv()
                into[...] = into[...] + got[...].astype(F32)
            return action

        for d in self.order():
            work[...] = block(d)
            ups, downs = self.passes(d, out.at[d], up.at[d], down.at[d])
            flight[d] = ups, downs
            below, above = self.between(d)
            if d > 1:
                when(below, take(ups, up.at[d], work))
            if d < last - 1:
                when(above, take(downs, down.at[d], work))

            def give(d=d):
                out[d] = work[...].astype(BF16)

            def keep():
                own[...] = work[...]

            when(zi != d, give)
            when(zi == d, keep)
            for item in flight[d]:
                if item is not None:
                    item.start()
            yield d
        for d in range(self.count):
            ups, downs = flight[d]
            if ups is not None:
                when(zi == d, take(ups, up.at[d], own))
            if downs is not None:
                when(zi == d, take(downs, down.at[d], own))


def drain(*steps):
    steps = list(steps)
    while steps:
        steps = [step for step in steps if next(step, step) is not step]


def advance(step, count=1):
    for _ in range(count):
        next(step, None)


def greet(peers):
    barrier = pltpu.get_barrier_semaphore()
    for peer in peers:
        pl.semaphore_signal(barrier, inc=1, device_id=peer, device_id_type=MESH)
    pl.semaphore_wait(barrier, len(peers))


def place():
    return lax.axis_index("seq"), lax.axis_index("head")


def at(ref, rows, row_count, lanes, lane_count):
    return ref.at[
        pl.ds(pl.multiple_of(rows, EDGE), row_count),
        pl.ds(pl.multiple_of(lanes, LANES), lane_count),
    ]


def sem(count):
    return pltpu.SemaphoreType.DMA((count,))


def call(body, name, cid, outs, scratch, args, spaces=None, limit=60, us=100):
    any_in = spaces or ()
    out_specs = [pl.BlockSpec(memory_space=ANY if kind == "any" else VM) for _, kind in outs]
    return pl.pallas_call(
        body,
        out_shape=[shape for shape, _ in outs],
        in_specs=[
            pl.BlockSpec(memory_space=ANY if i in any_in else VM) for i in range(len(args))
        ],
        out_specs=out_specs,
        scratch_shapes=scratch,
        compiler_params=pltpu.CompilerParams(
            collective_id=cid, has_side_effects=True, vmem_limit_bytes=limit << 20
        ),
        cost_estimate=pl.CostEstimate(
            flops=us * 10**6, bytes_accessed=us * 3 * 10**6, transcendentals=0
        ),
        name=name,
    )(*args)


def sds(shape, kind):
    return jax.ShapeDtypeStruct(shape, kind)


class Size:
    def __init__(self, mesh_sizes, tokens, x_weight, a_weight, gate_weight):
        self.S, self.H = mesh_sizes
        self.Z = self.S // 2
        self.R, self.D = tokens.shape
        self.T = self.S * self.R
        self.Ds, self.C = x_weight.shape
        self.HS = a_weight.shape[0]
        self.heads = self.H * self.C // self.HS
        self.F2 = gate_weight.shape[1]
        self.TB = self.T // self.H
        self.U = 2 * LANES
        self.NI = self.HS // self.H

    def fits(self):
        tiles = self.F2 // LANES
        return (
            self.S == 8
            and self.H == 4
            and self.Z == self.H
            and (2 * self.Ds) % LANES == 0
            and (2 * self.HS // self.S) % EDGE == 0
            and self.D == self.H * self.C
            and self.F2 % LANES == 0
            and 2 * (self.S - 1) < tiles <= 2 * self.S
            and self.T <= 1024
            and self.R % LANES == 0
            and self.C % LANES == 0
            and self.Ds % (2 * EDGE) == 0
            and (self.Ds // self.H) % EDGE == 0
            and self.NI % EDGE == 0
        )


def gate_weight_of(z, spread, mask, weight, k):
    rows = weight[pl.ds(pl.multiple_of(k * z.NI, EDGE), z.NI), :]
    return mm(spread[...], rows).astype(BF16) * mask[...]


def shifted(values, by, fill, row):
    count = values.shape[0]
    moved = pltpu.roll(values, by % count, 0)
    inside = row >= by if by > 0 else row < count + by
    return jnp.where(inside, moved, fill)


def scan_rows(prod, value, sign):
    row = lax.broadcasted_iota(jnp.int32, prod.shape, 0)
    by = 1
    while by < prod.shape[0]:
        value = prod * shifted(value, sign * by, 0.0, row) + value
        prod = prod * shifted(prod, sign * by, 1.0, row)
        by *= 2
    return prod, value


def decay_terms(a_pre, i_pre, rate, anchor):
    recall = jax.nn.sigmoid(a_pre)
    input_gate = jax.nn.sigmoid(i_pre)
    log_decay = -8.0 * recall * rate
    factor = jnp.exp(log_decay)
    one_minus = minus_expm1(2.0 * log_decay)
    root_value = jnp.sqrt(jnp.maximum(one_minus, SQUARE_FLOOR))
    root_scale = jnp.where(anchor, 1.0, root_value)
    return recall, input_gate, factor, one_minus, root_value, root_scale


def anchor_of(z, s, width):
    row = lax.broadcasted_iota(jnp.int32, (z.R, width), 0)
    return jnp.logical_and(row == 0, s == 0)


def vectors(conv_weight, conv_bias, a_bias, i_bias, decay):
    rows = [
        conv_weight.astype(F32),
        conv_bias.astype(F32)[None],
        a_bias.astype(F32)[None],
        i_bias.astype(F32)[None],
        jax.nn.softplus(decay)[None],
        jax.nn.sigmoid(decay)[None],
    ]
    stacked = jnp.concatenate(rows, axis=0)
    return jnp.pad(stacked, ((0, 16 - stacked.shape[0]), (0, 0)))


def head_maps(z):
    channel = jnp.arange(z.C)
    spread = (channel[:, None] // z.heads == jnp.arange(z.NI)[None, :]).astype(BF16)
    mask = (channel[:, None] % z.heads == channel[None, :] % z.heads).astype(BF16)
    return spread, mask


class Deal:
    def __init__(self, wire, z, s, h):
        self.wire, self.z, self.s, self.h = wire, z, s, h
        self.tiles = z.F2 // LANES
        self.sent = []

    def rows(self, owner):
        return pl.ds(pl.multiple_of(owner * self.z.Ds, EDGE), self.z.Ds)

    def post(self, src, dst, peer, part, goes, comes):
        wire = self.wire
        item = pltpu.make_async_remote_copy(
            src_ref=src,
            dst_ref=dst,
            send_sem=wire.send.at[wire.count],
            recv_sem=wire.recv.at[wire.count],
            device_id=(peer, self.h),
            device_id_type=MESH,
        )
        wire.count += 1
        self.sent.append((item, part, goes, comes))
        if part == 0:
            item.start()
        else:
            @pl.when(goes)
            def _():
                item.start()

    def out(self, src, dst, offsets):
        z = self.z
        for k in offsets:
            peer = self.s ^ k
            for part in range(2):
                tile = 2 * peer + part
                self.post(
                    at(src, 0, z.Ds, jnp.minimum(tile, self.tiles - 1) * LANES, LANES),
                    dst.at[self.rows(self.s), pl.ds(part * LANES, LANES)],
                    peer,
                    part,
                    tile < self.tiles,
                    2 * self.s + part < self.tiles,
                )

    def back(self, src, dst, offsets):
        z = self.z
        for k in offsets:
            peer = self.s ^ k
            for part in range(2):
                tile = 2 * self.s + part
                lane = jnp.minimum(tile, self.tiles - 1) * LANES
                self.post(
                    src.at[self.rows(peer), pl.ds(part * LANES, LANES)],
                    at(dst, 0, z.Ds, lane, LANES),
                    peer,
                    part,
                    tile < self.tiles,
                    2 * peer + part < self.tiles,
                )

    def back_own(self, src, dst):
        z, s = self.z, self.s
        at(dst, 0, z.Ds, 2 * s * LANES, LANES)[...] = src[self.rows(s), 0:LANES]

        @pl.when(2 * s + 1 < self.tiles)
        def _():
            lane = jnp.minimum(2 * s + 1, self.tiles - 1) * LANES
            at(dst, 0, z.Ds, lane, LANES)[...] = src[self.rows(s), LANES : 2 * LANES]

    def wait(self, sent=None):
        for item, part, goes, comes in self.sent if sent is None else sent:
            if part == 0:
                item.wait()
            else:
                @pl.when(goes)
                def _(item=item):
                    item.wait_send()

                @pl.when(comes)
                def _(item=item):
                    item.wait_recv()
        if sent is None:
            self.sent = []


class Own:
    def __init__(self, z, zeros, sems, s):
        self.z, self.zeros, self.sems, self.s = z, zeros, sems, s
        self.tiles = z.F2 // LANES
        self.count = 0

    def start(self, src, dst):
        z, s, sems = self.z, self.s, self.sems
        base = self.count * (z.S + 1)
        self.count += 1
        rows = pl.ds(pl.multiple_of(s * z.Ds, EDGE), z.Ds)
        first = pltpu.make_async_copy(
            at(src, 0, z.Ds, 2 * s * LANES, LANES), dst.at[rows, pl.ds(0, LANES)], sems.at[base]
        )
        second = pltpu.make_async_copy(
            at(src, 0, z.Ds, jnp.minimum(2 * s + 1, self.tiles - 1) * LANES, LANES),
            dst.at[rows, pl.ds(LANES, LANES)],
            sems.at[base + 1],
        )
        fill = []
        if self.zeros is not None:
            fill = [
                pltpu.make_async_copy(
                    self.zeros,
                    dst.at[pl.ds(z.Ds * r, z.Ds), pl.ds(LANES, LANES)],
                    sems.at[base + 1 + r],
                )
                for r in range(z.S)
            ]
        whole = 2 * s + 1 < self.tiles
        first.start()

        @pl.when(whole)
        def _():
            second.start()

        @pl.when(jnp.logical_not(whole))
        def _():
            for item in fill:
                item.start()
            if not fill:
                dst[:, LANES : 2 * LANES] = jnp.zeros((z.D, LANES), BF16)

        def wait():
            first.wait()

            @pl.when(whole)
            def _():
                second.wait()

            @pl.when(jnp.logical_not(whole))
            def _():
                for item in fill:
                    item.wait()

        return wait


def chain_scratch(z, rows, width):
    return [VM((rows, width), F32)] + [VM((z.Z, rows, width), BF16)] * 3 + [VM((rows, width), F32)]


def row_blocks(z, buf):
    return lambda index: buf.at[pl.ds(pl.multiple_of(index * z.R, EDGE), z.R), :]


def ahead_kernel(
    z, tok, gain, xw, yw, ow, vec, aw, iw, spread, mask, cot_in, gw, uw,
    xw2, yw2, ow2, tok2, fn2, rn, yb, pad, conv, a_o, i_o, st, entry_o, mix, res, cot, gc, uc,
    turned, x1, x2, x3, x4, x5, y1, y2, y3, y4, y5, sums, tot, part, got, zeros, edge, send, recv, own_sem,
):
    s, h = place()
    S, H, R, Ds, C, Z = z.S, z.H, z.R, z.Ds, z.C, z.Z
    DG = 2 * Ds
    Q = DG // H
    zi, xi = s // 2, s % 2
    after, before = lax.rem(s + 1, S), lax.rem(s + S - 1, S)
    greet(
        [(s ^ k, h) for k in range(1, S)]
        + [(s, h ^ j) for j in range(1, H)]
        + [(after, h), (before, h)]
    )
    wire = Wire(send, recv)
    g = Grid(s, h)
    chain = Chain(wire, Z, s, h)
    deal = Deal(wire, z, s, h)
    owned = Own(z, zeros, own_sem, s)
    half = pl.ds(pl.multiple_of(xi * Ds, EDGE), Ds)
    twins = [
        wire.copy(src, dst.at[half, :], (s ^ 1, h)) for src, dst in ((xw, xw2), (yw, yw2))
    ]
    turned[...] = tok[...].astype(F32).T.astype(BF16)
    quarter = pl.ds(pl.multiple_of(h * Q, EDGE), Q)
    my_lanes = pl.ds(pl.multiple_of(zi * R, LANES), R)

    def group(index):
        return pl.ds(pl.multiple_of(index * DG + h * Q, EDGE), Q)

    first = [
        wire.copy(turned.at[group(zi ^ kz), :], tok2.at[quarter, my_lanes], (s ^ (2 * kz), h))
        for kz in range(1, Z)
    ]
    column = turned[...].astype(F32)
    mean = jnp.sum(column * column, axis=0, keepdims=True) / z.D
    rn[zi] = jnp.broadcast_to(lax.rsqrt(mean + EPSILON), (8, R))
    for kz in range(1, Z):
        first.append(wire.copy(rn.at[zi], rn.at[zi], (s ^ (2 * kz), h)))
    tok2[quarter, my_lanes] = turned[group(zi), :]
    xw2[half, :] = xw[...]
    yw2[half, :] = yw[...]
    ow2[half, :] = ow[...]
    zeros[...] = jnp.zeros_like(zeros)
    pending = [owned.start(src, dst) for src, dst in ((gw, gc), (uw, uc))]
    W = z.D // H

    def corner(a, b, half):
        return halves(cot, a * R, R, b * W, W, half)

    corner(s, h, None)[...] = cot_in[:, pl.ds(pl.multiple_of(h * W, LANES), W)]
    cot_in_all = gather_all(wire, z, g, corner)
    for item in first:
        item.wait_recv()
    second = [
        wire.copy(tok2.at[quarter, :], tok2.at[quarter, :], (s, h ^ j)) for j in range(1, H)
    ]
    advance(cot_in_all, 1)
    deal.out(gw, gc, range(1, S))
    for item in second:
        item.wait_recv()
    for b in range(Z):
        cut = slice(b * R, b * R + R)
        fn2[:, cut] = (tok2[:, cut].astype(F32) * rn[b, 0:1, :] * gain[...]).astype(BF16)
    for item in twins:
        item.wait_recv()
    advance(cot_in_all, 2)
    twins = [wire.copy(ow, ow2.at[half, :], (s ^ 1, h))]

    def part_of(weight):
        return lambda d: mm(fn2[:, d * R : d * R + R].astype(F32).T.astype(BF16), weight[...])

    drain(
        chain.scatter(part_of(xw2), x1, x2, x3, x4, x5),
        chain.scatter(part_of(yw2), y1, y2, y3, y4, y5),
    )
    yb[...] = y5[...]
    x_low = x5[...].astype(BF16)
    edge[0] = x_low[R - EDGE : R, :]
    halo = wire.copy(edge.at[0], edge.at[1], (after, h))
    advance(cot_in_all, 3)
    deal.out(uw, uc, range(1, S))
    pad[pl.ds(EDGE, R), :] = x_low.astype(F32)
    halo.wait_recv()
    pad[pl.ds(0, EDGE), :] = jnp.where(s == 0, 0.0, edge[1].astype(F32))
    out = jnp.broadcast_to(vec[4:5, :], (R, C))
    for lag in range(CONV):
        out = out + vec[lag : lag + 1, :] * pad[pl.ds(EDGE - lag, R), :]
    conv[h] = out.astype(BF16)
    across = [wire.copy(conv.at[h], conv.at[h], (s, h ^ j)) for j in range(1, H)]
    advance(cot_in_all, 2)
    a_pre = jnp.broadcast_to(vec[5:6, :], (R, C))
    i_pre = jnp.broadcast_to(vec[6:7, :], (R, C))
    for j in range(H):
        if j:
            across[j - 1].wait_recv()
        k = h ^ j
        taken = conv[k]
        a_pre = a_pre + mm(taken, gate_weight_of(z, spread, mask, aw, k))
        i_pre = i_pre + mm(taken, gate_weight_of(z, spread, mask, iw, k))
    a_o[...] = a_pre
    i_o[...] = i_pre
    anchor = anchor_of(z, s, LANES)
    sums[s] = jnp.zeros((8, C), F32)
    for b in range(C // LANES):
        cut = pl.ds(b * LANES, LANES)
        recall, input_gate, factor, one_minus, root_value, root_scale = decay_terms(
            a_o[:, cut], i_o[:, cut], vec[7:8, cut], anchor
        )
        driven = conv[h, :, cut].astype(F32) * input_gate * root_scale
        prod, value = scan_rows(factor, driven, 1)
        st[:, cut] = value
        tot[:, cut] = prod
        sums[s, 0:1, cut] = prod[R - 1 : R, :]
        sums[s, 1:2, cut] = value[R - 1 : R, :]
    ends = [wire.copy(sums.at[s], sums.at[s], (s ^ k, h)) for k in range(1, S)]
    advance(cot_in_all, 2)
    for item in ends:
        item.wait_recv()
    entry = jnp.zeros((1, C), F32)
    for j in range(S - 1):
        entry = jnp.where(j < s, sums[j, 0:1, :] * entry + sums[j, 1:2, :], entry)
    entry_o[...] = jnp.broadcast_to(entry, (8, C))
    my_rows = pl.ds(pl.multiple_of(zi * R, EDGE), R)
    for b in range(C // LANES):
        cut = pl.ds(b * LANES, LANES)
        state = st[:, cut] + tot[:, cut] * entry_o[0:1, cut]
        st[:, cut] = state
        mix[my_rows, cut] = (state * gelu_pair(yb[:, cut])[0]).astype(BF16)
    arriving = chain.gather(row_blocks(z, mix))
    advance(arriving)
    advance(cot_in_all, 2)
    drain(arriving)
    twins[0].wait_recv()

    def out_part(head):
        rows = pl.ds(pl.multiple_of(head * R, EDGE), R)
        return mm(ow2[...], mix[rows, :], NT)

    heads = []
    for j in range(1, H):
        part[j] = out_part(h ^ j).astype(BF16)
        heads.append(wire.copy(part.at[j], got.at[j], (s, h ^ j)))
    total = out_part(h) + tok2[:, pl.ds(pl.multiple_of(h * R, LANES), R)].astype(F32)
    for j in range(1, H):
        heads[j - 1].wait_recv()
        total = total + got[j].astype(F32)
    res[...] = total
    drain(cot_in_all)
    for wait in pending:
        wait()
    deal.wait()
    wire.close()


def ahead(z, *args):
    S, H, R, D, Ds, C, Z = z.S, z.H, z.R, z.D, z.Ds, z.C, z.Z
    DG, TX = 2 * Ds, Z * R
    copies = 2 + 2 * (Z - 1) + (H - 1) + 1 + 4 * (Z - 1) + 1 + (H - 1) + (S - 1)
    copies += 2 * (Z - 1) + (H - 1) + 4 * (S - 1) + gather_copies(z)
    return call(
        functools.partial(ahead_kernel, z),
        "ahead",
        1,
        [
            (sds((DG, C), BF16), "vm"),
            (sds((DG, C), BF16), "vm"),
            (sds((DG, C), BF16), "vm"),
            (sds((DG, TX), BF16), "vm"),
            (sds((DG, TX), BF16), "vm"),
            (sds((Z, 8, R), F32), "vm"),
            (sds((R, C), F32), "vm"),
            (sds((EDGE + R, C), F32), "vm"),
            (sds((H, R, C), BF16), "vm"),
            (sds((R, C), F32), "vm"),
            (sds((R, C), F32), "vm"),
            (sds((R, C), F32), "vm"),
            (sds((8, C), F32), "vm"),
            (sds((TX, C), BF16), "vm"),
            (sds((DG, R), F32), "vm"),
            (sds((z.T, D), BF16), "vm"),
            (sds((D, z.U), BF16), "any"),
            (sds((D, z.U), BF16), "any"),
        ],
        [
            VM((D, R), BF16),
            *chain_scratch(z, R, C),
            *chain_scratch(z, R, C),
            VM((S, 8, C), F32),
            VM((R, C), F32),
            VM((H, DG, R), BF16),
            VM((H, DG, R), BF16),
            VM((Ds, LANES), BF16),
            VM((2, EDGE, C), BF16),
            sem(copies),
            sem(copies),
            sem(2 * (S + 1)),
        ],
        args,
        (11, 12),
    )


class Grid:
    def __init__(self, s, h):
        self.s, self.h = s, h
        self.x, self.y, self.core = (s ^ 1, h), (s, h ^ 2), (s, h ^ 1)

    def z(self, kz):
        return (self.s ^ (2 * kz), self.h)


def gather_all(wire, z, g, region):
    s, h, xi = g.s, g.h, g.s % 2
    chain = Chain(wire, z.Z, s, h)
    arrivals = chain.gather(lambda index: region(2 * index + xi, h, None))
    blocks, near, far, core = [], {}, {}, []

    def send(a, b, half, peer, held):
        return wire.copy(region(a, b, half), region(a, b, half), peer, held, held)

    def one(i):
        held, index = next(arrivals)
        a = 2 * index + xi
        blocks.append((held, a))
        near[0, i] = send(a, h, 0, g.x, held)
        near[1, i] = send(a, h, 1, g.y, held)
        far[0, i, 0] = send(a, h, 0, g.y, held)
        far[1, i, 0] = send(a, h, 1, g.x, held)
        core.append(send(a, h, None, g.core, held))

    def two(i):
        held, a = blocks[i]
        near[0, i].wait_recv()
        far[0, i, 1] = send(a ^ 1, h, 0, g.y, held)
        core.append(send(a ^ 1, h, 0, g.core, held))
        near[1, i].wait_recv()
        far[1, i, 1] = send(a, h ^ 2, 1, g.x, held)
        core.append(send(a, h ^ 2, 1, g.core, held))

    def three(i):
        held, a = blocks[i]
        far[0, i, 0].wait_recv()
        core.append(send(a, h ^ 2, 0, g.core, held))
        far[1, i, 0].wait_recv()
        core.append(send(a ^ 1, h, 1, g.core, held))

    def four(i):
        held, a = blocks[i]
        far[0, i, 1].wait_recv()
        core.append(send(a ^ 1, h ^ 2, 0, g.core, held))
        far[1, i, 1].wait_recv()
        core.append(send(a ^ 1, h ^ 2, 1, g.core, held))

    count = 2 * z.Z - 1
    stages = (one, two, three, four)
    for turn in range(count + 6):
        for lag, stage in enumerate(stages):
            if 0 <= turn - 2 * lag < count:
                stage(turn - 2 * lag)
        yield turn
    for item in core:
        item.wait_recv()


def gather_copies(z):
    return 2 * (z.Z - 1) + 13 * (2 * z.Z - 1)


class SumAll:
    def __init__(self, wire, z, g, region, bufs):
        self.wire, self.zz, self.g, self.region = wire, z, g, region
        self.from_core, self.hop1, self.hop2, self.up, self.down, self.own = bufs
        self.chain = Chain(wire, z.Z, g.s, g.h)
        self.flight = {}

    @staticmethod
    def copies(z):
        return z.Z * (4 + 4 + 2) + 4 * (z.Z - 1)

    @staticmethod
    def scratch(z, rows, lanes):
        half = rows // 2
        return [
            VM((z.Z, 4, rows, lanes), BF16),
            VM((z.Z, 4, half, lanes), BF16),
            VM((z.Z, 2, half, lanes), BF16),
            VM((z.Z, 2, half, lanes), BF16),
            VM((z.Z, 2, half, lanes), BF16),
            VM((2, half, lanes), F32),
        ]

    def put(self, a, b, half, dst, peer):
        return self.wire.copy(self.region(a, b, half), dst, peer)

    def add(self, a, b, half, got):
        spot = self.region(a, b, half)
        spot[...] = (spot[...].astype(F32) + got[...].astype(F32)).astype(BF16)

    def core(self, d):
        g = self.g
        for i in range(4):
            a, b = (2 * d + g.s % 2) ^ (i // 2), g.h ^ 1 ^ (2 * (i % 2))
            self.flight["core", d, i] = self.put(a, b, None, self.from_core.at[d, i], g.core)

    def first(self, d):
        g = self.g
        rows = self.hop1.shape[2]
        for i in (1, 3, 2, 0):
            self.flight["core", d, i].wait_recv()
            a, b = (2 * d + g.s % 2) ^ (i // 2), g.h ^ (2 * (i % 2))
            for half in range(2):
                self.add(a, b, half, self.from_core.at[d, i, pl.ds(half * rows, rows), :])
            if i % 2:
                key = i // 2
                self.flight["one", d, key] = self.put(a, b, 0, self.hop1.at[d, key], g.y)
            if i // 2:
                key = 2 + i % 2
                self.flight["one", d, key] = self.put(a, b, 1, self.hop1.at[d, key], g.x)

    def second(self, d):
        g = self.g
        a = 2 * d + g.s % 2
        for key in (1, 0):
            self.flight["one", d, key].wait_recv()
            self.add(a ^ key, g.h, 0, self.hop1.at[d, key])
        self.flight["two", d, 0] = self.put(a ^ 1, g.h, 0, self.hop2.at[d, 0], g.x)
        for key in (3, 2):
            self.flight["one", d, key].wait_recv()
            self.add(a, g.h ^ (2 * (key - 2)), 1, self.hop1.at[d, key])
        self.flight["two", d, 1] = self.put(a, g.h ^ 2, 1, self.hop2.at[d, 1], g.y)

    def third(self, d):
        g, chain = self.g, self.chain
        a, last = 2 * d + g.s % 2, self.zz.Z - 1
        below, above = chain.between(d)
        for half in range(2):
            self.flight["two", d, half].wait_recv()
            self.add(a, g.h, half, self.hop2.at[d, half])
            ups, downs = chain.passes(
                d, self.region(a, g.h, half), self.up.at[d, half], self.down.at[d, half]
            )
            self.flight["z", d, half] = ups, downs
            if d > 1:
                when(below, self.taken(ups, a, half, self.up.at[d, half]))
            if d < last - 1:
                when(above, self.taken(downs, a, half, self.down.at[d, half]))
            for item in (ups, downs):
                if item is not None:
                    item.start()

    def taken(self, item, a, half, got):
        def action():
            item.item.wait_recv()
            self.add(a, self.g.h, half, got)
        return action

    def finish(self, half):
        g, zi = self.g, self.g.s // 2
        own = self.own.at[half]
        own[...] = self.region(g.s, g.h, half)[...].astype(F32)

        def add(item, got):
            def action():
                item.item.wait_recv()
                own[...] = own[...] + got[...].astype(F32)
            return action

        for d in range(self.zz.Z):
            ups, downs = self.flight["z", d, half]
            if ups is not None:
                when(zi == d, add(ups, self.up.at[d, half]))
            if downs is not None:
                when(zi == d, add(downs, self.down.at[d, half]))
        return own[...]

    def run(self, produce):
        order = self.chain.order()
        steps = [lambda d: (produce(d), self.core(d)), self.first, self.second, self.third]
        count = len(order)
        for turn in range(count + len(steps) - 1):
            for stage in range(len(steps)):
                if 0 <= turn - stage < count:
                    steps[stage](order[turn - stage])
                    yield turn


def halves(ref, rows, row_count, lanes, lane_count, half):
    if half is not None:
        row_count //= 2
        rows = rows + half * row_count
    return at(ref, rows, row_count, lanes, lane_count)


def region_of(z, ref):
    return lambda a, b, half: halves(
        ref, a // 2 * 2 * z.Ds, 2 * z.Ds, (2 * b + a % 2) * z.R, z.R, half
    )


def feed_kernel(
    z, res, cot, gw, uw, dw_in, gain,
    gate_o, uwg_o, dwg_o, gsum_o, bg_o, hid, dw,
    xt, gwt, uwt, dwt, gwg, hg, gg, ug, gs, us, rs, part, back_g,
    c1, c2, c3, c4, c5, c6, stat, send, recv, own_sem,
):
    s, h = place()
    g = Grid(s, h)
    S, H, R, D, T, Ds = z.S, z.H, z.R, z.D, z.T, z.Ds
    DG = 2 * Ds
    zi, xi = s // 2, s % 2
    greet([(s ^ k, h) for k in range(1, S)] + [(s, h ^ j) for j in range(1, H)])
    wire = Wire(send, recv)
    deal = Deal(wire, z, s, h)
    tile = 256
    region_of(z, xt)(s, h, None)[...] = res[...].astype(BF16)
    spread = gather_all(wire, z, g, region_of(z, xt))
    advance(spread)
    deal.out(dw_in, dw, range(1, S))
    dealt_own = Own(z, None, own_sem, s).start(dw_in, dw)

    def turn(src, dst, scaled):
        for n in range(D // tile):
            cut = slice(n * tile, n * tile + tile)
            piece = src[cut, :].astype(F32)
            dst[:, cut] = (piece * gain[cut, :] if scaled else piece).T.astype(BF16)

    advance(spread)
    turn(gw, gwt, True)
    advance(spread, 2)
    turn(uw, uwt, True)
    drain(spread)
    dealt_own()
    deal.wait()
    turn(dw, dwt, False)
    for n in range(T // tile):
        cut = slice(n * tile, n * tile + tile)
        hg[:, cut] = mm(dwt[...], cot[cut, :], NT)
        square = jnp.zeros((1, tile), F32)
        for b in range(D // tile):
            piece = xt[b * tile : b * tile + tile, cut].astype(F32)
            square = square + jnp.sum(piece * piece, axis=0, keepdims=True)
        scale = lax.rsqrt(square / D + EPSILON)
        rs[:, cut] = jnp.broadcast_to(scale, (8, tile))
        gate = mm(gwt[...], xt[:, cut]) * scale
        up = mm(uwt[...], xt[:, cut]) * scale
        act, slope = gelu_pair(gate)
        hid[:, cut] = (act * up).astype(BF16)
        back = hg[:, cut]
        gate_grad = back * up * slope
        up_grad = back * act
        gg[:, cut] = gate_grad.astype(BF16)
        ug[:, cut] = up_grad.astype(BF16)
        gs[:, cut] = (gate_grad * scale).astype(BF16)
        us[:, cut] = (up_grad * scale).astype(BF16)
    second = SumAll(wire, z, g, region_of(z, part), (c1, c2, c3, c4, c5, c6))

    def produce(d):
        rows = pl.ds(d * DG, DG)
        part[rows, :] = (mm(gw[rows, :], gg[...]) + mm(uw[rows, :], ug[...])).astype(BF16)

    summing = second.run(produce)
    advance(summing, 3)
    for n in range(D // tile):
        cut = slice(n * tile, n * tile + tile)
        gwg[cut, :] = (mm(xt[cut, :], gs[...], NT) * gain[cut, :]).astype(BF16)
    deal.back(gwg, back_g, range(1, S))
    deal.back_own(gwg, back_g)
    drain(summing)
    for n in range(D // tile):
        cut = slice(n * tile, n * tile + tile)
        uwg_o[cut, :] = (mm(xt[cut, :], us[...], NT) * gain[cut, :]).astype(BF16)
        dwg_o[cut, :] = mm(hid[...], cot[:, cut]).T.astype(BF16)
    second_grad = jnp.concatenate([second.finish(0), second.finish(1)], axis=0)
    mine = pl.ds(pl.multiple_of((2 * h + xi) * R, LANES), R)
    group = pl.ds(pl.multiple_of(zi * DG, LANES), DG)
    scale = rs[0:1, mine]
    residual = res[...]
    gsum_o[...] = second_grad * residual * scale
    weighted = gain[group, :] * second_grad
    stat[zi] = jnp.broadcast_to(jnp.sum(weighted * residual, axis=0, keepdims=True), (8, R))
    ends = [wire.copy(stat.at[zi], stat.at[zi], g.z(kz)) for kz in range(1, z.Z)]
    direct = cot[mine, group].astype(F32).T + scale * weighted
    for item in ends:
        item.wait_recv()
    mean = jnp.sum(stat[:, 0:1, :], axis=0) / D
    grad = direct - residual * (scale * scale * scale * mean)
    lanes = pl.ds(pl.multiple_of(h * R, LANES), R)
    bg_o[:, lanes] = grad.astype(BF16)
    heads = [wire.copy(bg_o.at[:, lanes], bg_o.at[:, lanes], (s, h ^ j)) for j in range(1, H)]
    deal.wait()
    gate_o[...] = back_g[...].astype(F32)
    for item in heads:
        item.wait_recv()
    wire.close()


def feed(z, *args):
    S, H, R, D, T, U, Ds = z.S, z.H, z.R, z.D, z.T, z.U, z.Ds
    DG = 2 * Ds
    copies = gather_copies(z) + SumAll.copies(z) + (z.Z - 1) + (H - 1) + 4 * (S - 1)
    return call(
        functools.partial(feed_kernel, z),
        "feed",
        2,
        [
            (sds((Ds, z.F2), F32), "vm"),
            (sds((D, U), BF16), "vm"),
            (sds((D, U), BF16), "vm"),
            (sds((DG, R), F32), "vm"),
            (sds((DG, z.Z * R), BF16), "vm"),
            (sds((U, T), BF16), "vm"),
            (sds((D, U), BF16), "vm"),
        ],
        [VM((D, T), BF16)]
        + [VM((U, D), BF16)] * 3
        + [VM((D, U), BF16), VM((U, T), F32)]
        + [VM((U, T), BF16)] * 4
        + [VM((8, T), F32), VM((D, T), BF16), VM((Ds, z.F2), BF16)]
        + SumAll.scratch(z, DG, R)
        + [VM((z.Z, 8, R), F32), sem(copies), sem(copies), sem(2)],
        args,
        (4,),
    )


def exact(left, right, dims):
    return lax.dot_general(
        left, right, dims, precision=lax.Precision.HIGHEST, preferred_element_type=F32
    )


def back_kernel(
    z, bg, ow2, mix, yb, vec, a_pre, i_pre, st, entry, conv, pad, aw, iw, spread, mask,
    xw2, yw2, fn2, tok2, rn, gain, msum, res, hid, dw, uwg, dwg,
    mixed_o, owg_o, xwg_o, ywg_o, tg_o, gains_o, awg_o, iwg_o, vec_o, up_o, down_o,
    g1, g2, g3, g4, own, adj, tot, ag, ig, sums, late, cgr, cgs, ext, gath, part, got, stat, stat2, full,
    tgq, prod, gains, gains2, small, smallx, s1, s2, s3, s4, s5, smallg, vecs, twin_s, twin_r,
    back_u, back_d, mpart, m1, m2, m3, m4, m5, m6, send, recv,
):
    s, h = place()
    g = Grid(s, h)
    S, H, R, D, Ds, C, Z, T = z.S, z.H, z.R, z.D, z.Ds, z.C, z.Z, z.T
    DG, W = 2 * Ds, D // H
    Q = DG // H
    zi, xi = s // 2, s % 2
    after, before = lax.rem(s + 1, S), lax.rem(s + S - 1, S)
    greet(
        [(s ^ k, h) for k in range(1, S)]
        + [(s, h ^ j) for j in range(1, H)]
        + [(after, h), (before, h)]
    )
    wire = Wire(send, recv)
    chain = Chain(wire, Z, s, h)
    deal = Deal(wire, z, s, h)
    my_rows = pl.ds(pl.multiple_of(zi * R, EDGE), R)
    half = pl.ds(pl.multiple_of(xi * Ds, EDGE), Ds)
    other = pl.ds(pl.multiple_of((1 - xi) * Ds, EDGE), Ds)

    def corner(a, b, part_of):
        return halves(mpart, b * W, W, a * R, R, part_of)

    mixed = SumAll(wire, z, g, corner, (m1, m2, m3, m4, m5, m6))

    def produce_mixed(d):
        cut = pl.ds(d * 2 * R, 2 * R)
        mpart[:, cut] = mm(dw[...], hid[:, cut]).astype(BF16)

        @pl.when(h == d)
        def _():
            spot = region_of(z, mpart)(s, h, None)
            spot[...] = (spot[...].astype(F32) + res[...]).astype(BF16)

    mixing = mixed.run(produce_mixed)

    def block(d):
        return mm(bg[:, d * R : d * R + R].astype(F32).T.astype(BF16), ow2[...])

    summing = chain.scatter(block, g1, g2, g3, g4, own)
    for _ in range(Z):
        advance(summing)
        advance(mixing)
    drain(summing)
    deal.back(uwg, back_u, range(1, S))
    row = lax.broadcasted_iota(jnp.int32, (R, LANES), 0)
    anchor = anchor_of(z, s, LANES)
    sums[s] = jnp.zeros((8, C), F32)
    for b in range(C // LANES):
        cut = pl.ds(b * LANES, LANES)
        grad = own[:, cut]
        gate, slope = gelu_pair(yb[:, cut])
        gath[my_rows, pl.ds(C + b * LANES, LANES)] = (grad * st[:, cut] * slope).astype(BF16)
        factor = jnp.exp(-8.0 * jax.nn.sigmoid(a_pre[:, cut]) * vec[7:8, cut])
        ahead = shifted(factor, -1, 1.0, row)
        prods, value = scan_rows(ahead, grad * gate, -1)
        tot[:, cut] = prods
        adj[:, cut] = value
        sums[s, 0:1, cut] = factor[0:1, :] * prods[0:1, :]
        sums[s, 1:2, cut] = factor[0:1, :] * value[0:1, :]
    ends = [wire.copy(sums.at[s], sums.at[s], (s ^ k, h)) for k in range(1, S)]
    outer = mm(bg[...], mix[...])
    prod[:, 0:C] = outer
    twin_s[0] = prod[other, 0:C].astype(BF16)
    twins = [wire.copy(twin_s.at[0], twin_r.at[0], g.x)]
    owg_o[...] = prod[half, 0:C]
    advance(mixing, 2)
    for item in ends:
        item.wait_recv()
    deal.back(dwg, back_d, range(1, S))
    carry = jnp.zeros((1, C), F32)
    for j in range(S - 1, 0, -1):
        carry = jnp.where(j > s, sums[j, 0:1, :] * carry + sums[j, 1:2, :], carry)
    vec_o[...] = jnp.zeros_like(vec_o)
    late[...] = jnp.broadcast_to(carry, (8, C))
    for b in range(C // LANES):
        cut = pl.ds(b * LANES, LANES)
        adjoint = adj[:, cut] + tot[:, cut] * late[0:1, cut]
        rate = vec[7:8, cut]
        recall, input_gate, factor, one_minus, root_value, root_scale = decay_terms(
            a_pre[:, cut], i_pre[:, cut], rate, anchor
        )
        taken = conv[h, :, cut].astype(F32)
        state = st[:, cut]
        earlier = jnp.where(row == 0, entry[0:1, cut], shifted(state, 1, 0.0, row))
        live = jnp.logical_and(one_minus > SQUARE_FLOOR, jnp.logical_not(anchor))
        scale_grad = adjoint * taken * input_gate
        log_grad = adjoint * earlier * factor - jnp.where(
            live, scale_grad * factor * factor / root_value, 0.0
        )
        a_grad = (log_grad * (-8.0 * rate) * recall * (1.0 - recall)).astype(BF16)
        i_grad = (scale_grad * root_scale * (1.0 - input_gate)).astype(BF16)
        ag[:, cut] = a_grad
        ig[:, cut] = i_grad
        decay_sum = jnp.sum(log_grad * (-8.0 * recall), axis=0, keepdims=True)
        vec_o[5:6, cut] = jnp.sum(a_grad.astype(F32), axis=0, keepdims=True)
        vec_o[6:7, cut] = jnp.sum(i_grad.astype(F32), axis=0, keepdims=True)
        vec_o[7:8, cut] = decay_sum * vec[8:9, cut]
        ext[pl.ds(0, R), cut] = adjoint * input_gate * root_scale

    def gates_back(k):
        return mm(ag[...], gate_weight_of(z, spread, mask, aw, k), NT) + mm(
            ig[...], gate_weight_of(z, spread, mask, iw, k), NT
        )

    across = []
    for j in range(1, H):
        cgs[j] = gates_back(h ^ j).astype(BF16)
        across.append(wire.copy(cgs.at[j], cgr.at[j], (s, h ^ j)))
    conv_grad = ext[pl.ds(0, R), :] + gates_back(h)
    for k in range(H):
        turn = conv[k].astype(F32).T.astype(BF16)
        for spot, grad in ((0, ag), (z.HS, ig)):
            dense = mm(turn, grad[...]).astype(BF16) * mask[...]
            small[pl.ds(spot + k * z.NI, z.NI), :] = mm(spread[...], dense, TN).astype(BF16)
    advance(mixing, 2)
    for j in range(1, H):
        across[j - 1].wait_recv()
        conv_grad = conv_grad + cgr[j].astype(F32)
    ext[pl.ds(0, R), :] = conv_grad
    halo = wire.copy(ext.at[pl.ds(0, 8), :], ext.at[pl.ds(R, 8), :], (before, h))
    for lag in range(CONV):
        vec_o[lag : lag + 1, :] = jnp.sum(
            conv_grad * pad[pl.ds(EDGE - lag, R), :], axis=0, keepdims=True
        )
    vec_o[4:5, :] = jnp.sum(conv_grad, axis=0, keepdims=True)
    vecs[s] = vec_o[...]
    halo.wait_recv()
    ext[pl.ds(R, 8), :] = jnp.where(s == S - 1, 0.0, ext[pl.ds(R, 8), :])
    grad = jnp.zeros((R, C), F32)
    for lag in range(CONV):
        grad = grad + vec[lag : lag + 1, :] * ext[pl.ds(lag, R), :]
    gath[my_rows, pl.ds(0, C)] = grad.astype(BF16)
    rows_in = chain.gather(row_blocks(z, gath))
    advance(rows_in)
    pair = grad.astype(BF16).astype(F32) * pad[pl.ds(EDGE, R), :] + gath[
        my_rows, C : 2 * C
    ].astype(F32) * yb[...]
    stat[h] = exact(jnp.ones((8, C), F32), pair, NT)
    stats = [wire.copy(stat.at[h], stat.at[h], (s, h ^ j)) for j in range(1, H)]

    lesser = [wire.copy(vecs.at[s], vecs.at[s], (s ^ k, h)) for k in range(1, S)]
    eighth = small.shape[0] // S

    def share(x_index, z_index, count):
        start = (x_index * Z + z_index) * eighth
        return pl.ds(pl.multiple_of(start, EDGE), count * eighth)

    def sum_small():
        mine = share(xi, 0, Z)
        item = wire.copy(small.at[share(1 - xi, 0, Z), :], smallx, g.x)
        yield
        item.wait_recv()
        smallx[...] = (smallx[...].astype(F32) + small[mine, :].astype(F32)).astype(BF16)
        yield from chain.scatter(
            lambda d: smallx[pl.ds(d * eighth, eighth), :].astype(F32), s1, s2, s3, s4, s5
        )
        smallg[share(xi, zi, 1), :] = s5[...].astype(BF16)
        yield from chain.gather(lambda index: smallg.at[share(xi, index, 1), :])
        item = wire.copy(smallg.at[mine, :], smallg.at[mine, :], g.x)
        yield
        item.wait_recv()

    smaller = sum_small()
    advance(smaller)
    advance(mixing, 4)
    for item in stats:
        item.wait_recv()
    stat2[zi] = stat[0] + stat[1] + stat[2] + stat[3]
    stats = [wire.copy(stat2.at[zi], stat2.at[zi], g.z(kz)) for kz in range(1, Z)]
    advance(smaller, 2)
    drain(rows_in)

    def first_part():
        return mm(xw2[...], gath[:, 0:C], NT) + mm(yw2[...], gath[:, C : 2 * C], NT)

    prod[:, 0 : Z * R] = first_part()
    heads = []
    for j in range(1, H):
        rows = pl.ds(pl.multiple_of((h ^ j) * Q, EDGE), Q)
        part[j] = prod[rows, 0 : Z * R].astype(BF16)
        heads.append(wire.copy(part.at[j], got.at[j], (s, h ^ j)))
    quarter = pl.ds(pl.multiple_of(h * Q, EDGE), Q)
    total = prod[quarter, 0 : Z * R]
    for index, out in ((0, xwg_o), (1, ywg_o)):
        prod2 = mm(fn2[...], gath[:, index * C : index * C + C])
        prod[:, 0:C] = prod2
        twin_s[1 + index] = prod[other, 0:C].astype(BF16)
        twins.append(wire.copy(twin_s.at[1 + index], twin_r.at[1 + index], g.x))
        out[...] = prod[half, 0:C]
    for j in range(1, H):
        heads[j - 1].wait_recv()
        total = total + got[j].astype(F32)
    for item in stats:
        item.wait_recv()
    token = tok2[quarter, :].astype(F32)
    norm = jnp.concatenate([rn[b, 0:1, :] for b in range(Z)], axis=1)
    mean = jnp.concatenate([stat2[b, 0:1, :] for b in range(Z)], axis=1) / (norm * D)
    group = pl.ds(pl.multiple_of(zi * DG + h * Q, EDGE), Q)
    weighted = gain[group, :] * total
    grad = bg[quarter, :].astype(F32) + norm * weighted - token * (norm * norm * norm * mean)
    tgq[...] = grad.astype(BF16)

    def spot(z_index, head):
        return full.at[pl.ds(pl.multiple_of(z_index * DG + head * Q, EDGE), Q), :]

    outs = [
        wire.copy(
            tgq.at[:, pl.ds(pl.multiple_of((zi ^ kz) * R, LANES), R)], spot(zi, h), g.z(kz)
        )
        for kz in range(1, Z)
    ]
    spot(zi, h)[...] = tgq[:, pl.ds(pl.multiple_of(zi * R, LANES), R)]
    prod[...] = jnp.zeros_like(prod)
    prod[quarter, 0 : Z * R] = total * token * norm
    ones = jnp.ones((8, Z * R), F32)
    picked = lax.broadcasted_iota(jnp.int32, (8, DG), 0)
    gains[h] = jnp.where(
        picked == 0, exact(jnp.ones((8, R), F32), msum[...], NT), exact(ones, prod[:, 0 : Z * R], NT)
    )
    tally = [wire.copy(gains.at[h], gains.at[h], (s, h ^ j)) for j in range(1, H)]
    finals = []
    for kz in range(Z):
        if kz:
            outs[kz - 1].wait_recv()
        for j in range(1, H):
            finals.append(wire.copy(spot(zi ^ kz, h), spot(zi ^ kz, h), (s, h ^ j)))
    for item in tally:
        item.wait_recv()
    gains2[s] = gains[0] + gains[1] + gains[2] + gains[3]
    tally = [wire.copy(gains2.at[s], gains2.at[s], (s ^ k, h)) for k in range(1, S)]
    advance(smaller, 4)
    drain(mixing)
    advance(smaller, 3)
    for part_of in range(2):
        mixed_o[:, pl.ds(part_of * W // 2, W // 2)] = mixed.finish(part_of).T.astype(BF16)
    for item in lesser:
        item.wait_recv()
    vec_o[...] = jnp.sum(vecs[...], axis=0)
    for index, out in ((0, owg_o), (1, xwg_o), (2, ywg_o)):
        twins[index].wait_recv()
        out[...] = out[...] + twin_r[index].astype(F32)
    deal.back_own(uwg, back_u)
    deal.back_own(dwg, back_d)
    pending, deal.sent = deal.sent, []
    count = len(pending) // 2
    for index, (dst, out) in enumerate(((back_u, up_o), (back_d, down_o))):
        deal.wait(pending[index * count : index * count + count])
        out[...] = dst[...].astype(F32)
    drain(smaller)
    awg_o[...] = smallg[pl.ds(0, z.HS), :].astype(F32)
    iwg_o[...] = smallg[pl.ds(z.HS, z.HS), :].astype(F32)
    for item in tally:
        item.wait_recv()
    for b in range(Z):
        gains_o[b] = gains2[2 * b] + gains2[2 * b + 1]
    for item in finals:
        item.wait_recv()
    tg_o[...] = full[...].astype(F32).T
    wire.close()


def back(z, *args):
    S, H, R, D, Ds, C, Z, T = z.S, z.H, z.R, z.D, z.Ds, z.C, z.Z, z.T
    DG, W = 2 * Ds, D // H
    TX, Q = Z * R, DG // H
    copies = (
        4 * (Z - 1) + (S - 1) + 3 + (H - 1) + 1 + 2 * (Z - 1) + (H - 1) + (Z - 1) + (S - 1)
        + 2 + 4 * (Z - 1) + 4 * (S - 1) + (H - 1) + (Z - 1) + (H - 1) + Z * (H - 1) + (S - 1)
        + SumAll.copies(z)
    )
    small = 2 * z.HS
    return call(
        functools.partial(back_kernel, z),
        "back",
        3,
        [
            (sds((R, W), BF16), "vm"),
            (sds((Ds, C), F32), "vm"),
            (sds((Ds, C), F32), "vm"),
            (sds((Ds, C), F32), "vm"),
            (sds((R, D), F32), "vm"),
            (sds((Z, 8, DG), F32), "vm"),
            (sds((z.HS, C), F32), "vm"),
            (sds((z.HS, C), F32), "vm"),
            (sds((8, C), F32), "vm"),
            (sds((Ds, z.F2), F32), "vm"),
            (sds((Ds, z.F2), F32), "vm"),
        ],
        [
            *chain_scratch(z, R, C),
            VM((R, C), F32),
            VM((R, C), F32),
            VM((R, C), BF16),
            VM((R, C), BF16),
            VM((S, 8, C), F32),
            VM((8, C), F32),
            VM((H, R, C), BF16),
            VM((H, R, C), BF16),
            VM((R + 8, C), F32),
            VM((TX, 2 * C), BF16),
            VM((H, Q, TX), BF16),
            VM((H, Q, TX), BF16),
            VM((H, 8, R), F32),
            VM((Z, 8, R), F32),
            VM((D, R), BF16),
            VM((Q, TX), BF16),
            VM((DG, max(C, TX)), F32),
            VM((H, 8, DG), F32),
            VM((S, 8, DG), F32),
            VM((small, C), BF16),
            VM((small // 2, C), BF16),
            *chain_scratch(z, small // S, C),
            VM((small, C), BF16),
            VM((S, 8, C), F32),
            VM((3, Ds, C), BF16),
            VM((3, Ds, C), BF16),
            VM((Ds, z.F2), BF16),
            VM((Ds, z.F2), BF16),
            VM((D, T), BF16),
        ]
        + SumAll.scratch(z, W, R)
        + [sem(copies), sem(copies)],
        args,
    )


def dealt(
    z,
    tokens,
    norm_gain,
    x_weight,
    y_weight,
    conv_weight,
    conv_bias,
    a_weight,
    a_bias,
    i_weight,
    i_bias,
    decay,
    out_weight,
    mlp_gain,
    gate_weight,
    up_weight,
    down_weight,
    cotangent,
):
    s = lax.axis_index("seq")
    first_gain = norm_gain.astype(F32)[:, None]
    second_gain = mlp_gain.astype(F32)[:, None]
    gain_s = lax.dynamic_slice(first_gain, (s // 2 * 2 * z.Ds, 0), (2 * z.Ds, 1))
    vec = vectors(conv_weight, conv_bias, a_bias, i_bias, decay)
    spread, mask = head_maps(z)
    xw2, yw2, ow2, tok2, fn2, rn, yb, pad, conv, a_pre, i_pre, st, entry, mix, res, cot, gc, uc = (
        ahead(
            z, tokens, gain_s, x_weight, y_weight, out_weight, vec, a_weight, i_weight, spread,
            mask, cotangent, gate_weight, up_weight,
        )
    )
    gate_g, uwg, dwg, msum, bg, hid, dc = feed(z, res, cot, gc, uc, down_weight, second_gain)
    mixed, owg, xwg, ywg, tg, gains, awg, iwg, vec_sum, up_g, down_g = back(
        z, bg, ow2, mix, yb, vec, a_pre, i_pre, st, entry, conv, pad, a_weight, i_weight, spread,
        mask, xw2, yw2, fn2, tok2, rn, first_gain, msum, res, hid, dc, uwg, dwg,
    )
    return (
        mixed,
        tg,
        gains[:, 1, :].reshape(z.D),
        xwg,
        ywg,
        vec_sum[0:CONV],
        vec_sum[4],
        awg,
        vec_sum[5],
        iwg,
        vec_sum[6],
        vec_sum[7],
        owg,
        gains[:, 0, :].reshape(z.D),
        gate_g,
        up_g,
        down_g,
    )


def from_behind(x, axis, by):
    size = lax.axis_size(axis)
    pairs = [(i, i + by) for i in range(size) if 0 <= i + by < size]
    return lax.ppermute(x, axis, pairs)


def rms_norm(values, gain):
    return values * lax.rsqrt(jnp.mean(values * values, axis=-1, keepdims=True) + EPSILON) * gain


def linear_pair(earlier, later):
    return (later[0] * earlier[0], later[0] * earlier[1] + later[1])


def gelu_back(values, grad):
    return jax.vjp(jax.nn.gelu, values)[1](grad)[0]


def gathered_weights(
    tokens,
    norm_gain,
    x_weight,
    y_weight,
    conv_weight,
    conv_bias,
    a_weight,
    a_bias,
    i_weight,
    i_bias,
    decay,
    out_weight,
    mlp_gain,
    gate_weight,
    up_weight,
    down_weight,
    cotangent,
):
    row_count = tokens.shape[0]
    model_width = tokens.shape[1]
    lane_count = x_weight.shape[1]
    head_size = a_weight.shape[0]
    head_index = lax.axis_index("head")
    seq_index = lax.axis_index("seq")
    head_devices = lax.axis_size("head")
    float_type = jnp.float32
    half_type = jnp.bfloat16
    gathered = (
        lax.all_gather(x_weight, "seq", axis=0, tiled=True),
        lax.all_gather(y_weight, "seq", axis=0, tiled=True),
        lax.all_gather(out_weight, "seq", axis=0, tiled=True),
        lax.all_gather(gate_weight, "seq", axis=0, tiled=True),
        lax.all_gather(up_weight, "seq", axis=0, tiled=True),
        lax.all_gather(down_weight, "seq", axis=0, tiled=True),
    )
    x_full, y_full, out_full, gate_full, up_full, down_full = gathered
    tokens_wide = tokens.astype(float_type)
    first_gain = norm_gain.astype(float_type)
    first_norm = rms_norm(tokens_wide, first_gain)
    first_low = first_norm.astype(half_type)
    x_branch = jnp.dot(first_low, x_full, preferred_element_type=float_type).astype(half_type)
    y_branch = jnp.dot(first_low, y_full, preferred_element_type=float_type)
    y_gate = jax.nn.gelu(y_branch)
    left_edge = from_behind(x_branch[row_count - (CONV - 1) :], "seq", 1)
    padded = jnp.concatenate([left_edge, x_branch], axis=0).astype(float_type)
    conv_taps = conv_weight.astype(float_type)
    conv_out = conv_bias.astype(float_type) + sum(
        (
            conv_taps[lag_index] * padded[CONV - 1 - lag_index : CONV - 1 - lag_index + row_count]
            for lag_index in range(CONV)
        )
    )
    conv_low = conv_out.astype(half_type)
    conv_value = conv_low.astype(float_type)
    all_channels = lax.all_gather(conv_low, "head", axis=1, tiled=True)
    head_count = all_channels.shape[1] // head_size
    group_count = lane_count // head_count
    heads_view = all_channels.reshape(row_count, head_size, head_count)

    def block_gate(weight, bias):
        product = jnp.einsum(
            "tih,ijh->tjh",
            heads_view,
            weight.reshape(head_size, group_count, head_count),
            preferred_element_type=float_type,
        )
        return product.reshape(row_count, lane_count) + bias.astype(float_type)

    a_pre = block_gate(a_weight, a_bias)
    i_pre = block_gate(i_weight, i_bias)
    recall = jax.nn.sigmoid(a_pre)
    input_gate = jax.nn.sigmoid(i_pre)
    decay_rate = jax.nn.softplus(decay)
    log_decay = -8.0 * recall * decay_rate
    factor = jnp.exp(log_decay)
    double_decay = jnp.exp(2.0 * log_decay)
    one_minus = -jnp.expm1(2.0 * log_decay)
    root_value = jnp.sqrt(jnp.maximum(one_minus, SQUARE_FLOOR))
    position = seq_index * row_count + jnp.arange(row_count)
    anchor = (position == 0)[:, None]
    root_scale = jnp.where(anchor, 1.0, root_value)
    root_live = jnp.logical_and(one_minus > SQUARE_FLOOR, jnp.logical_not(anchor))
    driven = conv_value * input_gate * root_scale
    local_prod, local_state = lax.associative_scan(linear_pair, (factor, driven))

    def relay_step(turn_number, carried):
        return from_behind(local_prod[-1] * carried + local_state[-1], "seq", 1)

    state_entry = lax.fori_loop(
        0, lax.axis_size("seq") - 1, relay_step, jnp.zeros_like(local_state[-1])
    )
    state_all = local_state + local_prod * state_entry
    mixed_in = (state_all * y_gate).astype(half_type)
    branch_part = jnp.einsum("tc,dc->td", mixed_in, out_full, preferred_element_type=float_type)
    branch = lax.psum(branch_part, "head")
    residual = tokens_wide + branch
    second_gain = mlp_gain.astype(float_type)
    second_low = rms_norm(residual, second_gain).astype(half_type)
    gate_pre = jnp.dot(second_low, gate_full, preferred_element_type=float_type)
    up_pre = jnp.dot(second_low, up_full, preferred_element_type=float_type)
    gate_act = jax.nn.gelu(gate_pre)
    hidden = (gate_act * up_pre).astype(half_type)
    mlp_part = jnp.einsum("tf,df->td", hidden, down_full, preferred_element_type=float_type)
    own_columns = lax.psum_scatter(mlp_part, "head", scatter_dimension=1, tiled=True)
    column_count = model_width // head_devices
    mixed = (
        lax.dynamic_slice_in_dim(residual, head_index * column_count, column_count, 1) + own_columns
    ).astype(half_type)
    regathered = (
        lax.all_gather(x_weight, "seq", axis=0, tiled=True),
        lax.all_gather(y_weight, "seq", axis=0, tiled=True),
        lax.all_gather(out_weight, "seq", axis=0, tiled=True),
        lax.all_gather(gate_weight, "seq", axis=0, tiled=True),
        lax.all_gather(up_weight, "seq", axis=0, tiled=True),
        lax.all_gather(down_weight, "seq", axis=0, tiled=True),
    )
    x_full, y_full, out_full, gate_full, up_full, down_full = regathered
    hidden_grad = jnp.dot(cotangent, down_full, preferred_element_type=float_type)
    gate_grad = gelu_back(gate_pre, hidden_grad * up_pre).astype(half_type)
    up_grad = (hidden_grad * gate_act).astype(half_type)
    second_part = jnp.einsum(
        "tf,df->td", gate_grad, gate_full, preferred_element_type=float_type
    ) + jnp.einsum("tf,df->td", up_grad, up_full, preferred_element_type=float_type)
    second_grad = lax.psum(second_part, "head")
    resid_back, mlp_gain_term = jax.vjp(rms_norm, residual, second_gain)[1](second_grad)
    resid_grad = cotangent.astype(float_type) + resid_back
    branch_grad = resid_grad.astype(half_type)
    mixed_grad = jnp.dot(branch_grad, out_full, preferred_element_type=float_type)
    state_grad = mixed_grad * y_gate
    y_grad = gelu_back(y_branch, mixed_grad * state_all).astype(half_type)
    next_factor = jnp.concatenate([factor[1:], jnp.ones_like(factor[:1])], axis=0)
    back_prod, back_adjoint = lax.associative_scan(
        linear_pair, (next_factor[::-1], state_grad[::-1])
    )
    back_prod = back_prod[::-1]
    back_adjoint = back_adjoint[::-1]
    tail_prod = factor[0] * back_prod[0]
    tail_value = factor[0] * back_adjoint[0]

    def relay_back(turn_number, carried):
        return from_behind(tail_value + tail_prod * carried, "seq", -1)

    exit_carry = lax.fori_loop(0, lax.axis_size("seq") - 1, relay_back, jnp.zeros_like(tail_value))
    adjoint = back_adjoint + back_prod * exit_carry
    prev_state = jnp.concatenate([state_entry[None], state_all[:-1]], axis=0)
    scale_grad = adjoint * conv_value * input_gate
    log_grad = adjoint * prev_state * factor + jnp.where(
        root_live, -scale_grad * double_decay / root_value, 0.0
    )
    a_grad = (log_grad * (-8.0 * decay_rate) * recall * (1.0 - recall)).astype(half_type)
    i_grad = (adjoint * conv_value * root_scale * input_gate * (1.0 - input_gate)).astype(half_type)
    decay_term = jnp.sum(log_grad * (-8.0 * recall), axis=0) * jax.nn.sigmoid(decay)
    a_bias_term = jnp.sum(a_grad.astype(float_type), axis=0)
    i_bias_term = jnp.sum(i_grad.astype(float_type), axis=0)

    def gate_back(grad, weight):
        grad_view = grad.reshape(row_count, group_count, head_count)
        weight_term = jnp.einsum(
            "tih,tjh->ijh", heads_view, grad_view, preferred_element_type=float_type
        ).reshape(head_size, lane_count)
        input_term = jnp.einsum(
            "tjh,ijh->tih",
            grad_view,
            weight.reshape(head_size, group_count, head_count),
            preferred_element_type=float_type,
        )
        return (weight_term, input_term)

    a_wgrad, a_input = gate_back(a_grad, a_weight)
    i_wgrad, i_input = gate_back(i_grad, i_weight)
    gate_input_grad = lax.psum_scatter(
        (a_input + i_input).reshape(row_count, head_size * head_count),
        "head",
        scatter_dimension=1,
        tiled=True,
    )
    conv_grad = gate_input_grad + adjoint * input_gate * root_scale
    right_edge = from_behind(conv_grad[: CONV - 1], "seq", -1)
    extended_grad = jnp.concatenate([conv_grad, right_edge], axis=0)
    x_branch_grad = sum(
        (
            conv_taps[lag_index] * extended_grad[lag_index : lag_index + row_count]
            for lag_index in range(CONV)
        )
    ).astype(half_type)
    conv_wgrad = jnp.stack(
        [
            jnp.sum(
                conv_grad * padded[CONV - 1 - lag_index : CONV - 1 - lag_index + row_count], axis=0
            )
            for lag_index in range(CONV)
        ],
        axis=0,
    )
    conv_bgrad = jnp.sum(conv_grad, axis=0)
    first_part = jnp.einsum(
        "tc,dc->td", x_branch_grad, x_full, preferred_element_type=float_type
    ) + jnp.einsum("tc,dc->td", y_grad, y_full, preferred_element_type=float_type)
    first_grad = lax.psum(first_part, "head")
    tokens_back, norm_gain_term = jax.vjp(rms_norm, tokens_wide, first_gain)[1](first_grad)
    tokens_grad = resid_grad + tokens_back
    pairings = (
        (first_low, x_branch_grad),
        (first_low, y_grad),
        (branch_grad, mixed_in),
        (second_low, gate_grad),
        (second_low, up_grad),
        (cotangent, hidden),
    )
    products = tuple(
        (
            jnp.einsum("td,tc->dc", left, right, preferred_element_type=float_type)
            for left, right in pairings
        )
    )
    weight_sums = lax.psum_scatter(products, "seq", scatter_dimension=0, tiled=True)
    small_sums = lax.psum(
        (
            norm_gain_term,
            conv_wgrad,
            conv_bgrad,
            a_wgrad,
            a_bias_term,
            i_wgrad,
            i_bias_term,
            decay_term,
            mlp_gain_term,
        ),
        "seq",
    )
    return (
        mixed,
        tokens_grad,
        small_sums[0],
        weight_sums[0],
        weight_sums[1],
        small_sums[1],
        small_sums[2],
        small_sums[3],
        small_sums[4],
        small_sums[5],
        small_sums[6],
        small_sums[7],
        weight_sums[2],
        small_sums[8],
        weight_sums[3],
        weight_sums[4],
        weight_sums[5],
    )


def solution(mesh):
    sizes = mesh.shape["seq"], mesh.shape["head"]

    def body(*args):
        z = Size(sizes, args[0], args[2], args[6], args[13])
        return dealt(z, *args) if z.fits() else gathered_weights(*args)

    return jax.shard_map(
        body,
        mesh=mesh,
        in_specs=(
            P("seq", None),
            P(),
            P("seq", "head"),
            P("seq", "head"),
            P(None, "head"),
            P("head"),
            P(None, "head"),
            P("head"),
            P(None, "head"),
            P("head"),
            P("head"),
            P("seq", "head"),
            P(),
            P("seq", "head"),
            P("seq", "head"),
            P("seq", "head"),
            P("seq", None),
        ),
        out_specs=(
            P("seq", "head"),
            P("seq", None),
            P(),
            P("seq", "head"),
            P("seq", "head"),
            P(None, "head"),
            P("head"),
            P(None, "head"),
            P("head"),
            P(None, "head"),
            P("head"),
            P("head"),
            P("seq", "head"),
            P(),
            P("seq", "head"),
            P("seq", "head"),
            P("seq", "head"),
        ),
        check_vma=False,
    )
```

```python
import functools

import jax
import jax.numpy as jnp
from jax import lax
from jax.experimental import pallas as pl
from jax.experimental.pallas import tpu as pltpu
from jax.sharding import PartitionSpec as P

CONV = 4
EPSILON = 1e-06
SQUARE_FLOOR = 2.5e-07
MESH = pl.DeviceIdType.MESH
F32 = jnp.float32
BF16 = jnp.bfloat16
LANES = 128
EDGE = 16
VM = pltpu.VMEM
ANY = pl.ANY
NN = (((1,), (0,)), ((), ()))
NT = (((1,), (1,)), ((), ()))
TN = (((0,), (0,)), ((), ()))


def mm(left, right, dims=NN):
    return lax.dot_general(left, right, dims, preferred_element_type=F32)


def gelu_pair(values):
    scale = 0.7978845608028654
    square = values * values
    bend = jnp.tanh(scale * values * (1.0 + 0.044715 * square))
    half = 0.5 * (1.0 + bend)
    slope = half + 0.5 * values * (1.0 - bend * bend) * scale * (1.0 + 3.0 * 0.044715 * square)
    return values * half, slope


def minus_expm1(v):
    series = jnp.full_like(v, 1.0 / 40320.0)
    for divisor in (5040.0, 720.0, 120.0, 24.0, 6.0, 2.0, 1.0):
        series = series * v + 1.0 / divisor
    return jnp.where(v > -0.35, -v * series, 1.0 - jnp.exp(v))


def when(condition, action):
    if condition is None:
        action()
    else:
        pl.when(condition)(action)


class Copy:
    def __init__(self, item, goes, comes):
        self.item, self.goes, self.comes = item, goes, comes

    def start(self):
        when(self.goes, lambda: self.item.start())

    def wait_send(self):
        when(self.goes, lambda: self.item.wait_send())

    def wait_recv(self):
        when(self.comes, lambda: self.item.wait_recv())

    def arrived(self):
        self.item.wait_recv()


class Wire:
    def __init__(self, send, recv):
        self.send, self.recv, self.count, self.open = send, recv, 0, []

    def make(self, src, dst, peer, goes=None, comes=None):
        slot = self.count
        self.count += 1
        item = pltpu.make_async_remote_copy(
            src_ref=src,
            dst_ref=dst,
            send_sem=self.send.at[slot],
            recv_sem=self.recv.at[slot],
            device_id=peer,
            device_id_type=MESH,
        )
        copy = Copy(item, goes, comes)
        self.open.append(copy)
        return copy

    def copy(self, src, dst, peer, goes=None, comes=None):
        copy = self.make(src, dst, peer, goes, comes)
        copy.start()
        return copy

    def close(self):
        for item in self.open:
            item.wait_send()
        assert self.count <= self.send.shape[0], self.count


class Chain:
    def __init__(self, wire, count, s, h):
        self.wire, self.count, self.s, self.h, self.zi = wire, count, s, h, s // 2
        self.up = (jnp.minimum(s + 2, 2 * count - 2 + s % 2), h)
        self.down = (jnp.maximum(s - 2, s % 2), h)

    def gather(self, view):
        zi, last = self.zi, self.count - 1

        def hop(step, way):
            index = zi - way * step
            held = jnp.logical_and(index >= 0, index <= last)
            goes = jnp.logical_and(held, zi < last if way > 0 else zi > 0)
            here = index - way
            comes = jnp.logical_and(here >= 0, here <= last)
            block = view(jnp.clip(index, 0, last))
            peer = self.up if way > 0 else self.down
            return self.wire.copy(block, block, peer, goes, comes), comes, jnp.clip(here, 0, last)

        flight = [hop(0, 1), hop(0, -1)]
        yield None, zi
        for step in range(last):
            for side, way in enumerate((1, -1)):
                item, comes, index = flight[side]
                item.wait_recv()
                if step + 1 < last:
                    flight[side] = hop(step + 1, way)
                yield comes, index

    def order(self):
        count = self.count
        low = list(reversed(range(count // 2, count))) + list(range(count // 2))
        near = self.zi < count // 2
        return [jnp.where(near, d, count - 1 - d) for d in low]

    def passes(self, d, src, up, down):
        zi, last, wire = self.zi, self.count - 1, self.wire
        base = wire.count
        wire.count = base + d
        first = wire.make(src, up, self.up, zi < d, jnp.logical_and(zi > 0, zi <= d))
        wire.count = base + self.count + d
        second = wire.make(src, down, self.down, zi > d, jnp.logical_and(zi < last, zi >= d))
        wire.count = base
        return first, second

    def between(self, d):
        zi, last = self.zi, self.count - 1
        return jnp.logical_and(zi > 0, zi < d), jnp.logical_and(zi < last, zi > d)

    def ends(self, d):
        zi, last = self.zi, self.count - 1
        return jnp.logical_and(zi == d, zi > 0), jnp.logical_and(zi == d, zi < last)

    def scatter(self, block, work, out, up, down, own):
        zi = self.zi
        flight = []
        base = self.wire.count
        self.wire.count += 2 * self.count

        def take(item, got, into):
            def action():
                item.arrived()
                into[...] = into[...] + got[...].astype(F32)
            return action

        for d in self.order():
            work[...] = block(d)
            kept, self.wire.count = self.wire.count, base
            ups, downs = self.passes(d, out.at[d], up.at[d], down.at[d])
            self.wire.count = kept
            flight.append((d, ups, downs))
            below, above = self.between(d)
            when(below, take(ups, up.at[d], work))
            when(above, take(downs, down.at[d], work))

            def give(d=d):
                out[d] = work[...].astype(BF16)

            def keep():
                own[...] = work[...]

            when(zi != d, give)
            when(zi == d, keep)
            ups.start()
            downs.start()
            yield d
        for d, ups, downs in flight:
            below, above = self.ends(d)
            when(below, take(ups, up.at[d], own))
            when(above, take(downs, down.at[d], own))


class HeadGather:
    def __init__(self, wire, s, h, view):
        self.wire, self.s, self.h, self.view = wire, s, h, view
        self.items = {1: self.send(0, 1), 2: self.send(0, 2)}

    def send(self, j, to):
        block = self.view(self.h ^ j)
        return self.wire.copy(block, block, (self.s, self.h ^ to))

    def wait(self, j):
        if j == 2:
            self.items[2].wait_recv()
            self.items[3] = self.send(2, 1)
        else:
            self.items[j].wait_recv()

    def wait_all(self):
        for j in (2, 1, 3):
            self.wait(j)


def head_scatter(wire, s, h, block, out, got):
    core, other = (s, h ^ 1), (s, h ^ 2)
    flight = {}
    for j in (3, 1):
        out[j] = block(j).astype(BF16)
        flight[j] = wire.copy(out.at[j], got.at[j], core)
    part = block(2)
    flight[3].wait_recv()
    out[2] = (part + got[3].astype(F32)).astype(BF16)
    flight[2] = wire.copy(out.at[2], got.at[2], other)
    total = block(0)
    flight[1].wait_recv()
    total = total + got[1].astype(F32)

    def finish():
        flight[2].wait_recv()
        return total + got[2].astype(F32)

    return finish


def drain(*steps):
    steps = list(steps)
    while steps:
        steps = [step for step in steps if next(step, step) is not step]


def advance(step, count=1):
    for _ in range(count):
        next(step, None)


def greet(peers):
    barrier = pltpu.get_barrier_semaphore()
    for peer in peers:
        pl.semaphore_signal(barrier, inc=1, device_id=peer, device_id_type=MESH)
    pl.semaphore_wait(barrier, len(peers))


def place():
    return lax.axis_index("seq"), lax.axis_index("head")


def at(ref, rows, row_count, lanes, lane_count):
    return ref.at[
        pl.ds(pl.multiple_of(rows, EDGE), row_count),
        pl.ds(pl.multiple_of(lanes, LANES), lane_count),
    ]


def sem(count):
    return pltpu.SemaphoreType.DMA((count,))


def call(body, name, cid, outs, scratch, args, spaces=(), limit=62, us=150):
    return pl.pallas_call(
        body,
        out_shape=outs,
        in_specs=[
            pl.BlockSpec(memory_space=ANY if i in spaces else VM) for i in range(len(args))
        ],
        out_specs=[pl.BlockSpec(memory_space=VM) for _ in outs],
        scratch_shapes=scratch,
        compiler_params=pltpu.CompilerParams(
            collective_id=cid, has_side_effects=True, vmem_limit_bytes=limit << 20
        ),
        cost_estimate=pl.CostEstimate(
            flops=us * 10**6, bytes_accessed=us * 3 * 10**6, transcendentals=0
        ),
        name=name,
    )(*args)


def sds(shape, kind):
    return jax.ShapeDtypeStruct(shape, kind)


class Size:
    def __init__(self, mesh_sizes, tokens, x_weight, a_weight, gate_weight):
        self.S, self.H = mesh_sizes
        self.Z = self.S // 2
        self.R, self.D = tokens.shape
        self.T = self.S * self.R
        self.Ds, self.C = x_weight.shape
        self.HS = a_weight.shape[0]
        self.heads = self.H * self.C // self.HS
        self.F2 = gate_weight.shape[1]
        self.TB = self.T // self.H
        self.U = 2 * LANES
        self.NI = self.HS // self.H

    def fits(self):
        tiles = self.F2 // LANES
        return (
            self.S == 8
            and self.H == 4
            and self.Z == self.H
            and (2 * self.Ds) % LANES == 0
            and (2 * self.HS // self.S) % EDGE == 0
            and self.D == self.H * self.C
            and self.F2 % LANES == 0
            and 2 * (self.S - 1) < tiles <= 2 * self.S
            and self.T <= 1024
            and self.R % LANES == 0
            and self.C % LANES == 0
            and self.Ds % (2 * EDGE) == 0
            and (self.Ds // self.H) % EDGE == 0
            and self.NI % EDGE == 0
        )


def gate_weight_of(z, spread, mask, weight, k):
    rows = weight[pl.ds(pl.multiple_of(k * z.NI, EDGE), z.NI), :]
    return mm(spread[...], rows).astype(BF16) * mask[...]


def shifted(values, by, fill, row):
    count = values.shape[0]
    moved = pltpu.roll(values, by % count, 0)
    inside = row >= by if by > 0 else row < count + by
    return jnp.where(inside, moved, fill)


def scan_rows(prod, value, sign):
    row = lax.broadcasted_iota(jnp.int32, prod.shape, 0)
    by = 1
    while by < prod.shape[0]:
        value = prod * shifted(value, sign * by, 0.0, row) + value
        prod = prod * shifted(prod, sign * by, 1.0, row)
        by *= 2
    return prod, value


def decay_terms(a_pre, i_pre, rate, anchor):
    recall = jax.nn.sigmoid(a_pre)
    input_gate = jax.nn.sigmoid(i_pre)
    log_decay = -8.0 * recall * rate
    factor = jnp.exp(log_decay)
    one_minus = minus_expm1(2.0 * log_decay)
    root_value = jnp.sqrt(jnp.maximum(one_minus, SQUARE_FLOOR))
    root_scale = jnp.where(anchor, 1.0, root_value)
    return recall, input_gate, factor, one_minus, root_value, root_scale


def anchor_of(z, s, width):
    row = lax.broadcasted_iota(jnp.int32, (z.R, width), 0)
    return jnp.logical_and(row == 0, s == 0)


def vectors(conv_weight, conv_bias, a_bias, i_bias, decay):
    rows = [
        conv_weight.astype(F32),
        conv_bias.astype(F32)[None],
        a_bias.astype(F32)[None],
        i_bias.astype(F32)[None],
        jax.nn.softplus(decay)[None],
        jax.nn.sigmoid(decay)[None],
    ]
    stacked = jnp.concatenate(rows, axis=0)
    return jnp.pad(stacked, ((0, 16 - stacked.shape[0]), (0, 0)))


def head_maps(z):
    channel = jnp.arange(z.C)
    spread = (channel[:, None] // z.heads == jnp.arange(z.NI)[None, :]).astype(BF16)
    mask = (channel[:, None] % z.heads == channel[None, :] % z.heads).astype(BF16)
    return spread, mask


class Deal:
    def __init__(self, wire, z, s, h):
        self.wire, self.z, self.s, self.h = wire, z, s, h
        self.tiles = z.F2 // LANES
        self.sent = []

    def rows(self, owner):
        return pl.ds(pl.multiple_of(owner * self.z.Ds, EDGE), self.z.Ds)

    def post(self, src, dst, peer, part, goes, comes):
        wire = self.wire
        item = pltpu.make_async_remote_copy(
            src_ref=src,
            dst_ref=dst,
            send_sem=wire.send.at[wire.count],
            recv_sem=wire.recv.at[wire.count],
            device_id=(peer, self.h),
            device_id_type=MESH,
        )
        wire.count += 1
        self.sent.append((item, part, goes, comes))
        if part == 0:
            item.start()
        else:
            @pl.when(goes)
            def _():
                item.start()

    def out(self, src, dst, offsets):
        z = self.z
        for k in offsets:
            peer = self.s ^ k
            for part in range(2):
                tile = 2 * peer + part
                self.post(
                    at(src, 0, z.Ds, jnp.minimum(tile, self.tiles - 1) * LANES, LANES),
                    dst.at[self.rows(self.s), pl.ds(part * LANES, LANES)],
                    peer,
                    part,
                    tile < self.tiles,
                    2 * self.s + part < self.tiles,
                )

    def back(self, src, dst, offsets):
        z = self.z
        for k in offsets:
            peer = self.s ^ k
            for part in range(2):
                tile = 2 * self.s + part
                lane = jnp.minimum(tile, self.tiles - 1) * LANES
                self.post(
                    src.at[self.rows(peer), pl.ds(part * LANES, LANES)],
                    at(dst, 0, z.Ds, lane, LANES),
                    peer,
                    part,
                    tile < self.tiles,
                    2 * peer + part < self.tiles,
                )

    def steps(self, how, pairs):
        for src, dst in pairs:
            for offsets in ((4, 2), (5, 3), (6, 1), (7,)):
                how(src, dst, offsets)
                yield

    def back_own(self, src, dst):
        z, s = self.z, self.s
        at(dst, 0, z.Ds, 2 * s * LANES, LANES)[...] = src[self.rows(s), 0:LANES]

        @pl.when(2 * s + 1 < self.tiles)
        def _():
            lane = jnp.minimum(2 * s + 1, self.tiles - 1) * LANES
            at(dst, 0, z.Ds, lane, LANES)[...] = src[self.rows(s), LANES : 2 * LANES]

    def wait(self, sent=None):
        for item, part, goes, comes in self.sent if sent is None else sent:
            if part == 0:
                item.wait()
            else:
                @pl.when(goes)
                def _(item=item):
                    item.wait_send()

                @pl.when(comes)
                def _(item=item):
                    item.wait_recv()
        if sent is None:
            self.sent = []


def own_block(z, src, dst, sems, s):
    tiles = z.F2 // LANES
    rows = pl.ds(pl.multiple_of(s * z.Ds, EDGE), z.Ds)
    first = pltpu.make_async_copy(
        at(src, 0, z.Ds, 2 * s * LANES, LANES), dst.at[rows, pl.ds(0, LANES)], sems.at[0]
    )
    second = pltpu.make_async_copy(
        at(src, 0, z.Ds, jnp.minimum(2 * s + 1, tiles - 1) * LANES, LANES),
        dst.at[rows, pl.ds(LANES, LANES)],
        sems.at[1],
    )
    whole = 2 * s + 1 < tiles
    first.start()

    @pl.when(whole)
    def _():
        second.start()

    @pl.when(jnp.logical_not(whole))
    def _():
        dst[:, LANES : 2 * LANES] = jnp.zeros((z.D, LANES), BF16)

    def wait():
        first.wait()

        @pl.when(whole)
        def _():
            second.wait()

    return wait


def chain_scratch(z, rows, width):
    return [VM((rows, width), F32)] + [VM((z.Z, rows, width), BF16)] * 3 + [VM((rows, width), F32)]


def row_blocks(z, buf):
    return lambda index: buf.at[pl.ds(pl.multiple_of(index * z.R, EDGE), z.R), :]


class Grid:
    def __init__(self, s, h):
        self.s, self.h = s, h
        self.x, self.y, self.core = (s ^ 1, h), (s, h ^ 2), (s, h ^ 1)

    def z(self, kz):
        return (self.s ^ (2 * kz), self.h)


def gather_all(wire, z, g, region):
    s, h, xi = g.s, g.h, g.s % 2
    chain = Chain(wire, z.Z, s, h)
    arrivals = chain.gather(lambda index: region(2 * index + xi, h, None))
    mine = next(arrivals)
    yield None
    blocks, near, far, core = [], {}, {}, []

    def send(a, b, half, peer, held):
        return wire.copy(region(a, b, half), region(a, b, half), peer, held, held)

    def one(i):
        held, index = next(arrivals) if i else mine
        a = 2 * index + xi
        blocks.append((held, a))
        near[0, i] = send(a, h, 0, g.x, held)
        near[1, i] = send(a, h, 1, g.y, held)
        far[0, i, 0] = send(a, h, 0, g.y, held)
        far[1, i, 0] = send(a, h, 1, g.x, held)
        core.append(send(a, h, None, g.core, held))

    def two(i):
        held, a = blocks[i]
        near[0, i].wait_recv()
        far[0, i, 1] = send(a ^ 1, h, 0, g.y, held)
        core.append(send(a ^ 1, h, 0, g.core, held))
        near[1, i].wait_recv()
        far[1, i, 1] = send(a, h ^ 2, 1, g.x, held)
        core.append(send(a, h ^ 2, 1, g.core, held))

    def three(i):
        held, a = blocks[i]
        far[0, i, 0].wait_recv()
        core.append(send(a, h ^ 2, 0, g.core, held))
        far[1, i, 0].wait_recv()
        core.append(send(a ^ 1, h, 1, g.core, held))

    def four(i):
        held, a = blocks[i]
        far[0, i, 1].wait_recv()
        core.append(send(a ^ 1, h ^ 2, 0, g.core, held))
        far[1, i, 1].wait_recv()
        core.append(send(a ^ 1, h ^ 2, 1, g.core, held))

    count = 2 * z.Z - 1
    stages = (one, two, three, four)
    for turn in range(count + 6):
        for lag, stage in enumerate(stages):
            if 0 <= turn - 2 * lag < count:
                stage(turn - 2 * lag)
        yield turn
    for item in core:
        item.wait_recv()


def gather_copies(z):
    return 2 * (z.Z - 1) + 13 * (2 * z.Z - 1)


class SumAll:
    def __init__(self, wire, z, g, region, bufs):
        self.wire, self.zz, self.g, self.region = wire, z, g, region
        self.from_core, self.hop1, self.hop2, self.up, self.down, self.own = bufs
        self.chain = Chain(wire, z.Z, g.s, g.h)
        self.flight = {}
        self.base = wire.count
        wire.count += self.copies(z)

    @staticmethod
    def copies(z):
        return z.Z * (4 + 4 + 2) + 4 * z.Z

    @staticmethod
    def scratch(z, rows, lanes):
        half = rows // 2
        return [
            VM((z.Z, 4, rows, lanes), BF16),
            VM((z.Z, 4, half, lanes), BF16),
            VM((z.Z, 2, half, lanes), BF16),
            VM((z.Z, 2, half, lanes), BF16),
            VM((z.Z, 2, half, lanes), BF16),
            VM((2, half, lanes), F32),
        ]

    def put(self, a, b, half, dst, peer, slot):
        kept, self.wire.count = self.wire.count, self.base + slot
        item = self.wire.copy(self.region(a, b, half), dst, peer)
        self.wire.count = kept
        return item

    def add(self, a, b, half, got):
        spot = self.region(a, b, half)
        spot[...] = (spot[...].astype(F32) + got[...].astype(F32)).astype(BF16)

    def core(self, i, d):
        g = self.g
        for k in range(4):
            a, b = (2 * d + g.s % 2) ^ (k // 2), g.h ^ 1 ^ (2 * (k % 2))
            self.flight["core", i, k] = self.put(
                a, b, None, self.from_core.at[d, k], g.core, 10 * i + k
            )

    def first(self, i, d):
        g = self.g
        rows = self.hop1.shape[2]
        for k in (1, 3, 2, 0):
            self.flight["core", i, k].wait_recv()
            a, b = (2 * d + g.s % 2) ^ (k // 2), g.h ^ (2 * (k % 2))
            for half in range(2):
                self.add(a, b, half, self.from_core.at[d, k, pl.ds(half * rows, rows), :])
            if k % 2:
                key = k // 2
                self.flight["one", i, key] = self.put(
                    a, b, 0, self.hop1.at[d, key], g.y, 10 * i + 4 + key
                )
            if k // 2:
                key = 2 + k % 2
                self.flight["one", i, key] = self.put(
                    a, b, 1, self.hop1.at[d, key], g.x, 10 * i + 4 + key
                )

    def second(self, i, d):
        g = self.g
        a = 2 * d + g.s % 2
        for key in (1, 0):
            self.flight["one", i, key].wait_recv()
            self.add(a ^ key, g.h, 0, self.hop1.at[d, key])
        self.flight["two", i, 0] = self.put(
            a ^ 1, g.h, 0, self.hop2.at[d, 0], g.x, 10 * i + 8
        )
        for key in (3, 2):
            self.flight["one", i, key].wait_recv()
            self.add(a, g.h ^ (2 * (key - 2)), 1, self.hop1.at[d, key])
        self.flight["two", i, 1] = self.put(
            a, g.h ^ 2, 1, self.hop2.at[d, 1], g.y, 10 * i + 9
        )

    def third(self, i, d):
        g, chain = self.g, self.chain
        a, count = 2 * d + g.s % 2, self.zz.Z
        below, above = chain.between(d)
        for half in range(2):
            self.flight["two", i, half].wait_recv()
            self.add(a, g.h, half, self.hop2.at[d, half])
            kept = self.wire.count
            self.wire.count = self.base + 10 * count + 2 * count * half
            ups, downs = chain.passes(
                d, self.region(a, g.h, half), self.up.at[d, half], self.down.at[d, half]
            )
            self.wire.count = kept
            self.flight["z", i, half] = d, ups, downs
            when(below, self.taken(ups, a, half, self.up.at[d, half]))
            when(above, self.taken(downs, a, half, self.down.at[d, half]))
            ups.start()
            downs.start()

    def taken(self, item, a, half, got):
        def action():
            item.arrived()
            self.add(a, self.g.h, half, got)
        return action

    def finish(self, half):
        g = self.g
        own = self.own.at[half]
        own[...] = self.region(g.s, g.h, half)[...].astype(F32)

        def add(item, got):
            def action():
                item.arrived()
                own[...] = own[...] + got[...].astype(F32)
            return action

        for i in range(self.zz.Z):
            d, ups, downs = self.flight["z", i, half]
            below, above = self.chain.ends(d)
            when(below, add(ups, self.up.at[d, half]))
            when(above, add(downs, self.down.at[d, half]))
        return own[...]

    def run(self, produce):
        order = self.chain.order()
        steps = [
            lambda i, d: (produce(d), self.core(i, d)),
            self.first,
            self.second,
            self.third,
        ]
        count = len(order)
        for turn in range(count + len(steps) - 1):
            for stage in range(len(steps)):
                if 0 <= turn - stage < count:
                    steps[stage](turn - stage, order[turn - stage])
                    yield turn


def halves(ref, rows, row_count, lanes, lane_count, half):
    if half is not None:
        row_count //= 2
        rows = rows + half * row_count
    return at(ref, rows, row_count, lanes, lane_count)


def region_of(z, ref):
    return lambda a, b, half: halves(
        ref, a // 2 * 2 * z.Ds, 2 * z.Ds, (2 * b + a % 2) * z.R, z.R, half
    )


def front_kernel(
    z, tok, gain, xw, yw, ow, vec, aw, iw, spread, mask, cot_in, gain2, gw_in, uw_in, dw_in,
    xw2, yw2, ow2, tok2, fn2, rn, yb, pad, conv, a_o, i_o, st, entry_o, mix, res,
    back_g, uwg_o, dwg_o, gsum_o, bg_o, hid, dw,
    turned, fnt, x1, x2, x3, x4, x5, y1, y2, y3, y4, y5, sums, tot, part, got, edge,
    cot, gw, uw, xt, gwt, uwt, dwt, gwg, hg, gg, ug, gs, us, rs, wide,
    c1, c2, c3, c4, c5, c6, stat, send, recv, own_sem,
):
    s, h = place()
    S, H, R, D, T, Ds, C, Z = z.S, z.H, z.R, z.D, z.T, z.Ds, z.C, z.Z
    DG = 2 * Ds
    Q = DG // H
    zi, xi = s // 2, s % 2
    after, before = lax.rem(s + 1, S), lax.rem(s + S - 1, S)
    greet(
        [(s ^ k, h) for k in range(1, S)]
        + [(s, h ^ j) for j in range(1, H)]
        + [(after, h), (before, h)]
    )
    wire = Wire(send, recv)
    g = Grid(s, h)
    chain = Chain(wire, Z, s, h)
    deal = Deal(wire, z, s, h)
    pairs = ((gw_in, gw), (uw_in, uw), (dw_in, dw))
    dealing = deal.steps(deal.out, pairs)
    half = pl.ds(pl.multiple_of(xi * Ds, EDGE), Ds)
    twins = [
        wire.copy(src, dst.at[half, :], (s ^ 1, h)) for src, dst in ((xw, xw2), (yw, yw2))
    ]
    turned[...] = tok[...].astype(F32).T.astype(BF16)
    quarter = pl.ds(pl.multiple_of(h * Q, EDGE), Q)
    my_lanes = pl.ds(pl.multiple_of(zi * R, LANES), R)

    def group(index):
        return pl.ds(pl.multiple_of(index * DG + h * Q, EDGE), Q)

    first = [
        wire.copy(turned.at[group(zi ^ kz), :], tok2.at[quarter, my_lanes], (s ^ (2 * kz), h))
        for kz in range(1, Z)
    ]
    column = turned[...].astype(F32)
    mean = jnp.sum(column * column, axis=0, keepdims=True) / z.D
    rn[zi] = jnp.broadcast_to(lax.rsqrt(mean + EPSILON), (8, R))
    for kz in range(1, Z):
        first.append(wire.copy(rn.at[zi], rn.at[zi], (s ^ (2 * kz), h)))
    tok2[quarter, my_lanes] = turned[group(zi), :]
    xw2[half, :] = xw[...]
    yw2[half, :] = yw[...]
    ow2[half, :] = ow[...]
    pending = [
        own_block(z, src, dst, own_sem.at[pl.ds(2 * i, 2)], s)
        for i, (src, dst) in enumerate(pairs)
    ]
    W = z.D // H

    def corner(a, b, half):
        return halves(cot, a * R, R, b * W, W, half)

    corner(s, h, None)[...] = cot_in[:, pl.ds(pl.multiple_of(h * W, LANES), W)]
    cot_in_all = gather_all(wire, z, g, corner)
    advance(cot_in_all)
    advance(dealing, 2)
    for item in first:
        item.wait_recv()
    HeadGather(
        wire, s, h, lambda j: tok2.at[pl.ds(pl.multiple_of(j * Q, EDGE), Q), :]
    ).wait_all()
    for b in range(Z):
        cut = slice(b * R, b * R + R)
        fn2[:, cut] = (tok2[:, cut].astype(F32) * rn[b, 0:1, :] * gain[...]).astype(BF16)
    twins[0].wait_recv()
    twins.append(wire.copy(ow, ow2.at[half, :], (s ^ 1, h)))

    def x_part(d):
        lanes = pl.ds(pl.multiple_of(d * R, LANES), R)
        fnt[d] = fn2[:, lanes].astype(F32).T.astype(BF16)
        return mm(fnt[d], xw2[...])

    x_sum = chain.scatter(x_part, x1, x2, x3, x4, x5)
    advance(x_sum, Z)
    advance(cot_in_all)
    drain(x_sum)
    x_low = x5[...].astype(BF16)
    edge[0] = x_low[R - EDGE : R, :]
    halo = wire.copy(edge.at[0], edge.at[1], (after, h))
    twins[1].wait_recv()
    y_sum = chain.scatter(lambda d: mm(fnt[d], yw2[...]), y1, y2, y3, y4, y5)
    advance(y_sum, 1)
    advance(cot_in_all, 2)
    pad[pl.ds(EDGE, R), :] = x_low.astype(F32)
    halo.wait_recv()
    pad[pl.ds(0, EDGE), :] = jnp.where(s == 0, 0.0, edge[1].astype(F32))
    out = jnp.broadcast_to(vec[4:5, :], (R, C))
    for lag in range(CONV):
        out = out + vec[lag : lag + 1, :] * pad[pl.ds(EDGE - lag, R), :]
    conv[h] = out.astype(BF16)
    across = HeadGather(wire, s, h, lambda j: conv.at[j])
    advance(y_sum, 1)
    a_pre = jnp.broadcast_to(vec[5:6, :], (R, C))
    i_pre = jnp.broadcast_to(vec[6:7, :], (R, C))
    for j in (0, 2, 1, 3):
        if j:
            across.wait(j)
        k = h ^ j
        taken = conv[k]
        a_pre = a_pre + mm(taken, gate_weight_of(z, spread, mask, aw, k))
        i_pre = i_pre + mm(taken, gate_weight_of(z, spread, mask, iw, k))
    advance(y_sum, 1)
    a_o[...] = a_pre
    i_o[...] = i_pre
    anchor = anchor_of(z, s, LANES)
    sums[s] = jnp.zeros((8, C), F32)
    for b in range(C // LANES):
        cut = pl.ds(b * LANES, LANES)
        recall, input_gate, factor, one_minus, root_value, root_scale = decay_terms(
            a_o[:, cut], i_o[:, cut], vec[7:8, cut], anchor
        )
        driven = conv[h, :, cut].astype(F32) * input_gate * root_scale
        prod, value = scan_rows(factor, driven, 1)
        st[:, cut] = value
        tot[:, cut] = prod
        sums[s, 0:1, cut] = prod[R - 1 : R, :]
        sums[s, 1:2, cut] = value[R - 1 : R, :]
    ends = [wire.copy(sums.at[s], sums.at[s], (s ^ k, h)) for k in range(1, S)]
    advance(dealing, 1)
    advance(cot_in_all, 2)
    drain(y_sum)
    yb[...] = y5[...]
    for item in ends:
        item.wait_recv()
    entry = jnp.zeros((1, C), F32)
    for j in range(S - 1):
        entry = jnp.where(j < s, sums[j, 0:1, :] * entry + sums[j, 1:2, :], entry)
    entry_o[...] = jnp.broadcast_to(entry, (8, C))
    my_rows = pl.ds(pl.multiple_of(zi * R, EDGE), R)
    for b in range(C // LANES):
        cut = pl.ds(b * LANES, LANES)
        state = st[:, cut] + tot[:, cut] * entry_o[0:1, cut]
        st[:, cut] = state
        mix[my_rows, cut] = (state * gelu_pair(yb[:, cut])[0]).astype(BF16)
    arriving = chain.gather(row_blocks(z, mix))
    advance(arriving)
    advance(cot_in_all, 2)
    drain(arriving)
    twins[2].wait_recv()

    def out_part(j):
        rows = pl.ds(pl.multiple_of((h ^ j) * R, EDGE), R)
        return mm(ow2[...], mix[rows, :], NT)

    whole = head_scatter(wire, s, h, out_part, part, got)
    advance(dealing, 2)
    res[...] = whole() + tok2[:, pl.ds(pl.multiple_of(h * R, LANES), R)].astype(F32)


    tile = 256
    region_of(z, xt)(s, h, None)[...] = res[...].astype(BF16)
    spreading = gather_all(wire, z, g, region_of(z, xt))
    advance(spreading, 2)
    def turn(src, dst, scaled):
        for n in range(D // tile):
            cut = slice(n * tile, n * tile + tile)
            piece = src[cut, :].astype(F32)
            dst[:, cut] = (piece * gain2[cut, :] if scaled else piece).T.astype(BF16)

    drain(cot_in_all)
    advance(spreading, 3)
    advance(dealing, 2)
    advance(spreading, 2)
    advance(dealing, 2)
    drain(spreading, dealing)
    for wait in pending:
        wait()
    deal.wait()
    turn(gw, gwt, True)
    turn(uw, uwt, True)
    turn(dw, dwt, False)
    for n in range(T // tile):
        cut = slice(n * tile, n * tile + tile)
        hg[:, cut] = mm(dwt[...], cot[cut, :], NT)
        square = jnp.zeros((1, tile), F32)
        for b in range(D // tile):
            piece = xt[b * tile : b * tile + tile, cut].astype(F32)
            square = square + jnp.sum(piece * piece, axis=0, keepdims=True)
        scale = lax.rsqrt(square / D + EPSILON)
        rs[:, cut] = jnp.broadcast_to(scale, (8, tile))
        gate = mm(gwt[...], xt[:, cut]) * scale
        up = mm(uwt[...], xt[:, cut]) * scale
        act, slope = gelu_pair(gate)
        hid[:, cut] = (act * up).astype(BF16)
        back = hg[:, cut]
        gate_grad = back * up * slope
        up_grad = back * act
        gg[:, cut] = gate_grad.astype(BF16)
        ug[:, cut] = up_grad.astype(BF16)
        gs[:, cut] = (gate_grad * scale).astype(BF16)
        us[:, cut] = (up_grad * scale).astype(BF16)
    second = SumAll(wire, z, g, region_of(z, wide), (c1, c2, c3, c4, c5, c6))

    def produce(d):
        rows = pl.ds(pl.multiple_of(d * DG, LANES), DG)
        wide[rows, :] = (mm(gw[rows, :], gg[...]) + mm(uw[rows, :], ug[...])).astype(BF16)

    summing = second.run(produce)
    advance(summing, 3)
    for n in range(D // tile):
        cut = slice(n * tile, n * tile + tile)
        gwg[cut, :] = (mm(xt[cut, :], gs[...], NT) * gain2[cut, :]).astype(BF16)
    dealing = deal.steps(deal.back, ((gwg, back_g),))
    advance(dealing, 3)
    deal.back_own(gwg, back_g)
    advance(summing, 6)
    advance(dealing, 1)
    drain(summing)
    for n in range(D // tile):
        cut = slice(n * tile, n * tile + tile)
        uwg_o[cut, :] = (mm(xt[cut, :], us[...], NT) * gain2[cut, :]).astype(BF16)
        dwg_o[cut, :] = mm(hid[...], cot[:, cut]).T.astype(BF16)
    second_grad = jnp.concatenate([second.finish(0), second.finish(1)], axis=0)
    mine = pl.ds(pl.multiple_of((2 * h + xi) * R, LANES), R)
    group = pl.ds(pl.multiple_of(zi * DG, LANES), DG)
    scale = rs[0:1, mine]
    residual = res[...]
    gsum_o[...] = second_grad * residual * scale
    weighted = gain2[group, :] * second_grad
    stat[zi] = jnp.broadcast_to(jnp.sum(weighted * residual, axis=0, keepdims=True), (8, R))
    ends = [wire.copy(stat.at[zi], stat.at[zi], g.z(kz)) for kz in range(1, z.Z)]
    direct = cot[mine, group].astype(F32).T + scale * weighted
    for item in ends:
        item.wait_recv()
    mean = jnp.sum(stat[:, 0:1, :], axis=0) / D
    grad = direct - residual * (scale * scale * scale * mean)
    lanes = pl.ds(pl.multiple_of(h * R, LANES), R)
    bg_o[:, lanes] = grad.astype(BF16)
    HeadGather(
        wire, s, h, lambda j: bg_o.at[:, pl.ds(pl.multiple_of(j * R, LANES), R)]
    ).wait_all()
    deal.wait()
    wire.close()


def front(z, *args):
    S, H, R, D, T, U, Ds, C, Z = z.S, z.H, z.R, z.D, z.T, z.U, z.Ds, z.C, z.Z
    DG, TX = 2 * Ds, Z * R
    copies = 2 + 2 * (Z - 1) + (H - 1) + 1 + 4 * Z + 1 + (H - 1) + (S - 1)
    copies += 2 * (Z - 1) + (H - 1) + 8 * (S - 1) + 2 * gather_copies(z)
    copies += SumAll.copies(z) + (Z - 1) + (H - 1)
    return call(
        functools.partial(front_kernel, z),
        "front",
        1,
        [
            sds((DG, C), BF16),
            sds((DG, C), BF16),
            sds((DG, C), BF16),
            sds((DG, TX), BF16),
            sds((DG, TX), BF16),
            sds((Z, 8, R), F32),
            sds((R, C), F32),
            sds((EDGE + R, C), F32),
            sds((H, R, C), BF16),
            sds((R, C), F32),
            sds((R, C), F32),
            sds((R, C), F32),
            sds((8, C), F32),
            sds((TX, C), BF16),
            sds((DG, R), F32),
            sds((Ds, z.F2), BF16),
            sds((D, U), BF16),
            sds((D, U), BF16),
            sds((DG, R), F32),
            sds((DG, TX), BF16),
            sds((U, T), BF16),
            sds((D, U), BF16),
        ],
        [
            VM((D, R), BF16),
            VM((Z, R, DG), BF16),
            *chain_scratch(z, R, C),
            *chain_scratch(z, R, C),
            VM((S, 8, C), F32),
            VM((R, C), F32),
            VM((H, DG, R), BF16),
            VM((H, DG, R), BF16),
            VM((2, EDGE, C), BF16),
            VM((T, D), BF16),
            VM((D, U), BF16),
            VM((D, U), BF16),
            VM((D, T), BF16),
            VM((U, D), BF16),
            VM((U, D), BF16),
            VM((U, D), BF16),
            VM((D, U), BF16),
            VM((U, T), F32),
            VM((U, T), BF16),
            VM((U, T), BF16),
            VM((U, T), BF16),
            VM((U, T), BF16),
            VM((8, T), F32),
            VM((D, T), BF16),
            *SumAll.scratch(z, DG, R),
            VM((Z, 8, R), F32),
            sem(copies),
            sem(copies),
            sem(6),
        ],
        args,
        (12, 13, 14),
    )


def exact(left, right, dims):
    return lax.dot_general(
        left, right, dims, precision=lax.Precision.HIGHEST, preferred_element_type=F32
    )


def back_kernel(
    z, bg, ow2, mix, yb, vec, a_pre, i_pre, st, entry, conv, pad, aw, iw, spread, mask,
    xw2, yw2, fn2, tok2, rn, gain, msum, res, hid, dw, uwg, dwg,
    mixed_o, owg_o, xwg_o, ywg_o, twin_r, full, gains2, smallg, vec_o, back_u, back_d,
    g1, g2, g3, g4, own, adj, tot, ag, ig, sums, late, cgr, cgs, ext, gx, gy, part, got, stat, stat2,
    tgq, prod, prod2, gains, small, smallx, small_z, vecs, twin_s, mpart, m1, m2, m3, m4, m5, m6, send, recv,
):
    s, h = place()
    g = Grid(s, h)
    S, H, R, D, Ds, C, Z, T = z.S, z.H, z.R, z.D, z.Ds, z.C, z.Z, z.T
    DG, W = 2 * Ds, D // H
    Q = DG // H
    zi, xi = s // 2, s % 2
    after, before = lax.rem(s + 1, S), lax.rem(s + S - 1, S)
    greet(
        [(s ^ k, h) for k in range(1, S)]
        + [(s, h ^ j) for j in range(1, H)]
        + [(after, h), (before, h)]
    )
    wire = Wire(send, recv)
    chain = Chain(wire, Z, s, h)
    deal = Deal(wire, z, s, h)
    dealing = deal.steps(deal.back, ((uwg, back_u), (dwg, back_d)))
    my_rows = pl.ds(pl.multiple_of(zi * R, EDGE), R)
    half = pl.ds(pl.multiple_of(xi * Ds, EDGE), Ds)
    other = pl.ds(pl.multiple_of((1 - xi) * Ds, EDGE), Ds)

    def corner(a, b, part_of):
        return halves(mpart, b * W, W, a * R, R, part_of)

    mixed = SumAll(wire, z, g, corner, (m1, m2, m3, m4, m5, m6))

    def produce_mixed(d):
        cut = pl.ds(pl.multiple_of(d * 2 * R, LANES), 2 * R)
        mpart[:, cut] = mm(dw[...], hid[:, cut]).astype(BF16)

        @pl.when(h == d)
        def _():
            spot = region_of(z, mpart)(s, h, None)
            spot[...] = (spot[...].astype(F32) + res[...]).astype(BF16)

    mixing = mixed.run(produce_mixed)

    def block(d):
        lanes = pl.ds(pl.multiple_of(d * R, LANES), R)
        return mm(bg[:, lanes].astype(F32).T.astype(BF16), ow2[...])

    summing = chain.scatter(block, g1, g2, g3, g4, own)
    for _ in range(Z):
        advance(summing)
        advance(mixing, 2)
    drain(summing)
    row = lax.broadcasted_iota(jnp.int32, (R, LANES), 0)
    anchor = anchor_of(z, s, LANES)
    sums[s] = jnp.zeros((8, C), F32)
    for b in range(C // LANES):
        cut = pl.ds(b * LANES, LANES)
        grad = own[:, cut]
        gate, slope = gelu_pair(yb[:, cut])
        gy[my_rows, cut] = (grad * st[:, cut] * slope).astype(BF16)
        factor = jnp.exp(-8.0 * jax.nn.sigmoid(a_pre[:, cut]) * vec[7:8, cut])
        ahead = shifted(factor, -1, 1.0, row)
        prods, value = scan_rows(ahead, grad * gate, -1)
        tot[:, cut] = prods
        adj[:, cut] = value
        sums[s, 0:1, cut] = factor[0:1, :] * prods[0:1, :]
        sums[s, 1:2, cut] = factor[0:1, :] * value[0:1, :]
    ends = [wire.copy(sums.at[s], sums.at[s], (s ^ k, h)) for k in range(1, S)]
    y_rows = chain.gather(row_blocks(z, gy))
    advance(y_rows)
    advance(dealing, 0)
    twins = []

    def weight_grad(index, left, right, out):
        prod2[...] = mm(left[...], right[...])
        twin_s[index] = prod2[other, :].astype(BF16)
        twins.append(wire.copy(twin_s.at[index], twin_r.at[index], g.x))
        out[...] = prod2[half, :]

    weight_grad(0, bg, mix, owg_o)
    advance(mixing, 2)
    for item in ends:
        item.wait_recv()
    carry = jnp.zeros((1, C), F32)
    for j in range(S - 1, 0, -1):
        carry = jnp.where(j > s, sums[j, 0:1, :] * carry + sums[j, 1:2, :], carry)
    vec_o[...] = jnp.zeros_like(vec_o)
    late[...] = jnp.broadcast_to(carry, (8, C))
    for b in range(C // LANES):
        cut = pl.ds(b * LANES, LANES)
        adjoint = adj[:, cut] + tot[:, cut] * late[0:1, cut]
        rate = vec[7:8, cut]
        recall, input_gate, factor, one_minus, root_value, root_scale = decay_terms(
            a_pre[:, cut], i_pre[:, cut], rate, anchor
        )
        taken = conv[h, :, cut].astype(F32)
        state = st[:, cut]
        earlier = jnp.where(row == 0, entry[0:1, cut], shifted(state, 1, 0.0, row))
        live = jnp.logical_and(one_minus > SQUARE_FLOOR, jnp.logical_not(anchor))
        scale_grad = adjoint * taken * input_gate
        log_grad = adjoint * earlier * factor - jnp.where(
            live, scale_grad * factor * factor / root_value, 0.0
        )
        a_grad = (log_grad * (-8.0 * rate) * recall * (1.0 - recall)).astype(BF16)
        i_grad = (scale_grad * root_scale * (1.0 - input_gate)).astype(BF16)
        ag[:, cut] = a_grad
        ig[:, cut] = i_grad
        decay_sum = jnp.sum(log_grad * (-8.0 * recall), axis=0, keepdims=True)
        vec_o[5:6, cut] = jnp.sum(a_grad.astype(F32), axis=0, keepdims=True)
        vec_o[6:7, cut] = jnp.sum(i_grad.astype(F32), axis=0, keepdims=True)
        vec_o[7:8, cut] = decay_sum * vec[8:9, cut]
        ext[pl.ds(0, R), cut] = adjoint * input_gate * root_scale

    eighth = small.shape[0] // S

    def share(x_index, z_index, count):
        start = (x_index * Z + z_index) * eighth
        return pl.ds(pl.multiple_of(start, EDGE), count * eighth)

    def sum_small():
        mine = share(xi, 0, Z)
        item = wire.copy(small.at[share(1 - xi, 0, Z), :], smallx, g.x)
        yield
        item.wait_recv()
        smallx[...] = (smallx[...].astype(F32) + small[mine, :].astype(F32)).astype(BF16)

        def piece(index):
            return pl.ds(pl.multiple_of(index * eighth, EDGE), eighth)

        items = [
            wire.copy(smallx.at[piece(zi ^ kz), :], small_z.at[kz], g.z(kz))
            for kz in range(1, Z)
        ]
        yield
        total = smallx[piece(zi), :].astype(F32)
        for kz in range(1, Z):
            items[kz - 1].wait_recv()
            total = total + small_z[kz].astype(F32)
        spot = smallg.at[share(xi, zi, 1), :]
        spot[...] = total.astype(BF16)
        items = [wire.copy(spot, spot, g.z(kz)) for kz in range(1, Z)]
        yield
        for item in items:
            item.wait_recv()
        item = wire.copy(smallg.at[mine, :], smallg.at[mine, :], g.x)
        yield
        item.wait_recv()

    smaller = sum_small()
    def gates_back(j):
        return mm(ag[...], gate_weight_of(z, spread, mask, aw, h ^ j), NT) + mm(
            ig[...], gate_weight_of(z, spread, mask, iw, h ^ j), NT
        )

    advance(y_rows, 2)
    across = head_scatter(wire, s, h, gates_back, cgs, cgr)
    advance(y_rows, 2)
    advance(dealing, 4)
    for k in range(H):
        turn = conv[k].astype(F32).T.astype(BF16)
        for spot, grad in ((0, ag), (z.HS, ig)):
            dense = mm(turn, grad[...]).astype(BF16) * mask[...]
            small[pl.ds(spot + k * z.NI, z.NI), :] = mm(spread[...], dense, TN).astype(BF16)
    advance(smaller)
    advance(mixing, 2)
    conv_grad = ext[pl.ds(0, R), :] + across()
    ext[pl.ds(0, R), :] = conv_grad
    halo = wire.copy(ext.at[pl.ds(0, 8), :], ext.at[pl.ds(R, 8), :], (before, h))
    for lag in range(CONV):
        vec_o[lag : lag + 1, :] = jnp.sum(
            conv_grad * pad[pl.ds(EDGE - lag, R), :], axis=0, keepdims=True
        )
    vec_o[4:5, :] = jnp.sum(conv_grad, axis=0, keepdims=True)
    vecs[s] = vec_o[...]
    advance(mixing, 1)
    advance(smaller)
    halo.wait_recv()
    ext[pl.ds(R, 8), :] = jnp.where(s == S - 1, 0.0, ext[pl.ds(R, 8), :])
    grad = jnp.zeros((R, C), F32)
    for lag in range(CONV):
        grad = grad + vec[lag : lag + 1, :] * ext[pl.ds(lag, R), :]
    gx[my_rows, :] = grad.astype(BF16)
    rows_in = chain.gather(row_blocks(z, gx))
    advance(rows_in)
    advance(dealing, 2)
    advance(mixing, 1)
    pair = grad.astype(BF16).astype(F32) * pad[pl.ds(EDGE, R), :] + gy[my_rows, :].astype(F32) * yb[...]
    stat[h] = exact(jnp.ones((8, C), F32), pair, NT)
    stats = [wire.copy(stat.at[h], stat.at[h], (s, h ^ j)) for j in range(1, H)]

    lesser = [wire.copy(vecs.at[s], vecs.at[s], (s ^ k, h)) for k in range(1, S)]
    drain(y_rows)
    weight_grad(1, fn2, gy, ywg_o)
    prod[...] = mm(yw2[...], gy[...], NT)
    for item in stats:
        item.wait_recv()
    stat2[zi] = stat[0] + stat[1] + stat[2] + stat[3]
    stats = [wire.copy(stat2.at[zi], stat2.at[zi], g.z(kz)) for kz in range(1, Z)]
    advance(smaller)
    advance(mixing, 1)
    drain(rows_in)

    prod[...] = prod[...] + mm(xw2[...], gx[...], NT)

    def quarter_of(j):
        return prod[pl.ds(pl.multiple_of((h ^ j) * Q, EDGE), Q), :]

    heads = head_scatter(wire, s, h, quarter_of, part, got)
    advance(dealing, 2)
    advance(smaller)
    advance(mixing, 1)
    quarter = pl.ds(pl.multiple_of(h * Q, EDGE), Q)
    weight_grad(2, fn2, gx, xwg_o)
    total = heads()
    for item in stats:
        item.wait_recv()
    token = tok2[quarter, :].astype(F32)
    norm = jnp.concatenate([rn[b, 0:1, :] for b in range(Z)], axis=1)
    mean = jnp.concatenate([stat2[b, 0:1, :] for b in range(Z)], axis=1) / (norm * D)
    group = pl.ds(pl.multiple_of(zi * DG + h * Q, EDGE), Q)
    weighted = gain[group, :] * total
    grad = bg[quarter, :].astype(F32) + norm * weighted - token * (norm * norm * norm * mean)
    tgq[...] = grad.astype(BF16)

    def spot(z_index, head):
        return full.at[pl.ds(pl.multiple_of(z_index * DG + head * Q, EDGE), Q), :]

    outs = [
        wire.copy(
            tgq.at[:, pl.ds(pl.multiple_of((zi ^ kz) * R, LANES), R)], spot(zi, h), g.z(kz)
        )
        for kz in range(1, Z)
    ]
    spot(zi, h)[...] = tgq[:, pl.ds(pl.multiple_of(zi * R, LANES), R)]
    prod[...] = jnp.zeros_like(prod)
    prod[quarter, :] = total * token * norm
    ones = jnp.ones((8, Z * R), F32)
    picked = lax.broadcasted_iota(jnp.int32, (8, DG), 0)
    gains[h] = jnp.where(
        picked == 0, exact(jnp.ones((8, R), F32), msum[...], NT), exact(ones, prod[...], NT)
    )
    tally = [wire.copy(gains.at[h], gains.at[h], (s, h ^ j)) for j in range(1, H)]
    finals = []
    drain(dealing)
    for kz in range(Z):
        if kz:
            outs[kz - 1].wait_recv()
        finals.append(HeadGather(wire, s, h, lambda j, kz=kz: spot(zi ^ kz, j)))
    for item in tally:
        item.wait_recv()
    gains2[s] = gains[0] + gains[1] + gains[2] + gains[3]
    tally = [wire.copy(gains2.at[s], gains2.at[s], (s ^ k, h)) for k in range(1, S)]
    drain(mixing)
    for part_of in range(2):
        mixed_o[pl.ds(part_of * W // 2, W // 2), :] = mixed.finish(part_of)
    for item in lesser:
        item.wait_recv()
    vec_o[...] = jnp.sum(vecs[...], axis=0)
    for item in twins:
        item.wait_recv()
    deal.back_own(uwg, back_u)
    deal.back_own(dwg, back_d)
    drain(smaller)
    for item in tally:
        item.wait_recv()
    for item in finals:
        item.wait_all()
    deal.wait()
    wire.close()


def back(z, *args):
    S, H, R, D, Ds, C, Z, T = z.S, z.H, z.R, z.D, z.Ds, z.C, z.Z, z.T
    DG, W = 2 * Ds, D // H
    TX, Q = Z * R, DG // H
    copies = (
        2 * Z + (S - 1) + 3 + (H - 1) + 1 + 4 * (Z - 1) + (H - 1) + (Z - 1) + (S - 1)
        + 2 + 2 * (Z - 1) + 2 * (Z - 1) + 4 * (S - 1) + (H - 1) + (Z - 1) + (H - 1) + Z * (H - 1) + (S - 1)
        + SumAll.copies(z)
    )
    small = 2 * z.HS
    return call(
        functools.partial(back_kernel, z),
        "back",
        2,
        [
            sds((W, R), F32),
            sds((Ds, C), F32),
            sds((Ds, C), F32),
            sds((Ds, C), F32),
            sds((3, Ds, C), BF16),
            sds((D, R), BF16),
            sds((S, 8, DG), F32),
            sds((small, C), BF16),
            sds((8, C), F32),
            sds((Ds, z.F2), BF16),
            sds((Ds, z.F2), BF16),
        ],
        [
            *chain_scratch(z, R, C),
            VM((R, C), F32),
            VM((R, C), F32),
            VM((R, C), BF16),
            VM((R, C), BF16),
            VM((S, 8, C), F32),
            VM((8, C), F32),
            VM((H, R, C), BF16),
            VM((H, R, C), BF16),
            VM((R + 8, C), F32),
            VM((TX, C), BF16),
            VM((TX, C), BF16),
            VM((H, Q, TX), BF16),
            VM((H, Q, TX), BF16),
            VM((H, 8, R), F32),
            VM((Z, 8, R), F32),
            VM((Q, TX), BF16),
            VM((DG, TX), F32),
            VM((DG, C), F32),
            VM((H, 8, DG), F32),
            VM((small, C), BF16),
            VM((small // 2, C), BF16),
            VM((Z, small // S, C), BF16),
            VM((S, 8, C), F32),
            VM((3, Ds, C), BF16),
            VM((D, T), BF16),
        ]
        + SumAll.scratch(z, W, R)
        + [sem(copies), sem(copies)],
        args,
    )


def results_kernel(z, *refs):
    sources, count = 12, 17
    inputs, outs = refs[:sources], refs[sources : sources + count]
    held = refs[sources + count : 2 * sources + count]
    stage = refs[2 * sources + count : 2 * (sources + count)]
    in_sem, out_sem = refs[-2:]
    fetch = []
    for index in range(sources):
        copy = pltpu.make_async_copy(inputs[index], held[index], in_sem.at[index])
        copy.start()
        fetch.append(copy)
    mixed, owg, xwg, ywg, twins, full, gains, small, vec, back_g, back_u, back_d = held
    copies = []

    def need(*indexes):
        for index in indexes:
            fetch[index].wait()

    def emit(index, value):
        stage[index][...] = value
        copy = pltpu.make_async_copy(stage[index], outs[index], out_sem.at[index])
        copy.start()
        copies.append(copy)

    need(4, 1, 2, 3)
    for index, slot, src in ((12, 0, owg), (4, 1, ywg), (3, 2, xwg)):
        emit(index, src[...] + twins[slot].astype(F32))
    for index, at_input, src in ((14, 9, back_g), (15, 10, back_u), (16, 11, back_d)):
        need(at_input)
        emit(index, src[...].astype(F32))
    need(5, 0, 7, 8, 6)
    emit(1, full[...].astype(F32).T)
    emit(0, mixed[...].T.astype(BF16))
    emit(7, small[0 : z.HS, :].astype(F32))
    emit(9, small[z.HS : 2 * z.HS, :].astype(F32))
    for index, start, rows in ((5, 0, CONV), (6, 4, 1), (8, 5, 1), (10, 6, 1), (11, 7, 1)):
        emit(index, vec[start : start + rows, :])
    for index, row in ((2, 1), (13, 0)):
        cut = slice(row, row + 1)
        sums = [gains[2 * b, cut, :] + gains[2 * b + 1, cut, :] for b in range(z.Z)]
        emit(index, jnp.concatenate(sums, axis=1))
    for copy in copies:
        copy.wait()


def results(z, *args):
    R, D, Ds, C, F2 = z.R, z.D, z.Ds, z.C, z.F2
    row = sds((1, C), F32)
    outs = [
        sds((R, D // z.H), BF16),
        sds((R, D), F32),
        sds((1, D), F32),
        sds((Ds, C), F32),
        sds((Ds, C), F32),
        sds((CONV, C), F32),
        row,
        sds((z.HS, C), F32),
        row,
        sds((z.HS, C), F32),
        row,
        row,
        sds((Ds, C), F32),
        sds((1, D), F32),
        sds((Ds, F2), F32),
        sds((Ds, F2), F32),
        sds((Ds, F2), F32),
    ]
    return pl.pallas_call(
        functools.partial(results_kernel, z),
        out_shape=outs,
        in_specs=[pl.BlockSpec(memory_space=ANY)] * len(args),
        out_specs=[pl.BlockSpec(memory_space=ANY)] * len(outs),
        scratch_shapes=[VM(a.shape, a.dtype) for a in list(args) + outs]
        + [sem(len(args)), sem(len(outs))],
        compiler_params=pltpu.CompilerParams(vmem_limit_bytes=62 << 20),
        name="results",
    )(*args)


def dealt(
    z,
    tokens,
    norm_gain,
    x_weight,
    y_weight,
    conv_weight,
    conv_bias,
    a_weight,
    a_bias,
    i_weight,
    i_bias,
    decay,
    out_weight,
    mlp_gain,
    gate_weight,
    up_weight,
    down_weight,
    cotangent,
):
    s = lax.axis_index("seq")
    first_gain = norm_gain.astype(F32)[:, None]
    second_gain = mlp_gain.astype(F32)[:, None]
    gain_s = lax.dynamic_slice(first_gain, (s // 2 * 2 * z.Ds, 0), (2 * z.Ds, 1))
    vec = vectors(conv_weight, conv_bias, a_bias, i_bias, decay)
    spread, mask = head_maps(z)
    (
        xw2, yw2, ow2, tok2, fn2, rn, yb, pad, conv, a_pre, i_pre, st, entry, mix, res,
        back_g, uwg, dwg, msum, bg, hid, dc,
    ) = front(
        z, tokens, gain_s, x_weight, y_weight, out_weight, vec, a_weight, i_weight, spread, mask,
        cotangent, second_gain, gate_weight, up_weight, down_weight,
    )
    mixed, owg, xwg, ywg, twins, tg, gains, small, vec_sum, back_u, back_d = back(
        z, bg, ow2, mix, yb, vec, a_pre, i_pre, st, entry, conv, pad, a_weight, i_weight, spread,
        mask, xw2, yw2, fn2, tok2, rn, first_gain, msum, res, hid, dc, uwg, dwg,
    )
    (
        mixed, tg, first_g, xwg, ywg, conv_wg, conv_bg, awg, a_bg, iwg, i_bg, decay_g, owg,
        second_g, gate_g, up_g, down_g,
    ) = results(z, mixed, owg, xwg, ywg, twins, tg, gains, small, vec_sum, back_g, back_u, back_d)
    return (
        mixed,
        tg,
        first_g.reshape(z.D),
        xwg,
        ywg,
        conv_wg,
        conv_bg.reshape(z.C),
        awg,
        a_bg.reshape(z.C),
        iwg,
        i_bg.reshape(z.C),
        decay_g.reshape(z.C),
        owg,
        second_g.reshape(z.D),
        gate_g,
        up_g,
        down_g,
    )


def from_behind(x, axis, by):
    size = lax.axis_size(axis)
    pairs = [(i, i + by) for i in range(size) if 0 <= i + by < size]
    return lax.ppermute(x, axis, pairs)


def rms_norm(values, gain):
    return values * lax.rsqrt(jnp.mean(values * values, axis=-1, keepdims=True) + EPSILON) * gain


def linear_pair(earlier, later):
    return (later[0] * earlier[0], later[0] * earlier[1] + later[1])


def gelu_back(values, grad):
    return jax.vjp(jax.nn.gelu, values)[1](grad)[0]


def gathered_weights(
    tokens,
    norm_gain,
    x_weight,
    y_weight,
    conv_weight,
    conv_bias,
    a_weight,
    a_bias,
    i_weight,
    i_bias,
    decay,
    out_weight,
    mlp_gain,
    gate_weight,
    up_weight,
    down_weight,
    cotangent,
):
    row_count = tokens.shape[0]
    model_width = tokens.shape[1]
    lane_count = x_weight.shape[1]
    head_size = a_weight.shape[0]
    head_index = lax.axis_index("head")
    seq_index = lax.axis_index("seq")
    head_devices = lax.axis_size("head")
    float_type = jnp.float32
    half_type = jnp.bfloat16
    gathered = (
        lax.all_gather(x_weight, "seq", axis=0, tiled=True),
        lax.all_gather(y_weight, "seq", axis=0, tiled=True),
        lax.all_gather(out_weight, "seq", axis=0, tiled=True),
        lax.all_gather(gate_weight, "seq", axis=0, tiled=True),
        lax.all_gather(up_weight, "seq", axis=0, tiled=True),
        lax.all_gather(down_weight, "seq", axis=0, tiled=True),
    )
    x_full, y_full, out_full, gate_full, up_full, down_full = gathered
    tokens_wide = tokens.astype(float_type)
    first_gain = norm_gain.astype(float_type)
    first_norm = rms_norm(tokens_wide, first_gain)
    first_low = first_norm.astype(half_type)
    x_branch = jnp.dot(first_low, x_full, preferred_element_type=float_type).astype(half_type)
    y_branch = jnp.dot(first_low, y_full, preferred_element_type=float_type)
    y_gate = jax.nn.gelu(y_branch)
    left_edge = from_behind(x_branch[row_count - (CONV - 1) :], "seq", 1)
    padded = jnp.concatenate([left_edge, x_branch], axis=0).astype(float_type)
    conv_taps = conv_weight.astype(float_type)
    conv_out = conv_bias.astype(float_type) + sum(
        (
            conv_taps[lag_index] * padded[CONV - 1 - lag_index : CONV - 1 - lag_index + row_count]
            for lag_index in range(CONV)
        )
    )
    conv_low = conv_out.astype(half_type)
    conv_value = conv_low.astype(float_type)
    all_channels = lax.all_gather(conv_low, "head", axis=1, tiled=True)
    head_count = all_channels.shape[1] // head_size
    group_count = lane_count // head_count
    heads_view = all_channels.reshape(row_count, head_size, head_count)

    def block_gate(weight, bias):
        product = jnp.einsum(
            "tih,ijh->tjh",
            heads_view,
            weight.reshape(head_size, group_count, head_count),
            preferred_element_type=float_type,
        )
        return product.reshape(row_count, lane_count) + bias.astype(float_type)

    a_pre = block_gate(a_weight, a_bias)
    i_pre = block_gate(i_weight, i_bias)
    recall = jax.nn.sigmoid(a_pre)
    input_gate = jax.nn.sigmoid(i_pre)
    decay_rate = jax.nn.softplus(decay)
    log_decay = -8.0 * recall * decay_rate
    factor = jnp.exp(log_decay)
    double_decay = jnp.exp(2.0 * log_decay)
    one_minus = -jnp.expm1(2.0 * log_decay)
    root_value = jnp.sqrt(jnp.maximum(one_minus, SQUARE_FLOOR))
    position = seq_index * row_count + jnp.arange(row_count)
    anchor = (position == 0)[:, None]
    root_scale = jnp.where(anchor, 1.0, root_value)
    root_live = jnp.logical_and(one_minus > SQUARE_FLOOR, jnp.logical_not(anchor))
    driven = conv_value * input_gate * root_scale
    local_prod, local_state = lax.associative_scan(linear_pair, (factor, driven))

    def relay_step(turn_number, carried):
        return from_behind(local_prod[-1] * carried + local_state[-1], "seq", 1)

    state_entry = lax.fori_loop(
        0, lax.axis_size("seq") - 1, relay_step, jnp.zeros_like(local_state[-1])
    )
    state_all = local_state + local_prod * state_entry
    mixed_in = (state_all * y_gate).astype(half_type)
    branch_part = jnp.einsum("tc,dc->td", mixed_in, out_full, preferred_element_type=float_type)
    branch = lax.psum(branch_part, "head")
    residual = tokens_wide + branch
    second_gain = mlp_gain.astype(float_type)
    second_low = rms_norm(residual, second_gain).astype(half_type)
    gate_pre = jnp.dot(second_low, gate_full, preferred_element_type=float_type)
    up_pre = jnp.dot(second_low, up_full, preferred_element_type=float_type)
    gate_act = jax.nn.gelu(gate_pre)
    hidden = (gate_act * up_pre).astype(half_type)
    mlp_part = jnp.einsum("tf,df->td", hidden, down_full, preferred_element_type=float_type)
    own_columns = lax.psum_scatter(mlp_part, "head", scatter_dimension=1, tiled=True)
    column_count = model_width // head_devices
    mixed = (
        lax.dynamic_slice_in_dim(residual, head_index * column_count, column_count, 1) + own_columns
    ).astype(half_type)
    regathered = (
        lax.all_gather(x_weight, "seq", axis=0, tiled=True),
        lax.all_gather(y_weight, "seq", axis=0, tiled=True),
        lax.all_gather(out_weight, "seq", axis=0, tiled=True),
        lax.all_gather(gate_weight, "seq", axis=0, tiled=True),
        lax.all_gather(up_weight, "seq", axis=0, tiled=True),
        lax.all_gather(down_weight, "seq", axis=0, tiled=True),
    )
    x_full, y_full, out_full, gate_full, up_full, down_full = regathered
    hidden_grad = jnp.dot(cotangent, down_full, preferred_element_type=float_type)
    gate_grad = gelu_back(gate_pre, hidden_grad * up_pre).astype(half_type)
    up_grad = (hidden_grad * gate_act).astype(half_type)
    second_part = jnp.einsum(
        "tf,df->td", gate_grad, gate_full, preferred_element_type=float_type
    ) + jnp.einsum("tf,df->td", up_grad, up_full, preferred_element_type=float_type)
    second_grad = lax.psum(second_part, "head")
    resid_back, mlp_gain_term = jax.vjp(rms_norm, residual, second_gain)[1](second_grad)
    resid_grad = cotangent.astype(float_type) + resid_back
    branch_grad = resid_grad.astype(half_type)
    mixed_grad = jnp.dot(branch_grad, out_full, preferred_element_type=float_type)
    state_grad = mixed_grad * y_gate
    y_grad = gelu_back(y_branch, mixed_grad * state_all).astype(half_type)
    next_factor = jnp.concatenate([factor[1:], jnp.ones_like(factor[:1])], axis=0)
    back_prod, back_adjoint = lax.associative_scan(
        linear_pair, (next_factor[::-1], state_grad[::-1])
    )
    back_prod = back_prod[::-1]
    back_adjoint = back_adjoint[::-1]
    tail_prod = factor[0] * back_prod[0]
    tail_value = factor[0] * back_adjoint[0]

    def relay_back(turn_number, carried):
        return from_behind(tail_value + tail_prod * carried, "seq", -1)

    exit_carry = lax.fori_loop(0, lax.axis_size("seq") - 1, relay_back, jnp.zeros_like(tail_value))
    adjoint = back_adjoint + back_prod * exit_carry
    prev_state = jnp.concatenate([state_entry[None], state_all[:-1]], axis=0)
    scale_grad = adjoint * conv_value * input_gate
    log_grad = adjoint * prev_state * factor + jnp.where(
        root_live, -scale_grad * double_decay / root_value, 0.0
    )
    a_grad = (log_grad * (-8.0 * decay_rate) * recall * (1.0 - recall)).astype(half_type)
    i_grad = (adjoint * conv_value * root_scale * input_gate * (1.0 - input_gate)).astype(half_type)
    decay_term = jnp.sum(log_grad * (-8.0 * recall), axis=0) * jax.nn.sigmoid(decay)
    a_bias_term = jnp.sum(a_grad.astype(float_type), axis=0)
    i_bias_term = jnp.sum(i_grad.astype(float_type), axis=0)

    def gate_back(grad, weight):
        grad_view = grad.reshape(row_count, group_count, head_count)
        weight_term = jnp.einsum(
            "tih,tjh->ijh", heads_view, grad_view, preferred_element_type=float_type
        ).reshape(head_size, lane_count)
        input_term = jnp.einsum(
            "tjh,ijh->tih",
            grad_view,
            weight.reshape(head_size, group_count, head_count),
            preferred_element_type=float_type,
        )
        return (weight_term, input_term)

    a_wgrad, a_input = gate_back(a_grad, a_weight)
    i_wgrad, i_input = gate_back(i_grad, i_weight)
    gate_input_grad = lax.psum_scatter(
        (a_input + i_input).reshape(row_count, head_size * head_count),
        "head",
        scatter_dimension=1,
        tiled=True,
    )
    conv_grad = gate_input_grad + adjoint * input_gate * root_scale
    right_edge = from_behind(conv_grad[: CONV - 1], "seq", -1)
    extended_grad = jnp.concatenate([conv_grad, right_edge], axis=0)
    x_branch_grad = sum(
        (
            conv_taps[lag_index] * extended_grad[lag_index : lag_index + row_count]
            for lag_index in range(CONV)
        )
    ).astype(half_type)
    conv_wgrad = jnp.stack(
        [
            jnp.sum(
                conv_grad * padded[CONV - 1 - lag_index : CONV - 1 - lag_index + row_count], axis=0
            )
            for lag_index in range(CONV)
        ],
        axis=0,
    )
    conv_bgrad = jnp.sum(conv_grad, axis=0)
    first_part = jnp.einsum(
        "tc,dc->td", x_branch_grad, x_full, preferred_element_type=float_type
    ) + jnp.einsum("tc,dc->td", y_grad, y_full, preferred_element_type=float_type)
    first_grad = lax.psum(first_part, "head")
    tokens_back, norm_gain_term = jax.vjp(rms_norm, tokens_wide, first_gain)[1](first_grad)
    tokens_grad = resid_grad + tokens_back
    pairings = (
        (first_low, x_branch_grad),
        (first_low, y_grad),
        (branch_grad, mixed_in),
        (second_low, gate_grad),
        (second_low, up_grad),
        (cotangent, hidden),
    )
    products = tuple(
        (
            jnp.einsum("td,tc->dc", left, right, preferred_element_type=float_type)
            for left, right in pairings
        )
    )
    weight_sums = lax.psum_scatter(products, "seq", scatter_dimension=0, tiled=True)
    small_sums = lax.psum(
        (
            norm_gain_term,
            conv_wgrad,
            conv_bgrad,
            a_wgrad,
            a_bias_term,
            i_wgrad,
            i_bias_term,
            decay_term,
            mlp_gain_term,
        ),
        "seq",
    )
    return (
        mixed,
        tokens_grad,
        small_sums[0],
        weight_sums[0],
        weight_sums[1],
        small_sums[1],
        small_sums[2],
        small_sums[3],
        small_sums[4],
        small_sums[5],
        small_sums[6],
        small_sums[7],
        weight_sums[2],
        small_sums[8],
        weight_sums[3],
        weight_sums[4],
        weight_sums[5],
    )


def solution(mesh):
    sizes = mesh.shape["seq"], mesh.shape["head"]

    def body(*args):
        z = Size(sizes, args[0], args[2], args[6], args[13])
        return dealt(z, *args) if z.fits() else gathered_weights(*args)

    return jax.shard_map(
        body,
        mesh=mesh,
        in_specs=(
            P("seq", None),
            P(),
            P("seq", "head"),
            P("seq", "head"),
            P(None, "head"),
            P("head"),
            P(None, "head"),
            P("head"),
            P(None, "head"),
            P("head"),
            P("head"),
            P("seq", "head"),
            P(),
            P("seq", "head"),
            P("seq", "head"),
            P("seq", "head"),
            P("seq", None),
        ),
        out_specs=(
            P("seq", "head"),
            P("seq", None),
            P(),
            P("seq", "head"),
            P("seq", "head"),
            P(None, "head"),
            P("head"),
            P(None, "head"),
            P("head"),
            P(None, "head"),
            P("head"),
            P("head"),
            P("seq", "head"),
            P(),
            P("seq", "head"),
            P("seq", "head"),
            P("seq", "head"),
        ),
        check_vma=False,
    )
```

```python
import functools

import jax
import jax.numpy as jnp
from jax import lax
from jax.experimental import pallas as pl
from jax.experimental.pallas import tpu as pltpu
from jax.sharding import PartitionSpec as P

CONV = 4
EPSILON = 1e-06
SQUARE_FLOOR = 2.5e-07
MESH = pl.DeviceIdType.MESH
F32 = jnp.float32
BF16 = jnp.bfloat16
LANES = 128
EDGE = 16
VM = pltpu.VMEM
ANY = pl.ANY
NN = (((1,), (0,)), ((), ()))
NT = (((1,), (1,)), ((), ()))
TN = (((0,), (0,)), ((), ()))


def mm(left, right, dims=NN):
    return lax.dot_general(left, right, dims, preferred_element_type=F32)


def gelu_pair(values):
    scale = 0.7978845608028654
    square = values * values
    bend = jnp.tanh(scale * values * (1.0 + 0.044715 * square))
    half = 0.5 * (1.0 + bend)
    slope = half + 0.5 * values * (1.0 - bend * bend) * scale * (1.0 + 3.0 * 0.044715 * square)
    return values * half, slope


def minus_expm1(v):
    series = jnp.full_like(v, 1.0 / 40320.0)
    for divisor in (5040.0, 720.0, 120.0, 24.0, 6.0, 2.0, 1.0):
        series = series * v + 1.0 / divisor
    return jnp.where(v > -0.35, -v * series, 1.0 - jnp.exp(v))


def when(condition, action):
    if condition is None:
        action()
    else:
        pl.when(condition)(action)


class Copy:
    def __init__(self, item, goes, comes):
        self.item, self.goes, self.comes = item, goes, comes

    def start(self):
        when(self.goes, lambda: self.item.start())

    def wait_send(self):
        when(self.goes, lambda: self.item.wait_send())

    def wait_recv(self):
        when(self.comes, lambda: self.item.wait_recv())

    def arrived(self):
        self.item.wait_recv()


class Wire:
    def __init__(self, send, recv):
        self.send, self.recv, self.count, self.open = send, recv, 0, []

    def make(self, src, dst, peer, goes=None, comes=None):
        slot = self.count
        self.count += 1
        item = pltpu.make_async_remote_copy(
            src_ref=src,
            dst_ref=dst,
            send_sem=self.send.at[slot],
            recv_sem=self.recv.at[slot],
            device_id=peer,
            device_id_type=MESH,
        )
        copy = Copy(item, goes, comes)
        self.open.append(copy)
        return copy

    def copy(self, src, dst, peer, goes=None, comes=None):
        copy = self.make(src, dst, peer, goes, comes)
        copy.start()
        return copy

    def close(self):
        for item in self.open:
            item.wait_send()
        assert self.count <= self.send.shape[0], self.count


class Chain:
    def __init__(self, wire, count, s, h):
        self.wire, self.count, self.s, self.h, self.zi = wire, count, s, h, s // 2
        self.up = (jnp.minimum(s + 2, 2 * count - 2 + s % 2), h)
        self.down = (jnp.maximum(s - 2, s % 2), h)

    def gather(self, view):
        zi, last = self.zi, self.count - 1

        def hop(step, way):
            index = zi - way * step
            held = jnp.logical_and(index >= 0, index <= last)
            goes = jnp.logical_and(held, zi < last if way > 0 else zi > 0)
            here = index - way
            comes = jnp.logical_and(here >= 0, here <= last)
            block = view(jnp.clip(index, 0, last))
            peer = self.up if way > 0 else self.down
            return self.wire.copy(block, block, peer, goes, comes), comes, jnp.clip(here, 0, last)

        flight = [hop(0, 1), hop(0, -1)]
        yield None, zi
        for step in range(last):
            for side, way in enumerate((1, -1)):
                item, comes, index = flight[side]
                item.wait_recv()
                if step + 1 < last:
                    flight[side] = hop(step + 1, way)
                yield comes, index

    def order(self):
        count = self.count
        low = list(reversed(range(count // 2, count))) + list(range(count // 2))
        near = self.zi < count // 2
        return [jnp.where(near, d, count - 1 - d) for d in low]

    def passes(self, d, src, up, down):
        zi, last, wire = self.zi, self.count - 1, self.wire
        base = wire.count
        wire.count = base + d
        first = wire.make(src, up, self.up, zi < d, jnp.logical_and(zi > 0, zi <= d))
        wire.count = base + self.count + d
        second = wire.make(src, down, self.down, zi > d, jnp.logical_and(zi < last, zi >= d))
        wire.count = base
        return first, second

    def between(self, d):
        zi, last = self.zi, self.count - 1
        return jnp.logical_and(zi > 0, zi < d), jnp.logical_and(zi < last, zi > d)

    def ends(self, d):
        zi, last = self.zi, self.count - 1
        return jnp.logical_and(zi == d, zi > 0), jnp.logical_and(zi == d, zi < last)

    def scatter(self, block, work, out, up, down, own):
        zi = self.zi
        flight = []
        base = self.wire.count
        self.wire.count += 2 * self.count

        def take(item, got, into):
            def action():
                item.arrived()
                into[...] = into[...] + got[...].astype(F32)
            return action

        for d in self.order():
            work[...] = block(d)
            kept, self.wire.count = self.wire.count, base
            ups, downs = self.passes(d, out.at[d], up.at[d], down.at[d])
            self.wire.count = kept
            flight.append((d, ups, downs))
            below, above = self.between(d)
            when(below, take(ups, up.at[d], work))
            when(above, take(downs, down.at[d], work))

            def give(d=d):
                out[d] = work[...].astype(BF16)

            def keep():
                own[...] = work[...]

            when(zi != d, give)
            when(zi == d, keep)
            ups.start()
            downs.start()
            yield d
        for d, ups, downs in flight:
            below, above = self.ends(d)
            when(below, take(ups, up.at[d], own))
            when(above, take(downs, down.at[d], own))


class HeadGather:
    def __init__(self, wire, s, h, view):
        self.wire, self.s, self.h, self.view = wire, s, h, view
        self.items = {1: self.send(0, 1), 2: self.send(0, 2)}

    def send(self, j, to):
        block = self.view(self.h ^ j)
        return self.wire.copy(block, block, (self.s, self.h ^ to))

    def wait(self, j):
        if j == 2:
            self.items[2].wait_recv()
            self.items[3] = self.send(2, 1)
        else:
            self.items[j].wait_recv()

    def wait_all(self):
        for j in (2, 1, 3):
            self.wait(j)


def head_scatter(wire, s, h, block, out, got):
    core, other = (s, h ^ 1), (s, h ^ 2)
    flight = {}
    for j in (3, 1):
        out[j] = block(j).astype(BF16)
        flight[j] = wire.copy(out.at[j], got.at[j], core)
    part = block(2)
    flight[3].wait_recv()
    out[2] = (part + got[3].astype(F32)).astype(BF16)
    flight[2] = wire.copy(out.at[2], got.at[2], other)
    total = block(0)
    flight[1].wait_recv()
    total = total + got[1].astype(F32)

    def finish():
        flight[2].wait_recv()
        return total + got[2].astype(F32)

    return finish


def drain(*steps):
    steps = list(steps)
    while steps:
        steps = [step for step in steps if next(step, step) is not step]


def advance(step, count=1):
    for _ in range(count):
        next(step, None)


def greet(peers):
    barrier = pltpu.get_barrier_semaphore()
    for peer in peers:
        pl.semaphore_signal(barrier, inc=1, device_id=peer, device_id_type=MESH)
    pl.semaphore_wait(barrier, len(peers))


def place():
    return lax.axis_index("seq"), lax.axis_index("head")


def at(ref, rows, row_count, lanes, lane_count):
    return ref.at[
        pl.ds(pl.multiple_of(rows, EDGE), row_count),
        pl.ds(pl.multiple_of(lanes, LANES), lane_count),
    ]


def sem(count):
    return pltpu.SemaphoreType.DMA((count,))


def call(body, name, cid, outs, scratch, args, spaces=(), far=False, limit=62, us=150):
    return pl.pallas_call(
        body,
        out_shape=outs,
        in_specs=[
            pl.BlockSpec(memory_space=ANY if i in spaces else VM) for i in range(len(args))
        ],
        out_specs=[pl.BlockSpec(memory_space=ANY if far else VM) for _ in outs],
        scratch_shapes=scratch,
        compiler_params=pltpu.CompilerParams(
            collective_id=cid, has_side_effects=True, vmem_limit_bytes=limit << 20
        ),
        cost_estimate=pl.CostEstimate(
            flops=us * 10**6, bytes_accessed=us * 3 * 10**6, transcendentals=0
        ),
        name=name,
    )(*args)


def sds(shape, kind):
    return jax.ShapeDtypeStruct(shape, kind)


class Size:
    def __init__(self, mesh_sizes, tokens, x_weight, a_weight, gate_weight):
        self.S, self.H = mesh_sizes
        self.Z = self.S // 2
        self.R, self.D = tokens.shape
        self.T = self.S * self.R
        self.Ds, self.C = x_weight.shape
        self.HS = a_weight.shape[0]
        self.heads = self.H * self.C // self.HS
        self.F2 = gate_weight.shape[1]
        self.TB = self.T // self.H
        self.U = 2 * LANES
        self.NI = self.HS // self.H

    def fits(self):
        tiles = self.F2 // LANES
        return (
            self.S == 8
            and self.H == 4
            and self.Z == self.H
            and (2 * self.Ds) % LANES == 0
            and (2 * self.HS // self.S) % EDGE == 0
            and self.D == self.H * self.C
            and self.F2 % LANES == 0
            and 2 * (self.S - 1) < tiles <= 2 * self.S
            and self.T <= 1024
            and self.R % LANES == 0
            and self.C % LANES == 0
            and self.Ds % (2 * EDGE) == 0
            and (self.Ds // self.H) % EDGE == 0
            and self.NI % EDGE == 0
        )


def gate_weight_of(z, spread, mask, weight, k):
    rows = weight[pl.ds(pl.multiple_of(k * z.NI, EDGE), z.NI), :]
    return mm(spread[...], rows).astype(BF16) * mask[...]


def shifted(values, by, fill, row):
    count = values.shape[0]
    moved = pltpu.roll(values, by % count, 0)
    inside = row >= by if by > 0 else row < count + by
    return jnp.where(inside, moved, fill)


def scan_rows(prod, value, sign):
    row = lax.broadcasted_iota(jnp.int32, prod.shape, 0)
    by = 1
    while by < prod.shape[0]:
        value = prod * shifted(value, sign * by, 0.0, row) + value
        prod = prod * shifted(prod, sign * by, 1.0, row)
        by *= 2
    return prod, value


def decay_terms(a_pre, i_pre, rate, anchor):
    recall = jax.nn.sigmoid(a_pre)
    input_gate = jax.nn.sigmoid(i_pre)
    log_decay = -8.0 * recall * rate
    factor = jnp.exp(log_decay)
    one_minus = minus_expm1(2.0 * log_decay)
    root_value = jnp.sqrt(jnp.maximum(one_minus, SQUARE_FLOOR))
    root_scale = jnp.where(anchor, 1.0, root_value)
    return recall, input_gate, factor, one_minus, root_value, root_scale


def anchor_of(z, s, width):
    row = lax.broadcasted_iota(jnp.int32, (z.R, width), 0)
    return jnp.logical_and(row == 0, s == 0)


def head_maps(z, spread, mask):
    def parts(shape, axis):
        channel = lax.broadcasted_iota(jnp.int32, shape, axis).astype(F32)
        row = jnp.floor((channel + 0.5) * (1.0 / z.heads))
        return row, channel - row * z.heads

    across = lax.broadcasted_iota(jnp.int32, (z.C, z.NI), 1).astype(F32)
    spread[...] = jnp.where(parts((z.C, z.NI), 0)[0] == across, 1.0, 0.0).astype(BF16)
    same = parts((z.C, z.C), 0)[1] == parts((z.C, z.C), 1)[1]
    mask[...] = jnp.where(same, 1.0, 0.0).astype(BF16)


class Deal:
    def __init__(self, wire, z, s, h):
        self.wire, self.z, self.s, self.h = wire, z, s, h
        self.tiles = z.F2 // LANES
        self.sent = []

    def rows(self, owner):
        return pl.ds(pl.multiple_of(owner * self.z.Ds, EDGE), self.z.Ds)

    def post(self, src, dst, peer, part, goes, comes):
        wire = self.wire
        item = pltpu.make_async_remote_copy(
            src_ref=src,
            dst_ref=dst,
            send_sem=wire.send.at[wire.count],
            recv_sem=wire.recv.at[wire.count],
            device_id=(peer, self.h),
            device_id_type=MESH,
        )
        wire.count += 1
        self.sent.append((item, part, goes, comes))
        if part == 0:
            item.start()
        else:
            @pl.when(goes)
            def _():
                item.start()

    def out(self, src, dst, offsets):
        z = self.z
        for k in offsets:
            peer = self.s ^ k
            for part in range(2):
                tile = 2 * peer + part
                self.post(
                    at(src, 0, z.Ds, jnp.minimum(tile, self.tiles - 1) * LANES, LANES),
                    dst.at[self.rows(self.s), pl.ds(part * LANES, LANES)],
                    peer,
                    part,
                    tile < self.tiles,
                    2 * self.s + part < self.tiles,
                )

    def back(self, src, dst, offsets):
        z = self.z
        for k in offsets:
            peer = self.s ^ k
            for part in range(2):
                tile = 2 * self.s + part
                lane = jnp.minimum(tile, self.tiles - 1) * LANES
                self.post(
                    src.at[self.rows(peer), pl.ds(part * LANES, LANES)],
                    at(dst, 0, z.Ds, lane, LANES),
                    peer,
                    part,
                    tile < self.tiles,
                    2 * peer + part < self.tiles,
                )

    def steps(self, how, pairs):
        for src, dst in pairs:
            for offsets in ((4, 2), (5, 3), (6, 1), (7,)):
                how(src, dst, offsets)
                yield

    def back_own(self, src, dst):
        z, s = self.z, self.s
        at(dst, 0, z.Ds, 2 * s * LANES, LANES)[...] = src[self.rows(s), 0:LANES]

        @pl.when(2 * s + 1 < self.tiles)
        def _():
            lane = jnp.minimum(2 * s + 1, self.tiles - 1) * LANES
            at(dst, 0, z.Ds, lane, LANES)[...] = src[self.rows(s), LANES : 2 * LANES]

    def wait(self, sent=None):
        for item, part, goes, comes in self.sent if sent is None else sent:
            if part == 0:
                item.wait()
            else:
                @pl.when(goes)
                def _(item=item):
                    item.wait_send()

                @pl.when(comes)
                def _(item=item):
                    item.wait_recv()
        if sent is None:
            self.sent = []


def own_block(z, src, dst, sems, s):
    tiles = z.F2 // LANES
    rows = pl.ds(pl.multiple_of(s * z.Ds, EDGE), z.Ds)
    first = pltpu.make_async_copy(
        at(src, 0, z.Ds, 2 * s * LANES, LANES), dst.at[rows, pl.ds(0, LANES)], sems.at[0]
    )
    second = pltpu.make_async_copy(
        at(src, 0, z.Ds, jnp.minimum(2 * s + 1, tiles - 1) * LANES, LANES),
        dst.at[rows, pl.ds(LANES, LANES)],
        sems.at[1],
    )
    whole = 2 * s + 1 < tiles
    first.start()

    @pl.when(whole)
    def _():
        second.start()

    @pl.when(jnp.logical_not(whole))
    def _():
        dst[:, LANES : 2 * LANES] = jnp.zeros((z.D, LANES), BF16)

    def wait():
        first.wait()

        @pl.when(whole)
        def _():
            second.wait()

    return wait


def chain_scratch(z, rows, width):
    return [VM((rows, width), F32)] + [VM((z.Z, rows, width), BF16)] * 3 + [VM((rows, width), F32)]


def row_blocks(z, buf):
    return lambda index: buf.at[pl.ds(pl.multiple_of(index * z.R, EDGE), z.R), :]


class Grid:
    def __init__(self, s, h):
        self.s, self.h = s, h
        self.x, self.y, self.core = (s ^ 1, h), (s, h ^ 2), (s, h ^ 1)

    def z(self, kz):
        return (self.s ^ (2 * kz), self.h)


def gather_all(wire, z, g, region):
    s, h, xi = g.s, g.h, g.s % 2
    chain = Chain(wire, z.Z, s, h)
    arrivals = chain.gather(lambda index: region(2 * index + xi, h, None))
    mine = next(arrivals)
    yield None
    blocks, near, far, core = [], {}, {}, []

    def send(a, b, half, peer, held):
        return wire.copy(region(a, b, half), region(a, b, half), peer, held, held)

    def one(i):
        held, index = next(arrivals) if i else mine
        a = 2 * index + xi
        blocks.append((held, a))
        near[0, i] = send(a, h, 0, g.x, held)
        near[1, i] = send(a, h, 1, g.y, held)
        far[0, i, 0] = send(a, h, 0, g.y, held)
        far[1, i, 0] = send(a, h, 1, g.x, held)
        core.append(send(a, h, None, g.core, held))

    def two(i):
        held, a = blocks[i]
        near[0, i].wait_recv()
        far[0, i, 1] = send(a ^ 1, h, 0, g.y, held)
        core.append(send(a ^ 1, h, 0, g.core, held))
        near[1, i].wait_recv()
        far[1, i, 1] = send(a, h ^ 2, 1, g.x, held)
        core.append(send(a, h ^ 2, 1, g.core, held))

    def three(i):
        held, a = blocks[i]
        far[0, i, 0].wait_recv()
        core.append(send(a, h ^ 2, 0, g.core, held))
        far[1, i, 0].wait_recv()
        core.append(send(a ^ 1, h, 1, g.core, held))

    def four(i):
        held, a = blocks[i]
        far[0, i, 1].wait_recv()
        core.append(send(a ^ 1, h ^ 2, 0, g.core, held))
        far[1, i, 1].wait_recv()
        core.append(send(a ^ 1, h ^ 2, 1, g.core, held))

    count = 2 * z.Z - 1
    stages = (one, two, three, four)
    for turn in range(count + 6):
        for lag, stage in enumerate(stages):
            if 0 <= turn - 2 * lag < count:
                stage(turn - 2 * lag)
        yield turn
    for item in core:
        item.wait_recv()


def gather_copies(z):
    return 2 * (z.Z - 1) + 13 * (2 * z.Z - 1)


class SumAll:
    def __init__(self, wire, z, g, region, bufs):
        self.wire, self.zz, self.g, self.region = wire, z, g, region
        self.from_core, self.hop1, self.hop2, self.up, self.down, self.own = bufs
        self.chain = Chain(wire, z.Z, g.s, g.h)
        self.flight = {}
        self.base = wire.count
        wire.count += self.copies(z)

    @staticmethod
    def copies(z):
        return z.Z * (4 + 4 + 2) + 4 * z.Z

    @staticmethod
    def scratch(z, rows, lanes):
        half = rows // 2
        return [
            VM((z.Z, 4, rows, lanes), BF16),
            VM((z.Z, 4, half, lanes), BF16),
            VM((z.Z, 2, half, lanes), BF16),
            VM((z.Z, 2, half, lanes), BF16),
            VM((z.Z, 2, half, lanes), BF16),
            VM((2, half, lanes), F32),
        ]

    def put(self, a, b, half, dst, peer, slot):
        kept, self.wire.count = self.wire.count, self.base + slot
        item = self.wire.copy(self.region(a, b, half), dst, peer)
        self.wire.count = kept
        return item

    def add(self, a, b, half, got):
        spot = self.region(a, b, half)
        spot[...] = (spot[...].astype(F32) + got[...].astype(F32)).astype(BF16)

    def core(self, i, d):
        g = self.g
        for k in range(4):
            a, b = (2 * d + g.s % 2) ^ (k // 2), g.h ^ 1 ^ (2 * (k % 2))
            self.flight["core", i, k] = self.put(
                a, b, None, self.from_core.at[d, k], g.core, 10 * i + k
            )

    def first(self, i, d):
        g = self.g
        rows = self.hop1.shape[2]
        for k in (1, 3, 2, 0):
            self.flight["core", i, k].wait_recv()
            a, b = (2 * d + g.s % 2) ^ (k // 2), g.h ^ (2 * (k % 2))
            for half in range(2):
                self.add(a, b, half, self.from_core.at[d, k, pl.ds(half * rows, rows), :])
            if k % 2:
                key = k // 2
                self.flight["one", i, key] = self.put(
                    a, b, 0, self.hop1.at[d, key], g.y, 10 * i + 4 + key
                )
            if k // 2:
                key = 2 + k % 2
                self.flight["one", i, key] = self.put(
                    a, b, 1, self.hop1.at[d, key], g.x, 10 * i + 4 + key
                )

    def second(self, i, d):
        g = self.g
        a = 2 * d + g.s % 2
        for key in (1, 0):
            self.flight["one", i, key].wait_recv()
            self.add(a ^ key, g.h, 0, self.hop1.at[d, key])
        self.flight["two", i, 0] = self.put(
            a ^ 1, g.h, 0, self.hop2.at[d, 0], g.x, 10 * i + 8
        )
        for key in (3, 2):
            self.flight["one", i, key].wait_recv()
            self.add(a, g.h ^ (2 * (key - 2)), 1, self.hop1.at[d, key])
        self.flight["two", i, 1] = self.put(
            a, g.h ^ 2, 1, self.hop2.at[d, 1], g.y, 10 * i + 9
        )

    def third(self, i, d):
        g, chain = self.g, self.chain
        a, count = 2 * d + g.s % 2, self.zz.Z
        below, above = chain.between(d)
        for half in range(2):
            self.flight["two", i, half].wait_recv()
            self.add(a, g.h, half, self.hop2.at[d, half])
            kept = self.wire.count
            self.wire.count = self.base + 10 * count + 2 * count * half
            ups, downs = chain.passes(
                d, self.region(a, g.h, half), self.up.at[d, half], self.down.at[d, half]
            )
            self.wire.count = kept
            self.flight["z", i, half] = d, ups, downs
            when(below, self.taken(ups, a, half, self.up.at[d, half]))
            when(above, self.taken(downs, a, half, self.down.at[d, half]))
            ups.start()
            downs.start()

    def taken(self, item, a, half, got):
        def action():
            item.arrived()
            self.add(a, self.g.h, half, got)
        return action

    def finish(self, half):
        g = self.g
        own = self.own.at[half]
        own[...] = self.region(g.s, g.h, half)[...].astype(F32)

        def add(item, got):
            def action():
                item.arrived()
                own[...] = own[...] + got[...].astype(F32)
            return action

        for i in range(self.zz.Z):
            d, ups, downs = self.flight["z", i, half]
            below, above = self.chain.ends(d)
            when(below, add(ups, self.up.at[d, half]))
            when(above, add(downs, self.down.at[d, half]))
        return own[...]

    def run(self, produce):
        order = self.chain.order()
        steps = [
            lambda i, d: (produce(d), self.core(i, d)),
            self.first,
            self.second,
            self.third,
        ]
        count = len(order)
        for turn in range(count + len(steps) - 1):
            for stage in range(len(steps)):
                if 0 <= turn - stage < count:
                    steps[stage](turn - stage, order[turn - stage])
                    yield turn


def halves(ref, rows, row_count, lanes, lane_count, half):
    if half is not None:
        row_count //= 2
        rows = rows + half * row_count
    return at(ref, rows, row_count, lanes, lane_count)


def region_of(z, ref):
    return lambda a, b, half: halves(
        ref, a // 2 * 2 * z.Ds, 2 * z.Ds, (2 * b + a % 2) * z.R, z.R, half
    )


FRONT_RESULTS = 26


def front_kernel(
    z, tok, gain1, gain2, xw, yw, ow, conv_w, conv_b, a_b, i_b, rate, slope_d, aw, iw, cot_in,
    gw_in, uw_in, dw_in, *rest
):
    outs, rest = rest[:FRONT_RESULTS], rest[FRONT_RESULTS:]
    held, rest = rest[:FRONT_RESULTS], rest[FRONT_RESULTS:]
    (
        xw2, yw2, ow2, tok2, fn2, rn, yb, pad, conv, a_o, i_o, st, entry_o, mix, res,
        vec, mask, spread, gain_q, hid, dw, uwg_o, dwg_o, back_g, gsum_o, bg_o,
    ) = held
    (
        turned, fnt, x1, x2, x3, x4, x5, y1, y2, y3, y4, y5, sums, tot, part, got, edge, gains,
        cot, gw, uw, xt, gwt, uwt, dwt, gwg, hg, gg, ug, gs, us, rs, wide,
        c1, c2, c3, c4, c5, c6, stat, send, recv, own_sem, out_sem,
    ) = rest
    leaving = []

    def flush(first, last):
        for index in range(first, last):
            copy = pltpu.make_async_copy(held[index], outs[index], out_sem.at[index])
            copy.start()
            leaving.append(copy)

    s, h = place()
    S, H, R, D, T, Ds, C, Z = z.S, z.H, z.R, z.D, z.T, z.Ds, z.C, z.Z
    DG = 2 * Ds
    Q = DG // H
    zi, xi = s // 2, s % 2
    after, before = lax.rem(s + 1, S), lax.rem(s + S - 1, S)
    greet(
        [(s ^ k, h) for k in range(1, S)]
        + [(s, h ^ j) for j in range(1, H)]
        + [(after, h), (before, h)]
    )
    wire = Wire(send, recv)
    g = Grid(s, h)
    chain = Chain(wire, Z, s, h)
    deal = Deal(wire, z, s, h)
    pairs = ((gw_in, gw), (uw_in, uw), (dw_in, dw))
    dealing = deal.steps(deal.out, pairs)
    half = pl.ds(pl.multiple_of(xi * Ds, EDGE), Ds)
    twins = [wire.copy(xw, xw2.at[half, :], (s ^ 1, h))]
    turned[...] = tok[...].astype(F32).T.astype(BF16)
    quarter = pl.ds(pl.multiple_of(h * Q, EDGE), Q)
    my_lanes = pl.ds(pl.multiple_of(zi * R, LANES), R)

    def group(index):
        return pl.ds(pl.multiple_of(index * DG + h * Q, EDGE), Q)

    first = [
        wire.copy(turned.at[group(zi ^ kz), :], tok2.at[quarter, my_lanes], (s ^ (2 * kz), h))
        for kz in range(1, Z)
    ]
    column = turned[...].astype(F32)
    mean = jnp.sum(column * column, axis=0, keepdims=True) / z.D
    rn[zi] = jnp.broadcast_to(lax.rsqrt(mean + EPSILON), (8, R))
    for kz in range(1, Z):
        first.append(wire.copy(rn.at[zi], rn.at[zi], (s ^ (2 * kz), h)))
    tok2[quarter, my_lanes] = turned[group(zi), :]
    vec[...] = jnp.zeros_like(vec)
    vec[0:CONV, :] = conv_w[...].astype(F32)
    for index, ref in enumerate((conv_b, a_b, i_b, rate, slope_d)):
        vec[4 + index : 5 + index, :] = ref[...].astype(F32)[None, :]
    eight = lax.broadcasted_iota(jnp.int32, (8, D), 0)
    gains[...] = jnp.where(
        eight == 0, gain1[...].astype(F32)[None, :], gain2[...].astype(F32)[None, :]
    ).T
    gain_q[...] = gains[pl.ds(pl.multiple_of(zi * DG + h * Q, EDGE), Q), :]
    gain_s = gains[pl.ds(pl.multiple_of(zi * DG, EDGE), DG), 0:1]
    head_maps(z, spread, mask)
    xw2[half, :] = xw[...]
    yw2[half, :] = yw[...]
    ow2[half, :] = ow[...]
    pending = [
        own_block(z, src, dst, own_sem.at[pl.ds(2 * i, 2)], s)
        for i, (src, dst) in enumerate(pairs)
    ]
    W = z.D // H

    def corner(a, b, half):
        return halves(cot, a * R, R, b * W, W, half)

    corner(s, h, None)[...] = cot_in[:, pl.ds(pl.multiple_of(h * W, LANES), W)]
    cot_in_all = gather_all(wire, z, g, corner)
    advance(cot_in_all)
    advance(dealing, 2)
    for item in first:
        item.wait_recv()
    HeadGather(
        wire, s, h, lambda j: tok2.at[pl.ds(pl.multiple_of(j * Q, EDGE), Q), :]
    ).wait_all()
    for b in range(Z):
        cut = slice(b * R, b * R + R)
        fn2[:, cut] = (tok2[:, cut].astype(F32) * rn[b, 0:1, :] * gain_s).astype(BF16)
    twins[0].wait_recv()
    for src, dst in ((yw, yw2), (ow, ow2)):
        twins.append(wire.copy(src, dst.at[half, :], (s ^ 1, h)))

    def x_part(d):
        lanes = pl.ds(pl.multiple_of(d * R, LANES), R)
        fnt[d] = fn2[:, lanes].astype(F32).T.astype(BF16)
        return mm(fnt[d], xw2[...])

    x_sum = chain.scatter(x_part, x1, x2, x3, x4, x5)
    advance(x_sum, Z)
    advance(cot_in_all)
    drain(x_sum)
    x_low = x5[...].astype(BF16)
    edge[0] = x_low[R - EDGE : R, :]
    halo = wire.copy(edge.at[0], edge.at[1], (after, h))
    twins[1].wait_recv()
    y_sum = chain.scatter(lambda d: mm(fnt[d], yw2[...]), y1, y2, y3, y4, y5)
    advance(y_sum, 1)
    advance(cot_in_all, 2)
    pad[pl.ds(EDGE, R), :] = x_low.astype(F32)
    halo.wait_recv()
    pad[pl.ds(0, EDGE), :] = jnp.where(s == 0, 0.0, edge[1].astype(F32))
    out = jnp.broadcast_to(vec[4:5, :], (R, C))
    for lag in range(CONV):
        out = out + vec[lag : lag + 1, :] * pad[pl.ds(EDGE - lag, R), :]
    conv[h] = out.astype(BF16)
    across = HeadGather(wire, s, h, lambda j: conv.at[j])
    advance(y_sum, 1)
    a_pre = jnp.broadcast_to(vec[5:6, :], (R, C))
    i_pre = jnp.broadcast_to(vec[6:7, :], (R, C))
    for j in (0, 2, 1, 3):
        if j:
            across.wait(j)
        k = h ^ j
        taken = conv[k]
        a_pre = a_pre + mm(taken, gate_weight_of(z, spread, mask, aw, k))
        i_pre = i_pre + mm(taken, gate_weight_of(z, spread, mask, iw, k))
    advance(y_sum, 1)
    a_o[...] = a_pre
    i_o[...] = i_pre
    anchor = anchor_of(z, s, LANES)
    sums[s] = jnp.zeros((8, C), F32)
    for b in range(C // LANES):
        cut = pl.ds(b * LANES, LANES)
        recall, input_gate, factor, one_minus, root_value, root_scale = decay_terms(
            a_o[:, cut], i_o[:, cut], vec[7:8, cut], anchor
        )
        driven = conv[h, :, cut].astype(F32) * input_gate * root_scale
        prod, value = scan_rows(factor, driven, 1)
        st[:, cut] = value
        tot[:, cut] = prod
        sums[s, 0:1, cut] = prod[R - 1 : R, :]
        sums[s, 1:2, cut] = value[R - 1 : R, :]
    ends = [wire.copy(sums.at[s], sums.at[s], (s ^ k, h)) for k in range(1, S)]
    advance(dealing, 1)
    advance(cot_in_all, 2)
    drain(y_sum)
    yb[...] = y5[...]
    for item in ends:
        item.wait_recv()
    entry = jnp.zeros((1, C), F32)
    for j in range(S - 1):
        entry = jnp.where(j < s, sums[j, 0:1, :] * entry + sums[j, 1:2, :], entry)
    entry_o[...] = jnp.broadcast_to(entry, (8, C))
    my_rows = pl.ds(pl.multiple_of(zi * R, EDGE), R)
    for b in range(C // LANES):
        cut = pl.ds(b * LANES, LANES)
        state = st[:, cut] + tot[:, cut] * entry_o[0:1, cut]
        st[:, cut] = state
        mix[my_rows, cut] = (state * gelu_pair(yb[:, cut])[0]).astype(BF16)
    arriving = chain.gather(row_blocks(z, mix))
    advance(arriving)
    advance(cot_in_all, 2)
    drain(arriving)
    twins[2].wait_recv()

    def out_part(j):
        rows = pl.ds(pl.multiple_of((h ^ j) * R, EDGE), R)
        return mm(ow2[...], mix[rows, :], NT)

    whole = head_scatter(wire, s, h, out_part, part, got)
    advance(dealing, 2)
    res[...] = whole() + tok2[:, pl.ds(pl.multiple_of(h * R, LANES), R)].astype(F32)


    flush(0, 19)
    tile = 256
    region_of(z, xt)(s, h, None)[...] = res[...].astype(BF16)
    spreading = gather_all(wire, z, g, region_of(z, xt))
    advance(spreading, 2)
    def turn(src, dst, scaled):
        for n in range(D // tile):
            cut = slice(n * tile, n * tile + tile)
            piece = src[cut, :].astype(F32)
            dst[:, cut] = (piece * gains[cut, 1:2] if scaled else piece).T.astype(BF16)

    drain(cot_in_all)
    advance(spreading, 3)
    advance(dealing, 2)
    advance(spreading, 2)
    advance(dealing, 2)
    drain(spreading, dealing)
    for wait in pending:
        wait()
    deal.wait()
    turn(gw, gwt, True)
    turn(uw, uwt, True)
    turn(dw, dwt, False)
    for n in range(T // tile):
        cut = slice(n * tile, n * tile + tile)
        hg[:, cut] = mm(dwt[...], cot[cut, :], NT)
        square = jnp.zeros((1, tile), F32)
        for b in range(D // tile):
            piece = xt[b * tile : b * tile + tile, cut].astype(F32)
            square = square + jnp.sum(piece * piece, axis=0, keepdims=True)
        scale = lax.rsqrt(square / D + EPSILON)
        rs[:, cut] = jnp.broadcast_to(scale, (8, tile))
        gate = mm(gwt[...], xt[:, cut]) * scale
        up = mm(uwt[...], xt[:, cut]) * scale
        act, slope = gelu_pair(gate)
        hid[:, cut] = (act * up).astype(BF16)
        back = hg[:, cut]
        gate_grad = back * up * slope
        up_grad = back * act
        gg[:, cut] = gate_grad.astype(BF16)
        ug[:, cut] = up_grad.astype(BF16)
        gs[:, cut] = (gate_grad * scale).astype(BF16)
        us[:, cut] = (up_grad * scale).astype(BF16)
    second = SumAll(wire, z, g, region_of(z, wide), (c1, c2, c3, c4, c5, c6))

    def produce(d):
        rows = pl.ds(pl.multiple_of(d * DG, LANES), DG)
        wide[rows, :] = (mm(gw[rows, :], gg[...]) + mm(uw[rows, :], ug[...])).astype(BF16)

    summing = second.run(produce)
    advance(summing, 3)
    flush(19, 21)
    for n in range(D // tile):
        cut = slice(n * tile, n * tile + tile)
        gwg[cut, :] = (mm(xt[cut, :], gs[...], NT) * gains[cut, 1:2]).astype(BF16)
    dealing = deal.steps(deal.back, ((gwg, back_g),))
    advance(dealing, 3)
    deal.back_own(gwg, back_g)
    advance(summing, 6)
    advance(dealing, 1)
    drain(summing)
    for n in range(D // tile):
        cut = slice(n * tile, n * tile + tile)
        uwg_o[cut, :] = (mm(xt[cut, :], us[...], NT) * gains[cut, 1:2]).astype(BF16)
        dwg_o[cut, :] = mm(hid[...], cot[:, cut]).T.astype(BF16)
    flush(21, 23)
    second_grad = jnp.concatenate([second.finish(0), second.finish(1)], axis=0)
    mine = pl.ds(pl.multiple_of((2 * h + xi) * R, LANES), R)
    group = pl.ds(pl.multiple_of(zi * DG, LANES), DG)
    scale = rs[0:1, mine]
    residual = res[...]
    gsum_o[...] = second_grad * residual * scale
    weighted = gains[group, 1:2] * second_grad
    stat[zi] = jnp.broadcast_to(jnp.sum(weighted * residual, axis=0, keepdims=True), (8, R))
    ends = [wire.copy(stat.at[zi], stat.at[zi], g.z(kz)) for kz in range(1, z.Z)]
    direct = cot[mine, group].astype(F32).T + scale * weighted
    for item in ends:
        item.wait_recv()
    mean = jnp.sum(stat[:, 0:1, :], axis=0) / D
    grad = direct - residual * (scale * scale * scale * mean)
    lanes = pl.ds(pl.multiple_of(h * R, LANES), R)
    bg_o[:, lanes] = grad.astype(BF16)
    HeadGather(
        wire, s, h, lambda j: bg_o.at[:, pl.ds(pl.multiple_of(j * R, LANES), R)]
    ).wait_all()
    deal.wait()
    flush(23, 26)
    wire.close()
    for copy in leaving:
        copy.wait()


def front(z, *args):
    S, H, R, D, T, U, Ds, C, Z = z.S, z.H, z.R, z.D, z.T, z.U, z.Ds, z.C, z.Z
    DG, TX = 2 * Ds, Z * R
    copies = 2 + 2 * (Z - 1) + (H - 1) + 1 + 4 * Z + 1 + (H - 1) + (S - 1)
    copies += 2 * (Z - 1) + (H - 1) + 8 * (S - 1) + 2 * gather_copies(z)
    copies += SumAll.copies(z) + (Z - 1) + (H - 1)
    results = [
        sds((DG, C), BF16),
        sds((DG, C), BF16),
        sds((DG, C), BF16),
        sds((DG, TX), BF16),
        sds((DG, TX), BF16),
        sds((Z, 8, R), F32),
        sds((R, C), F32),
        sds((EDGE + R, C), F32),
        sds((H, R, C), BF16),
        sds((R, C), F32),
        sds((R, C), F32),
        sds((R, C), F32),
        sds((8, C), F32),
        sds((TX, C), BF16),
        sds((DG, R), F32),
        sds((EDGE, C), F32),
        sds((C, C), BF16),
        sds((C, z.NI), BF16),
        sds((DG // H, 8), F32),
        sds((U, T), BF16),
        sds((D, U), BF16),
        sds((D, U), BF16),
        sds((D, U), BF16),
        sds((Ds, z.F2), BF16),
        sds((DG, R), F32),
        sds((DG, TX), BF16),
    ]
    return call(
        functools.partial(front_kernel, z),
        "front",
        1,
        results,
        [VM(item.shape, item.dtype) for item in results]
        + [
            VM((D, R), BF16),
            VM((Z, R, DG), BF16),
            *chain_scratch(z, R, C),
            *chain_scratch(z, R, C),
            VM((S, 8, C), F32),
            VM((R, C), F32),
            VM((H, DG, R), BF16),
            VM((H, DG, R), BF16),
            VM((2, EDGE, C), BF16),
            VM((D, 8), F32),
            VM((T, D), BF16),
            VM((D, U), BF16),
            VM((D, U), BF16),
            VM((D, T), BF16),
            VM((U, D), BF16),
            VM((U, D), BF16),
            VM((U, D), BF16),
            VM((D, U), BF16),
            VM((U, T), F32),
            VM((U, T), BF16),
            VM((U, T), BF16),
            VM((U, T), BF16),
            VM((U, T), BF16),
            VM((8, T), F32),
            VM((D, T), BF16),
            *SumAll.scratch(z, DG, R),
            VM((Z, 8, R), F32),
            sem(copies),
            sem(copies),
            sem(6),
            sem(len(results)),
        ],
        args,
        (15, 16, 17),
        True,
    )


def exact(left, right, dims):
    return lax.dot_general(
        left, right, dims, precision=lax.Precision.HIGHEST, preferred_element_type=F32
    )


def back_kernel(
    z, far, held, fetch_sem, mixed_o, owg_o, xwg_o, ywg_o, twin_r, full, gains2, smallg, vec_o, back_u, back_d,
    g1, g2, g3, g4, own, adj, tot, ag, ig, sums, late, cgr, cgs, ext, gx, gy, part, got, stat, stat2,
    tgq, prod, prod2, gains, small, smallx, small_z, vecs, twin_s, mpart, m1, m2, m3, m4, m5, m6, send, recv,
):
    (
        bg, ow2, hid, dw, res, mix, yb, vec, a_pre, i_pre, st, entry, conv, pad, aw, iw, spread,
        mask, xw2, yw2, fn2, tok2, rn, gain, msum, uwg, dwg,
    ) = held
    fetch = [
        pltpu.make_async_copy(src, dst, fetch_sem.at[index])
        for index, (src, dst) in enumerate(zip(far, held))
    ]
    for copy in fetch:
        copy.start()
    s, h = place()
    g = Grid(s, h)
    S, H, R, D, Ds, C, Z, T = z.S, z.H, z.R, z.D, z.Ds, z.C, z.Z, z.T
    DG, W = 2 * Ds, D // H
    Q = DG // H
    zi, xi = s // 2, s % 2
    after, before = lax.rem(s + 1, S), lax.rem(s + S - 1, S)
    greet(
        [(s ^ k, h) for k in range(1, S)]
        + [(s, h ^ j) for j in range(1, H)]
        + [(after, h), (before, h)]
    )
    wire = Wire(send, recv)
    chain = Chain(wire, Z, s, h)
    deal = Deal(wire, z, s, h)
    dealing = deal.steps(deal.back, ((uwg, back_u), (dwg, back_d)))
    my_rows = pl.ds(pl.multiple_of(zi * R, EDGE), R)
    half = pl.ds(pl.multiple_of(xi * Ds, EDGE), Ds)
    other = pl.ds(pl.multiple_of((1 - xi) * Ds, EDGE), Ds)

    def corner(a, b, part_of):
        return halves(mpart, b * W, W, a * R, R, part_of)

    mixed = SumAll(wire, z, g, corner, (m1, m2, m3, m4, m5, m6))

    def produce_mixed(d):
        cut = pl.ds(pl.multiple_of(d * 2 * R, LANES), 2 * R)
        mpart[:, cut] = mm(dw[...], hid[:, cut]).astype(BF16)

        @pl.when(h == d)
        def _():
            spot = region_of(z, mpart)(s, h, None)
            spot[...] = (spot[...].astype(F32) + res[...]).astype(BF16)

    mixing = mixed.run(produce_mixed)

    def block(d):
        lanes = pl.ds(pl.multiple_of(d * R, LANES), R)
        return mm(bg[:, lanes].astype(F32).T.astype(BF16), ow2[...])

    for copy in fetch[:5]:
        copy.wait()
    summing = chain.scatter(block, g1, g2, g3, g4, own)
    for _ in range(Z):
        advance(summing)
        advance(mixing, 2)
    for copy in fetch[5:]:
        copy.wait()
    drain(summing)
    row = lax.broadcasted_iota(jnp.int32, (R, LANES), 0)
    anchor = anchor_of(z, s, LANES)
    sums[s] = jnp.zeros((8, C), F32)
    for b in range(C // LANES):
        cut = pl.ds(b * LANES, LANES)
        grad = own[:, cut]
        gate, slope = gelu_pair(yb[:, cut])
        gy[my_rows, cut] = (grad * st[:, cut] * slope).astype(BF16)
        factor = jnp.exp(-8.0 * jax.nn.sigmoid(a_pre[:, cut]) * vec[7:8, cut])
        ahead = shifted(factor, -1, 1.0, row)
        prods, value = scan_rows(ahead, grad * gate, -1)
        tot[:, cut] = prods
        adj[:, cut] = value
        sums[s, 0:1, cut] = factor[0:1, :] * prods[0:1, :]
        sums[s, 1:2, cut] = factor[0:1, :] * value[0:1, :]
    ends = [wire.copy(sums.at[s], sums.at[s], (s ^ k, h)) for k in range(1, S)]
    y_rows = chain.gather(row_blocks(z, gy))
    advance(y_rows)
    advance(dealing, 0)
    twins = []

    def weight_grad(index, left, right, out):
        prod2[...] = mm(left[...], right[...])
        twin_s[index] = prod2[other, :].astype(BF16)
        twins.append(wire.copy(twin_s.at[index], twin_r.at[index], g.x))
        out[...] = prod2[half, :]

    weight_grad(0, bg, mix, owg_o)
    advance(mixing, 2)
    for item in ends:
        item.wait_recv()
    carry = jnp.zeros((1, C), F32)
    for j in range(S - 1, 0, -1):
        carry = jnp.where(j > s, sums[j, 0:1, :] * carry + sums[j, 1:2, :], carry)
    vec_o[...] = jnp.zeros_like(vec_o)
    late[...] = jnp.broadcast_to(carry, (8, C))
    for b in range(C // LANES):
        cut = pl.ds(b * LANES, LANES)
        adjoint = adj[:, cut] + tot[:, cut] * late[0:1, cut]
        rate = vec[7:8, cut]
        recall, input_gate, factor, one_minus, root_value, root_scale = decay_terms(
            a_pre[:, cut], i_pre[:, cut], rate, anchor
        )
        taken = conv[h, :, cut].astype(F32)
        state = st[:, cut]
        earlier = jnp.where(row == 0, entry[0:1, cut], shifted(state, 1, 0.0, row))
        live = jnp.logical_and(one_minus > SQUARE_FLOOR, jnp.logical_not(anchor))
        scale_grad = adjoint * taken * input_gate
        log_grad = adjoint * earlier * factor - jnp.where(
            live, scale_grad * factor * factor / root_value, 0.0
        )
        a_grad = (log_grad * (-8.0 * rate) * recall * (1.0 - recall)).astype(BF16)
        i_grad = (scale_grad * root_scale * (1.0 - input_gate)).astype(BF16)
        ag[:, cut] = a_grad
        ig[:, cut] = i_grad
        decay_sum = jnp.sum(log_grad * (-8.0 * recall), axis=0, keepdims=True)
        vec_o[5:6, cut] = jnp.sum(a_grad.astype(F32), axis=0, keepdims=True)
        vec_o[6:7, cut] = jnp.sum(i_grad.astype(F32), axis=0, keepdims=True)
        vec_o[7:8, cut] = decay_sum * vec[8:9, cut]
        ext[pl.ds(0, R), cut] = adjoint * input_gate * root_scale

    eighth = small.shape[0] // S

    def share(x_index, z_index, count):
        start = (x_index * Z + z_index) * eighth
        return pl.ds(pl.multiple_of(start, EDGE), count * eighth)

    def sum_small():
        mine = share(xi, 0, Z)
        item = wire.copy(small.at[share(1 - xi, 0, Z), :], smallx, g.x)
        yield
        item.wait_recv()
        smallx[...] = (smallx[...].astype(F32) + small[mine, :].astype(F32)).astype(BF16)

        def piece(index):
            return pl.ds(pl.multiple_of(index * eighth, EDGE), eighth)

        items = [
            wire.copy(smallx.at[piece(zi ^ kz), :], small_z.at[kz], g.z(kz))
            for kz in range(1, Z)
        ]
        yield
        total = smallx[piece(zi), :].astype(F32)
        for kz in range(1, Z):
            items[kz - 1].wait_recv()
            total = total + small_z[kz].astype(F32)
        spot = smallg.at[share(xi, zi, 1), :]
        spot[...] = total.astype(BF16)
        items = [wire.copy(spot, spot, g.z(kz)) for kz in range(1, Z)]
        yield
        for item in items:
            item.wait_recv()
        item = wire.copy(smallg.at[mine, :], smallg.at[mine, :], g.x)
        yield
        item.wait_recv()

    smaller = sum_small()
    def gates_back(j):
        return mm(ag[...], gate_weight_of(z, spread, mask, aw, h ^ j), NT) + mm(
            ig[...], gate_weight_of(z, spread, mask, iw, h ^ j), NT
        )

    advance(y_rows, 2)
    across = head_scatter(wire, s, h, gates_back, cgs, cgr)
    advance(y_rows, 2)
    advance(dealing, 4)
    for k in range(H):
        turn = conv[k].astype(F32).T.astype(BF16)
        for spot, grad in ((0, ag), (z.HS, ig)):
            dense = mm(turn, grad[...]).astype(BF16) * mask[...]
            small[pl.ds(spot + k * z.NI, z.NI), :] = mm(spread[...], dense, TN).astype(BF16)
    advance(smaller)
    advance(mixing, 2)
    conv_grad = ext[pl.ds(0, R), :] + across()
    ext[pl.ds(0, R), :] = conv_grad
    halo = wire.copy(ext.at[pl.ds(0, 8), :], ext.at[pl.ds(R, 8), :], (before, h))
    for lag in range(CONV):
        vec_o[lag : lag + 1, :] = jnp.sum(
            conv_grad * pad[pl.ds(EDGE - lag, R), :], axis=0, keepdims=True
        )
    vec_o[4:5, :] = jnp.sum(conv_grad, axis=0, keepdims=True)
    vecs[s] = vec_o[...]
    advance(mixing, 1)
    advance(smaller)
    halo.wait_recv()
    ext[pl.ds(R, 8), :] = jnp.where(s == S - 1, 0.0, ext[pl.ds(R, 8), :])
    grad = jnp.zeros((R, C), F32)
    for lag in range(CONV):
        grad = grad + vec[lag : lag + 1, :] * ext[pl.ds(lag, R), :]
    gx[my_rows, :] = grad.astype(BF16)
    rows_in = chain.gather(row_blocks(z, gx))
    advance(rows_in)
    advance(dealing, 2)
    advance(mixing, 1)
    pair = grad.astype(BF16).astype(F32) * pad[pl.ds(EDGE, R), :] + gy[my_rows, :].astype(F32) * yb[...]
    stat[h] = exact(jnp.ones((8, C), F32), pair, NT)
    stats = [wire.copy(stat.at[h], stat.at[h], (s, h ^ j)) for j in range(1, H)]

    lesser = [wire.copy(vecs.at[s], vecs.at[s], (s ^ k, h)) for k in range(1, S)]
    drain(y_rows)
    weight_grad(1, fn2, gy, ywg_o)
    prod[...] = mm(yw2[...], gy[...], NT)
    for item in stats:
        item.wait_recv()
    stat2[zi] = stat[0] + stat[1] + stat[2] + stat[3]
    stats = [wire.copy(stat2.at[zi], stat2.at[zi], g.z(kz)) for kz in range(1, Z)]
    advance(smaller)
    advance(mixing, 1)
    drain(rows_in)

    prod[...] = prod[...] + mm(xw2[...], gx[...], NT)

    def quarter_of(j):
        return prod[pl.ds(pl.multiple_of((h ^ j) * Q, EDGE), Q), :]

    heads = head_scatter(wire, s, h, quarter_of, part, got)
    advance(dealing, 2)
    advance(smaller)
    advance(mixing, 1)
    quarter = pl.ds(pl.multiple_of(h * Q, EDGE), Q)
    weight_grad(2, fn2, gx, xwg_o)
    total = heads()
    for item in stats:
        item.wait_recv()
    token = tok2[quarter, :].astype(F32)
    norm = jnp.concatenate([rn[b, 0:1, :] for b in range(Z)], axis=1)
    mean = jnp.concatenate([stat2[b, 0:1, :] for b in range(Z)], axis=1) / (norm * D)
    weighted = gain[:, 0:1] * total
    grad = bg[quarter, :].astype(F32) + norm * weighted - token * (norm * norm * norm * mean)
    tgq[...] = grad.astype(BF16)

    def spot(z_index, head):
        return full.at[pl.ds(pl.multiple_of(z_index * DG + head * Q, EDGE), Q), :]

    outs = [
        wire.copy(
            tgq.at[:, pl.ds(pl.multiple_of((zi ^ kz) * R, LANES), R)], spot(zi, h), g.z(kz)
        )
        for kz in range(1, Z)
    ]
    spot(zi, h)[...] = tgq[:, pl.ds(pl.multiple_of(zi * R, LANES), R)]
    prod[...] = jnp.zeros_like(prod)
    prod[quarter, :] = total * token * norm
    ones = jnp.ones((8, Z * R), F32)
    picked = lax.broadcasted_iota(jnp.int32, (8, DG), 0)
    gains[h] = jnp.where(
        picked == 0, exact(jnp.ones((8, R), F32), msum[...], NT), exact(ones, prod[...], NT)
    )
    tally = [wire.copy(gains.at[h], gains.at[h], (s, h ^ j)) for j in range(1, H)]
    finals = []
    drain(dealing)
    for kz in range(Z):
        if kz:
            outs[kz - 1].wait_recv()
        finals.append(HeadGather(wire, s, h, lambda j, kz=kz: spot(zi ^ kz, j)))
    for item in tally:
        item.wait_recv()
    gains2[s] = gains[0] + gains[1] + gains[2] + gains[3]
    tally = [wire.copy(gains2.at[s], gains2.at[s], (s ^ k, h)) for k in range(1, S)]
    drain(mixing)
    for part_of in range(2):
        mixed_o[pl.ds(part_of * W // 2, W // 2), :] = mixed.finish(part_of)
    for item in lesser:
        item.wait_recv()
    vec_o[...] = jnp.sum(vecs[...], axis=0)
    for item in twins:
        item.wait_recv()
    deal.back_own(uwg, back_u)
    deal.back_own(dwg, back_d)
    drain(smaller)
    for item in tally:
        item.wait_recv()
    for item in finals:
        item.wait_all()
    deal.wait()
    wire.close()


def back(z, *args):
    S, H, R, D, Ds, C, Z, T = z.S, z.H, z.R, z.D, z.Ds, z.C, z.Z, z.T
    DG, W = 2 * Ds, D // H
    TX, Q = Z * R, DG // H
    copies = (
        2 * Z + (S - 1) + 3 + (H - 1) + 1 + 4 * (Z - 1) + (H - 1) + (Z - 1) + (S - 1)
        + 2 + 2 * (Z - 1) + 2 * (Z - 1) + 4 * (S - 1) + (H - 1) + (Z - 1) + (H - 1) + Z * (H - 1) + (S - 1)
        + SumAll.copies(z)
    )
    small = 2 * z.HS
    count = len(args)

    def body(*refs):
        far, rest = refs[:count], refs[count:]
        outs, held, rest = rest[:11], rest[11 : 11 + count], rest[11 + count :]
        back_kernel(z, far, held, rest[0], *outs, *rest[1:])

    return call(
        body,
        "back",
        2,
        [
            sds((W, R), F32),
            sds((Ds, C), F32),
            sds((Ds, C), F32),
            sds((Ds, C), F32),
            sds((3, Ds, C), BF16),
            sds((D, R), BF16),
            sds((S, 8, DG), F32),
            sds((small, C), BF16),
            sds((8, C), F32),
            sds((Ds, z.F2), BF16),
            sds((Ds, z.F2), BF16),
        ],
        [VM(a.shape, a.dtype) for a in args]
        + [sem(count)]
        + [
            *chain_scratch(z, R, C),
            VM((R, C), F32),
            VM((R, C), F32),
            VM((R, C), BF16),
            VM((R, C), BF16),
            VM((S, 8, C), F32),
            VM((8, C), F32),
            VM((H, R, C), BF16),
            VM((H, R, C), BF16),
            VM((R + 8, C), F32),
            VM((TX, C), BF16),
            VM((TX, C), BF16),
            VM((H, Q, TX), BF16),
            VM((H, Q, TX), BF16),
            VM((H, 8, R), F32),
            VM((Z, 8, R), F32),
            VM((Q, TX), BF16),
            VM((DG, TX), F32),
            VM((DG, C), F32),
            VM((H, 8, DG), F32),
            VM((small, C), BF16),
            VM((small // 2, C), BF16),
            VM((Z, small // S, C), BF16),
            VM((S, 8, C), F32),
            VM((3, Ds, C), BF16),
            VM((D, T), BF16),
        ]
        + SumAll.scratch(z, W, R)
        + [sem(copies), sem(copies)],
        args,
        range(count),
    )


def results_kernel(z, *refs):
    sources, count = 12, 17
    inputs, outs = refs[:sources], refs[sources : sources + count]
    held = refs[sources + count : 2 * sources + count]
    stage = refs[2 * sources + count : 2 * (sources + count)]
    in_sem, out_sem = refs[-2:]
    fetch = []
    for index in range(sources):
        copy = pltpu.make_async_copy(inputs[index], held[index], in_sem.at[index])
        copy.start()
        fetch.append(copy)
    mixed, owg, xwg, ywg, twins, full, gains, small, vec, back_g, back_u, back_d = held
    copies = []

    def need(*indexes):
        for index in indexes:
            fetch[index].wait()

    def emit(index, value):
        stage[index][...] = value
        copy = pltpu.make_async_copy(stage[index], outs[index], out_sem.at[index])
        copy.start()
        copies.append(copy)

    need(4, 1, 2, 3)
    for index, slot, src in ((12, 0, owg), (4, 1, ywg), (3, 2, xwg)):
        emit(index, src[...] + twins[slot].astype(F32))
    for index, at_input, src in ((14, 9, back_g), (15, 10, back_u), (16, 11, back_d)):
        need(at_input)
        emit(index, src[...].astype(F32))
    need(5, 0, 7, 8, 6)
    emit(1, full[...].astype(F32).T)
    emit(0, mixed[...].T.astype(BF16))
    emit(7, small[0 : z.HS, :].astype(F32))
    emit(9, small[z.HS : 2 * z.HS, :].astype(F32))
    emit(5, vec[0:CONV, :])
    for index, row in ((6, 4), (8, 5), (10, 6), (11, 7)):
        outs[index][...] = vec[row, :]
    for index, row in ((2, 1), (13, 0)):
        sums = [gains[2 * b, row, :] + gains[2 * b + 1, row, :] for b in range(z.Z)]
        outs[index][...] = jnp.concatenate(sums)
    for copy in copies:
        copy.wait()


def results(z, *args):
    R, D, Ds, C, F2 = z.R, z.D, z.Ds, z.C, z.F2
    row = sds((C,), F32)
    outs = [
        sds((R, D // z.H), BF16),
        sds((R, D), F32),
        sds((D,), F32),
        sds((Ds, C), F32),
        sds((Ds, C), F32),
        sds((CONV, C), F32),
        row,
        sds((z.HS, C), F32),
        row,
        sds((z.HS, C), F32),
        row,
        row,
        sds((Ds, C), F32),
        sds((D,), F32),
        sds((Ds, F2), F32),
        sds((Ds, F2), F32),
        sds((Ds, F2), F32),
    ]
    return pl.pallas_call(
        functools.partial(results_kernel, z),
        out_shape=outs,
        in_specs=[pl.BlockSpec(memory_space=ANY)] * len(args),
        out_specs=[
            pl.BlockSpec(memory_space=VM if len(out.shape) == 1 else ANY) for out in outs
        ],
        scratch_shapes=[VM(a.shape, a.dtype) for a in list(args) + outs]
        + [sem(len(args)), sem(len(outs))],
        compiler_params=pltpu.CompilerParams(vmem_limit_bytes=62 << 20),
        name="results",
    )(*args)


def dealt(
    z,
    tokens,
    norm_gain,
    x_weight,
    y_weight,
    conv_weight,
    conv_bias,
    a_weight,
    a_bias,
    i_weight,
    i_bias,
    decay,
    out_weight,
    mlp_gain,
    gate_weight,
    up_weight,
    down_weight,
    cotangent,
):
    (
        xw2, yw2, ow2, tok2, fn2, rn, yb, pad, conv, a_pre, i_pre, st, entry, mix, res,
        vec, mask, spread, gain_q, hid, dc, uwg, dwg, back_g, msum, bg,
    ) = front(
        z, tokens, norm_gain, mlp_gain, x_weight, y_weight, out_weight, conv_weight, conv_bias,
        a_bias, i_bias, jax.nn.softplus(decay), jax.nn.sigmoid(decay), a_weight, i_weight,
        cotangent, gate_weight, up_weight, down_weight,
    )
    mixed, owg, xwg, ywg, twins, tg, gains, small, vec_sum, back_u, back_d = back(
        z, bg, ow2, hid, dc, res, mix, yb, vec, a_pre, i_pre, st, entry, conv, pad, a_weight,
        i_weight, spread, mask, xw2, yw2, fn2, tok2, rn, gain_q, msum, uwg, dwg,
    )
    return tuple(
        results(z, mixed, owg, xwg, ywg, twins, tg, gains, small, vec_sum, back_g, back_u, back_d)
    )


def from_behind(x, axis, by):
    size = lax.axis_size(axis)
    pairs = [(i, i + by) for i in range(size) if 0 <= i + by < size]
    return lax.ppermute(x, axis, pairs)


def rms_norm(values, gain):
    return values * lax.rsqrt(jnp.mean(values * values, axis=-1, keepdims=True) + EPSILON) * gain


def linear_pair(earlier, later):
    return (later[0] * earlier[0], later[0] * earlier[1] + later[1])


def gelu_back(values, grad):
    return jax.vjp(jax.nn.gelu, values)[1](grad)[0]


def gathered_weights(
    tokens,
    norm_gain,
    x_weight,
    y_weight,
    conv_weight,
    conv_bias,
    a_weight,
    a_bias,
    i_weight,
    i_bias,
    decay,
    out_weight,
    mlp_gain,
    gate_weight,
    up_weight,
    down_weight,
    cotangent,
):
    row_count = tokens.shape[0]
    model_width = tokens.shape[1]
    lane_count = x_weight.shape[1]
    head_size = a_weight.shape[0]
    head_index = lax.axis_index("head")
    seq_index = lax.axis_index("seq")
    head_devices = lax.axis_size("head")
    float_type = jnp.float32
    half_type = jnp.bfloat16
    gathered = (
        lax.all_gather(x_weight, "seq", axis=0, tiled=True),
        lax.all_gather(y_weight, "seq", axis=0, tiled=True),
        lax.all_gather(out_weight, "seq", axis=0, tiled=True),
        lax.all_gather(gate_weight, "seq", axis=0, tiled=True),
        lax.all_gather(up_weight, "seq", axis=0, tiled=True),
        lax.all_gather(down_weight, "seq", axis=0, tiled=True),
    )
    x_full, y_full, out_full, gate_full, up_full, down_full = gathered
    tokens_wide = tokens.astype(float_type)
    first_gain = norm_gain.astype(float_type)
    first_norm = rms_norm(tokens_wide, first_gain)
    first_low = first_norm.astype(half_type)
    x_branch = jnp.dot(first_low, x_full, preferred_element_type=float_type).astype(half_type)
    y_branch = jnp.dot(first_low, y_full, preferred_element_type=float_type)
    y_gate = jax.nn.gelu(y_branch)
    left_edge = from_behind(x_branch[row_count - (CONV - 1) :], "seq", 1)
    padded = jnp.concatenate([left_edge, x_branch], axis=0).astype(float_type)
    conv_taps = conv_weight.astype(float_type)
    conv_out = conv_bias.astype(float_type) + sum(
        (
            conv_taps[lag_index] * padded[CONV - 1 - lag_index : CONV - 1 - lag_index + row_count]
            for lag_index in range(CONV)
        )
    )
    conv_low = conv_out.astype(half_type)
    conv_value = conv_low.astype(float_type)
    all_channels = lax.all_gather(conv_low, "head", axis=1, tiled=True)
    head_count = all_channels.shape[1] // head_size
    group_count = lane_count // head_count
    heads_view = all_channels.reshape(row_count, head_size, head_count)

    def block_gate(weight, bias):
        product = jnp.einsum(
            "tih,ijh->tjh",
            heads_view,
            weight.reshape(head_size, group_count, head_count),
            preferred_element_type=float_type,
        )
        return product.reshape(row_count, lane_count) + bias.astype(float_type)

    a_pre = block_gate(a_weight, a_bias)
    i_pre = block_gate(i_weight, i_bias)
    recall = jax.nn.sigmoid(a_pre)
    input_gate = jax.nn.sigmoid(i_pre)
    decay_rate = jax.nn.softplus(decay)
    log_decay = -8.0 * recall * decay_rate
    factor = jnp.exp(log_decay)
    double_decay = jnp.exp(2.0 * log_decay)
    one_minus = -jnp.expm1(2.0 * log_decay)
    root_value = jnp.sqrt(jnp.maximum(one_minus, SQUARE_FLOOR))
    position = seq_index * row_count + jnp.arange(row_count)
    anchor = (position == 0)[:, None]
    root_scale = jnp.where(anchor, 1.0, root_value)
    root_live = jnp.logical_and(one_minus > SQUARE_FLOOR, jnp.logical_not(anchor))
    driven = conv_value * input_gate * root_scale
    local_prod, local_state = lax.associative_scan(linear_pair, (factor, driven))

    def relay_step(turn_number, carried):
        return from_behind(local_prod[-1] * carried + local_state[-1], "seq", 1)

    state_entry = lax.fori_loop(
        0, lax.axis_size("seq") - 1, relay_step, jnp.zeros_like(local_state[-1])
    )
    state_all = local_state + local_prod * state_entry
    mixed_in = (state_all * y_gate).astype(half_type)
    branch_part = jnp.einsum("tc,dc->td", mixed_in, out_full, preferred_element_type=float_type)
    branch = lax.psum(branch_part, "head")
    residual = tokens_wide + branch
    second_gain = mlp_gain.astype(float_type)
    second_low = rms_norm(residual, second_gain).astype(half_type)
    gate_pre = jnp.dot(second_low, gate_full, preferred_element_type=float_type)
    up_pre = jnp.dot(second_low, up_full, preferred_element_type=float_type)
    gate_act = jax.nn.gelu(gate_pre)
    hidden = (gate_act * up_pre).astype(half_type)
    mlp_part = jnp.einsum("tf,df->td", hidden, down_full, preferred_element_type=float_type)
    own_columns = lax.psum_scatter(mlp_part, "head", scatter_dimension=1, tiled=True)
    column_count = model_width // head_devices
    mixed = (
        lax.dynamic_slice_in_dim(residual, head_index * column_count, column_count, 1) + own_columns
    ).astype(half_type)
    regathered = (
        lax.all_gather(x_weight, "seq", axis=0, tiled=True),
        lax.all_gather(y_weight, "seq", axis=0, tiled=True),
        lax.all_gather(out_weight, "seq", axis=0, tiled=True),
        lax.all_gather(gate_weight, "seq", axis=0, tiled=True),
        lax.all_gather(up_weight, "seq", axis=0, tiled=True),
        lax.all_gather(down_weight, "seq", axis=0, tiled=True),
    )
    x_full, y_full, out_full, gate_full, up_full, down_full = regathered
    hidden_grad = jnp.dot(cotangent, down_full, preferred_element_type=float_type)
    gate_grad = gelu_back(gate_pre, hidden_grad * up_pre).astype(half_type)
    up_grad = (hidden_grad * gate_act).astype(half_type)
    second_part = jnp.einsum(
        "tf,df->td", gate_grad, gate_full, preferred_element_type=float_type
    ) + jnp.einsum("tf,df->td", up_grad, up_full, preferred_element_type=float_type)
    second_grad = lax.psum(second_part, "head")
    resid_back, mlp_gain_term = jax.vjp(rms_norm, residual, second_gain)[1](second_grad)
    resid_grad = cotangent.astype(float_type) + resid_back
    branch_grad = resid_grad.astype(half_type)
    mixed_grad = jnp.dot(branch_grad, out_full, preferred_element_type=float_type)
    state_grad = mixed_grad * y_gate
    y_grad = gelu_back(y_branch, mixed_grad * state_all).astype(half_type)
    next_factor = jnp.concatenate([factor[1:], jnp.ones_like(factor[:1])], axis=0)
    back_prod, back_adjoint = lax.associative_scan(
        linear_pair, (next_factor[::-1], state_grad[::-1])
    )
    back_prod = back_prod[::-1]
    back_adjoint = back_adjoint[::-1]
    tail_prod = factor[0] * back_prod[0]
    tail_value = factor[0] * back_adjoint[0]

    def relay_back(turn_number, carried):
        return from_behind(tail_value + tail_prod * carried, "seq", -1)

    exit_carry = lax.fori_loop(0, lax.axis_size("seq") - 1, relay_back, jnp.zeros_like(tail_value))
    adjoint = back_adjoint + back_prod * exit_carry
    prev_state = jnp.concatenate([state_entry[None], state_all[:-1]], axis=0)
    scale_grad = adjoint * conv_value * input_gate
    log_grad = adjoint * prev_state * factor + jnp.where(
        root_live, -scale_grad * double_decay / root_value, 0.0
    )
    a_grad = (log_grad * (-8.0 * decay_rate) * recall * (1.0 - recall)).astype(half_type)
    i_grad = (adjoint * conv_value * root_scale * input_gate * (1.0 - input_gate)).astype(half_type)
    decay_term = jnp.sum(log_grad * (-8.0 * recall), axis=0) * jax.nn.sigmoid(decay)
    a_bias_term = jnp.sum(a_grad.astype(float_type), axis=0)
    i_bias_term = jnp.sum(i_grad.astype(float_type), axis=0)

    def gate_back(grad, weight):
        grad_view = grad.reshape(row_count, group_count, head_count)
        weight_term = jnp.einsum(
            "tih,tjh->ijh", heads_view, grad_view, preferred_element_type=float_type
        ).reshape(head_size, lane_count)
        input_term = jnp.einsum(
            "tjh,ijh->tih",
            grad_view,
            weight.reshape(head_size, group_count, head_count),
            preferred_element_type=float_type,
        )
        return (weight_term, input_term)

    a_wgrad, a_input = gate_back(a_grad, a_weight)
    i_wgrad, i_input = gate_back(i_grad, i_weight)
    gate_input_grad = lax.psum_scatter(
        (a_input + i_input).reshape(row_count, head_size * head_count),
        "head",
        scatter_dimension=1,
        tiled=True,
    )
    conv_grad = gate_input_grad + adjoint * input_gate * root_scale
    right_edge = from_behind(conv_grad[: CONV - 1], "seq", -1)
    extended_grad = jnp.concatenate([conv_grad, right_edge], axis=0)
    x_branch_grad = sum(
        (
            conv_taps[lag_index] * extended_grad[lag_index : lag_index + row_count]
            for lag_index in range(CONV)
        )
    ).astype(half_type)
    conv_wgrad = jnp.stack(
        [
            jnp.sum(
                conv_grad * padded[CONV - 1 - lag_index : CONV - 1 - lag_index + row_count], axis=0
            )
            for lag_index in range(CONV)
        ],
        axis=0,
    )
    conv_bgrad = jnp.sum(conv_grad, axis=0)
    first_part = jnp.einsum(
        "tc,dc->td", x_branch_grad, x_full, preferred_element_type=float_type
    ) + jnp.einsum("tc,dc->td", y_grad, y_full, preferred_element_type=float_type)
    first_grad = lax.psum(first_part, "head")
    tokens_back, norm_gain_term = jax.vjp(rms_norm, tokens_wide, first_gain)[1](first_grad)
    tokens_grad = resid_grad + tokens_back
    pairings = (
        (first_low, x_branch_grad),
        (first_low, y_grad),
        (branch_grad, mixed_in),
        (second_low, gate_grad),
        (second_low, up_grad),
        (cotangent, hidden),
    )
    products = tuple(
        (
            jnp.einsum("td,tc->dc", left, right, preferred_element_type=float_type)
            for left, right in pairings
        )
    )
    weight_sums = lax.psum_scatter(products, "seq", scatter_dimension=0, tiled=True)
    small_sums = lax.psum(
        (
            norm_gain_term,
            conv_wgrad,
            conv_bgrad,
            a_wgrad,
            a_bias_term,
            i_wgrad,
            i_bias_term,
            decay_term,
            mlp_gain_term,
        ),
        "seq",
    )
    return (
        mixed,
        tokens_grad,
        small_sums[0],
        weight_sums[0],
        weight_sums[1],
        small_sums[1],
        small_sums[2],
        small_sums[3],
        small_sums[4],
        small_sums[5],
        small_sums[6],
        small_sums[7],
        weight_sums[2],
        small_sums[8],
        weight_sums[3],
        weight_sums[4],
        weight_sums[5],
    )


def solution(mesh):
    sizes = mesh.shape["seq"], mesh.shape["head"]

    def body(*args):
        z = Size(sizes, args[0], args[2], args[6], args[13])
        return dealt(z, *args) if z.fits() else gathered_weights(*args)

    return jax.shard_map(
        body,
        mesh=mesh,
        in_specs=(
            P("seq", None),
            P(),
            P("seq", "head"),
            P("seq", "head"),
            P(None, "head"),
            P("head"),
            P(None, "head"),
            P("head"),
            P(None, "head"),
            P("head"),
            P("head"),
            P("seq", "head"),
            P(),
            P("seq", "head"),
            P("seq", "head"),
            P("seq", "head"),
            P("seq", None),
        ),
        out_specs=(
            P("seq", "head"),
            P("seq", None),
            P(),
            P("seq", "head"),
            P("seq", "head"),
            P(None, "head"),
            P("head"),
            P(None, "head"),
            P("head"),
            P(None, "head"),
            P("head"),
            P("head"),
            P("seq", "head"),
            P(),
            P("seq", "head"),
            P("seq", "head"),
            P("seq", "head"),
        ),
        check_vma=False,
    )
```

```python
import functools

import jax
import jax.numpy as jnp
from jax import lax
from jax.experimental import pallas as pl
from jax.experimental.pallas import tpu as pltpu
from jax.sharding import PartitionSpec as P

CONV = 4
EPSILON = 1e-06
SQUARE_FLOOR = 2.5e-07
MESH = pl.DeviceIdType.MESH
F32 = jnp.float32
BF16 = jnp.bfloat16
LANES = 128
EDGE = 16
VM = pltpu.VMEM
ANY = pl.ANY
NN = (((1,), (0,)), ((), ()))
NT = (((1,), (1,)), ((), ()))
TN = (((0,), (0,)), ((), ()))


def mm(left, right, dims=NN):
    return lax.dot_general(left, right, dims, preferred_element_type=F32)


def gelu_pair(values):
    scale = 0.7978845608028654
    square = values * values
    bend = jnp.tanh(scale * values * (1.0 + 0.044715 * square))
    half = 0.5 * (1.0 + bend)
    slope = half + 0.5 * values * (1.0 - bend * bend) * scale * (1.0 + 3.0 * 0.044715 * square)
    return values * half, slope


def minus_expm1(v):
    series = jnp.full_like(v, 1.0 / 40320.0)
    for divisor in (5040.0, 720.0, 120.0, 24.0, 6.0, 2.0, 1.0):
        series = series * v + 1.0 / divisor
    return jnp.where(v > -0.35, -v * series, 1.0 - jnp.exp(v))


def when(condition, action):
    if condition is None:
        action()
    else:
        pl.when(condition)(action)


class Copy:
    def __init__(self, item, goes, comes):
        self.item, self.goes, self.comes = item, goes, comes

    def start(self):
        when(self.goes, lambda: self.item.start())

    def wait_send(self):
        when(self.goes, lambda: self.item.wait_send())

    def wait_recv(self):
        when(self.comes, lambda: self.item.wait_recv())

    def arrived(self):
        self.item.wait_recv()


class Wire:
    def __init__(self, send, recv):
        self.send, self.recv, self.count, self.open = send, recv, 0, []

    def make(self, src, dst, peer, goes=None, comes=None):
        slot = self.count
        self.count += 1
        item = pltpu.make_async_remote_copy(
            src_ref=src,
            dst_ref=dst,
            send_sem=self.send.at[slot],
            recv_sem=self.recv.at[slot],
            device_id=peer,
            device_id_type=MESH,
        )
        copy = Copy(item, goes, comes)
        self.open.append(copy)
        return copy

    def copy(self, src, dst, peer, goes=None, comes=None):
        copy = self.make(src, dst, peer, goes, comes)
        copy.start()
        return copy

    def close(self):
        for item in self.open:
            item.wait_send()
        assert self.count <= self.send.shape[0], self.count


class Chain:
    def __init__(self, wire, count, s, h):
        self.wire, self.count, self.s, self.h, self.zi = wire, count, s, h, s // 2
        self.up = (jnp.minimum(s + 2, 2 * count - 2 + s % 2), h)
        self.down = (jnp.maximum(s - 2, s % 2), h)

    def gather(self, view):
        zi, last = self.zi, self.count - 1

        def hop(step, way):
            index = zi - way * step
            held = jnp.logical_and(index >= 0, index <= last)
            goes = jnp.logical_and(held, zi < last if way > 0 else zi > 0)
            here = index - way
            comes = jnp.logical_and(here >= 0, here <= last)
            block = view(jnp.clip(index, 0, last))
            peer = self.up if way > 0 else self.down
            return self.wire.copy(block, block, peer, goes, comes), comes, jnp.clip(here, 0, last)

        flight = [hop(0, 1), hop(0, -1)]
        yield None, zi
        for step in range(last):
            for side, way in enumerate((1, -1)):
                item, comes, index = flight[side]
                item.wait_recv()
                if step + 1 < last:
                    flight[side] = hop(step + 1, way)
                yield comes, index

    def order(self):
        count = self.count
        low = list(reversed(range(count // 2, count))) + list(range(count // 2))
        near = self.zi < count // 2
        return [jnp.where(near, d, count - 1 - d) for d in low]

    def passes(self, d, src, up, down):
        zi, last, wire = self.zi, self.count - 1, self.wire
        base = wire.count
        wire.count = base + d
        first = wire.make(src, up, self.up, zi < d, jnp.logical_and(zi > 0, zi <= d))
        wire.count = base + self.count + d
        second = wire.make(src, down, self.down, zi > d, jnp.logical_and(zi < last, zi >= d))
        wire.count = base
        return first, second

    def between(self, d):
        zi, last = self.zi, self.count - 1
        return jnp.logical_and(zi > 0, zi < d), jnp.logical_and(zi < last, zi > d)

    def ends(self, d):
        zi, last = self.zi, self.count - 1
        return jnp.logical_and(zi == d, zi > 0), jnp.logical_and(zi == d, zi < last)

    def scatter(self, block, work, out, up, down, own):
        zi = self.zi
        flight = []
        base = self.wire.count
        self.wire.count += 2 * self.count

        def take(item, got, into):
            def action():
                item.arrived()
                into[...] = into[...] + got[...].astype(F32)
            return action

        for d in self.order():
            work[...] = block(d)
            kept, self.wire.count = self.wire.count, base
            ups, downs = self.passes(d, out.at[d], up.at[d], down.at[d])
            self.wire.count = kept
            flight.append((d, ups, downs))
            below, above = self.between(d)
            when(below, take(ups, up.at[d], work))
            when(above, take(downs, down.at[d], work))

            def give(d=d):
                out[d] = work[...].astype(BF16)

            def keep():
                own[...] = work[...]

            when(zi != d, give)
            when(zi == d, keep)
            ups.start()
            downs.start()
            yield d
        for d, ups, downs in flight:
            below, above = self.ends(d)
            when(below, take(ups, up.at[d], own))
            when(above, take(downs, down.at[d], own))


class HeadGather:
    def __init__(self, wire, s, h, view):
        self.wire, self.s, self.h, self.view = wire, s, h, view
        self.items = {1: self.send(0, 1), 2: self.send(0, 2)}

    def send(self, j, to):
        block = self.view(self.h ^ j)
        return self.wire.copy(block, block, (self.s, self.h ^ to))

    def wait(self, j):
        if j == 2:
            self.items[2].wait_recv()
            self.items[3] = self.send(2, 1)
        else:
            self.items[j].wait_recv()

    def wait_all(self):
        for j in (2, 1, 3):
            self.wait(j)


def head_scatter(wire, s, h, block, out, got):
    core, other = (s, h ^ 1), (s, h ^ 2)
    flight = {}
    for j in (3, 1):
        out[j] = block(j).astype(BF16)
        flight[j] = wire.copy(out.at[j], got.at[j], core)
    part = block(2)
    flight[3].wait_recv()
    out[2] = (part + got[3].astype(F32)).astype(BF16)
    flight[2] = wire.copy(out.at[2], got.at[2], other)
    total = block(0)
    flight[1].wait_recv()
    total = total + got[1].astype(F32)

    def finish():
        flight[2].wait_recv()
        return total + got[2].astype(F32)

    return finish


def drain(*steps):
    steps = list(steps)
    while steps:
        steps = [step for step in steps if next(step, step) is not step]


def advance(step, count=1):
    for _ in range(count):
        next(step, None)


def greet(peers):
    barrier = pltpu.get_barrier_semaphore()
    for peer in peers:
        pl.semaphore_signal(barrier, inc=1, device_id=peer, device_id_type=MESH)
    pl.semaphore_wait(barrier, len(peers))


def place():
    return lax.axis_index("seq"), lax.axis_index("head")


def at(ref, rows, row_count, lanes, lane_count):
    return ref.at[
        pl.ds(pl.multiple_of(rows, EDGE), row_count),
        pl.ds(pl.multiple_of(lanes, LANES), lane_count),
    ]


def sem(count):
    return pltpu.SemaphoreType.DMA((count,))


def call(body, name, cid, outs, scratch, args, spaces=(), far=False, limit=62, us=150):
    return pl.pallas_call(
        body,
        out_shape=outs,
        in_specs=[
            pl.BlockSpec(memory_space=ANY if i in spaces else VM) for i in range(len(args))
        ],
        out_specs=[pl.BlockSpec(memory_space=ANY if far else VM) for _ in outs],
        scratch_shapes=scratch,
        compiler_params=pltpu.CompilerParams(
            collective_id=cid, has_side_effects=True, vmem_limit_bytes=limit << 20
        ),
        cost_estimate=pl.CostEstimate(
            flops=us * 10**6, bytes_accessed=us * 3 * 10**6, transcendentals=0
        ),
        name=name,
    )(*args)


def sds(shape, kind):
    return jax.ShapeDtypeStruct(shape, kind)


class Size:
    def __init__(self, mesh_sizes, tokens, x_weight, a_weight, gate_weight):
        self.S, self.H = mesh_sizes
        self.Z = self.S // 2
        self.R, self.D = tokens.shape
        self.T = self.S * self.R
        self.Ds, self.C = x_weight.shape
        self.HS = a_weight.shape[0]
        self.heads = self.H * self.C // self.HS
        self.F2 = gate_weight.shape[1]
        self.TB = self.T // self.H
        self.U = 2 * LANES
        self.NI = self.HS // self.H

    def fits(self):
        tiles = self.F2 // LANES
        return (
            self.S == 8
            and self.H == 4
            and self.Z == self.H
            and (2 * self.Ds) % LANES == 0
            and (2 * self.HS // self.S) % EDGE == 0
            and self.D == self.H * self.C
            and self.F2 % LANES == 0
            and 2 * (self.S - 1) < tiles <= 2 * self.S
            and self.T <= 1024
            and self.R % LANES == 0
            and self.C % LANES == 0
            and self.Ds % (2 * EDGE) == 0
            and (self.Ds // self.H) % EDGE == 0
            and self.NI % EDGE == 0
        )


def gate_weight_of(z, spread, mask, weight, k):
    rows = weight[pl.ds(pl.multiple_of(k * z.NI, EDGE), z.NI), :]
    return mm(spread[...], rows).astype(BF16) * mask[...]


def shifted(values, by, fill, row):
    count = values.shape[0]
    moved = pltpu.roll(values, by % count, 0)
    inside = row >= by if by > 0 else row < count + by
    return jnp.where(inside, moved, fill)


def scan_rows(prod, value, sign):
    row = lax.broadcasted_iota(jnp.int32, prod.shape, 0)
    by = 1
    while by < prod.shape[0]:
        value = prod * shifted(value, sign * by, 0.0, row) + value
        prod = prod * shifted(prod, sign * by, 1.0, row)
        by *= 2
    return prod, value


def decay_terms(a_pre, i_pre, rate, anchor):
    recall = jax.nn.sigmoid(a_pre)
    input_gate = jax.nn.sigmoid(i_pre)
    log_decay = -8.0 * recall * rate
    factor = jnp.exp(log_decay)
    one_minus = minus_expm1(2.0 * log_decay)
    root_value = jnp.sqrt(jnp.maximum(one_minus, SQUARE_FLOOR))
    root_scale = jnp.where(anchor, 1.0, root_value)
    return recall, input_gate, factor, one_minus, root_value, root_scale


def anchor_of(z, s, width):
    row = lax.broadcasted_iota(jnp.int32, (z.R, width), 0)
    return jnp.logical_and(row == 0, s == 0)


def head_maps(z, spread, mask):
    def parts(shape, axis):
        channel = lax.broadcasted_iota(jnp.int32, shape, axis).astype(F32)
        row = jnp.floor((channel + 0.5) * (1.0 / z.heads))
        return row, channel - row * z.heads

    across = lax.broadcasted_iota(jnp.int32, (z.C, z.NI), 1).astype(F32)
    spread[...] = jnp.where(parts((z.C, z.NI), 0)[0] == across, 1.0, 0.0).astype(BF16)
    same = parts((z.C, z.C), 0)[1] == parts((z.C, z.C), 1)[1]
    mask[...] = jnp.where(same, 1.0, 0.0).astype(BF16)


def softplus(values):
    small = jnp.exp(-jnp.abs(values))
    series = jnp.full_like(small, 1.0 / 9.0)
    for order in range(8, 0, -1):
        series = 1.0 / order - small * series
    tail = jnp.where(small < 0.1, small * series, jnp.log(1.0 + small))
    return jnp.maximum(values, 0.0) + tail


class Deal:
    def __init__(self, wire, z, s, h):
        self.wire, self.z, self.s, self.h = wire, z, s, h
        self.tiles = z.F2 // LANES
        self.sent = []

    def rows(self, owner):
        return pl.ds(pl.multiple_of(owner * self.z.Ds, EDGE), self.z.Ds)

    def post(self, src, dst, peer, part, goes, comes):
        wire = self.wire
        item = pltpu.make_async_remote_copy(
            src_ref=src,
            dst_ref=dst,
            send_sem=wire.send.at[wire.count],
            recv_sem=wire.recv.at[wire.count],
            device_id=(peer, self.h),
            device_id_type=MESH,
        )
        wire.count += 1
        self.sent.append((item, part, goes, comes))
        if part == 0:
            item.start()
        else:
            @pl.when(goes)
            def _():
                item.start()

    def out(self, src, dst, offsets):
        z = self.z
        for k in offsets:
            peer = self.s ^ k
            for part in range(2):
                tile = 2 * peer + part
                self.post(
                    at(src, 0, z.Ds, jnp.minimum(tile, self.tiles - 1) * LANES, LANES),
                    dst.at[self.rows(self.s), pl.ds(part * LANES, LANES)],
                    peer,
                    part,
                    tile < self.tiles,
                    2 * self.s + part < self.tiles,
                )

    def back(self, src, dst, offsets):
        z = self.z
        for k in offsets:
            peer = self.s ^ k
            for part in range(2):
                tile = 2 * self.s + part
                lane = jnp.minimum(tile, self.tiles - 1) * LANES
                self.post(
                    src.at[self.rows(peer), pl.ds(part * LANES, LANES)],
                    at(dst, 0, z.Ds, lane, LANES),
                    peer,
                    part,
                    tile < self.tiles,
                    2 * peer + part < self.tiles,
                )

    def steps(self, how, pairs, start=0):
        plan = [(pair, k) for pair in pairs for k in ((4, 2), (5, 3), (6, 1), (7,))]
        for (src, dst), offsets in plan[start:]:
            how(src, dst, offsets)
            yield

    def back_own(self, src, dst):
        z, s = self.z, self.s
        at(dst, 0, z.Ds, 2 * s * LANES, LANES)[...] = src[self.rows(s), 0:LANES]

        @pl.when(2 * s + 1 < self.tiles)
        def _():
            lane = jnp.minimum(2 * s + 1, self.tiles - 1) * LANES
            at(dst, 0, z.Ds, lane, LANES)[...] = src[self.rows(s), LANES : 2 * LANES]

    def wait(self, sent=None):
        for item, part, goes, comes in self.sent if sent is None else sent:
            if part == 0:
                item.wait()
            else:
                @pl.when(goes)
                def _(item=item):
                    item.wait_send()

                @pl.when(comes)
                def _(item=item):
                    item.wait_recv()
        if sent is None:
            self.sent = []


def own_block(z, src, dst, sems, s):
    tiles = z.F2 // LANES
    rows = pl.ds(pl.multiple_of(s * z.Ds, EDGE), z.Ds)
    first = pltpu.make_async_copy(
        at(src, 0, z.Ds, 2 * s * LANES, LANES), dst.at[rows, pl.ds(0, LANES)], sems.at[0]
    )
    second = pltpu.make_async_copy(
        at(src, 0, z.Ds, jnp.minimum(2 * s + 1, tiles - 1) * LANES, LANES),
        dst.at[rows, pl.ds(LANES, LANES)],
        sems.at[1],
    )
    whole = 2 * s + 1 < tiles
    first.start()

    @pl.when(whole)
    def _():
        second.start()

    @pl.when(jnp.logical_not(whole))
    def _():
        dst[:, LANES : 2 * LANES] = jnp.zeros((z.D, LANES), BF16)

    def wait():
        first.wait()

        @pl.when(whole)
        def _():
            second.wait()

    return wait


def chain_scratch(z, rows, width):
    return [VM((rows, width), F32)] + [VM((z.Z, rows, width), BF16)] * 3 + [VM((rows, width), F32)]


def row_blocks(z, buf, part=None):
    count = z.R if part is None else z.R // 2
    first = 0 if part is None else part * count
    return lambda index: buf.at[pl.ds(pl.multiple_of(index * z.R + first, EDGE), count), :]


def scatter_halves(chain, z, block, stash, bufs):
    count = z.R // 2

    def cut(buf, part):
        rows = pl.ds(part * count, count)
        return buf.at[:, rows, :] if len(buf.shape) == 3 else buf.at[rows, :]

    def first(d):
        whole = block(d)
        stash[...] = whole[count:, :]
        return whole[:count, :]

    return [
        chain.scatter(source, *(cut(buf, part) for buf in bufs))
        for part, source in enumerate((first, lambda d: stash[...]))
    ]


class Grid:
    def __init__(self, s, h):
        self.s, self.h = s, h
        self.x, self.y, self.core = (s ^ 1, h), (s, h ^ 2), (s, h ^ 1)

    def z(self, kz):
        return (self.s ^ (2 * kz), self.h)


def gather_all(wire, z, g, region):
    s, h, xi = g.s, g.h, g.s % 2
    chain = Chain(wire, z.Z, s, h)
    arrivals = chain.gather(lambda index: region(2 * index + xi, h, None))
    mine = next(arrivals)
    yield None
    blocks, near, far, core = [], {}, {}, []

    def send(a, b, half, peer, held):
        return wire.copy(region(a, b, half), region(a, b, half), peer, held, held)

    def one(i):
        held, index = next(arrivals) if i else mine
        a = 2 * index + xi
        blocks.append((held, a))
        near[0, i] = send(a, h, 0, g.x, held)
        near[1, i] = send(a, h, 1, g.y, held)
        far[0, i, 0] = send(a, h, 0, g.y, held)
        far[1, i, 0] = send(a, h, 1, g.x, held)
        core.append(send(a, h, None, g.core, held))

    def two(i):
        held, a = blocks[i]
        near[0, i].wait_recv()
        far[0, i, 1] = send(a ^ 1, h, 0, g.y, held)
        core.append(send(a ^ 1, h, 0, g.core, held))
        near[1, i].wait_recv()
        far[1, i, 1] = send(a, h ^ 2, 1, g.x, held)
        core.append(send(a, h ^ 2, 1, g.core, held))

    def three(i):
        held, a = blocks[i]
        far[0, i, 0].wait_recv()
        core.append(send(a, h ^ 2, 0, g.core, held))
        far[1, i, 0].wait_recv()
        core.append(send(a ^ 1, h, 1, g.core, held))

    def four(i):
        held, a = blocks[i]
        far[0, i, 1].wait_recv()
        core.append(send(a ^ 1, h ^ 2, 0, g.core, held))
        far[1, i, 1].wait_recv()
        core.append(send(a ^ 1, h ^ 2, 1, g.core, held))

    count = 2 * z.Z - 1
    stages = (one, two, three, four)
    for turn in range(count + 6):
        for lag, stage in enumerate(stages):
            if 0 <= turn - 2 * lag < count:
                stage(turn - 2 * lag)
        yield turn
    for item in core:
        item.wait_recv()


def gather_copies(z):
    return 2 * (z.Z - 1) + 13 * (2 * z.Z - 1)


class SumAll:
    def __init__(self, wire, z, g, region, bufs):
        self.wire, self.zz, self.g, self.region = wire, z, g, region
        self.from_core, self.hop1, self.hop2, self.up, self.down, self.own = bufs
        self.chain = Chain(wire, z.Z, g.s, g.h)
        self.flight = {}
        self.base = wire.count
        wire.count += self.copies(z)

    @staticmethod
    def copies(z):
        return z.Z * (4 + 4 + 2) + 4 * z.Z

    @staticmethod
    def scratch(z, rows, lanes):
        half = rows // 2
        return [
            VM((z.Z, 4, rows, lanes), BF16),
            VM((z.Z, 4, half, lanes), BF16),
            VM((z.Z, 2, half, lanes), BF16),
            VM((z.Z, 2, half, lanes), BF16),
            VM((z.Z, 2, half, lanes), BF16),
            VM((2, half, lanes), F32),
        ]

    def put(self, a, b, half, dst, peer, slot):
        kept, self.wire.count = self.wire.count, self.base + slot
        item = self.wire.copy(self.region(a, b, half), dst, peer)
        self.wire.count = kept
        return item

    def add(self, a, b, half, got):
        spot = self.region(a, b, half)
        spot[...] = (spot[...].astype(F32) + got[...].astype(F32)).astype(BF16)

    def core(self, i, d):
        g = self.g
        for k in range(4):
            a, b = (2 * d + g.s % 2) ^ (k // 2), g.h ^ 1 ^ (2 * (k % 2))
            self.flight["core", i, k] = self.put(
                a, b, None, self.from_core.at[d, k], g.core, 10 * i + k
            )

    def first(self, i, d):
        g = self.g
        rows = self.hop1.shape[2]
        for k in (1, 3, 2, 0):
            self.flight["core", i, k].wait_recv()
            a, b = (2 * d + g.s % 2) ^ (k // 2), g.h ^ (2 * (k % 2))
            for half in range(2):
                self.add(a, b, half, self.from_core.at[d, k, pl.ds(half * rows, rows), :])
            if k % 2:
                key = k // 2
                self.flight["one", i, key] = self.put(
                    a, b, 0, self.hop1.at[d, key], g.y, 10 * i + 4 + key
                )
            if k // 2:
                key = 2 + k % 2
                self.flight["one", i, key] = self.put(
                    a, b, 1, self.hop1.at[d, key], g.x, 10 * i + 4 + key
                )

    def second(self, i, d):
        g = self.g
        a = 2 * d + g.s % 2
        for key in (1, 0):
            self.flight["one", i, key].wait_recv()
            self.add(a ^ key, g.h, 0, self.hop1.at[d, key])
        self.flight["two", i, 0] = self.put(
            a ^ 1, g.h, 0, self.hop2.at[d, 0], g.x, 10 * i + 8
        )
        for key in (3, 2):
            self.flight["one", i, key].wait_recv()
            self.add(a, g.h ^ (2 * (key - 2)), 1, self.hop1.at[d, key])
        self.flight["two", i, 1] = self.put(
            a, g.h ^ 2, 1, self.hop2.at[d, 1], g.y, 10 * i + 9
        )

    def third(self, i, d):
        g, chain = self.g, self.chain
        a, count = 2 * d + g.s % 2, self.zz.Z
        below, above = chain.between(d)
        for half in range(2):
            self.flight["two", i, half].wait_recv()
            self.add(a, g.h, half, self.hop2.at[d, half])
            kept = self.wire.count
            self.wire.count = self.base + 10 * count + 2 * count * half
            ups, downs = chain.passes(
                d, self.region(a, g.h, half), self.up.at[d, half], self.down.at[d, half]
            )
            self.wire.count = kept
            self.flight["z", i, half] = d, ups, downs
            when(below, self.taken(ups, a, half, self.up.at[d, half]))
            when(above, self.taken(downs, a, half, self.down.at[d, half]))
            ups.start()
            downs.start()

    def taken(self, item, a, half, got):
        def action():
            item.arrived()
            self.add(a, self.g.h, half, got)
        return action

    def finish(self, half):
        g = self.g
        own = self.own.at[half]
        own[...] = self.region(g.s, g.h, half)[...].astype(F32)

        def add(item, got):
            def action():
                item.arrived()
                own[...] = own[...] + got[...].astype(F32)
            return action

        for i in range(self.zz.Z):
            d, ups, downs = self.flight["z", i, half]
            below, above = self.chain.ends(d)
            when(below, add(ups, self.up.at[d, half]))
            when(above, add(downs, self.down.at[d, half]))
        return own[...]

    def run(self, produce):
        order = self.chain.order()
        steps = [
            lambda i, d: (produce(d), self.core(i, d)),
            self.first,
            self.second,
            self.third,
        ]
        count = len(order)
        for turn in range(count + len(steps) - 1):
            for stage in range(len(steps)):
                if 0 <= turn - stage < count:
                    steps[stage](turn - stage, order[turn - stage])
                    yield turn


def halves(ref, rows, row_count, lanes, lane_count, half):
    if half is not None:
        row_count //= 2
        rows = rows + half * row_count
    return at(ref, rows, row_count, lanes, lane_count)


def region_of(z, ref):
    return lambda a, b, half: halves(
        ref, a // 2 * 2 * z.Ds, 2 * z.Ds, (2 * b + a % 2) * z.R, z.R, half
    )


FRONT_RESULTS = 27


def front_kernel(
    z, tok, gain1, gain2, xw, yw, ow, conv_w, conv_b, a_b, i_b, decay, aw, iw, cot_in,
    gw_in, uw_in, dw_in, *rest
):
    outs, rest = rest[:FRONT_RESULTS], rest[FRONT_RESULTS:]
    held, rest = rest[:FRONT_RESULTS], rest[FRONT_RESULTS:]
    (
        xw2, yw2, ow2, tok2, fn2, rn, yb, pad, conv, a_o, i_o, st, entry_o, mix, res,
        vec, mask, spread, gain_q, hid, dw, uwg_o, dwg_o, back_g, gsum_o, bg_o, back_u,
    ) = held
    (
        turned, fnt, stash, x1, x2, x3, x4, x5, y1, y2, y3, y4, y5, sums, tot, part, got, edge, gains,
        cot, gw, uw, xt, gwt, uwt, dwt, gwg, hg, gg, ug, gs, us, rs, wide,
        c1, c2, c3, c4, c5, c6, stat, send, recv, own_sem, out_sem,
    ) = rest
    leaving = []

    def flush(first, last):
        for index in range(first, last):
            copy = pltpu.make_async_copy(held[index], outs[index], out_sem.at[index])
            copy.start()
            leaving.append(copy)

    s, h = place()
    S, H, R, D, T, Ds, C, Z = z.S, z.H, z.R, z.D, z.T, z.Ds, z.C, z.Z
    DG = 2 * Ds
    Q = DG // H
    zi, xi = s // 2, s % 2
    after, before = lax.rem(s + 1, S), lax.rem(s + S - 1, S)
    greet(
        [(s ^ k, h) for k in range(1, S)]
        + [(s, h ^ j) for j in range(1, H)]
        + [(after, h), (before, h)]
    )
    wire = Wire(send, recv)
    g = Grid(s, h)
    chain = Chain(wire, Z, s, h)
    deal = Deal(wire, z, s, h)
    pairs = ((gw_in, gw), (uw_in, uw), (dw_in, dw))
    dealing = deal.steps(deal.out, pairs)
    advance(dealing)
    half = pl.ds(pl.multiple_of(xi * Ds, EDGE), Ds)
    twins = [wire.copy(xw, xw2.at[half, :], (s ^ 1, h))]
    turned[...] = tok[...].astype(F32).T.astype(BF16)
    quarter = pl.ds(pl.multiple_of(h * Q, EDGE), Q)
    my_lanes = pl.ds(pl.multiple_of(zi * R, LANES), R)

    def group(index):
        return pl.ds(pl.multiple_of(index * DG + h * Q, EDGE), Q)

    first = [
        wire.copy(turned.at[group(zi ^ kz), :], tok2.at[quarter, my_lanes], (s ^ (2 * kz), h))
        for kz in range(1, Z)
    ]
    column = turned[...].astype(F32)
    mean = jnp.sum(column * column, axis=0, keepdims=True) / z.D
    rn[zi] = jnp.broadcast_to(lax.rsqrt(mean + EPSILON), (8, R))
    for kz in range(1, Z):
        first.append(wire.copy(rn.at[zi], rn.at[zi], (s ^ (2 * kz), h)))
    tok2[quarter, my_lanes] = turned[group(zi), :]
    vec[...] = jnp.zeros_like(vec)
    vec[0:CONV, :] = conv_w[...].astype(F32)
    for index, ref in enumerate((conv_b, a_b, i_b)):
        vec[4 + index : 5 + index, :] = ref[...].astype(F32)[None, :]
    vec[7:8, :] = softplus(decay[...][None, :])
    vec[8:9, :] = jax.nn.sigmoid(decay[...][None, :])
    eight = lax.broadcasted_iota(jnp.int32, (8, D), 0)
    gains[...] = jnp.where(
        eight == 0, gain1[...].astype(F32)[None, :], gain2[...].astype(F32)[None, :]
    ).T
    gain_q[...] = gains[pl.ds(pl.multiple_of(zi * DG + h * Q, EDGE), Q), :]
    gain_s = gains[pl.ds(pl.multiple_of(zi * DG, EDGE), DG), 0:1]
    head_maps(z, spread, mask)
    xw2[half, :] = xw[...]
    yw2[half, :] = yw[...]
    ow2[half, :] = ow[...]
    pending = [
        own_block(z, src, dst, own_sem.at[pl.ds(2 * i, 2)], s)
        for i, (src, dst) in enumerate(pairs)
    ]
    W = z.D // H

    def corner(a, b, half):
        return halves(cot, a * R, R, b * W, W, half)

    corner(s, h, None)[...] = cot_in[:, pl.ds(pl.multiple_of(h * W, LANES), W)]
    cot_in_all = gather_all(wire, z, g, corner)
    advance(cot_in_all)
    advance(dealing, 2)
    for item in first:
        item.wait_recv()
    HeadGather(
        wire, s, h, lambda j: tok2.at[pl.ds(pl.multiple_of(j * Q, EDGE), Q), :]
    ).wait_all()
    for b in range(Z):
        cut = slice(b * R, b * R + R)
        fn2[:, cut] = (tok2[:, cut].astype(F32) * rn[b, 0:1, :] * gain_s).astype(BF16)
    twins[0].wait_recv()
    for src, dst in ((yw, yw2), (ow, ow2)):
        twins.append(wire.copy(src, dst.at[half, :], (s ^ 1, h)))

    def x_part(d):
        lanes = pl.ds(pl.multiple_of(d * R, LANES), R)
        fnt[d] = fn2[:, lanes].astype(F32).T.astype(BF16)
        return mm(fnt[d], xw2[...])

    x_sum = scatter_halves(chain, z, x_part, stash, (x1, x2, x3, x4, x5))
    for _ in range(Z):
        for step in x_sum:
            advance(step)
    advance(cot_in_all, 1)
    advance(dealing, 0)
    drain(*x_sum)
    x_low = x5[...].astype(BF16)
    edge[0] = x_low[R - EDGE : R, :]
    halo = wire.copy(edge.at[0], edge.at[1], (after, h))
    twins[1].wait_recv()
    y_sum = chain.scatter(lambda d: mm(fnt[d], yw2[...]), y1, y2, y3, y4, y5)
    advance(y_sum, 1)
    advance(dealing, 1)
    advance(cot_in_all, 2)
    pad[pl.ds(EDGE, R), :] = x_low.astype(F32)
    halo.wait_recv()
    pad[pl.ds(0, EDGE), :] = jnp.where(s == 0, 0.0, edge[1].astype(F32))
    out = jnp.broadcast_to(vec[4:5, :], (R, C))
    for lag in range(CONV):
        out = out + vec[lag : lag + 1, :] * pad[pl.ds(EDGE - lag, R), :]
    conv[h] = out.astype(BF16)
    across = HeadGather(wire, s, h, lambda j: conv.at[j])
    advance(dealing, 1)
    advance(cot_in_all, 2)
    advance(y_sum, 1)
    a_pre = jnp.broadcast_to(vec[5:6, :], (R, C))
    i_pre = jnp.broadcast_to(vec[6:7, :], (R, C))
    for j in (0, 2, 1, 3):
        if j:
            across.wait(j)
        k = h ^ j
        taken = conv[k]
        a_pre = a_pre + mm(taken, gate_weight_of(z, spread, mask, aw, k))
        i_pre = i_pre + mm(taken, gate_weight_of(z, spread, mask, iw, k))
    advance(y_sum, 1)
    a_o[...] = a_pre
    i_o[...] = i_pre
    anchor = anchor_of(z, s, LANES)
    sums[s] = jnp.zeros((8, C), F32)
    for b in range(C // LANES):
        cut = pl.ds(b * LANES, LANES)
        recall, input_gate, factor, one_minus, root_value, root_scale = decay_terms(
            a_o[:, cut], i_o[:, cut], vec[7:8, cut], anchor
        )
        driven = conv[h, :, cut].astype(F32) * input_gate * root_scale
        prod, value = scan_rows(factor, driven, 1)
        st[:, cut] = value
        tot[:, cut] = prod
        sums[s, 0:1, cut] = prod[R - 1 : R, :]
        sums[s, 1:2, cut] = value[R - 1 : R, :]
    ends = [wire.copy(sums.at[s], sums.at[s], (s ^ k, h)) for k in range(1, S)]
    advance(dealing, 0)
    advance(cot_in_all, 2)
    drain(y_sum)
    yb[...] = y5[...]
    for item in ends:
        item.wait_recv()
    entry = jnp.zeros((1, C), F32)
    for j in range(S - 1):
        entry = jnp.where(j < s, sums[j, 0:1, :] * entry + sums[j, 1:2, :], entry)
    entry_o[...] = jnp.broadcast_to(entry, (8, C))
    my_rows = pl.ds(pl.multiple_of(zi * R, EDGE), R)
    for b in range(C // LANES):
        cut = pl.ds(b * LANES, LANES)
        state = st[:, cut] + tot[:, cut] * entry_o[0:1, cut]
        st[:, cut] = state
        mix[my_rows, cut] = (state * gelu_pair(yb[:, cut])[0]).astype(BF16)
    arriving = [chain.gather(row_blocks(z, mix, part_of)) for part_of in range(2)]
    for step in arriving:
        advance(step)
    advance(dealing, 1)
    advance(cot_in_all, 3)
    drain(*arriving)
    twins[2].wait_recv()

    def out_part(j):
        rows = pl.ds(pl.multiple_of((h ^ j) * R, EDGE), R)
        return mm(ow2[...], mix[rows, :], NT)

    whole = head_scatter(wire, s, h, out_part, part, got)
    advance(dealing, 2)
    advance(cot_in_all, 3)
    res[...] = whole() + tok2[:, pl.ds(pl.multiple_of(h * R, LANES), R)].astype(F32)


    flush(0, 19)
    tile = 256
    region_of(z, xt)(s, h, None)[...] = res[...].astype(BF16)
    spreading = gather_all(wire, z, g, region_of(z, xt))
    advance(spreading, 2)
    def turn(src, dst, scaled):
        for n in range(D // tile):
            cut = slice(n * tile, n * tile + tile)
            piece = src[cut, :].astype(F32)
            dst[:, cut] = (piece * gains[cut, 1:2] if scaled else piece).T.astype(BF16)

    advance(spreading, 3)
    advance(dealing, 2)
    advance(spreading, 2)
    advance(dealing, 2)
    drain(spreading, dealing, cot_in_all)
    for wait in pending:
        wait()
    posted, deal.sent = deal.sent, []
    count = len(posted) // 3
    deal.wait(posted[: 2 * count])
    turn(gw, gwt, True)
    turn(uw, uwt, True)
    for n in range(T // tile):
        cut = slice(n * tile, n * tile + tile)
        square = jnp.zeros((1, tile), F32)
        for b in range(D // tile):
            piece = xt[b * tile : b * tile + tile, cut].astype(F32)
            square = square + jnp.sum(piece * piece, axis=0, keepdims=True)
        rs[:, cut] = jnp.broadcast_to(lax.rsqrt(square / D + EPSILON), (8, tile))
    deal.wait(posted[2 * count :])
    turn(dw, dwt, False)
    for n in range(T // tile):
        cut = slice(n * tile, n * tile + tile)
        hg[:, cut] = mm(dwt[...], cot[cut, :], NT)
        scale = rs[0:1, cut]
        gate = mm(gwt[...], xt[:, cut]) * scale
        up = mm(uwt[...], xt[:, cut]) * scale
        act, slope = gelu_pair(gate)
        hid[:, cut] = (act * up).astype(BF16)
        back = hg[:, cut]
        gate_grad = back * up * slope
        up_grad = back * act
        gg[:, cut] = gate_grad.astype(BF16)
        ug[:, cut] = up_grad.astype(BF16)
        gs[:, cut] = (gate_grad * scale).astype(BF16)
        us[:, cut] = (up_grad * scale).astype(BF16)
    second = SumAll(wire, z, g, region_of(z, wide), (c1, c2, c3, c4, c5, c6))

    def produce(d):
        rows = pl.ds(pl.multiple_of(d * DG, LANES), DG)
        wide[rows, :] = (mm(gw[rows, :], gg[...]) + mm(uw[rows, :], ug[...])).astype(BF16)

    summing = second.run(produce)
    advance(summing, 3)
    flush(19, 21)
    for n in range(D // tile):
        cut = slice(n * tile, n * tile + tile)
        gwg[cut, :] = (mm(xt[cut, :], gs[...], NT) * gains[cut, 1:2]).astype(BF16)
    dealing = deal.steps(deal.back, ((gwg, back_g),))
    advance(dealing, 3)
    deal.back_own(gwg, back_g)
    advance(summing, 6)
    advance(dealing, 1)
    drain(summing)
    for n in range(D // tile):
        cut = slice(n * tile, n * tile + tile)
        uwg_o[cut, :] = (mm(xt[cut, :], us[...], NT) * gains[cut, 1:2]).astype(BF16)
        dwg_o[cut, :] = mm(hid[...], cot[:, cut]).T.astype(BF16)
    flush(21, 23)
    rising = deal.steps(deal.back, ((uwg_o, back_u),))
    second_grad = jnp.concatenate([second.finish(0), second.finish(1)], axis=0)
    mine = pl.ds(pl.multiple_of((2 * h + xi) * R, LANES), R)
    group = pl.ds(pl.multiple_of(zi * DG, LANES), DG)
    scale = rs[0:1, mine]
    residual = res[...]
    gsum_o[...] = second_grad * residual * scale
    weighted = gains[group, 1:2] * second_grad
    stat[zi] = jnp.broadcast_to(jnp.sum(weighted * residual, axis=0, keepdims=True), (8, R))
    ends = [wire.copy(stat.at[zi], stat.at[zi], g.z(kz)) for kz in range(1, z.Z)]
    direct = cot[mine, group].astype(F32).T + scale * weighted
    for item in ends:
        item.wait_recv()
    advance(rising, 2)
    mean = jnp.sum(stat[:, 0:1, :], axis=0) / D
    grad = direct - residual * (scale * scale * scale * mean)
    lanes = pl.ds(pl.multiple_of(h * R, LANES), R)
    bg_o[:, lanes] = grad.astype(BF16)
    HeadGather(
        wire, s, h, lambda j: bg_o.at[:, pl.ds(pl.multiple_of(j * R, LANES), R)]
    ).wait_all()
    deal.wait()
    flush(23, 27)
    wire.close()
    for copy in leaving:
        copy.wait()


def front(z, *args):
    S, H, R, D, T, U, Ds, C, Z = z.S, z.H, z.R, z.D, z.T, z.U, z.Ds, z.C, z.Z
    DG, TX = 2 * Ds, Z * R
    copies = 2 + 2 * (Z - 1) + (H - 1) + 1 + 6 * Z + 1 + (H - 1) + (S - 1)
    copies += 4 * (Z - 1) + (H - 1) + 8 * (S - 1) + 8 + 2 * gather_copies(z)
    copies += SumAll.copies(z) + (Z - 1) + (H - 1)
    results = [
        sds((DG, C), BF16),
        sds((DG, C), BF16),
        sds((DG, C), BF16),
        sds((DG, TX), BF16),
        sds((DG, TX), BF16),
        sds((Z, 8, R), F32),
        sds((R, C), F32),
        sds((EDGE + R, C), F32),
        sds((H, R, C), BF16),
        sds((R, C), F32),
        sds((R, C), F32),
        sds((R, C), F32),
        sds((8, C), F32),
        sds((TX, C), BF16),
        sds((DG, R), F32),
        sds((EDGE, C), F32),
        sds((C, C), BF16),
        sds((C, z.NI), BF16),
        sds((DG // H, 8), F32),
        sds((U, T), BF16),
        sds((D, U), BF16),
        sds((D, U), BF16),
        sds((D, U), BF16),
        sds((Ds, z.F2), BF16),
        sds((DG, R), F32),
        sds((DG, TX), BF16),
        sds((Ds, z.F2), BF16),
    ]
    return call(
        functools.partial(front_kernel, z),
        "front",
        1,
        results,
        [VM(item.shape, item.dtype) for item in results]
        + [
            VM((D, R), BF16),
            VM((Z, R, DG), BF16),
            VM((R // 2, C), F32),
            *chain_scratch(z, R, C),
            *chain_scratch(z, R, C),
            VM((S, 8, C), F32),
            VM((R, C), F32),
            VM((H, DG, R), BF16),
            VM((H, DG, R), BF16),
            VM((2, EDGE, C), BF16),
            VM((D, 8), F32),
            VM((T, D), BF16),
            VM((D, U), BF16),
            VM((D, U), BF16),
            VM((D, T), BF16),
            VM((U, D), BF16),
            VM((U, D), BF16),
            VM((U, D), BF16),
            VM((D, U), BF16),
            VM((U, T), F32),
            VM((U, T), BF16),
            VM((U, T), BF16),
            VM((U, T), BF16),
            VM((U, T), BF16),
            VM((8, T), F32),
            VM((D, T), BF16),
            *SumAll.scratch(z, DG, R),
            VM((Z, 8, R), F32),
            sem(copies),
            sem(copies),
            sem(6),
            sem(len(results)),
        ],
        args,
        (14, 15, 16),
        True,
    )


def exact(left, right, dims):
    return lax.dot_general(
        left, right, dims, precision=lax.Precision.HIGHEST, preferred_element_type=F32
    )


def back_kernel(
    z, far, held, fetch_sem, mixed_o, owg_o, xwg_o, ywg_o, twin_r, full, gains2, smallg, vec_o, back_u, back_d,
    stash, g1, g2, g3, g4, own, adj, tot, ag, ig, sums, late, cgr, cgs, ext, gx, gy, part, got, stat, stat2,
    tgq, prod, prod2, gains, small, smallx, small_z, vecs, twin_s, mpart, m1, m2, m3, m4, m5, m6, send, recv,
):
    (
        bg, ow2, hid, dw, res, mix, yb, vec, a_pre, i_pre, st, entry, conv, pad, aw, iw, spread,
        mask, xw2, yw2, fn2, tok2, rn, gain, msum, uwg, dwg,
    ) = held
    fetch = [
        pltpu.make_async_copy(src, dst, fetch_sem.at[index])
        for index, (src, dst) in enumerate(zip(far, held))
    ]
    begun = pltpu.make_async_copy(far[-1], back_u, fetch_sem.at[len(held)])
    begun.start()
    for copy in fetch:
        copy.start()
    begun.wait()
    s, h = place()
    g = Grid(s, h)
    S, H, R, D, Ds, C, Z, T = z.S, z.H, z.R, z.D, z.Ds, z.C, z.Z, z.T
    DG, W = 2 * Ds, D // H
    Q = DG // H
    zi, xi = s // 2, s % 2
    after, before = lax.rem(s + 1, S), lax.rem(s + S - 1, S)
    greet(
        [(s ^ k, h) for k in range(1, S)]
        + [(s, h ^ j) for j in range(1, H)]
        + [(after, h), (before, h)]
    )
    wire = Wire(send, recv)
    chain = Chain(wire, Z, s, h)
    deal = Deal(wire, z, s, h)
    dealing = deal.steps(deal.back, ((uwg, back_u), (dwg, back_d)), 2)
    my_rows = pl.ds(pl.multiple_of(zi * R, EDGE), R)
    half = pl.ds(pl.multiple_of(xi * Ds, EDGE), Ds)
    other = pl.ds(pl.multiple_of((1 - xi) * Ds, EDGE), Ds)

    def corner(a, b, part_of):
        return halves(mpart, b * W, W, a * R, R, part_of)

    mixed = SumAll(wire, z, g, corner, (m1, m2, m3, m4, m5, m6))

    def produce_mixed(d):
        cut = pl.ds(pl.multiple_of(d * 2 * R, LANES), 2 * R)
        mpart[:, cut] = mm(dw[...], hid[:, cut]).astype(BF16)

        @pl.when(h == d)
        def _():
            spot = region_of(z, mpart)(s, h, None)
            spot[...] = (spot[...].astype(F32) + res[...]).astype(BF16)

    mixing = mixed.run(produce_mixed)

    def block(d):
        lanes = pl.ds(pl.multiple_of(d * R, LANES), R)
        return mm(bg[:, lanes].astype(F32).T.astype(BF16), ow2[...])

    for copy in fetch[:5]:
        copy.wait()
    summing = scatter_halves(chain, z, block, stash, (g1, g2, g3, g4, own))
    for _ in range(Z):
        for step in summing:
            advance(step)
        advance(mixing, 2)
    for copy in fetch[5:]:
        copy.wait()
    drain(*summing)
    row = lax.broadcasted_iota(jnp.int32, (R, LANES), 0)
    anchor = anchor_of(z, s, LANES)
    sums[s] = jnp.zeros((8, C), F32)
    for b in range(C // LANES):
        cut = pl.ds(b * LANES, LANES)
        grad = own[:, cut]
        gate, slope = gelu_pair(yb[:, cut])
        gy[my_rows, cut] = (grad * st[:, cut] * slope).astype(BF16)
        factor = jnp.exp(-8.0 * jax.nn.sigmoid(a_pre[:, cut]) * vec[7:8, cut])
        ahead = shifted(factor, -1, 1.0, row)
        prods, value = scan_rows(ahead, grad * gate, -1)
        tot[:, cut] = prods
        adj[:, cut] = value
        sums[s, 0:1, cut] = factor[0:1, :] * prods[0:1, :]
        sums[s, 1:2, cut] = factor[0:1, :] * value[0:1, :]
    ends = [wire.copy(sums.at[s], sums.at[s], (s ^ k, h)) for k in range(1, S)]
    y_rows = chain.gather(row_blocks(z, gy))
    advance(y_rows)
    advance(dealing, 0)
    twins = []

    def weight_grad(index, left, right, out):
        prod2[...] = mm(left[...], right[...])
        twin_s[index] = prod2[other, :].astype(BF16)
        twins.append(wire.copy(twin_s.at[index], twin_r.at[index], g.x))
        out[...] = prod2[half, :]

    weight_grad(0, bg, mix, owg_o)
    advance(mixing, 2)
    for item in ends:
        item.wait_recv()
    carry = jnp.zeros((1, C), F32)
    for j in range(S - 1, 0, -1):
        carry = jnp.where(j > s, sums[j, 0:1, :] * carry + sums[j, 1:2, :], carry)
    vec_o[...] = jnp.zeros_like(vec_o)
    late[...] = jnp.broadcast_to(carry, (8, C))
    for b in range(C // LANES):
        cut = pl.ds(b * LANES, LANES)
        adjoint = adj[:, cut] + tot[:, cut] * late[0:1, cut]
        rate = vec[7:8, cut]
        recall, input_gate, factor, one_minus, root_value, root_scale = decay_terms(
            a_pre[:, cut], i_pre[:, cut], rate, anchor
        )
        taken = conv[h, :, cut].astype(F32)
        state = st[:, cut]
        earlier = jnp.where(row == 0, entry[0:1, cut], shifted(state, 1, 0.0, row))
        live = jnp.logical_and(one_minus > SQUARE_FLOOR, jnp.logical_not(anchor))
        scale_grad = adjoint * taken * input_gate
        log_grad = adjoint * earlier * factor - jnp.where(
            live, scale_grad * factor * factor / root_value, 0.0
        )
        a_grad = (log_grad * (-8.0 * rate) * recall * (1.0 - recall)).astype(BF16)
        i_grad = (scale_grad * root_scale * (1.0 - input_gate)).astype(BF16)
        ag[:, cut] = a_grad
        ig[:, cut] = i_grad
        decay_sum = jnp.sum(log_grad * (-8.0 * recall), axis=0, keepdims=True)
        vec_o[5:6, cut] = jnp.sum(a_grad.astype(F32), axis=0, keepdims=True)
        vec_o[6:7, cut] = jnp.sum(i_grad.astype(F32), axis=0, keepdims=True)
        vec_o[7:8, cut] = decay_sum * vec[8:9, cut]
        ext[pl.ds(0, R), cut] = adjoint * input_gate * root_scale

    eighth = small.shape[0] // S

    def share(x_index, z_index, count):
        start = (x_index * Z + z_index) * eighth
        return pl.ds(pl.multiple_of(start, EDGE), count * eighth)

    def sum_small():
        mine = share(xi, 0, Z)
        item = wire.copy(small.at[share(1 - xi, 0, Z), :], smallx, g.x)
        yield
        item.wait_recv()
        smallx[...] = (smallx[...].astype(F32) + small[mine, :].astype(F32)).astype(BF16)

        def piece(index):
            return pl.ds(pl.multiple_of(index * eighth, EDGE), eighth)

        items = [
            wire.copy(smallx.at[piece(zi ^ kz), :], small_z.at[kz], g.z(kz))
            for kz in range(1, Z)
        ]
        yield
        total = smallx[piece(zi), :].astype(F32)
        for kz in range(1, Z):
            items[kz - 1].wait_recv()
            total = total + small_z[kz].astype(F32)
        spot = smallg.at[share(xi, zi, 1), :]
        spot[...] = total.astype(BF16)
        items = [wire.copy(spot, spot, g.z(kz)) for kz in range(1, Z)]
        yield
        for item in items:
            item.wait_recv()
        item = wire.copy(smallg.at[mine, :], smallg.at[mine, :], g.x)
        yield
        item.wait_recv()

    smaller = sum_small()
    def gates_back(j):
        return mm(ag[...], gate_weight_of(z, spread, mask, aw, h ^ j), NT) + mm(
            ig[...], gate_weight_of(z, spread, mask, iw, h ^ j), NT
        )

    advance(y_rows, 2)
    across = head_scatter(wire, s, h, gates_back, cgs, cgr)
    advance(y_rows, 2)
    advance(dealing, 3)
    for k in range(H):
        turn = conv[k].astype(F32).T.astype(BF16)
        for spot, grad in ((0, ag), (z.HS, ig)):
            dense = mm(turn, grad[...]).astype(BF16) * mask[...]
            small[pl.ds(spot + k * z.NI, z.NI), :] = mm(spread[...], dense, TN).astype(BF16)
    advance(smaller)
    advance(mixing, 2)
    conv_grad = ext[pl.ds(0, R), :] + across()
    ext[pl.ds(0, R), :] = conv_grad
    halo = wire.copy(ext.at[pl.ds(0, 8), :], ext.at[pl.ds(R, 8), :], (before, h))
    for lag in range(CONV):
        vec_o[lag : lag + 1, :] = jnp.sum(
            conv_grad * pad[pl.ds(EDGE - lag, R), :], axis=0, keepdims=True
        )
    vec_o[4:5, :] = jnp.sum(conv_grad, axis=0, keepdims=True)
    vecs[s] = vec_o[...]
    advance(mixing, 1)
    advance(smaller)
    halo.wait_recv()
    ext[pl.ds(R, 8), :] = jnp.where(s == S - 1, 0.0, ext[pl.ds(R, 8), :])
    grad = jnp.zeros((R, C), F32)
    for lag in range(CONV):
        grad = grad + vec[lag : lag + 1, :] * ext[pl.ds(lag, R), :]
    gx[my_rows, :] = grad.astype(BF16)
    rows_in = [chain.gather(row_blocks(z, gx, part_of)) for part_of in range(2)]
    for step in rows_in:
        advance(step)
    advance(dealing, 0)
    advance(mixing, 1)
    pair = grad.astype(BF16).astype(F32) * pad[pl.ds(EDGE, R), :] + gy[my_rows, :].astype(F32) * yb[...]
    stat[h] = exact(jnp.ones((8, C), F32), pair, NT)
    stats = [wire.copy(stat.at[h], stat.at[h], (s, h ^ j)) for j in range(1, H)]

    lesser = [wire.copy(vecs.at[s], vecs.at[s], (s ^ k, h)) for k in range(1, S)]
    drain(y_rows)
    weight_grad(1, fn2, gy, ywg_o)
    prod[...] = mm(yw2[...], gy[...], NT)
    for item in stats:
        item.wait_recv()
    stat2[zi] = stat[0] + stat[1] + stat[2] + stat[3]
    stats = [wire.copy(stat2.at[zi], stat2.at[zi], g.z(kz)) for kz in range(1, Z)]
    advance(smaller)
    advance(mixing, 1)
    drain(*rows_in)

    prod[...] = prod[...] + mm(xw2[...], gx[...], NT)

    def quarter_of(j):
        return prod[pl.ds(pl.multiple_of((h ^ j) * Q, EDGE), Q), :]

    heads = head_scatter(wire, s, h, quarter_of, part, got)
    advance(dealing, 3)
    advance(smaller)
    advance(mixing, 1)
    quarter = pl.ds(pl.multiple_of(h * Q, EDGE), Q)
    weight_grad(2, fn2, gx, xwg_o)
    total = heads()
    for item in stats:
        item.wait_recv()
    token = tok2[quarter, :].astype(F32)
    norm = jnp.concatenate([rn[b, 0:1, :] for b in range(Z)], axis=1)
    mean = jnp.concatenate([stat2[b, 0:1, :] for b in range(Z)], axis=1) / (norm * D)
    weighted = gain[:, 0:1] * total
    grad = bg[quarter, :].astype(F32) + norm * weighted - token * (norm * norm * norm * mean)
    tgq[...] = grad.astype(BF16)

    def spot(z_index, head):
        return full.at[pl.ds(pl.multiple_of(z_index * DG + head * Q, EDGE), Q), :]

    outs = [
        wire.copy(
            tgq.at[:, pl.ds(pl.multiple_of((zi ^ kz) * R, LANES), R)], spot(zi, h), g.z(kz)
        )
        for kz in range(1, Z)
    ]
    spot(zi, h)[...] = tgq[:, pl.ds(pl.multiple_of(zi * R, LANES), R)]
    prod[...] = jnp.zeros_like(prod)
    prod[quarter, :] = total * token * norm
    ones = jnp.ones((8, Z * R), F32)
    picked = lax.broadcasted_iota(jnp.int32, (8, DG), 0)
    gains[h] = jnp.where(
        picked == 0, exact(jnp.ones((8, R), F32), msum[...], NT), exact(ones, prod[...], NT)
    )
    tally = [wire.copy(gains.at[h], gains.at[h], (s, h ^ j)) for j in range(1, H)]
    finals = []
    drain(dealing)
    for kz in range(Z):
        if kz:
            outs[kz - 1].wait_recv()
        finals.append(HeadGather(wire, s, h, lambda j, kz=kz: spot(zi ^ kz, j)))
    for item in tally:
        item.wait_recv()
    gains2[s] = gains[0] + gains[1] + gains[2] + gains[3]
    tally = [wire.copy(gains2.at[s], gains2.at[s], (s ^ k, h)) for k in range(1, S)]
    drain(mixing)
    for part_of in range(2):
        mixed_o[pl.ds(part_of * W // 2, W // 2), :] = mixed.finish(part_of)
    for item in lesser:
        item.wait_recv()
    vec_o[...] = jnp.sum(vecs[...], axis=0)
    for item in twins:
        item.wait_recv()
    deal.back_own(uwg, back_u)
    deal.back_own(dwg, back_d)
    drain(smaller)
    for item in tally:
        item.wait_recv()
    for item in finals:
        item.wait_all()
    deal.wait()
    wire.close()


def back(z, *args):
    S, H, R, D, Ds, C, Z, T = z.S, z.H, z.R, z.D, z.Ds, z.C, z.Z, z.T
    DG, W = 2 * Ds, D // H
    TX, Q = Z * R, DG // H
    copies = (
        4 * Z + (S - 1) + 3 + (H - 1) + 1 + 6 * (Z - 1) + (H - 1) + (Z - 1) + (S - 1)
        + 2 + 2 * (Z - 1) + 2 * (Z - 1) + 4 * (S - 1) + (H - 1) + (Z - 1) + (H - 1) + Z * (H - 1) + (S - 1)
        + SumAll.copies(z)
    )
    small = 2 * z.HS
    count = len(args)

    def body(*refs):
        far, rest = refs[:count], refs[count:]
        outs, held, rest = rest[:11], rest[11 : 10 + count], rest[10 + count :]
        back_kernel(z, far, held, rest[0], *outs, *rest[1:])

    return call(
        body,
        "back",
        2,
        [
            sds((W, R), F32),
            sds((Ds, C), F32),
            sds((Ds, C), F32),
            sds((Ds, C), F32),
            sds((3, Ds, C), BF16),
            sds((D, R), BF16),
            sds((S, 8, DG), F32),
            sds((small, C), BF16),
            sds((8, C), F32),
            sds((Ds, z.F2), BF16),
            sds((Ds, z.F2), BF16),
        ],
        [VM(a.shape, a.dtype) for a in args[:-1]]
        + [sem(count)]
        + [
            VM((R // 2, C), F32),
            *chain_scratch(z, R, C),
            VM((R, C), F32),
            VM((R, C), F32),
            VM((R, C), BF16),
            VM((R, C), BF16),
            VM((S, 8, C), F32),
            VM((8, C), F32),
            VM((H, R, C), BF16),
            VM((H, R, C), BF16),
            VM((R + 8, C), F32),
            VM((TX, C), BF16),
            VM((TX, C), BF16),
            VM((H, Q, TX), BF16),
            VM((H, Q, TX), BF16),
            VM((H, 8, R), F32),
            VM((Z, 8, R), F32),
            VM((Q, TX), BF16),
            VM((DG, TX), F32),
            VM((DG, C), F32),
            VM((H, 8, DG), F32),
            VM((small, C), BF16),
            VM((small // 2, C), BF16),
            VM((Z, small // S, C), BF16),
            VM((S, 8, C), F32),
            VM((3, Ds, C), BF16),
            VM((D, T), BF16),
        ]
        + SumAll.scratch(z, W, R)
        + [sem(copies), sem(copies)],
        args,
        range(count),
    )


def results_kernel(z, *refs):
    sources, count = 12, 17
    inputs, outs = refs[:sources], refs[sources : sources + count]
    held = refs[sources + count : 2 * sources + count]
    stage = refs[2 * sources + count : 2 * (sources + count)]
    in_sem, out_sem = refs[-2:]
    fetch = []
    for index in range(sources):
        copy = pltpu.make_async_copy(inputs[index], held[index], in_sem.at[index])
        copy.start()
        fetch.append(copy)
    mixed, owg, xwg, ywg, twins, full, gains, small, vec, back_g, back_u, back_d = held
    copies = []

    def need(*indexes):
        for index in indexes:
            fetch[index].wait()

    def emit(index, value):
        stage[index][...] = value
        copy = pltpu.make_async_copy(stage[index], outs[index], out_sem.at[index])
        copy.start()
        copies.append(copy)

    need(4, 1, 2, 3)
    for index, slot, src in ((12, 0, owg), (4, 1, ywg), (3, 2, xwg)):
        emit(index, src[...] + twins[slot].astype(F32))
    for index, at_input, src in ((14, 9, back_g), (15, 10, back_u), (16, 11, back_d)):
        need(at_input)
        emit(index, src[...].astype(F32))
    need(5, 0, 7, 8, 6)
    emit(1, full[...].astype(F32).T)
    emit(0, mixed[...].T.astype(BF16))
    emit(7, small[0 : z.HS, :].astype(F32))
    emit(9, small[z.HS : 2 * z.HS, :].astype(F32))
    emit(5, vec[0:CONV, :])
    for index, row in ((6, 4), (8, 5), (10, 6), (11, 7)):
        outs[index][...] = vec[row, :]
    for index, row in ((2, 1), (13, 0)):
        sums = [gains[2 * b, row, :] + gains[2 * b + 1, row, :] for b in range(z.Z)]
        outs[index][...] = jnp.concatenate(sums)
    for copy in copies:
        copy.wait()


def results(z, *args):
    R, D, Ds, C, F2 = z.R, z.D, z.Ds, z.C, z.F2
    row = sds((C,), F32)
    outs = [
        sds((R, D // z.H), BF16),
        sds((R, D), F32),
        sds((D,), F32),
        sds((Ds, C), F32),
        sds((Ds, C), F32),
        sds((CONV, C), F32),
        row,
        sds((z.HS, C), F32),
        row,
        sds((z.HS, C), F32),
        row,
        row,
        sds((Ds, C), F32),
        sds((D,), F32),
        sds((Ds, F2), F32),
        sds((Ds, F2), F32),
        sds((Ds, F2), F32),
    ]
    return pl.pallas_call(
        functools.partial(results_kernel, z),
        out_shape=outs,
        in_specs=[pl.BlockSpec(memory_space=ANY)] * len(args),
        out_specs=[
            pl.BlockSpec(memory_space=VM if len(out.shape) == 1 else ANY) for out in outs
        ],
        scratch_shapes=[VM(a.shape, a.dtype) for a in list(args) + outs]
        + [sem(len(args)), sem(len(outs))],
        compiler_params=pltpu.CompilerParams(vmem_limit_bytes=62 << 20),
        name="results",
    )(*args)


def dealt(
    z,
    tokens,
    norm_gain,
    x_weight,
    y_weight,
    conv_weight,
    conv_bias,
    a_weight,
    a_bias,
    i_weight,
    i_bias,
    decay,
    out_weight,
    mlp_gain,
    gate_weight,
    up_weight,
    down_weight,
    cotangent,
):
    (
        xw2, yw2, ow2, tok2, fn2, rn, yb, pad, conv, a_pre, i_pre, st, entry, mix, res,
        vec, mask, spread, gain_q, hid, dc, uwg, dwg, back_g, msum, bg, up_part,
    ) = front(
        z, tokens, norm_gain, mlp_gain, x_weight, y_weight, out_weight, conv_weight, conv_bias,
        a_bias, i_bias, decay, a_weight, i_weight,
        cotangent, gate_weight, up_weight, down_weight,
    )
    mixed, owg, xwg, ywg, twins, tg, gains, small, vec_sum, back_u, back_d = back(
        z, bg, ow2, hid, dc, res, mix, yb, vec, a_pre, i_pre, st, entry, conv, pad, a_weight,
        i_weight, spread, mask, xw2, yw2, fn2, tok2, rn, gain_q, msum, uwg, dwg, up_part,
    )
    return tuple(
        results(z, mixed, owg, xwg, ywg, twins, tg, gains, small, vec_sum, back_g, back_u, back_d)
    )


def from_behind(x, axis, by):
    size = lax.axis_size(axis)
    pairs = [(i, i + by) for i in range(size) if 0 <= i + by < size]
    return lax.ppermute(x, axis, pairs)


def rms_norm(values, gain):
    return values * lax.rsqrt(jnp.mean(values * values, axis=-1, keepdims=True) + EPSILON) * gain


def linear_pair(earlier, later):
    return (later[0] * earlier[0], later[0] * earlier[1] + later[1])


def gelu_back(values, grad):
    return jax.vjp(jax.nn.gelu, values)[1](grad)[0]


def gathered_weights(
    tokens,
    norm_gain,
    x_weight,
    y_weight,
    conv_weight,
    conv_bias,
    a_weight,
    a_bias,
    i_weight,
    i_bias,
    decay,
    out_weight,
    mlp_gain,
    gate_weight,
    up_weight,
    down_weight,
    cotangent,
):
    row_count = tokens.shape[0]
    model_width = tokens.shape[1]
    lane_count = x_weight.shape[1]
    head_size = a_weight.shape[0]
    head_index = lax.axis_index("head")
    seq_index = lax.axis_index("seq")
    head_devices = lax.axis_size("head")
    float_type = jnp.float32
    half_type = jnp.bfloat16
    gathered = (
        lax.all_gather(x_weight, "seq", axis=0, tiled=True),
        lax.all_gather(y_weight, "seq", axis=0, tiled=True),
        lax.all_gather(out_weight, "seq", axis=0, tiled=True),
        lax.all_gather(gate_weight, "seq", axis=0, tiled=True),
        lax.all_gather(up_weight, "seq", axis=0, tiled=True),
        lax.all_gather(down_weight, "seq", axis=0, tiled=True),
    )
    x_full, y_full, out_full, gate_full, up_full, down_full = gathered
    tokens_wide = tokens.astype(float_type)
    first_gain = norm_gain.astype(float_type)
    first_norm = rms_norm(tokens_wide, first_gain)
    first_low = first_norm.astype(half_type)
    x_branch = jnp.dot(first_low, x_full, preferred_element_type=float_type).astype(half_type)
    y_branch = jnp.dot(first_low, y_full, preferred_element_type=float_type)
    y_gate = jax.nn.gelu(y_branch)
    left_edge = from_behind(x_branch[row_count - (CONV - 1) :], "seq", 1)
    padded = jnp.concatenate([left_edge, x_branch], axis=0).astype(float_type)
    conv_taps = conv_weight.astype(float_type)
    conv_out = conv_bias.astype(float_type) + sum(
        (
            conv_taps[lag_index] * padded[CONV - 1 - lag_index : CONV - 1 - lag_index + row_count]
            for lag_index in range(CONV)
        )
    )
    conv_low = conv_out.astype(half_type)
    conv_value = conv_low.astype(float_type)
    all_channels = lax.all_gather(conv_low, "head", axis=1, tiled=True)
    head_count = all_channels.shape[1] // head_size
    group_count = lane_count // head_count
    heads_view = all_channels.reshape(row_count, head_size, head_count)

    def block_gate(weight, bias):
        product = jnp.einsum(
            "tih,ijh->tjh",
            heads_view,
            weight.reshape(head_size, group_count, head_count),
            preferred_element_type=float_type,
        )
        return product.reshape(row_count, lane_count) + bias.astype(float_type)

    a_pre = block_gate(a_weight, a_bias)
    i_pre = block_gate(i_weight, i_bias)
    recall = jax.nn.sigmoid(a_pre)
    input_gate = jax.nn.sigmoid(i_pre)
    decay_rate = jax.nn.softplus(decay)
    log_decay = -8.0 * recall * decay_rate
    factor = jnp.exp(log_decay)
    double_decay = jnp.exp(2.0 * log_decay)
    one_minus = -jnp.expm1(2.0 * log_decay)
    root_value = jnp.sqrt(jnp.maximum(one_minus, SQUARE_FLOOR))
    position = seq_index * row_count + jnp.arange(row_count)
    anchor = (position == 0)[:, None]
    root_scale = jnp.where(anchor, 1.0, root_value)
    root_live = jnp.logical_and(one_minus > SQUARE_FLOOR, jnp.logical_not(anchor))
    driven = conv_value * input_gate * root_scale
    local_prod, local_state = lax.associative_scan(linear_pair, (factor, driven))

    def relay_step(turn_number, carried):
        return from_behind(local_prod[-1] * carried + local_state[-1], "seq", 1)

    state_entry = lax.fori_loop(
        0, lax.axis_size("seq") - 1, relay_step, jnp.zeros_like(local_state[-1])
    )
    state_all = local_state + local_prod * state_entry
    mixed_in = (state_all * y_gate).astype(half_type)
    branch_part = jnp.einsum("tc,dc->td", mixed_in, out_full, preferred_element_type=float_type)
    branch = lax.psum(branch_part, "head")
    residual = tokens_wide + branch
    second_gain = mlp_gain.astype(float_type)
    second_low = rms_norm(residual, second_gain).astype(half_type)
    gate_pre = jnp.dot(second_low, gate_full, preferred_element_type=float_type)
    up_pre = jnp.dot(second_low, up_full, preferred_element_type=float_type)
    gate_act = jax.nn.gelu(gate_pre)
    hidden = (gate_act * up_pre).astype(half_type)
    mlp_part = jnp.einsum("tf,df->td", hidden, down_full, preferred_element_type=float_type)
    own_columns = lax.psum_scatter(mlp_part, "head", scatter_dimension=1, tiled=True)
    column_count = model_width // head_devices
    mixed = (
        lax.dynamic_slice_in_dim(residual, head_index * column_count, column_count, 1) + own_columns
    ).astype(half_type)
    regathered = (
        lax.all_gather(x_weight, "seq", axis=0, tiled=True),
        lax.all_gather(y_weight, "seq", axis=0, tiled=True),
        lax.all_gather(out_weight, "seq", axis=0, tiled=True),
        lax.all_gather(gate_weight, "seq", axis=0, tiled=True),
        lax.all_gather(up_weight, "seq", axis=0, tiled=True),
        lax.all_gather(down_weight, "seq", axis=0, tiled=True),
    )
    x_full, y_full, out_full, gate_full, up_full, down_full = regathered
    hidden_grad = jnp.dot(cotangent, down_full, preferred_element_type=float_type)
    gate_grad = gelu_back(gate_pre, hidden_grad * up_pre).astype(half_type)
    up_grad = (hidden_grad * gate_act).astype(half_type)
    second_part = jnp.einsum(
        "tf,df->td", gate_grad, gate_full, preferred_element_type=float_type
    ) + jnp.einsum("tf,df->td", up_grad, up_full, preferred_element_type=float_type)
    second_grad = lax.psum(second_part, "head")
    resid_back, mlp_gain_term = jax.vjp(rms_norm, residual, second_gain)[1](second_grad)
    resid_grad = cotangent.astype(float_type) + resid_back
    branch_grad = resid_grad.astype(half_type)
    mixed_grad = jnp.dot(branch_grad, out_full, preferred_element_type=float_type)
    state_grad = mixed_grad * y_gate
    y_grad = gelu_back(y_branch, mixed_grad * state_all).astype(half_type)
    next_factor = jnp.concatenate([factor[1:], jnp.ones_like(factor[:1])], axis=0)
    back_prod, back_adjoint = lax.associative_scan(
        linear_pair, (next_factor[::-1], state_grad[::-1])
    )
    back_prod = back_prod[::-1]
    back_adjoint = back_adjoint[::-1]
    tail_prod = factor[0] * back_prod[0]
    tail_value = factor[0] * back_adjoint[0]

    def relay_back(turn_number, carried):
        return from_behind(tail_value + tail_prod * carried, "seq", -1)

    exit_carry = lax.fori_loop(0, lax.axis_size("seq") - 1, relay_back, jnp.zeros_like(tail_value))
    adjoint = back_adjoint + back_prod * exit_carry
    prev_state = jnp.concatenate([state_entry[None], state_all[:-1]], axis=0)
    scale_grad = adjoint * conv_value * input_gate
    log_grad = adjoint * prev_state * factor + jnp.where(
        root_live, -scale_grad * double_decay / root_value, 0.0
    )
    a_grad = (log_grad * (-8.0 * decay_rate) * recall * (1.0 - recall)).astype(half_type)
    i_grad = (adjoint * conv_value * root_scale * input_gate * (1.0 - input_gate)).astype(half_type)
    decay_term = jnp.sum(log_grad * (-8.0 * recall), axis=0) * jax.nn.sigmoid(decay)
    a_bias_term = jnp.sum(a_grad.astype(float_type), axis=0)
    i_bias_term = jnp.sum(i_grad.astype(float_type), axis=0)

    def gate_back(grad, weight):
        grad_view = grad.reshape(row_count, group_count, head_count)
        weight_term = jnp.einsum(
            "tih,tjh->ijh", heads_view, grad_view, preferred_element_type=float_type
        ).reshape(head_size, lane_count)
        input_term = jnp.einsum(
            "tjh,ijh->tih",
            grad_view,
            weight.reshape(head_size, group_count, head_count),
            preferred_element_type=float_type,
        )
        return (weight_term, input_term)

    a_wgrad, a_input = gate_back(a_grad, a_weight)
    i_wgrad, i_input = gate_back(i_grad, i_weight)
    gate_input_grad = lax.psum_scatter(
        (a_input + i_input).reshape(row_count, head_size * head_count),
        "head",
        scatter_dimension=1,
        tiled=True,
    )
    conv_grad = gate_input_grad + adjoint * input_gate * root_scale
    right_edge = from_behind(conv_grad[: CONV - 1], "seq", -1)
    extended_grad = jnp.concatenate([conv_grad, right_edge], axis=0)
    x_branch_grad = sum(
        (
            conv_taps[lag_index] * extended_grad[lag_index : lag_index + row_count]
            for lag_index in range(CONV)
        )
    ).astype(half_type)
    conv_wgrad = jnp.stack(
        [
            jnp.sum(
                conv_grad * padded[CONV - 1 - lag_index : CONV - 1 - lag_index + row_count], axis=0
            )
            for lag_index in range(CONV)
        ],
        axis=0,
    )
    conv_bgrad = jnp.sum(conv_grad, axis=0)
    first_part = jnp.einsum(
        "tc,dc->td", x_branch_grad, x_full, preferred_element_type=float_type
    ) + jnp.einsum("tc,dc->td", y_grad, y_full, preferred_element_type=float_type)
    first_grad = lax.psum(first_part, "head")
    tokens_back, norm_gain_term = jax.vjp(rms_norm, tokens_wide, first_gain)[1](first_grad)
    tokens_grad = resid_grad + tokens_back
    pairings = (
        (first_low, x_branch_grad),
        (first_low, y_grad),
        (branch_grad, mixed_in),
        (second_low, gate_grad),
        (second_low, up_grad),
        (cotangent, hidden),
    )
    products = tuple(
        (
            jnp.einsum("td,tc->dc", left, right, preferred_element_type=float_type)
            for left, right in pairings
        )
    )
    weight_sums = lax.psum_scatter(products, "seq", scatter_dimension=0, tiled=True)
    small_sums = lax.psum(
        (
            norm_gain_term,
            conv_wgrad,
            conv_bgrad,
            a_wgrad,
            a_bias_term,
            i_wgrad,
            i_bias_term,
            decay_term,
            mlp_gain_term,
        ),
        "seq",
    )
    return (
        mixed,
        tokens_grad,
        small_sums[0],
        weight_sums[0],
        weight_sums[1],
        small_sums[1],
        small_sums[2],
        small_sums[3],
        small_sums[4],
        small_sums[5],
        small_sums[6],
        small_sums[7],
        weight_sums[2],
        small_sums[8],
        weight_sums[3],
        weight_sums[4],
        weight_sums[5],
    )


def solution(mesh):
    sizes = mesh.shape["seq"], mesh.shape["head"]

    def body(*args):
        z = Size(sizes, args[0], args[2], args[6], args[13])
        return dealt(z, *args) if z.fits() else gathered_weights(*args)

    return jax.shard_map(
        body,
        mesh=mesh,
        in_specs=(
            P("seq", None),
            P(),
            P("seq", "head"),
            P("seq", "head"),
            P(None, "head"),
            P("head"),
            P(None, "head"),
            P("head"),
            P(None, "head"),
            P("head"),
            P("head"),
            P("seq", "head"),
            P(),
            P("seq", "head"),
            P("seq", "head"),
            P("seq", "head"),
            P("seq", None),
        ),
        out_specs=(
            P("seq", "head"),
            P("seq", None),
            P(),
            P("seq", "head"),
            P("seq", "head"),
            P(None, "head"),
            P("head"),
            P(None, "head"),
            P("head"),
            P(None, "head"),
            P("head"),
            P("head"),
            P("seq", "head"),
            P(),
            P("seq", "head"),
            P("seq", "head"),
            P("seq", "head"),
        ),
        check_vma=False,
    )
```

```python
import functools

import jax
import jax.numpy as jnp
from jax import lax
from jax.experimental import pallas as pl
from jax.experimental.pallas import tpu as pltpu
from jax.sharding import PartitionSpec as P

CONV = 4
EPSILON = 1e-06
SQUARE_FLOOR = 2.5e-07
MESH = pl.DeviceIdType.MESH
F32 = jnp.float32
BF16 = jnp.bfloat16
LANES = 128
EDGE = 16
VM = pltpu.VMEM
ANY = pl.ANY
NN = (((1,), (0,)), ((), ()))
NT = (((1,), (1,)), ((), ()))
TN = (((0,), (0,)), ((), ()))


def mm(left, right, dims=NN):
    return lax.dot_general(left, right, dims, preferred_element_type=F32)


def gelu_pair(values):
    scale = 0.7978845608028654
    square = values * values
    bend = jnp.tanh(scale * values * (1.0 + 0.044715 * square))
    half = 0.5 * (1.0 + bend)
    slope = half + 0.5 * values * (1.0 - bend * bend) * scale * (1.0 + 3.0 * 0.044715 * square)
    return values * half, slope


def minus_expm1(v):
    series = jnp.full_like(v, 1.0 / 40320.0)
    for divisor in (5040.0, 720.0, 120.0, 24.0, 6.0, 2.0, 1.0):
        series = series * v + 1.0 / divisor
    return jnp.where(v > -0.35, -v * series, 1.0 - jnp.exp(v))


def when(condition, action):
    if condition is None:
        action()
    else:
        pl.when(condition)(action)


class Copy:
    def __init__(self, item, goes, comes):
        self.item, self.goes, self.comes = item, goes, comes

    def start(self):
        when(self.goes, lambda: self.item.start())

    def wait_send(self):
        when(self.goes, lambda: self.item.wait_send())

    def wait_recv(self):
        when(self.comes, lambda: self.item.wait_recv())

    def arrived(self):
        self.item.wait_recv()


class Wire:
    def __init__(self, send, recv):
        self.send, self.recv, self.count, self.open = send, recv, 0, []

    def make(self, src, dst, peer, goes=None, comes=None):
        slot = self.count
        self.count += 1
        item = pltpu.make_async_remote_copy(
            src_ref=src,
            dst_ref=dst,
            send_sem=self.send.at[slot],
            recv_sem=self.recv.at[slot],
            device_id=peer,
            device_id_type=MESH,
        )
        copy = Copy(item, goes, comes)
        self.open.append(copy)
        return copy

    def copy(self, src, dst, peer, goes=None, comes=None):
        copy = self.make(src, dst, peer, goes, comes)
        copy.start()
        return copy

    def close(self):
        for item in self.open:
            item.wait_send()
        assert self.count <= self.send.shape[0], self.count


class Chain:
    def __init__(self, wire, count, s, h):
        self.wire, self.count, self.s, self.h, self.zi = wire, count, s, h, s // 2
        self.up = (jnp.minimum(s + 2, 2 * count - 2 + s % 2), h)
        self.down = (jnp.maximum(s - 2, s % 2), h)

    def gather(self, view):
        zi, last = self.zi, self.count - 1

        def hop(step, way):
            index = zi - way * step
            held = jnp.logical_and(index >= 0, index <= last)
            goes = jnp.logical_and(held, zi < last if way > 0 else zi > 0)
            here = index - way
            comes = jnp.logical_and(here >= 0, here <= last)
            block = view(jnp.clip(index, 0, last))
            peer = self.up if way > 0 else self.down
            return self.wire.copy(block, block, peer, goes, comes), comes, jnp.clip(here, 0, last)

        flight = [hop(0, 1), hop(0, -1)]
        yield None, zi
        for step in range(last):
            for side, way in enumerate((1, -1)):
                item, comes, index = flight[side]
                item.wait_recv()
                if step + 1 < last:
                    flight[side] = hop(step + 1, way)
                yield comes, index

    def order(self):
        count = self.count
        low = list(reversed(range(count // 2, count))) + list(range(count // 2))
        near = self.zi < count // 2
        return [jnp.where(near, d, count - 1 - d) for d in low]

    def passes(self, d, src, up, down):
        zi, last, wire = self.zi, self.count - 1, self.wire
        base = wire.count
        wire.count = base + d
        first = wire.make(src, up, self.up, zi < d, jnp.logical_and(zi > 0, zi <= d))
        wire.count = base + self.count + d
        second = wire.make(src, down, self.down, zi > d, jnp.logical_and(zi < last, zi >= d))
        wire.count = base
        return first, second

    def between(self, d):
        zi, last = self.zi, self.count - 1
        return jnp.logical_and(zi > 0, zi < d), jnp.logical_and(zi < last, zi > d)

    def ends(self, d):
        zi, last = self.zi, self.count - 1
        return jnp.logical_and(zi == d, zi > 0), jnp.logical_and(zi == d, zi < last)

    def scatter(self, block, work, out, up, down, own):
        zi = self.zi
        flight = []
        base = self.wire.count
        self.wire.count += 2 * self.count

        def take(item, got, into):
            def action():
                item.arrived()
                into[...] = into[...] + got[...].astype(F32)
            return action

        for d in self.order():
            work[...] = block(d)
            kept, self.wire.count = self.wire.count, base
            ups, downs = self.passes(d, out.at[d], up.at[d], down.at[d])
            self.wire.count = kept
            flight.append((d, ups, downs))
            below, above = self.between(d)
            when(below, take(ups, up.at[d], work))
            when(above, take(downs, down.at[d], work))

            def give(d=d):
                out[d] = work[...].astype(BF16)

            def keep():
                own[...] = work[...]

            when(zi != d, give)
            when(zi == d, keep)
            ups.start()
            downs.start()
            yield d
        for d, ups, downs in flight:
            below, above = self.ends(d)
            when(below, take(ups, up.at[d], own))
            when(above, take(downs, down.at[d], own))


class HeadGather:
    def __init__(self, wire, s, h, view):
        self.wire, self.s, self.h, self.view = wire, s, h, view
        self.items = {1: self.send(0, 1), 2: self.send(0, 2)}

    def send(self, j, to):
        block = self.view(self.h ^ j)
        return self.wire.copy(block, block, (self.s, self.h ^ to))

    def wait(self, j):
        if j == 2:
            self.items[2].wait_recv()
            self.items[3] = self.send(2, 1)
        else:
            self.items[j].wait_recv()

    def wait_all(self):
        for j in (2, 1, 3):
            self.wait(j)


def head_scatter(wire, s, h, block, out, got):
    core, other = (s, h ^ 1), (s, h ^ 2)
    flight = {}
    for j in (3, 1):
        out[j] = block(j).astype(BF16)
        flight[j] = wire.copy(out.at[j], got.at[j], core)
    part = block(2)
    flight[3].wait_recv()
    out[2] = (part + got[3].astype(F32)).astype(BF16)
    flight[2] = wire.copy(out.at[2], got.at[2], other)
    total = block(0)
    flight[1].wait_recv()
    total = total + got[1].astype(F32)

    def finish():
        flight[2].wait_recv()
        return total + got[2].astype(F32)

    return finish


def drain(*steps):
    steps = list(steps)
    while steps:
        steps = [step for step in steps if next(step, step) is not step]


def advance(step, count=1):
    for _ in range(count):
        next(step, None)


def greet(peers):
    barrier = pltpu.get_barrier_semaphore()
    for peer in peers:
        pl.semaphore_signal(barrier, inc=1, device_id=peer, device_id_type=MESH)
    pl.semaphore_wait(barrier, len(peers))


def place():
    return lax.axis_index("seq"), lax.axis_index("head")


def at(ref, rows, row_count, lanes, lane_count):
    return ref.at[
        pl.ds(pl.multiple_of(rows, EDGE), row_count),
        pl.ds(pl.multiple_of(lanes, LANES), lane_count),
    ]


def sem(count):
    return pltpu.SemaphoreType.DMA((count,))


def call(body, name, cid, outs, scratch, args, spaces=(), far=False, limit=62, us=150):
    return pl.pallas_call(
        body,
        out_shape=outs,
        in_specs=[
            pl.BlockSpec(memory_space=ANY if i in spaces else VM) for i in range(len(args))
        ],
        out_specs=[pl.BlockSpec(memory_space=ANY if far else VM) for _ in outs],
        scratch_shapes=scratch,
        compiler_params=pltpu.CompilerParams(
            collective_id=cid, has_side_effects=True, vmem_limit_bytes=limit << 20
        ),
        cost_estimate=pl.CostEstimate(
            flops=us * 10**6, bytes_accessed=us * 3 * 10**6, transcendentals=0
        ),
        name=name,
    )(*args)


def sds(shape, kind):
    return jax.ShapeDtypeStruct(shape, kind)


class Size:
    def __init__(self, mesh_sizes, tokens, x_weight, a_weight, gate_weight):
        self.S, self.H = mesh_sizes
        self.Z = self.S // 2
        self.R, self.D = tokens.shape
        self.T = self.S * self.R
        self.Ds, self.C = x_weight.shape
        self.HS = a_weight.shape[0]
        self.heads = self.H * self.C // self.HS
        self.F2 = gate_weight.shape[1]
        self.TB = self.T // self.H
        self.U = 2 * LANES
        self.NI = self.HS // self.H

    def fits(self):
        tiles = self.F2 // LANES
        return (
            self.S == 8
            and self.H == 4
            and self.Z == self.H
            and (2 * self.Ds) % LANES == 0
            and (2 * self.HS // self.S) % EDGE == 0
            and self.D == self.H * self.C
            and self.F2 % LANES == 0
            and 2 * (self.S - 1) < tiles <= 2 * self.S
            and self.T <= 1024
            and self.R % LANES == 0
            and self.C % LANES == 0
            and self.Ds % (2 * EDGE) == 0
            and (self.Ds // self.H) % EDGE == 0
            and self.NI % EDGE == 0
        )


def gate_weight_of(z, spread, mask, weight, k):
    rows = weight[pl.ds(pl.multiple_of(k * z.NI, EDGE), z.NI), :]
    return mm(spread[...], rows).astype(BF16) * mask[...]


def shifted(values, by, fill, row):
    count = values.shape[0]
    moved = pltpu.roll(values, by % count, 0)
    inside = row >= by if by > 0 else row < count + by
    return jnp.where(inside, moved, fill)


def scan_rows(prod, value, sign):
    row = lax.broadcasted_iota(jnp.int32, prod.shape, 0)
    by = 1
    while by < prod.shape[0]:
        value = prod * shifted(value, sign * by, 0.0, row) + value
        prod = prod * shifted(prod, sign * by, 1.0, row)
        by *= 2
    return prod, value


def decay_terms(a_pre, i_pre, rate, anchor):
    recall = jax.nn.sigmoid(a_pre)
    input_gate = jax.nn.sigmoid(i_pre)
    log_decay = -8.0 * recall * rate
    factor = jnp.exp(log_decay)
    one_minus = minus_expm1(2.0 * log_decay)
    root_value = jnp.sqrt(jnp.maximum(one_minus, SQUARE_FLOOR))
    root_scale = jnp.where(anchor, 1.0, root_value)
    return recall, input_gate, factor, one_minus, root_value, root_scale


def anchor_of(z, s, width):
    row = lax.broadcasted_iota(jnp.int32, (z.R, width), 0)
    return jnp.logical_and(row == 0, s == 0)


def head_maps(z, spread, mask):
    def parts(shape, axis):
        channel = lax.broadcasted_iota(jnp.int32, shape, axis).astype(F32)
        row = jnp.floor((channel + 0.5) * (1.0 / z.heads))
        return row, channel - row * z.heads

    across = lax.broadcasted_iota(jnp.int32, (z.C, z.NI), 1).astype(F32)
    spread[...] = jnp.where(parts((z.C, z.NI), 0)[0] == across, 1.0, 0.0).astype(BF16)
    same = parts((z.C, z.C), 0)[1] == parts((z.C, z.C), 1)[1]
    mask[...] = jnp.where(same, 1.0, 0.0).astype(BF16)


def softplus(values):
    small = jnp.exp(-jnp.abs(values))
    series = jnp.full_like(small, 1.0 / 9.0)
    for order in range(8, 0, -1):
        series = 1.0 / order - small * series
    tail = jnp.where(small < 0.1, small * series, jnp.log(1.0 + small))
    return jnp.maximum(values, 0.0) + tail


class Deal:
    def __init__(self, wire, z, s, h):
        self.wire, self.z, self.s, self.h = wire, z, s, h
        self.tiles = z.F2 // LANES
        self.sent = []

    def rows(self, owner):
        return pl.ds(pl.multiple_of(owner * self.z.Ds, EDGE), self.z.Ds)

    def post(self, src, dst, peer, part, goes, comes):
        wire = self.wire
        item = pltpu.make_async_remote_copy(
            src_ref=src,
            dst_ref=dst,
            send_sem=wire.send.at[wire.count],
            recv_sem=wire.recv.at[wire.count],
            device_id=(peer, self.h),
            device_id_type=MESH,
        )
        wire.count += 1
        self.sent.append((item, part, goes, comes))
        if part == 0:
            item.start()
        else:
            @pl.when(goes)
            def _():
                item.start()

    def out(self, src, dst, offsets):
        z = self.z
        for k in offsets:
            peer = self.s ^ k
            for part in range(2):
                tile = 2 * peer + part
                self.post(
                    at(src, 0, z.Ds, jnp.minimum(tile, self.tiles - 1) * LANES, LANES),
                    dst.at[self.rows(self.s), pl.ds(part * LANES, LANES)],
                    peer,
                    part,
                    tile < self.tiles,
                    2 * self.s + part < self.tiles,
                )

    def back(self, src, dst, offsets):
        z = self.z
        for k in offsets:
            peer = self.s ^ k
            for part in range(2):
                tile = 2 * self.s + part
                lane = jnp.minimum(tile, self.tiles - 1) * LANES
                self.post(
                    src.at[self.rows(peer), pl.ds(part * LANES, LANES)],
                    at(dst, 0, z.Ds, lane, LANES),
                    peer,
                    part,
                    tile < self.tiles,
                    2 * peer + part < self.tiles,
                )

    def steps(self, how, pairs, start=0):
        plan = [(pair, k) for pair in pairs for k in ((4, 2), (5, 3), (6, 1), (7,))]
        for (src, dst), offsets in plan[start:]:
            how(src, dst, offsets)
            yield

    def back_own(self, src, dst):
        z, s = self.z, self.s
        at(dst, 0, z.Ds, 2 * s * LANES, LANES)[...] = src[self.rows(s), 0:LANES]

        @pl.when(2 * s + 1 < self.tiles)
        def _():
            lane = jnp.minimum(2 * s + 1, self.tiles - 1) * LANES
            at(dst, 0, z.Ds, lane, LANES)[...] = src[self.rows(s), LANES : 2 * LANES]

    def wait(self, sent=None):
        for item, part, goes, comes in self.sent if sent is None else sent:
            if part == 0:
                item.wait()
            else:
                @pl.when(goes)
                def _(item=item):
                    item.wait_send()

                @pl.when(comes)
                def _(item=item):
                    item.wait_recv()
        if sent is None:
            self.sent = []


def own_block(z, src, dst, sems, s):
    tiles = z.F2 // LANES
    rows = pl.ds(pl.multiple_of(s * z.Ds, EDGE), z.Ds)
    first = pltpu.make_async_copy(
        at(src, 0, z.Ds, 2 * s * LANES, LANES), dst.at[rows, pl.ds(0, LANES)], sems.at[0]
    )
    second = pltpu.make_async_copy(
        at(src, 0, z.Ds, jnp.minimum(2 * s + 1, tiles - 1) * LANES, LANES),
        dst.at[rows, pl.ds(LANES, LANES)],
        sems.at[1],
    )
    whole = 2 * s + 1 < tiles
    first.start()

    @pl.when(whole)
    def _():
        second.start()

    @pl.when(jnp.logical_not(whole))
    def _():
        dst[:, LANES : 2 * LANES] = jnp.zeros((z.D, LANES), BF16)

    def wait():
        first.wait()

        @pl.when(whole)
        def _():
            second.wait()

    return wait


def chain_scratch(z, rows, width):
    return [VM((rows, width), F32)] + [VM((z.Z, rows, width), BF16)] * 3 + [VM((rows, width), F32)]


def row_blocks(z, buf, part=None):
    count = z.R if part is None else z.R // 2
    first = 0 if part is None else part * count
    return lambda index: buf.at[pl.ds(pl.multiple_of(index * z.R + first, EDGE), count), :]


def scatter_halves(chain, z, block, stash, bufs):
    count = z.R // 2

    def cut(buf, part):
        rows = pl.ds(part * count, count)
        return buf.at[:, rows, :] if len(buf.shape) == 3 else buf.at[rows, :]

    def first(d):
        whole = block(d)
        stash[...] = whole[count:, :]
        return whole[:count, :]

    return [
        chain.scatter(source, *(cut(buf, part) for buf in bufs))
        for part, source in enumerate((first, lambda d: stash[...]))
    ]


class Grid:
    def __init__(self, s, h):
        self.s, self.h = s, h
        self.x, self.y, self.core = (s ^ 1, h), (s, h ^ 2), (s, h ^ 1)

    def z(self, kz):
        return (self.s ^ (2 * kz), self.h)


def gather_all(wire, z, g, region):
    s, h, xi = g.s, g.h, g.s % 2
    chain = Chain(wire, z.Z, s, h)
    arrivals = chain.gather(lambda index: region(2 * index + xi, h, None))
    mine = next(arrivals)
    yield None
    blocks, near, far, core = [], {}, {}, []

    def send(a, b, half, peer, held):
        return wire.copy(region(a, b, half), region(a, b, half), peer, held, held)

    def one(i):
        held, index = next(arrivals) if i else mine
        a = 2 * index + xi
        blocks.append((held, a))
        near[0, i] = send(a, h, 0, g.x, held)
        near[1, i] = send(a, h, 1, g.y, held)
        far[0, i, 0] = send(a, h, 0, g.y, held)
        far[1, i, 0] = send(a, h, 1, g.x, held)
        core.append(send(a, h, None, g.core, held))

    def two(i):
        held, a = blocks[i]
        near[0, i].wait_recv()
        far[0, i, 1] = send(a ^ 1, h, 0, g.y, held)
        core.append(send(a ^ 1, h, 0, g.core, held))
        near[1, i].wait_recv()
        far[1, i, 1] = send(a, h ^ 2, 1, g.x, held)
        core.append(send(a, h ^ 2, 1, g.core, held))

    def three(i):
        held, a = blocks[i]
        far[0, i, 0].wait_recv()
        core.append(send(a, h ^ 2, 0, g.core, held))
        far[1, i, 0].wait_recv()
        core.append(send(a ^ 1, h, 1, g.core, held))

    def four(i):
        held, a = blocks[i]
        far[0, i, 1].wait_recv()
        core.append(send(a ^ 1, h ^ 2, 0, g.core, held))
        far[1, i, 1].wait_recv()
        core.append(send(a ^ 1, h ^ 2, 1, g.core, held))

    count = 2 * z.Z - 1
    stages = (one, two, three, four)
    for turn in range(count + 6):
        for lag, stage in enumerate(stages):
            if 0 <= turn - 2 * lag < count:
                stage(turn - 2 * lag)
        yield turn
    for item in core:
        item.wait_recv()


def gather_copies(z):
    return 2 * (z.Z - 1) + 13 * (2 * z.Z - 1)


class SumAll:
    def __init__(self, wire, z, g, region, bufs):
        self.wire, self.zz, self.g, self.region = wire, z, g, region
        self.from_core, self.hop1, self.hop2, self.up, self.down, self.own = bufs
        self.chain = Chain(wire, z.Z, g.s, g.h)
        self.flight = {}
        self.base = wire.count
        wire.count += self.copies(z)

    @staticmethod
    def copies(z):
        return z.Z * (4 + 4 + 2) + 4 * z.Z

    @staticmethod
    def scratch(z, rows, lanes):
        half = rows // 2
        return [
            VM((z.Z, 4, rows, lanes), BF16),
            VM((z.Z, 4, half, lanes), BF16),
            VM((z.Z, 2, half, lanes), BF16),
            VM((z.Z, 2, half, lanes), BF16),
            VM((z.Z, 2, half, lanes), BF16),
            VM((2, half, lanes), F32),
        ]

    def put(self, a, b, half, dst, peer, slot):
        kept, self.wire.count = self.wire.count, self.base + slot
        item = self.wire.copy(self.region(a, b, half), dst, peer)
        self.wire.count = kept
        return item

    def add(self, a, b, half, got):
        spot = self.region(a, b, half)
        spot[...] = (spot[...].astype(F32) + got[...].astype(F32)).astype(BF16)

    def core(self, i, d):
        g = self.g
        for k in range(4):
            a, b = (2 * d + g.s % 2) ^ (k // 2), g.h ^ 1 ^ (2 * (k % 2))
            self.flight["core", i, k] = self.put(
                a, b, None, self.from_core.at[d, k], g.core, 10 * i + k
            )

    def first(self, i, d):
        g = self.g
        rows = self.hop1.shape[2]
        for k in (1, 3, 2, 0):
            self.flight["core", i, k].wait_recv()
            a, b = (2 * d + g.s % 2) ^ (k // 2), g.h ^ (2 * (k % 2))
            for half in range(2):
                self.add(a, b, half, self.from_core.at[d, k, pl.ds(half * rows, rows), :])
            if k % 2:
                key = k // 2
                self.flight["one", i, key] = self.put(
                    a, b, 0, self.hop1.at[d, key], g.y, 10 * i + 4 + key
                )
            if k // 2:
                key = 2 + k % 2
                self.flight["one", i, key] = self.put(
                    a, b, 1, self.hop1.at[d, key], g.x, 10 * i + 4 + key
                )

    def second(self, i, d):
        g = self.g
        a = 2 * d + g.s % 2
        for key in (1, 0):
            self.flight["one", i, key].wait_recv()
            self.add(a ^ key, g.h, 0, self.hop1.at[d, key])
        self.flight["two", i, 0] = self.put(
            a ^ 1, g.h, 0, self.hop2.at[d, 0], g.x, 10 * i + 8
        )
        for key in (3, 2):
            self.flight["one", i, key].wait_recv()
            self.add(a, g.h ^ (2 * (key - 2)), 1, self.hop1.at[d, key])
        self.flight["two", i, 1] = self.put(
            a, g.h ^ 2, 1, self.hop2.at[d, 1], g.y, 10 * i + 9
        )

    def third(self, i, d):
        g, chain = self.g, self.chain
        a, count = 2 * d + g.s % 2, self.zz.Z
        below, above = chain.between(d)
        for half in range(2):
            self.flight["two", i, half].wait_recv()
            self.add(a, g.h, half, self.hop2.at[d, half])
            kept = self.wire.count
            self.wire.count = self.base + 10 * count + 2 * count * half
            ups, downs = chain.passes(
                d, self.region(a, g.h, half), self.up.at[d, half], self.down.at[d, half]
            )
            self.wire.count = kept
            self.flight["z", i, half] = d, ups, downs
            when(below, self.taken(ups, a, half, self.up.at[d, half]))
            when(above, self.taken(downs, a, half, self.down.at[d, half]))
            ups.start()
            downs.start()

    def taken(self, item, a, half, got):
        def action():
            item.arrived()
            self.add(a, self.g.h, half, got)
        return action

    def finish(self, half):
        g = self.g
        own = self.own.at[half]
        own[...] = self.region(g.s, g.h, half)[...].astype(F32)

        def add(item, got):
            def action():
                item.arrived()
                own[...] = own[...] + got[...].astype(F32)
            return action

        for i in range(self.zz.Z):
            d, ups, downs = self.flight["z", i, half]
            below, above = self.chain.ends(d)
            when(below, add(ups, self.up.at[d, half]))
            when(above, add(downs, self.down.at[d, half]))
        return own[...]

    def run(self, produce):
        order = self.chain.order()
        steps = [
            lambda i, d: (produce(d), self.core(i, d)),
            self.first,
            self.second,
            self.third,
        ]
        count = len(order)
        for turn in range(count + len(steps) - 1):
            for stage in range(len(steps)):
                if 0 <= turn - stage < count:
                    steps[stage](turn - stage, order[turn - stage])
                    yield turn


def halves(ref, rows, row_count, lanes, lane_count, half):
    if half is not None:
        row_count //= 2
        rows = rows + half * row_count
    return at(ref, rows, row_count, lanes, lane_count)


def region_of(z, ref):
    return lambda a, b, half: halves(
        ref, a // 2 * 2 * z.Ds, 2 * z.Ds, (2 * b + a % 2) * z.R, z.R, half
    )


FRONT_RESULTS = 27


def front_kernel(
    z, tok, gain1, gain2, xw, yw, ow, conv_w, conv_b, a_b, i_b, decay, aw, iw, cot_in,
    gw_in, uw_in, dw_in, *rest
):
    outs, rest = rest[:FRONT_RESULTS], rest[FRONT_RESULTS:]
    held, rest = rest[:FRONT_RESULTS], rest[FRONT_RESULTS:]
    (
        xw2, yw2, ow2, tok2, fn2, rn, yb, pad, conv, a_o, i_o, st, entry_o, mix, res,
        vec, mask, spread, gain_q, hid, dw, uwg_o, dwg_o, gsum_o, bg_o, back_g, back_u,
    ) = held
    (
        turned, fnt, stash, x1, x2, x3, x4, x5, y1, y2, y3, y4, y5, sums, tot, part, got, edge, gains,
        cot, gw, uw, xt, gwt, uwt, dwt, gwg, hg, gg, ug, gs, us, rs, wide,
        c1, c2, c3, c4, c5, c6, stat, send, recv, own_sem, out_sem,
    ) = rest
    leaving = []

    def flush(first, last):
        for index in range(first, last):
            copy = pltpu.make_async_copy(held[index], outs[index], out_sem.at[index])
            copy.start()
            leaving.append(copy)

    s, h = place()
    S, H, R, D, T, Ds, C, Z = z.S, z.H, z.R, z.D, z.T, z.Ds, z.C, z.Z
    DG = 2 * Ds
    Q = DG // H
    zi, xi = s // 2, s % 2
    after, before = lax.rem(s + 1, S), lax.rem(s + S - 1, S)
    greet(
        [(s ^ k, h) for k in range(1, S)]
        + [(s, h ^ j) for j in range(1, H)]
        + [(after, h), (before, h)]
    )
    wire = Wire(send, recv)
    g = Grid(s, h)
    chain = Chain(wire, Z, s, h)
    deal = Deal(wire, z, s, h)
    pairs = ((gw_in, gw), (uw_in, uw), (dw_in, dw))
    dealing = deal.steps(deal.out, pairs)
    advance(dealing)
    half = pl.ds(pl.multiple_of(xi * Ds, EDGE), Ds)
    twins = [wire.copy(xw, xw2.at[half, :], (s ^ 1, h))]
    turned[...] = tok[...].astype(F32).T.astype(BF16)
    quarter = pl.ds(pl.multiple_of(h * Q, EDGE), Q)
    my_lanes = pl.ds(pl.multiple_of(zi * R, LANES), R)

    def group(index):
        return pl.ds(pl.multiple_of(index * DG + h * Q, EDGE), Q)

    first = [
        wire.copy(turned.at[group(zi ^ kz), :], tok2.at[quarter, my_lanes], (s ^ (2 * kz), h))
        for kz in range(1, Z)
    ]
    column = turned[...].astype(F32)
    mean = jnp.sum(column * column, axis=0, keepdims=True) / z.D
    rn[zi] = jnp.broadcast_to(lax.rsqrt(mean + EPSILON), (8, R))
    for kz in range(1, Z):
        first.append(wire.copy(rn.at[zi], rn.at[zi], (s ^ (2 * kz), h)))
    tok2[quarter, my_lanes] = turned[group(zi), :]
    vec[...] = jnp.zeros_like(vec)
    vec[0:CONV, :] = conv_w[...].astype(F32)
    for index, ref in enumerate((conv_b, a_b, i_b)):
        vec[4 + index : 5 + index, :] = ref[...].astype(F32)[None, :]
    vec[7:8, :] = softplus(decay[...][None, :])
    vec[8:9, :] = jax.nn.sigmoid(decay[...][None, :])
    eight = lax.broadcasted_iota(jnp.int32, (8, D), 0)
    gains[...] = jnp.where(
        eight == 0, gain1[...].astype(F32)[None, :], gain2[...].astype(F32)[None, :]
    ).T
    gain_q[...] = gains[pl.ds(pl.multiple_of(zi * DG + h * Q, EDGE), Q), :]
    gain_s = gains[pl.ds(pl.multiple_of(zi * DG, EDGE), DG), 0:1]
    head_maps(z, spread, mask)
    xw2[half, :] = xw[...]
    yw2[half, :] = yw[...]
    ow2[half, :] = ow[...]
    pending = [
        own_block(z, src, dst, own_sem.at[pl.ds(2 * i, 2)], s)
        for i, (src, dst) in enumerate(pairs)
    ]
    W = z.D // H

    def corner(a, b, half):
        return halves(cot, a * R, R, b * W, W, half)

    corner(s, h, None)[...] = cot_in[:, pl.ds(pl.multiple_of(h * W, LANES), W)]
    cot_in_all = gather_all(wire, z, g, corner)
    advance(cot_in_all)
    advance(dealing, 2)
    for item in first:
        item.wait_recv()
    HeadGather(
        wire, s, h, lambda j: tok2.at[pl.ds(pl.multiple_of(j * Q, EDGE), Q), :]
    ).wait_all()
    for b in range(Z):
        cut = slice(b * R, b * R + R)
        fn2[:, cut] = (tok2[:, cut].astype(F32) * rn[b, 0:1, :] * gain_s).astype(BF16)
    twins[0].wait_recv()
    for src, dst in ((yw, yw2), (ow, ow2)):
        twins.append(wire.copy(src, dst.at[half, :], (s ^ 1, h)))

    def x_part(d):
        lanes = pl.ds(pl.multiple_of(d * R, LANES), R)
        fnt[d] = fn2[:, lanes].astype(F32).T.astype(BF16)
        return mm(fnt[d], xw2[...])

    x_sum = scatter_halves(chain, z, x_part, stash, (x1, x2, x3, x4, x5))
    for _ in range(Z):
        for step in x_sum:
            advance(step)
    advance(cot_in_all, 1)
    advance(dealing, 0)
    drain(*x_sum)
    x_low = x5[...].astype(BF16)
    edge[0] = x_low[R - EDGE : R, :]
    halo = wire.copy(edge.at[0], edge.at[1], (after, h))
    twins[1].wait_recv()
    y_sum = chain.scatter(lambda d: mm(fnt[d], yw2[...]), y1, y2, y3, y4, y5)
    advance(y_sum, 1)
    advance(dealing, 1)
    advance(cot_in_all, 2)
    pad[pl.ds(EDGE, R), :] = x_low.astype(F32)
    halo.wait_recv()
    pad[pl.ds(0, EDGE), :] = jnp.where(s == 0, 0.0, edge[1].astype(F32))
    out = jnp.broadcast_to(vec[4:5, :], (R, C))
    for lag in range(CONV):
        out = out + vec[lag : lag + 1, :] * pad[pl.ds(EDGE - lag, R), :]
    conv[h] = out.astype(BF16)
    across = HeadGather(wire, s, h, lambda j: conv.at[j])
    advance(dealing, 1)
    advance(cot_in_all, 2)
    advance(y_sum, 1)
    a_pre = jnp.broadcast_to(vec[5:6, :], (R, C))
    i_pre = jnp.broadcast_to(vec[6:7, :], (R, C))
    for j in (0, 2, 1, 3):
        if j:
            across.wait(j)
        k = h ^ j
        taken = conv[k]
        a_pre = a_pre + mm(taken, gate_weight_of(z, spread, mask, aw, k))
        i_pre = i_pre + mm(taken, gate_weight_of(z, spread, mask, iw, k))
    advance(y_sum, 1)
    a_o[...] = a_pre
    i_o[...] = i_pre
    anchor = anchor_of(z, s, LANES)
    sums[s] = jnp.zeros((8, C), F32)
    for b in range(C // LANES):
        cut = pl.ds(b * LANES, LANES)
        recall, input_gate, factor, one_minus, root_value, root_scale = decay_terms(
            a_o[:, cut], i_o[:, cut], vec[7:8, cut], anchor
        )
        driven = conv[h, :, cut].astype(F32) * input_gate * root_scale
        prod, value = scan_rows(factor, driven, 1)
        st[:, cut] = value
        tot[:, cut] = prod
        sums[s, 0:1, cut] = prod[R - 1 : R, :]
        sums[s, 1:2, cut] = value[R - 1 : R, :]
    ends = [wire.copy(sums.at[s], sums.at[s], (s ^ k, h)) for k in range(1, S)]
    advance(dealing, 0)
    advance(cot_in_all, 2)
    drain(y_sum)
    yb[...] = y5[...]
    for item in ends:
        item.wait_recv()
    entry = jnp.zeros((1, C), F32)
    for j in range(S - 1):
        entry = jnp.where(j < s, sums[j, 0:1, :] * entry + sums[j, 1:2, :], entry)
    entry_o[...] = jnp.broadcast_to(entry, (8, C))
    my_rows = pl.ds(pl.multiple_of(zi * R, EDGE), R)
    for b in range(C // LANES):
        cut = pl.ds(b * LANES, LANES)
        state = st[:, cut] + tot[:, cut] * entry_o[0:1, cut]
        st[:, cut] = state
        mix[my_rows, cut] = (state * gelu_pair(yb[:, cut])[0]).astype(BF16)
    arriving = [chain.gather(row_blocks(z, mix, part_of)) for part_of in range(2)]
    for step in arriving:
        advance(step)
    advance(dealing, 1)
    advance(cot_in_all, 3)
    drain(*arriving)
    twins[2].wait_recv()

    def out_part(j):
        rows = pl.ds(pl.multiple_of((h ^ j) * R, EDGE), R)
        return mm(ow2[...], mix[rows, :], NT)

    whole = head_scatter(wire, s, h, out_part, part, got)
    advance(dealing, 2)
    advance(cot_in_all, 3)
    res[...] = whole() + tok2[:, pl.ds(pl.multiple_of(h * R, LANES), R)].astype(F32)


    flush(0, 19)
    tile = 256
    region_of(z, xt)(s, h, None)[...] = res[...].astype(BF16)
    spreading = gather_all(wire, z, g, region_of(z, xt))
    advance(spreading, 2)
    def turn(src, dst, scaled):
        for n in range(D // tile):
            cut = slice(n * tile, n * tile + tile)
            piece = src[cut, :].astype(F32)
            dst[:, cut] = (piece * gains[cut, 1:2] if scaled else piece).T.astype(BF16)

    advance(spreading, 3)
    advance(dealing, 2)
    advance(spreading, 2)
    advance(dealing, 2)
    drain(spreading, dealing, cot_in_all)
    for wait in pending:
        wait()
    posted, deal.sent = deal.sent, []
    count = len(posted) // 3
    deal.wait(posted[: 2 * count])
    turn(gw, gwt, True)
    turn(uw, uwt, True)
    for n in range(T // tile):
        cut = slice(n * tile, n * tile + tile)
        square = jnp.zeros((1, tile), F32)
        for b in range(D // tile):
            piece = xt[b * tile : b * tile + tile, cut].astype(F32)
            square = square + jnp.sum(piece * piece, axis=0, keepdims=True)
        rs[:, cut] = jnp.broadcast_to(lax.rsqrt(square / D + EPSILON), (8, tile))
    deal.wait(posted[2 * count :])
    turn(dw, dwt, False)
    for n in range(T // tile):
        cut = slice(n * tile, n * tile + tile)
        hg[:, cut] = mm(dwt[...], cot[cut, :], NT)
        scale = rs[0:1, cut]
        gate = mm(gwt[...], xt[:, cut]) * scale
        up = mm(uwt[...], xt[:, cut]) * scale
        act, slope = gelu_pair(gate)
        hid[:, cut] = (act * up).astype(BF16)
        back = hg[:, cut]
        gate_grad = back * up * slope
        up_grad = back * act
        gg[:, cut] = gate_grad.astype(BF16)
        ug[:, cut] = up_grad.astype(BF16)
        gs[:, cut] = (gate_grad * scale).astype(BF16)
        us[:, cut] = (up_grad * scale).astype(BF16)
    second = SumAll(wire, z, g, region_of(z, wide), (c1, c2, c3, c4, c5, c6))

    def produce(d):
        rows = pl.ds(pl.multiple_of(d * DG, LANES), DG)
        wide[rows, :] = (mm(gw[rows, :], gg[...]) + mm(uw[rows, :], ug[...])).astype(BF16)

    summing = second.run(produce)
    advance(summing, 3)
    flush(19, 21)
    for n in range(D // tile):
        cut = slice(n * tile, n * tile + tile)
        gwg[cut, :] = (mm(xt[cut, :], gs[...], NT) * gains[cut, 1:2]).astype(BF16)
    dealing = deal.steps(deal.back, ((gwg, back_g),))
    advance(dealing, 3)
    deal.back_own(gwg, back_g)
    advance(summing, 6)
    advance(dealing, 1)
    drain(summing)
    for n in range(D // tile):
        cut = slice(n * tile, n * tile + tile)
        uwg_o[cut, :] = (mm(xt[cut, :], us[...], NT) * gains[cut, 1:2]).astype(BF16)
        dwg_o[cut, :] = mm(hid[...], cot[:, cut]).T.astype(BF16)
    flush(21, 23)
    rising = deal.steps(deal.back, ((uwg_o, back_u),))
    second_grad = jnp.concatenate([second.finish(0), second.finish(1)], axis=0)
    mine = pl.ds(pl.multiple_of((2 * h + xi) * R, LANES), R)
    group = pl.ds(pl.multiple_of(zi * DG, LANES), DG)
    scale = rs[0:1, mine]
    residual = res[...]
    gsum_o[...] = second_grad * residual * scale
    weighted = gains[group, 1:2] * second_grad
    stat[zi] = jnp.broadcast_to(jnp.sum(weighted * residual, axis=0, keepdims=True), (8, R))
    ends = [wire.copy(stat.at[zi], stat.at[zi], g.z(kz)) for kz in range(1, z.Z)]
    direct = cot[mine, group].astype(F32).T + scale * weighted
    for item in ends:
        item.wait_recv()
    advance(rising, 3)
    mean = jnp.sum(stat[:, 0:1, :], axis=0) / D
    grad = direct - residual * (scale * scale * scale * mean)
    lanes = pl.ds(pl.multiple_of(h * R, LANES), R)
    bg_o[:, lanes] = grad.astype(BF16)
    HeadGather(
        wire, s, h, lambda j: bg_o.at[:, pl.ds(pl.multiple_of(j * R, LANES), R)]
    ).wait_all()
    flush(23, 25)
    deal.wait()
    flush(25, 27)
    wire.close()
    for copy in leaving:
        copy.wait()


def front(z, *args):
    S, H, R, D, T, U, Ds, C, Z = z.S, z.H, z.R, z.D, z.T, z.U, z.Ds, z.C, z.Z
    DG, TX = 2 * Ds, Z * R
    copies = 2 + 2 * (Z - 1) + (H - 1) + 1 + 6 * Z + 1 + (H - 1) + (S - 1)
    copies += 4 * (Z - 1) + (H - 1) + 8 * (S - 1) + 12 + 2 * gather_copies(z)
    copies += SumAll.copies(z) + (Z - 1) + (H - 1)
    results = [
        sds((DG, C), BF16),
        sds((DG, C), BF16),
        sds((DG, C), BF16),
        sds((DG, TX), BF16),
        sds((DG, TX), BF16),
        sds((Z, 8, R), F32),
        sds((R, C), F32),
        sds((EDGE + R, C), F32),
        sds((H, R, C), BF16),
        sds((R, C), F32),
        sds((R, C), F32),
        sds((R, C), F32),
        sds((8, C), F32),
        sds((TX, C), BF16),
        sds((DG, R), F32),
        sds((EDGE, C), F32),
        sds((C, C), BF16),
        sds((C, z.NI), BF16),
        sds((DG // H, 8), F32),
        sds((U, T), BF16),
        sds((D, U), BF16),
        sds((D, U), BF16),
        sds((D, U), BF16),
        sds((DG, R), F32),
        sds((DG, TX), BF16),
        sds((Ds, z.F2), BF16),
        sds((Ds, z.F2), BF16),
    ]
    return call(
        functools.partial(front_kernel, z),
        "front",
        1,
        results,
        [VM(item.shape, item.dtype) for item in results]
        + [
            VM((D, R), BF16),
            VM((Z, R, DG), BF16),
            VM((R // 2, C), F32),
            *chain_scratch(z, R, C),
            *chain_scratch(z, R, C),
            VM((S, 8, C), F32),
            VM((R, C), F32),
            VM((H, DG, R), BF16),
            VM((H, DG, R), BF16),
            VM((2, EDGE, C), BF16),
            VM((D, 8), F32),
            VM((T, D), BF16),
            VM((D, U), BF16),
            VM((D, U), BF16),
            VM((D, T), BF16),
            VM((U, D), BF16),
            VM((U, D), BF16),
            VM((U, D), BF16),
            VM((D, U), BF16),
            VM((U, T), F32),
            VM((U, T), BF16),
            VM((U, T), BF16),
            VM((U, T), BF16),
            VM((U, T), BF16),
            VM((8, T), F32),
            VM((D, T), BF16),
            *SumAll.scratch(z, DG, R),
            VM((Z, 8, R), F32),
            sem(copies),
            sem(copies),
            sem(6),
            sem(len(results)),
        ],
        args,
        (14, 15, 16),
        True,
    )


def exact(left, right, dims):
    return lax.dot_general(
        left, right, dims, precision=lax.Precision.HIGHEST, preferred_element_type=F32
    )


def back_kernel(
    z, far, held, fetch_sem, mixed_o, owg_o, xwg_o, ywg_o, twin_r, full, gains2, smallg, vec_o, back_u, back_d,
    stash, g1, g2, g3, g4, own, adj, tot, ag, ig, sums, late, cgr, cgs, ext, gx, gy, part, got, stat, stat2,
    tgq, prod, prod2, gains, small, smallx, small_z, vecs, twin_s, mpart, m1, m2, m3, m4, m5, m6, send, recv,
):
    (
        bg, ow2, hid, dw, res, mix, yb, vec, a_pre, i_pre, st, entry, conv, pad, aw, iw, spread,
        mask, xw2, yw2, fn2, tok2, rn, gain, msum, uwg, dwg,
    ) = held
    fetch = [
        pltpu.make_async_copy(src, dst, fetch_sem.at[index])
        for index, (src, dst) in enumerate(zip(far, held))
    ]
    begun = pltpu.make_async_copy(far[-1], back_u, fetch_sem.at[len(held)])
    begun.start()
    for copy in fetch:
        copy.start()
    begun.wait()
    s, h = place()
    g = Grid(s, h)
    S, H, R, D, Ds, C, Z, T = z.S, z.H, z.R, z.D, z.Ds, z.C, z.Z, z.T
    DG, W = 2 * Ds, D // H
    Q = DG // H
    zi, xi = s // 2, s % 2
    after, before = lax.rem(s + 1, S), lax.rem(s + S - 1, S)
    greet(
        [(s ^ k, h) for k in range(1, S)]
        + [(s, h ^ j) for j in range(1, H)]
        + [(after, h), (before, h)]
    )
    wire = Wire(send, recv)
    chain = Chain(wire, Z, s, h)
    deal = Deal(wire, z, s, h)
    dealing = deal.steps(deal.back, ((uwg, back_u), (dwg, back_d)), 3)
    my_rows = pl.ds(pl.multiple_of(zi * R, EDGE), R)
    half = pl.ds(pl.multiple_of(xi * Ds, EDGE), Ds)
    other = pl.ds(pl.multiple_of((1 - xi) * Ds, EDGE), Ds)

    def corner(a, b, part_of):
        return halves(mpart, b * W, W, a * R, R, part_of)

    mixed = SumAll(wire, z, g, corner, (m1, m2, m3, m4, m5, m6))

    def produce_mixed(d):
        cut = pl.ds(pl.multiple_of(d * 2 * R, LANES), 2 * R)
        mpart[:, cut] = mm(dw[...], hid[:, cut]).astype(BF16)

        @pl.when(h == d)
        def _():
            spot = region_of(z, mpart)(s, h, None)
            spot[...] = (spot[...].astype(F32) + res[...]).astype(BF16)

    mixing = mixed.run(produce_mixed)

    def block(d):
        lanes = pl.ds(pl.multiple_of(d * R, LANES), R)
        return mm(bg[:, lanes].astype(F32).T.astype(BF16), ow2[...])

    for copy in fetch[:5]:
        copy.wait()
    summing = scatter_halves(chain, z, block, stash, (g1, g2, g3, g4, own))
    for _ in range(Z):
        for step in summing:
            advance(step)
        advance(mixing, 2)
    for copy in fetch[5:]:
        copy.wait()
    drain(*summing)
    row = lax.broadcasted_iota(jnp.int32, (R, LANES), 0)
    anchor = anchor_of(z, s, LANES)
    sums[s] = jnp.zeros((8, C), F32)
    for b in range(C // LANES):
        cut = pl.ds(b * LANES, LANES)
        grad = own[:, cut]
        gate, slope = gelu_pair(yb[:, cut])
        gy[my_rows, cut] = (grad * st[:, cut] * slope).astype(BF16)
        factor = jnp.exp(-8.0 * jax.nn.sigmoid(a_pre[:, cut]) * vec[7:8, cut])
        ahead = shifted(factor, -1, 1.0, row)
        prods, value = scan_rows(ahead, grad * gate, -1)
        tot[:, cut] = prods
        adj[:, cut] = value
        sums[s, 0:1, cut] = factor[0:1, :] * prods[0:1, :]
        sums[s, 1:2, cut] = factor[0:1, :] * value[0:1, :]
    ends = [wire.copy(sums.at[s], sums.at[s], (s ^ k, h)) for k in range(1, S)]
    y_rows = chain.gather(row_blocks(z, gy))
    advance(y_rows)
    advance(dealing, 0)
    twins = []

    def weight_grad(index, left, right, out):
        prod2[...] = mm(left[...], right[...])
        twin_s[index] = prod2[other, :].astype(BF16)
        twins.append(wire.copy(twin_s.at[index], twin_r.at[index], g.x))
        out[...] = prod2[half, :]

    weight_grad(0, bg, mix, owg_o)
    advance(mixing, 2)
    for item in ends:
        item.wait_recv()
    carry = jnp.zeros((1, C), F32)
    for j in range(S - 1, 0, -1):
        carry = jnp.where(j > s, sums[j, 0:1, :] * carry + sums[j, 1:2, :], carry)
    vec_o[...] = jnp.zeros_like(vec_o)
    late[...] = jnp.broadcast_to(carry, (8, C))
    for b in range(C // LANES):
        cut = pl.ds(b * LANES, LANES)
        adjoint = adj[:, cut] + tot[:, cut] * late[0:1, cut]
        rate = vec[7:8, cut]
        recall, input_gate, factor, one_minus, root_value, root_scale = decay_terms(
            a_pre[:, cut], i_pre[:, cut], rate, anchor
        )
        taken = conv[h, :, cut].astype(F32)
        state = st[:, cut]
        earlier = jnp.where(row == 0, entry[0:1, cut], shifted(state, 1, 0.0, row))
        live = jnp.logical_and(one_minus > SQUARE_FLOOR, jnp.logical_not(anchor))
        scale_grad = adjoint * taken * input_gate
        log_grad = adjoint * earlier * factor - jnp.where(
            live, scale_grad * factor * factor / root_value, 0.0
        )
        a_grad = (log_grad * (-8.0 * rate) * recall * (1.0 - recall)).astype(BF16)
        i_grad = (scale_grad * root_scale * (1.0 - input_gate)).astype(BF16)
        ag[:, cut] = a_grad
        ig[:, cut] = i_grad
        decay_sum = jnp.sum(log_grad * (-8.0 * recall), axis=0, keepdims=True)
        vec_o[5:6, cut] = jnp.sum(a_grad.astype(F32), axis=0, keepdims=True)
        vec_o[6:7, cut] = jnp.sum(i_grad.astype(F32), axis=0, keepdims=True)
        vec_o[7:8, cut] = decay_sum * vec[8:9, cut]
        ext[pl.ds(0, R), cut] = adjoint * input_gate * root_scale

    eighth = small.shape[0] // S

    def share(x_index, z_index, count):
        start = (x_index * Z + z_index) * eighth
        return pl.ds(pl.multiple_of(start, EDGE), count * eighth)

    def sum_small():
        mine = share(xi, 0, Z)
        item = wire.copy(small.at[share(1 - xi, 0, Z), :], smallx, g.x)
        yield
        item.wait_recv()
        smallx[...] = (smallx[...].astype(F32) + small[mine, :].astype(F32)).astype(BF16)

        def piece(index):
            return pl.ds(pl.multiple_of(index * eighth, EDGE), eighth)

        items = [
            wire.copy(smallx.at[piece(zi ^ kz), :], small_z.at[kz], g.z(kz))
            for kz in range(1, Z)
        ]
        yield
        total = smallx[piece(zi), :].astype(F32)
        for kz in range(1, Z):
            items[kz - 1].wait_recv()
            total = total + small_z[kz].astype(F32)
        spot = smallg.at[share(xi, zi, 1), :]
        spot[...] = total.astype(BF16)
        items = [wire.copy(spot, spot, g.z(kz)) for kz in range(1, Z)]
        yield
        for item in items:
            item.wait_recv()
        item = wire.copy(smallg.at[mine, :], smallg.at[mine, :], g.x)
        yield
        item.wait_recv()

    smaller = sum_small()
    def gates_back(j):
        return mm(ag[...], gate_weight_of(z, spread, mask, aw, h ^ j), NT) + mm(
            ig[...], gate_weight_of(z, spread, mask, iw, h ^ j), NT
        )

    advance(y_rows, 2)
    across = head_scatter(wire, s, h, gates_back, cgs, cgr)
    advance(y_rows, 2)
    advance(dealing, 3)
    for k in range(H):
        turn = conv[k].astype(F32).T.astype(BF16)
        for spot, grad in ((0, ag), (z.HS, ig)):
            dense = mm(turn, grad[...]).astype(BF16) * mask[...]
            small[pl.ds(spot + k * z.NI, z.NI), :] = mm(spread[...], dense, TN).astype(BF16)
    advance(smaller)
    advance(mixing, 2)
    conv_grad = ext[pl.ds(0, R), :] + across()
    ext[pl.ds(0, R), :] = conv_grad
    halo = wire.copy(ext.at[pl.ds(0, 8), :], ext.at[pl.ds(R, 8), :], (before, h))
    for lag in range(CONV):
        vec_o[lag : lag + 1, :] = jnp.sum(
            conv_grad * pad[pl.ds(EDGE - lag, R), :], axis=0, keepdims=True
        )
    vec_o[4:5, :] = jnp.sum(conv_grad, axis=0, keepdims=True)
    vecs[s] = vec_o[...]
    advance(mixing, 1)
    advance(smaller)
    halo.wait_recv()
    ext[pl.ds(R, 8), :] = jnp.where(s == S - 1, 0.0, ext[pl.ds(R, 8), :])
    grad = jnp.zeros((R, C), F32)
    for lag in range(CONV):
        grad = grad + vec[lag : lag + 1, :] * ext[pl.ds(lag, R), :]
    gx[my_rows, :] = grad.astype(BF16)
    rows_in = [chain.gather(row_blocks(z, gx, part_of)) for part_of in range(2)]
    for step in rows_in:
        advance(step)
    advance(dealing, 0)
    advance(mixing, 1)
    pair = grad.astype(BF16).astype(F32) * pad[pl.ds(EDGE, R), :] + gy[my_rows, :].astype(F32) * yb[...]
    stat[h] = exact(jnp.ones((8, C), F32), pair, NT)
    stats = [wire.copy(stat.at[h], stat.at[h], (s, h ^ j)) for j in range(1, H)]

    lesser = [wire.copy(vecs.at[s], vecs.at[s], (s ^ k, h)) for k in range(1, S)]
    drain(y_rows)
    weight_grad(1, fn2, gy, ywg_o)
    prod[...] = mm(yw2[...], gy[...], NT)
    for item in stats:
        item.wait_recv()
    stat2[zi] = stat[0] + stat[1] + stat[2] + stat[3]
    stats = [wire.copy(stat2.at[zi], stat2.at[zi], g.z(kz)) for kz in range(1, Z)]
    advance(smaller)
    advance(mixing, 1)
    drain(*rows_in)

    prod[...] = prod[...] + mm(xw2[...], gx[...], NT)

    def quarter_of(j):
        return prod[pl.ds(pl.multiple_of((h ^ j) * Q, EDGE), Q), :]

    heads = head_scatter(wire, s, h, quarter_of, part, got)
    advance(dealing, 3)
    advance(smaller)
    advance(mixing, 1)
    quarter = pl.ds(pl.multiple_of(h * Q, EDGE), Q)
    weight_grad(2, fn2, gx, xwg_o)
    total = heads()
    for item in stats:
        item.wait_recv()
    token = tok2[quarter, :].astype(F32)
    norm = jnp.concatenate([rn[b, 0:1, :] for b in range(Z)], axis=1)
    mean = jnp.concatenate([stat2[b, 0:1, :] for b in range(Z)], axis=1) / (norm * D)
    weighted = gain[:, 0:1] * total
    grad = bg[quarter, :].astype(F32) + norm * weighted - token * (norm * norm * norm * mean)
    tgq[...] = grad.astype(BF16)

    def spot(z_index, head):
        return full.at[pl.ds(pl.multiple_of(z_index * DG + head * Q, EDGE), Q), :]

    outs = [
        wire.copy(
            tgq.at[:, pl.ds(pl.multiple_of((zi ^ kz) * R, LANES), R)], spot(zi, h), g.z(kz)
        )
        for kz in range(1, Z)
    ]
    spot(zi, h)[...] = tgq[:, pl.ds(pl.multiple_of(zi * R, LANES), R)]
    prod[...] = jnp.zeros_like(prod)
    prod[quarter, :] = total * token * norm
    ones = jnp.ones((8, Z * R), F32)
    picked = lax.broadcasted_iota(jnp.int32, (8, DG), 0)
    gains[h] = jnp.where(
        picked == 0, exact(jnp.ones((8, R), F32), msum[...], NT), exact(ones, prod[...], NT)
    )
    tally = [wire.copy(gains.at[h], gains.at[h], (s, h ^ j)) for j in range(1, H)]
    finals = []
    drain(dealing)
    for kz in range(Z):
        if kz:
            outs[kz - 1].wait_recv()
        finals.append(HeadGather(wire, s, h, lambda j, kz=kz: spot(zi ^ kz, j)))
    for item in tally:
        item.wait_recv()
    gains2[s] = gains[0] + gains[1] + gains[2] + gains[3]
    tally = [wire.copy(gains2.at[s], gains2.at[s], (s ^ k, h)) for k in range(1, S)]
    drain(mixing)
    for part_of in range(2):
        mixed_o[pl.ds(part_of * W // 2, W // 2), :] = mixed.finish(part_of)
    for item in lesser:
        item.wait_recv()
    vec_o[...] = jnp.sum(vecs[...], axis=0)
    for item in twins:
        item.wait_recv()
    deal.back_own(uwg, back_u)
    deal.back_own(dwg, back_d)
    drain(smaller)
    for item in tally:
        item.wait_recv()
    for item in finals:
        item.wait_all()
    deal.wait()
    wire.close()


def back(z, *args):
    S, H, R, D, Ds, C, Z, T = z.S, z.H, z.R, z.D, z.Ds, z.C, z.Z, z.T
    DG, W = 2 * Ds, D // H
    TX, Q = Z * R, DG // H
    copies = (
        4 * Z + (S - 1) + 3 + (H - 1) + 1 + 6 * (Z - 1) + (H - 1) + (Z - 1) + (S - 1)
        + 2 + 2 * (Z - 1) + 2 * (Z - 1) + 4 * (S - 1) + (H - 1) + (Z - 1) + (H - 1) + Z * (H - 1) + (S - 1)
        + SumAll.copies(z)
    )
    small = 2 * z.HS
    count = len(args)

    def body(*refs):
        far, rest = refs[:count], refs[count:]
        outs, held, rest = rest[:11], rest[11 : 10 + count], rest[10 + count :]
        back_kernel(z, far, held, rest[0], *outs, *rest[1:])

    return call(
        body,
        "back",
        2,
        [
            sds((W, R), F32),
            sds((Ds, C), F32),
            sds((Ds, C), F32),
            sds((Ds, C), F32),
            sds((3, Ds, C), BF16),
            sds((D, R), BF16),
            sds((S, 8, DG), F32),
            sds((small, C), BF16),
            sds((8, C), F32),
            sds((Ds, z.F2), BF16),
            sds((Ds, z.F2), BF16),
        ],
        [VM(a.shape, a.dtype) for a in args[:-1]]
        + [sem(count)]
        + [
            VM((R // 2, C), F32),
            *chain_scratch(z, R, C),
            VM((R, C), F32),
            VM((R, C), F32),
            VM((R, C), BF16),
            VM((R, C), BF16),
            VM((S, 8, C), F32),
            VM((8, C), F32),
            VM((H, R, C), BF16),
            VM((H, R, C), BF16),
            VM((R + 8, C), F32),
            VM((TX, C), BF16),
            VM((TX, C), BF16),
            VM((H, Q, TX), BF16),
            VM((H, Q, TX), BF16),
            VM((H, 8, R), F32),
            VM((Z, 8, R), F32),
            VM((Q, TX), BF16),
            VM((DG, TX), F32),
            VM((DG, C), F32),
            VM((H, 8, DG), F32),
            VM((small, C), BF16),
            VM((small // 2, C), BF16),
            VM((Z, small // S, C), BF16),
            VM((S, 8, C), F32),
            VM((3, Ds, C), BF16),
            VM((D, T), BF16),
        ]
        + SumAll.scratch(z, W, R)
        + [sem(copies), sem(copies)],
        args,
        range(count),
    )


def results_kernel(z, *refs):
    sources, count = 12, 17
    inputs, outs = refs[:sources], refs[sources : sources + count]
    held = refs[sources + count : 2 * sources + count]
    stage = refs[2 * sources + count : 2 * (sources + count)]
    in_sem, out_sem = refs[-2:]
    fetch = {}
    for index in (4, 1, 2, 3, 9, 10, 11, 5, 0, 7, 8, 6):
        copy = pltpu.make_async_copy(inputs[index], held[index], in_sem.at[index])
        copy.start()
        fetch[index] = copy
    mixed, owg, xwg, ywg, twins, full, gains, small, vec, back_g, back_u, back_d = held
    copies = []

    def need(*indexes):
        for index in indexes:
            fetch[index].wait()

    def emit(index, value):
        stage[index][...] = value
        copy = pltpu.make_async_copy(stage[index], outs[index], out_sem.at[index])
        copy.start()
        copies.append(copy)

    need(4, 1, 2, 3)
    for index, slot, src in ((12, 0, owg), (4, 1, ywg), (3, 2, xwg)):
        emit(index, src[...] + twins[slot].astype(F32))
    for index, at_input, src in ((14, 9, back_g), (15, 10, back_u), (16, 11, back_d)):
        need(at_input)
        emit(index, src[...].astype(F32))
    need(5, 0, 7, 8, 6)
    emit(1, full[...].astype(F32).T)
    emit(0, mixed[...].T.astype(BF16))
    emit(7, small[0 : z.HS, :].astype(F32))
    emit(9, small[z.HS : 2 * z.HS, :].astype(F32))
    emit(5, vec[0:CONV, :])
    for index, row in ((6, 4), (8, 5), (10, 6), (11, 7)):
        outs[index][...] = vec[row, :]
    for index, row in ((2, 1), (13, 0)):
        sums = [gains[2 * b, row, :] + gains[2 * b + 1, row, :] for b in range(z.Z)]
        outs[index][...] = jnp.concatenate(sums)
    for copy in copies:
        copy.wait()


def results(z, *args):
    R, D, Ds, C, F2 = z.R, z.D, z.Ds, z.C, z.F2
    row = sds((C,), F32)
    outs = [
        sds((R, D // z.H), BF16),
        sds((R, D), F32),
        sds((D,), F32),
        sds((Ds, C), F32),
        sds((Ds, C), F32),
        sds((CONV, C), F32),
        row,
        sds((z.HS, C), F32),
        row,
        sds((z.HS, C), F32),
        row,
        row,
        sds((Ds, C), F32),
        sds((D,), F32),
        sds((Ds, F2), F32),
        sds((Ds, F2), F32),
        sds((Ds, F2), F32),
    ]
    return pl.pallas_call(
        functools.partial(results_kernel, z),
        out_shape=outs,
        in_specs=[pl.BlockSpec(memory_space=ANY)] * len(args),
        out_specs=[
            pl.BlockSpec(memory_space=VM if len(out.shape) == 1 else ANY) for out in outs
        ],
        scratch_shapes=[VM(a.shape, a.dtype) for a in list(args) + outs]
        + [sem(len(args)), sem(len(outs))],
        compiler_params=pltpu.CompilerParams(vmem_limit_bytes=62 << 20),
        name="results",
    )(*args)


def dealt(
    z,
    tokens,
    norm_gain,
    x_weight,
    y_weight,
    conv_weight,
    conv_bias,
    a_weight,
    a_bias,
    i_weight,
    i_bias,
    decay,
    out_weight,
    mlp_gain,
    gate_weight,
    up_weight,
    down_weight,
    cotangent,
):
    (
        xw2, yw2, ow2, tok2, fn2, rn, yb, pad, conv, a_pre, i_pre, st, entry, mix, res,
        vec, mask, spread, gain_q, hid, dc, uwg, dwg, msum, bg, back_g, up_part,
    ) = front(
        z, tokens, norm_gain, mlp_gain, x_weight, y_weight, out_weight, conv_weight, conv_bias,
        a_bias, i_bias, decay, a_weight, i_weight,
        cotangent, gate_weight, up_weight, down_weight,
    )
    mixed, owg, xwg, ywg, twins, tg, gains, small, vec_sum, back_u, back_d = back(
        z, bg, ow2, hid, dc, res, mix, yb, vec, a_pre, i_pre, st, entry, conv, pad, a_weight,
        i_weight, spread, mask, xw2, yw2, fn2, tok2, rn, gain_q, msum, uwg, dwg, up_part,
    )
    return tuple(
        results(z, mixed, owg, xwg, ywg, twins, tg, gains, small, vec_sum, back_g, back_u, back_d)
    )


def from_behind(x, axis, by):
    size = lax.axis_size(axis)
    pairs = [(i, i + by) for i in range(size) if 0 <= i + by < size]
    return lax.ppermute(x, axis, pairs)


def rms_norm(values, gain):
    return values * lax.rsqrt(jnp.mean(values * values, axis=-1, keepdims=True) + EPSILON) * gain


def linear_pair(earlier, later):
    return (later[0] * earlier[0], later[0] * earlier[1] + later[1])


def gelu_back(values, grad):
    return jax.vjp(jax.nn.gelu, values)[1](grad)[0]


def gathered_weights(
    tokens,
    norm_gain,
    x_weight,
    y_weight,
    conv_weight,
    conv_bias,
    a_weight,
    a_bias,
    i_weight,
    i_bias,
    decay,
    out_weight,
    mlp_gain,
    gate_weight,
    up_weight,
    down_weight,
    cotangent,
):
    row_count = tokens.shape[0]
    model_width = tokens.shape[1]
    lane_count = x_weight.shape[1]
    head_size = a_weight.shape[0]
    head_index = lax.axis_index("head")
    seq_index = lax.axis_index("seq")
    head_devices = lax.axis_size("head")
    float_type = jnp.float32
    half_type = jnp.bfloat16
    gathered = (
        lax.all_gather(x_weight, "seq", axis=0, tiled=True),
        lax.all_gather(y_weight, "seq", axis=0, tiled=True),
        lax.all_gather(out_weight, "seq", axis=0, tiled=True),
        lax.all_gather(gate_weight, "seq", axis=0, tiled=True),
        lax.all_gather(up_weight, "seq", axis=0, tiled=True),
        lax.all_gather(down_weight, "seq", axis=0, tiled=True),
    )
    x_full, y_full, out_full, gate_full, up_full, down_full = gathered
    tokens_wide = tokens.astype(float_type)
    first_gain = norm_gain.astype(float_type)
    first_norm = rms_norm(tokens_wide, first_gain)
    first_low = first_norm.astype(half_type)
    x_branch = jnp.dot(first_low, x_full, preferred_element_type=float_type).astype(half_type)
    y_branch = jnp.dot(first_low, y_full, preferred_element_type=float_type)
    y_gate = jax.nn.gelu(y_branch)
    left_edge = from_behind(x_branch[row_count - (CONV - 1) :], "seq", 1)
    padded = jnp.concatenate([left_edge, x_branch], axis=0).astype(float_type)
    conv_taps = conv_weight.astype(float_type)
    conv_out = conv_bias.astype(float_type) + sum(
        (
            conv_taps[lag_index] * padded[CONV - 1 - lag_index : CONV - 1 - lag_index + row_count]
            for lag_index in range(CONV)
        )
    )
    conv_low = conv_out.astype(half_type)
    conv_value = conv_low.astype(float_type)
    all_channels = lax.all_gather(conv_low, "head", axis=1, tiled=True)
    head_count = all_channels.shape[1] // head_size
    group_count = lane_count // head_count
    heads_view = all_channels.reshape(row_count, head_size, head_count)

    def block_gate(weight, bias):
        product = jnp.einsum(
            "tih,ijh->tjh",
            heads_view,
            weight.reshape(head_size, group_count, head_count),
            preferred_element_type=float_type,
        )
        return product.reshape(row_count, lane_count) + bias.astype(float_type)

    a_pre = block_gate(a_weight, a_bias)
    i_pre = block_gate(i_weight, i_bias)
    recall = jax.nn.sigmoid(a_pre)
    input_gate = jax.nn.sigmoid(i_pre)
    decay_rate = jax.nn.softplus(decay)
    log_decay = -8.0 * recall * decay_rate
    factor = jnp.exp(log_decay)
    double_decay = jnp.exp(2.0 * log_decay)
    one_minus = -jnp.expm1(2.0 * log_decay)
    root_value = jnp.sqrt(jnp.maximum(one_minus, SQUARE_FLOOR))
    position = seq_index * row_count + jnp.arange(row_count)
    anchor = (position == 0)[:, None]
    root_scale = jnp.where(anchor, 1.0, root_value)
    root_live = jnp.logical_and(one_minus > SQUARE_FLOOR, jnp.logical_not(anchor))
    driven = conv_value * input_gate * root_scale
    local_prod, local_state = lax.associative_scan(linear_pair, (factor, driven))

    def relay_step(turn_number, carried):
        return from_behind(local_prod[-1] * carried + local_state[-1], "seq", 1)

    state_entry = lax.fori_loop(
        0, lax.axis_size("seq") - 1, relay_step, jnp.zeros_like(local_state[-1])
    )
    state_all = local_state + local_prod * state_entry
    mixed_in = (state_all * y_gate).astype(half_type)
    branch_part = jnp.einsum("tc,dc->td", mixed_in, out_full, preferred_element_type=float_type)
    branch = lax.psum(branch_part, "head")
    residual = tokens_wide + branch
    second_gain = mlp_gain.astype(float_type)
    second_low = rms_norm(residual, second_gain).astype(half_type)
    gate_pre = jnp.dot(second_low, gate_full, preferred_element_type=float_type)
    up_pre = jnp.dot(second_low, up_full, preferred_element_type=float_type)
    gate_act = jax.nn.gelu(gate_pre)
    hidden = (gate_act * up_pre).astype(half_type)
    mlp_part = jnp.einsum("tf,df->td", hidden, down_full, preferred_element_type=float_type)
    own_columns = lax.psum_scatter(mlp_part, "head", scatter_dimension=1, tiled=True)
    column_count = model_width // head_devices
    mixed = (
        lax.dynamic_slice_in_dim(residual, head_index * column_count, column_count, 1) + own_columns
    ).astype(half_type)
    regathered = (
        lax.all_gather(x_weight, "seq", axis=0, tiled=True),
        lax.all_gather(y_weight, "seq", axis=0, tiled=True),
        lax.all_gather(out_weight, "seq", axis=0, tiled=True),
        lax.all_gather(gate_weight, "seq", axis=0, tiled=True),
        lax.all_gather(up_weight, "seq", axis=0, tiled=True),
        lax.all_gather(down_weight, "seq", axis=0, tiled=True),
    )
    x_full, y_full, out_full, gate_full, up_full, down_full = regathered
    hidden_grad = jnp.dot(cotangent, down_full, preferred_element_type=float_type)
    gate_grad = gelu_back(gate_pre, hidden_grad * up_pre).astype(half_type)
    up_grad = (hidden_grad * gate_act).astype(half_type)
    second_part = jnp.einsum(
        "tf,df->td", gate_grad, gate_full, preferred_element_type=float_type
    ) + jnp.einsum("tf,df->td", up_grad, up_full, preferred_element_type=float_type)
    second_grad = lax.psum(second_part, "head")
    resid_back, mlp_gain_term = jax.vjp(rms_norm, residual, second_gain)[1](second_grad)
    resid_grad = cotangent.astype(float_type) + resid_back
    branch_grad = resid_grad.astype(half_type)
    mixed_grad = jnp.dot(branch_grad, out_full, preferred_element_type=float_type)
    state_grad = mixed_grad * y_gate
    y_grad = gelu_back(y_branch, mixed_grad * state_all).astype(half_type)
    next_factor = jnp.concatenate([factor[1:], jnp.ones_like(factor[:1])], axis=0)
    back_prod, back_adjoint = lax.associative_scan(
        linear_pair, (next_factor[::-1], state_grad[::-1])
    )
    back_prod = back_prod[::-1]
    back_adjoint = back_adjoint[::-1]
    tail_prod = factor[0] * back_prod[0]
    tail_value = factor[0] * back_adjoint[0]

    def relay_back(turn_number, carried):
        return from_behind(tail_value + tail_prod * carried, "seq", -1)

    exit_carry = lax.fori_loop(0, lax.axis_size("seq") - 1, relay_back, jnp.zeros_like(tail_value))
    adjoint = back_adjoint + back_prod * exit_carry
    prev_state = jnp.concatenate([state_entry[None], state_all[:-1]], axis=0)
    scale_grad = adjoint * conv_value * input_gate
    log_grad = adjoint * prev_state * factor + jnp.where(
        root_live, -scale_grad * double_decay / root_value, 0.0
    )
    a_grad = (log_grad * (-8.0 * decay_rate) * recall * (1.0 - recall)).astype(half_type)
    i_grad = (adjoint * conv_value * root_scale * input_gate * (1.0 - input_gate)).astype(half_type)
    decay_term = jnp.sum(log_grad * (-8.0 * recall), axis=0) * jax.nn.sigmoid(decay)
    a_bias_term = jnp.sum(a_grad.astype(float_type), axis=0)
    i_bias_term = jnp.sum(i_grad.astype(float_type), axis=0)

    def gate_back(grad, weight):
        grad_view = grad.reshape(row_count, group_count, head_count)
        weight_term = jnp.einsum(
            "tih,tjh->ijh", heads_view, grad_view, preferred_element_type=float_type
        ).reshape(head_size, lane_count)
        input_term = jnp.einsum(
            "tjh,ijh->tih",
            grad_view,
            weight.reshape(head_size, group_count, head_count),
            preferred_element_type=float_type,
        )
        return (weight_term, input_term)

    a_wgrad, a_input = gate_back(a_grad, a_weight)
    i_wgrad, i_input = gate_back(i_grad, i_weight)
    gate_input_grad = lax.psum_scatter(
        (a_input + i_input).reshape(row_count, head_size * head_count),
        "head",
        scatter_dimension=1,
        tiled=True,
    )
    conv_grad = gate_input_grad + adjoint * input_gate * root_scale
    right_edge = from_behind(conv_grad[: CONV - 1], "seq", -1)
    extended_grad = jnp.concatenate([conv_grad, right_edge], axis=0)
    x_branch_grad = sum(
        (
            conv_taps[lag_index] * extended_grad[lag_index : lag_index + row_count]
            for lag_index in range(CONV)
        )
    ).astype(half_type)
    conv_wgrad = jnp.stack(
        [
            jnp.sum(
                conv_grad * padded[CONV - 1 - lag_index : CONV - 1 - lag_index + row_count], axis=0
            )
            for lag_index in range(CONV)
        ],
        axis=0,
    )
    conv_bgrad = jnp.sum(conv_grad, axis=0)
    first_part = jnp.einsum(
        "tc,dc->td", x_branch_grad, x_full, preferred_element_type=float_type
    ) + jnp.einsum("tc,dc->td", y_grad, y_full, preferred_element_type=float_type)
    first_grad = lax.psum(first_part, "head")
    tokens_back, norm_gain_term = jax.vjp(rms_norm, tokens_wide, first_gain)[1](first_grad)
    tokens_grad = resid_grad + tokens_back
    pairings = (
        (first_low, x_branch_grad),
        (first_low, y_grad),
        (branch_grad, mixed_in),
        (second_low, gate_grad),
        (second_low, up_grad),
        (cotangent, hidden),
    )
    products = tuple(
        (
            jnp.einsum("td,tc->dc", left, right, preferred_element_type=float_type)
            for left, right in pairings
        )
    )
    weight_sums = lax.psum_scatter(products, "seq", scatter_dimension=0, tiled=True)
    small_sums = lax.psum(
        (
            norm_gain_term,
            conv_wgrad,
            conv_bgrad,
            a_wgrad,
            a_bias_term,
            i_wgrad,
            i_bias_term,
            decay_term,
            mlp_gain_term,
        ),
        "seq",
    )
    return (
        mixed,
        tokens_grad,
        small_sums[0],
        weight_sums[0],
        weight_sums[1],
        small_sums[1],
        small_sums[2],
        small_sums[3],
        small_sums[4],
        small_sums[5],
        small_sums[6],
        small_sums[7],
        weight_sums[2],
        small_sums[8],
        weight_sums[3],
        weight_sums[4],
        weight_sums[5],
    )


def solution(mesh):
    sizes = mesh.shape["seq"], mesh.shape["head"]

    def body(*args):
        z = Size(sizes, args[0], args[2], args[6], args[13])
        return dealt(z, *args) if z.fits() else gathered_weights(*args)

    return jax.shard_map(
        body,
        mesh=mesh,
        in_specs=(
            P("seq", None),
            P(),
            P("seq", "head"),
            P("seq", "head"),
            P(None, "head"),
            P("head"),
            P(None, "head"),
            P("head"),
            P(None, "head"),
            P("head"),
            P("head"),
            P("seq", "head"),
            P(),
            P("seq", "head"),
            P("seq", "head"),
            P("seq", "head"),
            P("seq", None),
        ),
        out_specs=(
            P("seq", "head"),
            P("seq", None),
            P(),
            P("seq", "head"),
            P("seq", "head"),
            P(None, "head"),
            P("head"),
            P(None, "head"),
            P("head"),
            P(None, "head"),
            P("head"),
            P("head"),
            P("seq", "head"),
            P(),
            P("seq", "head"),
            P("seq", "head"),
            P("seq", "head"),
        ),
        check_vma=False,
    )
```

```python
import functools

import jax
import jax.numpy as jnp
from jax import lax
from jax.experimental import pallas as pl
from jax.experimental.pallas import tpu as pltpu
from jax.sharding import PartitionSpec as P

CONV = 4
EPSILON = 1e-06
SQUARE_FLOOR = 2.5e-07
MESH = pl.DeviceIdType.MESH
F32 = jnp.float32
BF16 = jnp.bfloat16
LANES = 128
EDGE = 16
VM = pltpu.VMEM
ANY = pl.ANY
NN = (((1,), (0,)), ((), ()))
NT = (((1,), (1,)), ((), ()))
TN = (((0,), (0,)), ((), ()))


def mm(left, right, dims=NN):
    return lax.dot_general(left, right, dims, preferred_element_type=F32)


def gelu_pair(values):
    scale = 0.7978845608028654
    square = values * values
    bend = jnp.tanh(scale * values * (1.0 + 0.044715 * square))
    half = 0.5 * (1.0 + bend)
    slope = half + 0.5 * values * (1.0 - bend * bend) * scale * (1.0 + 3.0 * 0.044715 * square)
    return values * half, slope


def minus_expm1(v):
    series = jnp.full_like(v, 1.0 / 40320.0)
    for divisor in (5040.0, 720.0, 120.0, 24.0, 6.0, 2.0, 1.0):
        series = series * v + 1.0 / divisor
    return jnp.where(v > -0.35, -v * series, 1.0 - jnp.exp(v))


def when(condition, action):
    if condition is None:
        action()
    else:
        pl.when(condition)(action)


class Copy:
    def __init__(self, item, goes, comes):
        self.item, self.goes, self.comes = item, goes, comes

    def start(self):
        when(self.goes, lambda: self.item.start())

    def wait_send(self):
        when(self.goes, lambda: self.item.wait_send())

    def wait_recv(self):
        when(self.comes, lambda: self.item.wait_recv())

    def arrived(self):
        self.item.wait_recv()


class Wire:
    def __init__(self, send, recv):
        self.send, self.recv, self.count, self.open = send, recv, 0, []

    def make(self, src, dst, peer, goes=None, comes=None):
        slot = self.count
        self.count += 1
        item = pltpu.make_async_remote_copy(
            src_ref=src,
            dst_ref=dst,
            send_sem=self.send.at[slot],
            recv_sem=self.recv.at[slot],
            device_id=peer,
            device_id_type=MESH,
        )
        copy = Copy(item, goes, comes)
        self.open.append(copy)
        return copy

    def copy(self, src, dst, peer, goes=None, comes=None):
        copy = self.make(src, dst, peer, goes, comes)
        copy.start()
        return copy

    def close(self):
        for item in self.open:
            item.wait_send()
        assert self.count <= self.send.shape[0], self.count


class Chain:
    def __init__(self, wire, count, s, h):
        self.wire, self.count, self.s, self.h, self.zi = wire, count, s, h, s // 2
        self.up = (jnp.minimum(s + 2, 2 * count - 2 + s % 2), h)
        self.down = (jnp.maximum(s - 2, s % 2), h)

    def gather(self, view):
        zi, last = self.zi, self.count - 1

        def hop(step, way):
            index = zi - way * step
            held = jnp.logical_and(index >= 0, index <= last)
            goes = jnp.logical_and(held, zi < last if way > 0 else zi > 0)
            here = index - way
            comes = jnp.logical_and(here >= 0, here <= last)
            block = view(jnp.clip(index, 0, last))
            peer = self.up if way > 0 else self.down
            return self.wire.copy(block, block, peer, goes, comes), comes, jnp.clip(here, 0, last)

        flight = [hop(0, 1), hop(0, -1)]
        yield None, zi
        for step in range(last):
            for side, way in enumerate((1, -1)):
                item, comes, index = flight[side]
                item.wait_recv()
                if step + 1 < last:
                    flight[side] = hop(step + 1, way)
                yield comes, index

    def order(self):
        count = self.count
        low = list(reversed(range(count // 2, count))) + list(range(count // 2))
        near = self.zi < count // 2
        return [jnp.where(near, d, count - 1 - d) for d in low]

    def passes(self, d, src, up, down):
        zi, last, wire = self.zi, self.count - 1, self.wire
        base = wire.count
        wire.count = base + d
        first = wire.make(src, up, self.up, zi < d, jnp.logical_and(zi > 0, zi <= d))
        wire.count = base + self.count + d
        second = wire.make(src, down, self.down, zi > d, jnp.logical_and(zi < last, zi >= d))
        wire.count = base
        return first, second

    def between(self, d):
        zi, last = self.zi, self.count - 1
        return jnp.logical_and(zi > 0, zi < d), jnp.logical_and(zi < last, zi > d)

    def ends(self, d):
        zi, last = self.zi, self.count - 1
        return jnp.logical_and(zi == d, zi > 0), jnp.logical_and(zi == d, zi < last)

    def scatter(self, block, work, out, up, down, own):
        zi = self.zi
        flight = []
        base = self.wire.count
        self.wire.count += 2 * self.count

        def take(item, got, into):
            def action():
                item.arrived()
                into[...] = into[...] + got[...].astype(F32)
            return action

        for d in self.order():
            work[...] = block(d)
            kept, self.wire.count = self.wire.count, base
            ups, downs = self.passes(d, out.at[d], up.at[d], down.at[d])
            self.wire.count = kept
            flight.append((d, ups, downs))
            below, above = self.between(d)
            when(below, take(ups, up.at[d], work))
            when(above, take(downs, down.at[d], work))

            def give(d=d):
                out[d] = work[...].astype(BF16)

            def keep():
                own[...] = work[...]

            when(zi != d, give)
            when(zi == d, keep)
            ups.start()
            downs.start()
            yield d
        for d, ups, downs in flight:
            below, above = self.ends(d)
            when(below, take(ups, up.at[d], own))
            when(above, take(downs, down.at[d], own))


class HeadGather:
    def __init__(self, wire, s, h, view):
        self.wire, self.s, self.h, self.view = wire, s, h, view
        self.items = {1: self.send(0, 1), 2: self.send(0, 2)}

    def send(self, j, to):
        block = self.view(self.h ^ j)
        return self.wire.copy(block, block, (self.s, self.h ^ to))

    def wait(self, j):
        if j == 2:
            self.items[2].wait_recv()
            self.items[3] = self.send(2, 1)
        else:
            self.items[j].wait_recv()

    def wait_all(self):
        for j in (2, 1, 3):
            self.wait(j)


def head_scatter(wire, s, h, block, out, got):
    core, other = (s, h ^ 1), (s, h ^ 2)
    flight = {}
    for j in (3, 1):
        out[j] = block(j).astype(BF16)
        flight[j] = wire.copy(out.at[j], got.at[j], core)
    part = block(2)
    flight[3].wait_recv()
    out[2] = (part + got[3].astype(F32)).astype(BF16)
    flight[2] = wire.copy(out.at[2], got.at[2], other)
    total = block(0)
    flight[1].wait_recv()
    total = total + got[1].astype(F32)

    def finish():
        flight[2].wait_recv()
        return total + got[2].astype(F32)

    return finish


def drain(*steps):
    steps = list(steps)
    while steps:
        steps = [step for step in steps if next(step, step) is not step]


def advance(step, count=1):
    for _ in range(count):
        next(step, None)


def greet(peers):
    barrier = pltpu.get_barrier_semaphore()
    for peer in peers:
        pl.semaphore_signal(barrier, inc=1, device_id=peer, device_id_type=MESH)
    pl.semaphore_wait(barrier, len(peers))


def place():
    return lax.axis_index("seq"), lax.axis_index("head")


def at(ref, rows, row_count, lanes, lane_count):
    return ref.at[
        pl.ds(pl.multiple_of(rows, EDGE), row_count),
        pl.ds(pl.multiple_of(lanes, LANES), lane_count),
    ]


def sem(count):
    return pltpu.SemaphoreType.DMA((count,))


def call(body, name, cid, outs, scratch, args, spaces=(), far=False, limit=62, us=150):
    return pl.pallas_call(
        body,
        out_shape=outs,
        in_specs=[
            pl.BlockSpec(memory_space=ANY if i in spaces else VM) for i in range(len(args))
        ],
        out_specs=[pl.BlockSpec(memory_space=ANY if far else VM) for _ in outs],
        scratch_shapes=scratch,
        compiler_params=pltpu.CompilerParams(
            collective_id=cid, has_side_effects=True, vmem_limit_bytes=limit << 20
        ),
        cost_estimate=pl.CostEstimate(
            flops=us * 10**6, bytes_accessed=us * 3 * 10**6, transcendentals=0
        ),
        name=name,
    )(*args)


def sds(shape, kind):
    return jax.ShapeDtypeStruct(shape, kind)


class Size:
    def __init__(self, mesh_sizes, tokens, x_weight, a_weight, gate_weight):
        self.S, self.H = mesh_sizes
        self.Z = self.S // 2
        self.R, self.D = tokens.shape
        self.T = self.S * self.R
        self.Ds, self.C = x_weight.shape
        self.HS = a_weight.shape[0]
        self.heads = self.H * self.C // self.HS
        self.F2 = gate_weight.shape[1]
        self.TB = self.T // self.H
        self.U = 2 * LANES
        self.NI = self.HS // self.H

    def fits(self):
        tiles = self.F2 // LANES
        return (
            self.S == 8
            and self.H == 4
            and self.Z == self.H
            and (2 * self.Ds) % LANES == 0
            and (2 * self.HS // self.S) % EDGE == 0
            and self.D == self.H * self.C
            and self.F2 % LANES == 0
            and 2 * (self.S - 1) < tiles <= 2 * self.S
            and self.T <= 1024
            and self.R % LANES == 0
            and self.C % LANES == 0
            and self.Ds % (2 * EDGE) == 0
            and (self.Ds // self.H) % EDGE == 0
            and self.NI % EDGE == 0
        )


def gate_weight_of(z, spread, mask, weight, k):
    rows = weight[pl.ds(pl.multiple_of(k * z.NI, EDGE), z.NI), :]
    return mm(spread[...], rows).astype(BF16) * mask[...]


def shifted(values, by, fill, row):
    count = values.shape[0]
    moved = pltpu.roll(values, by % count, 0)
    inside = row >= by if by > 0 else row < count + by
    return jnp.where(inside, moved, fill)


def scan_rows(prod, value, sign):
    row = lax.broadcasted_iota(jnp.int32, prod.shape, 0)
    by = 1
    while by < prod.shape[0]:
        value = prod * shifted(value, sign * by, 0.0, row) + value
        prod = prod * shifted(prod, sign * by, 1.0, row)
        by *= 2
    return prod, value


def decay_terms(a_pre, i_pre, rate, anchor):
    recall = jax.nn.sigmoid(a_pre)
    input_gate = jax.nn.sigmoid(i_pre)
    log_decay = -8.0 * recall * rate
    factor = jnp.exp(log_decay)
    one_minus = minus_expm1(2.0 * log_decay)
    root_value = jnp.sqrt(jnp.maximum(one_minus, SQUARE_FLOOR))
    root_scale = jnp.where(anchor, 1.0, root_value)
    return recall, input_gate, factor, one_minus, root_value, root_scale


def anchor_of(z, s, width):
    row = lax.broadcasted_iota(jnp.int32, (z.R, width), 0)
    return jnp.logical_and(row == 0, s == 0)


def head_maps(z, spread, mask):
    def parts(shape, axis):
        channel = lax.broadcasted_iota(jnp.int32, shape, axis).astype(F32)
        row = jnp.floor((channel + 0.5) * (1.0 / z.heads))
        return row, channel - row * z.heads

    across = lax.broadcasted_iota(jnp.int32, (z.C, z.NI), 1).astype(F32)
    spread[...] = jnp.where(parts((z.C, z.NI), 0)[0] == across, 1.0, 0.0).astype(BF16)
    same = parts((z.C, z.C), 0)[1] == parts((z.C, z.C), 1)[1]
    mask[...] = jnp.where(same, 1.0, 0.0).astype(BF16)


def softplus(values):
    small = jnp.exp(-jnp.abs(values))
    series = jnp.full_like(small, 1.0 / 9.0)
    for order in range(8, 0, -1):
        series = 1.0 / order - small * series
    tail = jnp.where(small < 0.1, small * series, jnp.log(1.0 + small))
    return jnp.maximum(values, 0.0) + tail


class Deal:
    def __init__(self, wire, z, s, h):
        self.wire, self.z, self.s, self.h = wire, z, s, h
        self.tiles = z.F2 // LANES
        self.sent = []

    def rows(self, owner):
        return pl.ds(pl.multiple_of(owner * self.z.Ds, EDGE), self.z.Ds)

    def post(self, src, dst, peer, part, goes, comes):
        wire = self.wire
        item = pltpu.make_async_remote_copy(
            src_ref=src,
            dst_ref=dst,
            send_sem=wire.send.at[wire.count],
            recv_sem=wire.recv.at[wire.count],
            device_id=(peer, self.h),
            device_id_type=MESH,
        )
        wire.count += 1
        self.sent.append((item, part, goes, comes))
        if part == 0:
            item.start()
        else:
            @pl.when(goes)
            def _():
                item.start()

    def out(self, src, dst, offsets):
        z = self.z
        for k in offsets:
            peer = self.s ^ k
            for part in range(2):
                tile = 2 * peer + part
                self.post(
                    at(src, 0, z.Ds, jnp.minimum(tile, self.tiles - 1) * LANES, LANES),
                    dst.at[self.rows(self.s), pl.ds(part * LANES, LANES)],
                    peer,
                    part,
                    tile < self.tiles,
                    2 * self.s + part < self.tiles,
                )

    def back(self, src, dst, offsets):
        z = self.z
        for k in offsets:
            peer = self.s ^ k
            for part in range(2):
                tile = 2 * self.s + part
                lane = jnp.minimum(tile, self.tiles - 1) * LANES
                self.post(
                    src.at[self.rows(peer), pl.ds(part * LANES, LANES)],
                    at(dst, 0, z.Ds, lane, LANES),
                    peer,
                    part,
                    tile < self.tiles,
                    2 * peer + part < self.tiles,
                )

    def steps(self, how, pairs, start=0):
        plan = [(pair, k) for pair in pairs for k in ((4, 2), (5, 3), (6, 1), (7,))]
        for (src, dst), offsets in plan[start:]:
            how(src, dst, offsets)
            yield

    def back_own(self, src, dst):
        z, s = self.z, self.s
        at(dst, 0, z.Ds, 2 * s * LANES, LANES)[...] = src[self.rows(s), 0:LANES]

        @pl.when(2 * s + 1 < self.tiles)
        def _():
            lane = jnp.minimum(2 * s + 1, self.tiles - 1) * LANES
            at(dst, 0, z.Ds, lane, LANES)[...] = src[self.rows(s), LANES : 2 * LANES]

    def wait(self, sent=None):
        for item, part, goes, comes in self.sent if sent is None else sent:
            if part == 0:
                item.wait()
            else:
                @pl.when(goes)
                def _(item=item):
                    item.wait_send()

                @pl.when(comes)
                def _(item=item):
                    item.wait_recv()
        if sent is None:
            self.sent = []


def own_block(z, src, dst, sems, s):
    tiles = z.F2 // LANES
    rows = pl.ds(pl.multiple_of(s * z.Ds, EDGE), z.Ds)
    first = pltpu.make_async_copy(
        at(src, 0, z.Ds, 2 * s * LANES, LANES), dst.at[rows, pl.ds(0, LANES)], sems.at[0]
    )
    second = pltpu.make_async_copy(
        at(src, 0, z.Ds, jnp.minimum(2 * s + 1, tiles - 1) * LANES, LANES),
        dst.at[rows, pl.ds(LANES, LANES)],
        sems.at[1],
    )
    whole = 2 * s + 1 < tiles
    first.start()

    @pl.when(whole)
    def _():
        second.start()

    @pl.when(jnp.logical_not(whole))
    def _():
        dst[:, LANES : 2 * LANES] = jnp.zeros((z.D, LANES), BF16)

    def wait():
        first.wait()

        @pl.when(whole)
        def _():
            second.wait()

    return wait


def chain_scratch(z, rows, width):
    return [VM((rows, width), F32)] + [VM((z.Z, rows, width), BF16)] * 3 + [VM((rows, width), F32)]


def row_blocks(z, buf, part=None):
    count = z.R if part is None else z.R // 2
    first = 0 if part is None else part * count
    return lambda index: buf.at[pl.ds(pl.multiple_of(index * z.R + first, EDGE), count), :]


def scatter_halves(chain, z, block, stash, bufs):
    count = z.R // 2

    def cut(buf, part):
        rows = pl.ds(part * count, count)
        return buf.at[:, rows, :] if len(buf.shape) == 3 else buf.at[rows, :]

    def first(d):
        whole = block(d)
        stash[...] = whole[count:, :]
        return whole[:count, :]

    return [
        chain.scatter(source, *(cut(buf, part) for buf in bufs))
        for part, source in enumerate((first, lambda d: stash[...]))
    ]


class Grid:
    def __init__(self, s, h):
        self.s, self.h = s, h
        self.x, self.y, self.core = (s ^ 1, h), (s, h ^ 2), (s, h ^ 1)

    def z(self, kz):
        return (self.s ^ (2 * kz), self.h)


def gather_all(wire, z, g, region):
    s, h, xi = g.s, g.h, g.s % 2
    chain = Chain(wire, z.Z, s, h)
    arrivals = chain.gather(lambda index: region(2 * index + xi, h, None))
    mine = next(arrivals)
    yield None
    blocks, near, far, core = [], {}, {}, []

    def send(a, b, half, peer, held):
        return wire.copy(region(a, b, half), region(a, b, half), peer, held, held)

    def one(i):
        held, index = next(arrivals) if i else mine
        a = 2 * index + xi
        blocks.append((held, a))
        near[0, i] = send(a, h, 0, g.x, held)
        near[1, i] = send(a, h, 1, g.y, held)
        far[0, i, 0] = send(a, h, 0, g.y, held)
        far[1, i, 0] = send(a, h, 1, g.x, held)
        core.append(send(a, h, None, g.core, held))

    def two(i):
        held, a = blocks[i]
        near[0, i].wait_recv()
        far[0, i, 1] = send(a ^ 1, h, 0, g.y, held)
        core.append(send(a ^ 1, h, 0, g.core, held))
        near[1, i].wait_recv()
        far[1, i, 1] = send(a, h ^ 2, 1, g.x, held)
        core.append(send(a, h ^ 2, 1, g.core, held))

    def three(i):
        held, a = blocks[i]
        far[0, i, 0].wait_recv()
        core.append(send(a, h ^ 2, 0, g.core, held))
        far[1, i, 0].wait_recv()
        core.append(send(a ^ 1, h, 1, g.core, held))

    def four(i):
        held, a = blocks[i]
        far[0, i, 1].wait_recv()
        core.append(send(a ^ 1, h ^ 2, 0, g.core, held))
        far[1, i, 1].wait_recv()
        core.append(send(a ^ 1, h ^ 2, 1, g.core, held))

    count = 2 * z.Z - 1
    stages = (one, two, three, four)
    for turn in range(count + 6):
        for lag, stage in enumerate(stages):
            if 0 <= turn - 2 * lag < count:
                stage(turn - 2 * lag)
        yield turn
    for item in core:
        item.wait_recv()


def gather_copies(z):
    return 2 * (z.Z - 1) + 13 * (2 * z.Z - 1)


class SumAll:
    def __init__(self, wire, z, g, region, bufs):
        self.wire, self.zz, self.g, self.region = wire, z, g, region
        self.from_core, self.hop1, self.hop2, self.up, self.down, self.own = bufs
        self.chain = Chain(wire, z.Z, g.s, g.h)
        self.flight = {}
        self.base = wire.count
        wire.count += self.copies(z)

    @staticmethod
    def copies(z):
        return z.Z * (4 + 4 + 2) + 4 * z.Z

    @staticmethod
    def scratch(z, rows, lanes):
        half = rows // 2
        return [
            VM((z.Z, 4, rows, lanes), BF16),
            VM((z.Z, 4, half, lanes), BF16),
            VM((z.Z, 2, half, lanes), BF16),
            VM((z.Z, 2, half, lanes), BF16),
            VM((z.Z, 2, half, lanes), BF16),
            VM((2, half, lanes), F32),
        ]

    def put(self, a, b, half, dst, peer, slot):
        kept, self.wire.count = self.wire.count, self.base + slot
        item = self.wire.copy(self.region(a, b, half), dst, peer)
        self.wire.count = kept
        return item

    def add(self, a, b, half, got):
        spot = self.region(a, b, half)
        spot[...] = (spot[...].astype(F32) + got[...].astype(F32)).astype(BF16)

    def core(self, i, d):
        g = self.g
        for k in range(4):
            a, b = (2 * d + g.s % 2) ^ (k // 2), g.h ^ 1 ^ (2 * (k % 2))
            self.flight["core", i, k] = self.put(
                a, b, None, self.from_core.at[d, k], g.core, 10 * i + k
            )

    def first(self, i, d):
        g = self.g
        rows = self.hop1.shape[2]
        for k in (1, 3, 2, 0):
            self.flight["core", i, k].wait_recv()
            a, b = (2 * d + g.s % 2) ^ (k // 2), g.h ^ (2 * (k % 2))
            for half in range(2):
                self.add(a, b, half, self.from_core.at[d, k, pl.ds(half * rows, rows), :])
            if k % 2:
                key = k // 2
                self.flight["one", i, key] = self.put(
                    a, b, 0, self.hop1.at[d, key], g.y, 10 * i + 4 + key
                )
            if k // 2:
                key = 2 + k % 2
                self.flight["one", i, key] = self.put(
                    a, b, 1, self.hop1.at[d, key], g.x, 10 * i + 4 + key
                )

    def second(self, i, d):
        g = self.g
        a = 2 * d + g.s % 2
        for key in (1, 0):
            self.flight["one", i, key].wait_recv()
            self.add(a ^ key, g.h, 0, self.hop1.at[d, key])
        self.flight["two", i, 0] = self.put(
            a ^ 1, g.h, 0, self.hop2.at[d, 0], g.x, 10 * i + 8
        )
        for key in (3, 2):
            self.flight["one", i, key].wait_recv()
            self.add(a, g.h ^ (2 * (key - 2)), 1, self.hop1.at[d, key])
        self.flight["two", i, 1] = self.put(
            a, g.h ^ 2, 1, self.hop2.at[d, 1], g.y, 10 * i + 9
        )

    def third(self, i, d):
        g, chain = self.g, self.chain
        a, count = 2 * d + g.s % 2, self.zz.Z
        below, above = chain.between(d)
        for half in range(2):
            self.flight["two", i, half].wait_recv()
            self.add(a, g.h, half, self.hop2.at[d, half])
            kept = self.wire.count
            self.wire.count = self.base + 10 * count + 2 * count * half
            ups, downs = chain.passes(
                d, self.region(a, g.h, half), self.up.at[d, half], self.down.at[d, half]
            )
            self.wire.count = kept
            self.flight["z", i, half] = d, ups, downs
            when(below, self.taken(ups, a, half, self.up.at[d, half]))
            when(above, self.taken(downs, a, half, self.down.at[d, half]))
            ups.start()
            downs.start()

    def taken(self, item, a, half, got):
        def action():
            item.arrived()
            self.add(a, self.g.h, half, got)
        return action

    def finish(self, half):
        g = self.g
        own = self.own.at[half]
        own[...] = self.region(g.s, g.h, half)[...].astype(F32)

        def add(item, got):
            def action():
                item.arrived()
                own[...] = own[...] + got[...].astype(F32)
            return action

        for i in range(self.zz.Z):
            d, ups, downs = self.flight["z", i, half]
            below, above = self.chain.ends(d)
            when(below, add(ups, self.up.at[d, half]))
            when(above, add(downs, self.down.at[d, half]))
        return own[...]

    def run(self, produce):
        order = self.chain.order()
        steps = [
            lambda i, d: (produce(d), self.core(i, d)),
            self.first,
            self.second,
            self.third,
        ]
        count = len(order)
        for turn in range(count + len(steps) - 1):
            for stage in range(len(steps)):
                if 0 <= turn - stage < count:
                    steps[stage](turn - stage, order[turn - stage])
                    yield turn


def halves(ref, rows, row_count, lanes, lane_count, half):
    if half is not None:
        row_count //= 2
        rows = rows + half * row_count
    return at(ref, rows, row_count, lanes, lane_count)


def region_of(z, ref):
    return lambda a, b, half: halves(
        ref, a // 2 * 2 * z.Ds, 2 * z.Ds, (2 * b + a % 2) * z.R, z.R, half
    )


FRONT_RESULTS = 27


def front_kernel(
    z, tok, gain1, gain2, xw, yw, ow, conv_w, conv_b, a_b, i_b, decay, aw, iw, cot_in,
    gw_in, uw_in, dw_in, *rest
):
    outs, rest = rest[:FRONT_RESULTS], rest[FRONT_RESULTS:]
    held, rest = rest[:FRONT_RESULTS], rest[FRONT_RESULTS:]
    (
        xw2, yw2, ow2, tok2, fn2, rn, yb, pad, conv, a_o, i_o, st, entry_o, mix, res,
        vec, mask, spread, gain_q, hid, dw, uwg_o, dwg_o, gsum_o, bg_o, back_g, back_u,
    ) = held
    (
        turned, fnt, stash, x1, x2, x3, x4, x5, y1, y2, y3, y4, y5, sums, tot, part, got, edge, gains,
        cot, gw, uw, xt, gwt, uwt, dwt, gwg, hg, gg, ug, gs, us, rs, wide,
        c1, c2, c3, c4, c5, c6, stat, send, recv, own_sem, out_sem,
    ) = rest
    leaving = []

    def flush(first, last):
        for index in range(first, last):
            copy = pltpu.make_async_copy(held[index], outs[index], out_sem.at[index])
            copy.start()
            leaving.append(copy)

    s, h = place()
    S, H, R, D, T, Ds, C, Z = z.S, z.H, z.R, z.D, z.T, z.Ds, z.C, z.Z
    DG = 2 * Ds
    Q = DG // H
    zi, xi = s // 2, s % 2
    after, before = lax.rem(s + 1, S), lax.rem(s + S - 1, S)
    greet(
        [(s ^ k, h) for k in range(1, S)]
        + [(s, h ^ j) for j in range(1, H)]
        + [(after, h), (before, h)]
    )
    wire = Wire(send, recv)
    g = Grid(s, h)
    chain = Chain(wire, Z, s, h)
    deal = Deal(wire, z, s, h)
    pairs = ((gw_in, gw), (uw_in, uw), (dw_in, dw))
    dealing = deal.steps(deal.out, pairs)
    advance(dealing)
    half = pl.ds(pl.multiple_of(xi * Ds, EDGE), Ds)
    twins = [wire.copy(xw, xw2.at[half, :], (s ^ 1, h))]
    turned[...] = tok[...].astype(F32).T.astype(BF16)
    quarter = pl.ds(pl.multiple_of(h * Q, EDGE), Q)
    my_lanes = pl.ds(pl.multiple_of(zi * R, LANES), R)

    def group(index):
        return pl.ds(pl.multiple_of(index * DG + h * Q, EDGE), Q)

    first = [
        wire.copy(turned.at[group(zi ^ kz), :], tok2.at[quarter, my_lanes], (s ^ (2 * kz), h))
        for kz in range(1, Z)
    ]
    column = turned[...].astype(F32)
    mean = jnp.sum(column * column, axis=0, keepdims=True) / z.D
    rn[zi] = jnp.broadcast_to(lax.rsqrt(mean + EPSILON), (8, R))
    for kz in range(1, Z):
        first.append(wire.copy(rn.at[zi], rn.at[zi], (s ^ (2 * kz), h)))
    tok2[quarter, my_lanes] = turned[group(zi), :]
    vec[...] = jnp.zeros_like(vec)
    vec[0:CONV, :] = conv_w[...].astype(F32)
    for index, ref in enumerate((conv_b, a_b, i_b)):
        vec[4 + index : 5 + index, :] = ref[...].astype(F32)[None, :]
    vec[7:8, :] = softplus(decay[...][None, :])
    vec[8:9, :] = jax.nn.sigmoid(decay[...][None, :])
    eight = lax.broadcasted_iota(jnp.int32, (8, D), 0)
    gains[...] = jnp.where(
        eight == 0, gain1[...].astype(F32)[None, :], gain2[...].astype(F32)[None, :]
    ).T
    gain_q[...] = gains[pl.ds(pl.multiple_of(zi * DG + h * Q, EDGE), Q), :]
    gain_s = gains[pl.ds(pl.multiple_of(zi * DG, EDGE), DG), 0:1]
    head_maps(z, spread, mask)
    xw2[half, :] = xw[...]
    yw2[half, :] = yw[...]
    ow2[half, :] = ow[...]
    pending = [
        own_block(z, src, dst, own_sem.at[pl.ds(2 * i, 2)], s)
        for i, (src, dst) in enumerate(pairs)
    ]
    W = z.D // H

    def corner(a, b, half):
        return halves(cot, a * R, R, b * W, W, half)

    corner(s, h, None)[...] = cot_in[:, pl.ds(pl.multiple_of(h * W, LANES), W)]
    cot_in_all = gather_all(wire, z, g, corner)
    advance(cot_in_all)
    advance(dealing, 2)
    for item in first:
        item.wait_recv()
    HeadGather(
        wire, s, h, lambda j: tok2.at[pl.ds(pl.multiple_of(j * Q, EDGE), Q), :]
    ).wait_all()
    for b in range(Z):
        cut = slice(b * R, b * R + R)
        fn2[:, cut] = (tok2[:, cut].astype(F32) * rn[b, 0:1, :] * gain_s).astype(BF16)
    twins[0].wait_recv()
    for src, dst in ((yw, yw2), (ow, ow2)):
        twins.append(wire.copy(src, dst.at[half, :], (s ^ 1, h)))

    def x_part(d):
        lanes = pl.ds(pl.multiple_of(d * R, LANES), R)
        fnt[d] = fn2[:, lanes].astype(F32).T.astype(BF16)
        return mm(fnt[d], xw2[...])

    x_sum = scatter_halves(chain, z, x_part, stash, (x1, x2, x3, x4, x5))
    for _ in range(Z):
        for step in x_sum:
            advance(step)
    advance(cot_in_all, 1)
    advance(dealing, 0)
    drain(*x_sum)
    x_low = x5[...].astype(BF16)
    edge[0] = x_low[R - EDGE : R, :]
    halo = wire.copy(edge.at[0], edge.at[1], (after, h))
    twins[1].wait_recv()
    y_sum = chain.scatter(lambda d: mm(fnt[d], yw2[...]), y1, y2, y3, y4, y5)
    advance(y_sum, 1)
    advance(dealing, 1)
    advance(cot_in_all, 2)
    pad[pl.ds(EDGE, R), :] = x_low.astype(F32)
    halo.wait_recv()
    pad[pl.ds(0, EDGE), :] = jnp.where(s == 0, 0.0, edge[1].astype(F32))
    out = jnp.broadcast_to(vec[4:5, :], (R, C))
    for lag in range(CONV):
        out = out + vec[lag : lag + 1, :] * pad[pl.ds(EDGE - lag, R), :]
    conv[h] = out.astype(BF16)
    across = HeadGather(wire, s, h, lambda j: conv.at[j])
    advance(dealing, 1)
    advance(cot_in_all, 2)
    advance(y_sum, 1)
    a_pre = jnp.broadcast_to(vec[5:6, :], (R, C))
    i_pre = jnp.broadcast_to(vec[6:7, :], (R, C))
    for j in (0, 2, 1, 3):
        if j:
            across.wait(j)
        k = h ^ j
        taken = conv[k]
        a_pre = a_pre + mm(taken, gate_weight_of(z, spread, mask, aw, k))
        i_pre = i_pre + mm(taken, gate_weight_of(z, spread, mask, iw, k))
    advance(y_sum, 1)
    a_o[...] = a_pre
    i_o[...] = i_pre
    anchor = anchor_of(z, s, LANES)
    sums[s] = jnp.zeros((8, C), F32)
    for b in range(C // LANES):
        cut = pl.ds(b * LANES, LANES)
        recall, input_gate, factor, one_minus, root_value, root_scale = decay_terms(
            a_o[:, cut], i_o[:, cut], vec[7:8, cut], anchor
        )
        driven = conv[h, :, cut].astype(F32) * input_gate * root_scale
        prod, value = scan_rows(factor, driven, 1)
        st[:, cut] = value
        tot[:, cut] = prod
        sums[s, 0:1, cut] = prod[R - 1 : R, :]
        sums[s, 1:2, cut] = value[R - 1 : R, :]
    ends = [wire.copy(sums.at[s], sums.at[s], (s ^ k, h)) for k in range(1, S)]
    advance(dealing, 0)
    advance(cot_in_all, 2)
    drain(y_sum)
    yb[...] = y5[...]
    for item in ends:
        item.wait_recv()
    entry = jnp.zeros((1, C), F32)
    for j in range(S - 1):
        entry = jnp.where(j < s, sums[j, 0:1, :] * entry + sums[j, 1:2, :], entry)
    entry_o[...] = jnp.broadcast_to(entry, (8, C))
    my_rows = pl.ds(pl.multiple_of(zi * R, EDGE), R)
    for b in range(C // LANES):
        cut = pl.ds(b * LANES, LANES)
        state = st[:, cut] + tot[:, cut] * entry_o[0:1, cut]
        st[:, cut] = state
        mix[my_rows, cut] = (state * gelu_pair(yb[:, cut])[0]).astype(BF16)
    arriving = [chain.gather(row_blocks(z, mix, part_of)) for part_of in range(2)]
    for step in arriving:
        advance(step)
    advance(dealing, 1)
    advance(cot_in_all, 3)
    drain(*arriving)
    twins[2].wait_recv()

    def out_part(j):
        rows = pl.ds(pl.multiple_of((h ^ j) * R, EDGE), R)
        return mm(ow2[...], mix[rows, :], NT)

    whole = head_scatter(wire, s, h, out_part, part, got)
    advance(dealing, 2)
    advance(cot_in_all, 3)
    res[...] = whole() + tok2[:, pl.ds(pl.multiple_of(h * R, LANES), R)].astype(F32)


    flush(0, 19)
    tile = 256
    region_of(z, xt)(s, h, None)[...] = res[...].astype(BF16)
    spreading = gather_all(wire, z, g, region_of(z, xt))
    advance(spreading, 2)
    def turn(src, dst, scaled):
        for n in range(D // tile):
            cut = slice(n * tile, n * tile + tile)
            piece = src[cut, :].astype(F32)
            dst[:, cut] = (piece * gains[cut, 1:2] if scaled else piece).T.astype(BF16)

    advance(spreading, 3)
    advance(dealing, 2)
    advance(spreading, 2)
    advance(dealing, 2)
    drain(spreading, dealing, cot_in_all)
    for wait in pending:
        wait()
    posted, deal.sent = deal.sent, []
    count = len(posted) // 3
    deal.wait(posted[: 2 * count])
    turn(gw, gwt, True)
    turn(uw, uwt, True)
    for n in range(T // tile):
        cut = slice(n * tile, n * tile + tile)
        square = jnp.zeros((1, tile), F32)
        for b in range(D // tile):
            piece = xt[b * tile : b * tile + tile, cut].astype(F32)
            square = square + jnp.sum(piece * piece, axis=0, keepdims=True)
        rs[:, cut] = jnp.broadcast_to(lax.rsqrt(square / D + EPSILON), (8, tile))
    deal.wait(posted[2 * count :])
    turn(dw, dwt, False)
    for n in range(T // tile):
        cut = slice(n * tile, n * tile + tile)
        hg[:, cut] = mm(dwt[...], cot[cut, :], NT)
        scale = rs[0:1, cut]
        gate = mm(gwt[...], xt[:, cut]) * scale
        up = mm(uwt[...], xt[:, cut]) * scale
        act, slope = gelu_pair(gate)
        hid[:, cut] = (act * up).astype(BF16)
        back = hg[:, cut]
        gate_grad = back * up * slope
        up_grad = back * act
        gg[:, cut] = gate_grad.astype(BF16)
        ug[:, cut] = up_grad.astype(BF16)
        gs[:, cut] = (gate_grad * scale).astype(BF16)
        us[:, cut] = (up_grad * scale).astype(BF16)
    second = SumAll(wire, z, g, region_of(z, wide), (c1, c2, c3, c4, c5, c6))

    def produce(d):
        rows = pl.ds(pl.multiple_of(d * DG, LANES), DG)
        wide[rows, :] = (mm(gw[rows, :], gg[...]) + mm(uw[rows, :], ug[...])).astype(BF16)

    summing = second.run(produce)
    advance(summing, 3)
    flush(19, 21)
    for n in range(D // tile):
        cut = slice(n * tile, n * tile + tile)
        gwg[cut, :] = (mm(xt[cut, :], gs[...], NT) * gains[cut, 1:2]).astype(BF16)
    dealing = deal.steps(deal.back, ((gwg, back_g),))
    advance(dealing, 3)
    deal.back_own(gwg, back_g)
    advance(summing, 6)
    advance(dealing, 1)
    drain(summing)
    for n in range(D // tile):
        cut = slice(n * tile, n * tile + tile)
        uwg_o[cut, :] = (mm(xt[cut, :], us[...], NT) * gains[cut, 1:2]).astype(BF16)
        dwg_o[cut, :] = mm(hid[...], cot[:, cut]).T.astype(BF16)
    flush(21, 23)
    rising = deal.steps(deal.back, ((uwg_o, back_u),))
    second_grad = jnp.concatenate([second.finish(0), second.finish(1)], axis=0)
    mine = pl.ds(pl.multiple_of((2 * h + xi) * R, LANES), R)
    group = pl.ds(pl.multiple_of(zi * DG, LANES), DG)
    scale = rs[0:1, mine]
    residual = res[...]
    gsum_o[...] = second_grad * residual * scale
    weighted = gains[group, 1:2] * second_grad
    stat[zi] = jnp.broadcast_to(jnp.sum(weighted * residual, axis=0, keepdims=True), (8, R))
    ends = [wire.copy(stat.at[zi], stat.at[zi], g.z(kz)) for kz in range(1, z.Z)]
    direct = cot[mine, group].astype(F32).T + scale * weighted
    for item in ends:
        item.wait_recv()
    advance(rising, 3)
    mean = jnp.sum(stat[:, 0:1, :], axis=0) / D
    grad = direct - residual * (scale * scale * scale * mean)
    lanes = pl.ds(pl.multiple_of(h * R, LANES), R)
    bg_o[:, lanes] = grad.astype(BF16)
    HeadGather(
        wire, s, h, lambda j: bg_o.at[:, pl.ds(pl.multiple_of(j * R, LANES), R)]
    ).wait_all()
    flush(23, 25)
    deal.wait()
    flush(25, 27)
    wire.close()
    for copy in leaving:
        copy.wait()


def front(z, *args):
    S, H, R, D, T, U, Ds, C, Z = z.S, z.H, z.R, z.D, z.T, z.U, z.Ds, z.C, z.Z
    DG, TX = 2 * Ds, Z * R
    copies = 2 + 2 * (Z - 1) + (H - 1) + 1 + 6 * Z + 1 + (H - 1) + (S - 1)
    copies += 4 * (Z - 1) + (H - 1) + 8 * (S - 1) + 12 + 2 * gather_copies(z)
    copies += SumAll.copies(z) + (Z - 1) + (H - 1)
    results = [
        sds((DG, C), BF16),
        sds((DG, C), BF16),
        sds((DG, C), BF16),
        sds((DG, TX), BF16),
        sds((DG, TX), BF16),
        sds((Z, 8, R), F32),
        sds((R, C), F32),
        sds((EDGE + R, C), F32),
        sds((H, R, C), BF16),
        sds((R, C), F32),
        sds((R, C), F32),
        sds((R, C), F32),
        sds((8, C), F32),
        sds((TX, C), BF16),
        sds((DG, R), F32),
        sds((EDGE, C), F32),
        sds((C, C), BF16),
        sds((C, z.NI), BF16),
        sds((DG // H, 8), F32),
        sds((U, T), BF16),
        sds((D, U), BF16),
        sds((D, U), BF16),
        sds((D, U), BF16),
        sds((DG, R), F32),
        sds((DG, TX), BF16),
        sds((Ds, z.F2), BF16),
        sds((Ds, z.F2), BF16),
    ]
    return call(
        functools.partial(front_kernel, z),
        "front",
        1,
        results,
        [VM(item.shape, item.dtype) for item in results]
        + [
            VM((D, R), BF16),
            VM((Z, R, DG), BF16),
            VM((R // 2, C), F32),
            *chain_scratch(z, R, C),
            *chain_scratch(z, R, C),
            VM((S, 8, C), F32),
            VM((R, C), F32),
            VM((H, DG, R), BF16),
            VM((H, DG, R), BF16),
            VM((2, EDGE, C), BF16),
            VM((D, 8), F32),
            VM((T, D), BF16),
            VM((D, U), BF16),
            VM((D, U), BF16),
            VM((D, T), BF16),
            VM((U, D), BF16),
            VM((U, D), BF16),
            VM((U, D), BF16),
            VM((D, U), BF16),
            VM((U, T), F32),
            VM((U, T), BF16),
            VM((U, T), BF16),
            VM((U, T), BF16),
            VM((U, T), BF16),
            VM((8, T), F32),
            VM((D, T), BF16),
            *SumAll.scratch(z, DG, R),
            VM((Z, 8, R), F32),
            sem(copies),
            sem(copies),
            sem(6),
            sem(len(results)),
        ],
        args,
        (14, 15, 16),
        True,
    )


def exact(left, right, dims):
    return lax.dot_general(
        left, right, dims, precision=lax.Precision.HIGHEST, preferred_element_type=F32
    )


def back_kernel(
    z, far, held, fetch_sem, leave, mixed_o, owg_o, xwg_o, ywg_o, twin_r, full, gains2, smallg, vec_o, back_u, back_d,
    stash, g1, g2, g3, g4, own, adj, tot, ag, ig, sums, late, cgr, cgs, ext, gx, gy, part, got, stat, stat2,
    tgq, prod, prod2, gains, small, smallx, small_z, vecs, twin_s, mpart, m1, m2, m3, m4, m5, m6, send, recv,
):
    (
        bg, ow2, hid, dw, res, mix, yb, vec, a_pre, i_pre, st, entry, conv, pad, aw, iw, spread,
        mask, xw2, yw2, fn2, tok2, rn, gain, msum, uwg, dwg,
    ) = held
    fetch = [
        pltpu.make_async_copy(src, dst, fetch_sem.at[index])
        for index, (src, dst) in enumerate(zip(far, held))
    ]
    begun = pltpu.make_async_copy(far[-1], back_u, fetch_sem.at[len(held)])
    begun.start()
    for copy in fetch:
        copy.start()
    begun.wait()
    s, h = place()
    g = Grid(s, h)
    S, H, R, D, Ds, C, Z, T = z.S, z.H, z.R, z.D, z.Ds, z.C, z.Z, z.T
    DG, W = 2 * Ds, D // H
    Q = DG // H
    zi, xi = s // 2, s % 2
    after, before = lax.rem(s + 1, S), lax.rem(s + S - 1, S)
    greet(
        [(s ^ k, h) for k in range(1, S)]
        + [(s, h ^ j) for j in range(1, H)]
        + [(after, h), (before, h)]
    )
    wire = Wire(send, recv)
    chain = Chain(wire, Z, s, h)
    deal = Deal(wire, z, s, h)
    dealing = deal.steps(deal.back, ((uwg, back_u), (dwg, back_d)), 3)
    my_rows = pl.ds(pl.multiple_of(zi * R, EDGE), R)
    half = pl.ds(pl.multiple_of(xi * Ds, EDGE), Ds)
    other = pl.ds(pl.multiple_of((1 - xi) * Ds, EDGE), Ds)

    def corner(a, b, part_of):
        return halves(mpart, b * W, W, a * R, R, part_of)

    mixed = SumAll(wire, z, g, corner, (m1, m2, m3, m4, m5, m6))

    def produce_mixed(d):
        cut = pl.ds(pl.multiple_of(d * 2 * R, LANES), 2 * R)
        mpart[:, cut] = mm(dw[...], hid[:, cut]).astype(BF16)

        @pl.when(h == d)
        def _():
            spot = region_of(z, mpart)(s, h, None)
            spot[...] = (spot[...].astype(F32) + res[...]).astype(BF16)

    mixing = mixed.run(produce_mixed)

    def block(d):
        lanes = pl.ds(pl.multiple_of(d * R, LANES), R)
        return mm(bg[:, lanes].astype(F32).T.astype(BF16), ow2[...])

    for copy in fetch[:5]:
        copy.wait()
    summing = scatter_halves(chain, z, block, stash, (g1, g2, g3, g4, own))
    for _ in range(Z):
        for step in summing:
            advance(step)
        advance(mixing, 2)
    for copy in fetch[5:]:
        copy.wait()
    drain(*summing)
    row = lax.broadcasted_iota(jnp.int32, (R, LANES), 0)
    anchor = anchor_of(z, s, LANES)
    sums[s] = jnp.zeros((8, C), F32)
    for b in range(C // LANES):
        cut = pl.ds(b * LANES, LANES)
        grad = own[:, cut]
        gate, slope = gelu_pair(yb[:, cut])
        gy[my_rows, cut] = (grad * st[:, cut] * slope).astype(BF16)
        factor = jnp.exp(-8.0 * jax.nn.sigmoid(a_pre[:, cut]) * vec[7:8, cut])
        ahead = shifted(factor, -1, 1.0, row)
        prods, value = scan_rows(ahead, grad * gate, -1)
        tot[:, cut] = prods
        adj[:, cut] = value
        sums[s, 0:1, cut] = factor[0:1, :] * prods[0:1, :]
        sums[s, 1:2, cut] = factor[0:1, :] * value[0:1, :]
    ends = [wire.copy(sums.at[s], sums.at[s], (s ^ k, h)) for k in range(1, S)]
    y_rows = chain.gather(row_blocks(z, gy))
    advance(y_rows)
    advance(dealing, 0)
    twins = []

    def weight_grad(index, left, right, out):
        prod2[...] = mm(left[...], right[...])
        twin_s[index] = prod2[other, :].astype(BF16)
        twins.append(wire.copy(twin_s.at[index], twin_r.at[index], g.x))
        out[...] = prod2[half, :]

    weight_grad(0, bg, mix, owg_o)
    leave(1)
    advance(mixing, 2)
    for item in ends:
        item.wait_recv()
    carry = jnp.zeros((1, C), F32)
    for j in range(S - 1, 0, -1):
        carry = jnp.where(j > s, sums[j, 0:1, :] * carry + sums[j, 1:2, :], carry)
    vec_o[...] = jnp.zeros_like(vec_o)
    late[...] = jnp.broadcast_to(carry, (8, C))
    for b in range(C // LANES):
        cut = pl.ds(b * LANES, LANES)
        adjoint = adj[:, cut] + tot[:, cut] * late[0:1, cut]
        rate = vec[7:8, cut]
        recall, input_gate, factor, one_minus, root_value, root_scale = decay_terms(
            a_pre[:, cut], i_pre[:, cut], rate, anchor
        )
        taken = conv[h, :, cut].astype(F32)
        state = st[:, cut]
        earlier = jnp.where(row == 0, entry[0:1, cut], shifted(state, 1, 0.0, row))
        live = jnp.logical_and(one_minus > SQUARE_FLOOR, jnp.logical_not(anchor))
        scale_grad = adjoint * taken * input_gate
        log_grad = adjoint * earlier * factor - jnp.where(
            live, scale_grad * factor * factor / root_value, 0.0
        )
        a_grad = (log_grad * (-8.0 * rate) * recall * (1.0 - recall)).astype(BF16)
        i_grad = (scale_grad * root_scale * (1.0 - input_gate)).astype(BF16)
        ag[:, cut] = a_grad
        ig[:, cut] = i_grad
        decay_sum = jnp.sum(log_grad * (-8.0 * recall), axis=0, keepdims=True)
        vec_o[5:6, cut] = jnp.sum(a_grad.astype(F32), axis=0, keepdims=True)
        vec_o[6:7, cut] = jnp.sum(i_grad.astype(F32), axis=0, keepdims=True)
        vec_o[7:8, cut] = decay_sum * vec[8:9, cut]
        ext[pl.ds(0, R), cut] = adjoint * input_gate * root_scale

    eighth = small.shape[0] // S

    def share(x_index, z_index, count):
        start = (x_index * Z + z_index) * eighth
        return pl.ds(pl.multiple_of(start, EDGE), count * eighth)

    def sum_small():
        mine = share(xi, 0, Z)
        item = wire.copy(small.at[share(1 - xi, 0, Z), :], smallx, g.x)
        yield
        item.wait_recv()
        smallx[...] = (smallx[...].astype(F32) + small[mine, :].astype(F32)).astype(BF16)

        def piece(index):
            return pl.ds(pl.multiple_of(index * eighth, EDGE), eighth)

        items = [
            wire.copy(smallx.at[piece(zi ^ kz), :], small_z.at[kz], g.z(kz))
            for kz in range(1, Z)
        ]
        yield
        total = smallx[piece(zi), :].astype(F32)
        for kz in range(1, Z):
            items[kz - 1].wait_recv()
            total = total + small_z[kz].astype(F32)
        spot = smallg.at[share(xi, zi, 1), :]
        spot[...] = total.astype(BF16)
        items = [wire.copy(spot, spot, g.z(kz)) for kz in range(1, Z)]
        yield
        for item in items:
            item.wait_recv()
        item = wire.copy(smallg.at[mine, :], smallg.at[mine, :], g.x)
        yield
        item.wait_recv()

    smaller = sum_small()
    def gates_back(j):
        return mm(ag[...], gate_weight_of(z, spread, mask, aw, h ^ j), NT) + mm(
            ig[...], gate_weight_of(z, spread, mask, iw, h ^ j), NT
        )

    advance(y_rows, 2)
    across = head_scatter(wire, s, h, gates_back, cgs, cgr)
    advance(y_rows, 2)
    advance(dealing, 3)
    for k in range(H):
        turn = conv[k].astype(F32).T.astype(BF16)
        for spot, grad in ((0, ag), (z.HS, ig)):
            dense = mm(turn, grad[...]).astype(BF16) * mask[...]
            small[pl.ds(spot + k * z.NI, z.NI), :] = mm(spread[...], dense, TN).astype(BF16)
    advance(smaller)
    advance(mixing, 2)
    conv_grad = ext[pl.ds(0, R), :] + across()
    ext[pl.ds(0, R), :] = conv_grad
    halo = wire.copy(ext.at[pl.ds(0, 8), :], ext.at[pl.ds(R, 8), :], (before, h))
    for lag in range(CONV):
        vec_o[lag : lag + 1, :] = jnp.sum(
            conv_grad * pad[pl.ds(EDGE - lag, R), :], axis=0, keepdims=True
        )
    vec_o[4:5, :] = jnp.sum(conv_grad, axis=0, keepdims=True)
    vecs[s] = vec_o[...]
    advance(mixing, 1)
    advance(smaller)
    halo.wait_recv()
    ext[pl.ds(R, 8), :] = jnp.where(s == S - 1, 0.0, ext[pl.ds(R, 8), :])
    grad = jnp.zeros((R, C), F32)
    for lag in range(CONV):
        grad = grad + vec[lag : lag + 1, :] * ext[pl.ds(lag, R), :]
    gx[my_rows, :] = grad.astype(BF16)
    rows_in = [chain.gather(row_blocks(z, gx, part_of)) for part_of in range(2)]
    for step in rows_in:
        advance(step)
    advance(dealing, 0)
    advance(mixing, 1)
    pair = grad.astype(BF16).astype(F32) * pad[pl.ds(EDGE, R), :] + gy[my_rows, :].astype(F32) * yb[...]
    stat[h] = exact(jnp.ones((8, C), F32), pair, NT)
    stats = [wire.copy(stat.at[h], stat.at[h], (s, h ^ j)) for j in range(1, H)]

    lesser = [wire.copy(vecs.at[s], vecs.at[s], (s ^ k, h)) for k in range(1, S)]
    drain(y_rows)
    weight_grad(1, fn2, gy, ywg_o)
    leave(3)
    prod[...] = mm(yw2[...], gy[...], NT)
    for item in stats:
        item.wait_recv()
    stat2[zi] = stat[0] + stat[1] + stat[2] + stat[3]
    stats = [wire.copy(stat2.at[zi], stat2.at[zi], g.z(kz)) for kz in range(1, Z)]
    advance(smaller)
    advance(mixing, 1)
    drain(*rows_in)

    prod[...] = prod[...] + mm(xw2[...], gx[...], NT)

    def quarter_of(j):
        return prod[pl.ds(pl.multiple_of((h ^ j) * Q, EDGE), Q), :]

    heads = head_scatter(wire, s, h, quarter_of, part, got)
    advance(dealing, 3)
    advance(smaller)
    advance(mixing, 1)
    quarter = pl.ds(pl.multiple_of(h * Q, EDGE), Q)
    weight_grad(2, fn2, gx, xwg_o)
    leave(2)
    total = heads()
    for item in stats:
        item.wait_recv()
    token = tok2[quarter, :].astype(F32)
    norm = jnp.concatenate([rn[b, 0:1, :] for b in range(Z)], axis=1)
    mean = jnp.concatenate([stat2[b, 0:1, :] for b in range(Z)], axis=1) / (norm * D)
    weighted = gain[:, 0:1] * total
    grad = bg[quarter, :].astype(F32) + norm * weighted - token * (norm * norm * norm * mean)
    tgq[...] = grad.astype(BF16)

    def spot(z_index, head):
        return full.at[pl.ds(pl.multiple_of(z_index * DG + head * Q, EDGE), Q), :]

    outs = [
        wire.copy(
            tgq.at[:, pl.ds(pl.multiple_of((zi ^ kz) * R, LANES), R)], spot(zi, h), g.z(kz)
        )
        for kz in range(1, Z)
    ]
    spot(zi, h)[...] = tgq[:, pl.ds(pl.multiple_of(zi * R, LANES), R)]
    prod[...] = jnp.zeros_like(prod)
    prod[quarter, :] = total * token * norm
    ones = jnp.ones((8, Z * R), F32)
    picked = lax.broadcasted_iota(jnp.int32, (8, DG), 0)
    gains[h] = jnp.where(
        picked == 0, exact(jnp.ones((8, R), F32), msum[...], NT), exact(ones, prod[...], NT)
    )
    tally = [wire.copy(gains.at[h], gains.at[h], (s, h ^ j)) for j in range(1, H)]
    finals = []
    drain(dealing)
    for kz in range(Z):
        if kz:
            outs[kz - 1].wait_recv()
        finals.append(HeadGather(wire, s, h, lambda j, kz=kz: spot(zi ^ kz, j)))
    for item in tally:
        item.wait_recv()
    gains2[s] = gains[0] + gains[1] + gains[2] + gains[3]
    tally = [wire.copy(gains2.at[s], gains2.at[s], (s ^ k, h)) for k in range(1, S)]
    drain(mixing)
    for part_of in range(2):
        mixed_o[pl.ds(part_of * W // 2, W // 2), :] = mixed.finish(part_of)
    for item in lesser:
        item.wait_recv()
    vec_o[...] = jnp.sum(vecs[...], axis=0)
    for item in twins:
        item.wait_recv()
    leave(0, 4, 8)
    deal.back_own(uwg, back_u)
    deal.back_own(dwg, back_d)
    drain(smaller)
    for item in tally:
        item.wait_recv()
    leave(6, 7)
    for item in finals:
        item.wait_all()
    leave(5)
    deal.wait()
    leave(9, 10)
    wire.close()


def back(z, *args):
    S, H, R, D, Ds, C, Z, T = z.S, z.H, z.R, z.D, z.Ds, z.C, z.Z, z.T
    DG, W = 2 * Ds, D // H
    TX, Q = Z * R, DG // H
    copies = (
        4 * Z + (S - 1) + 3 + (H - 1) + 1 + 6 * (Z - 1) + (H - 1) + (Z - 1) + (S - 1)
        + 2 + 2 * (Z - 1) + 2 * (Z - 1) + 4 * (S - 1) + (H - 1) + (Z - 1) + (H - 1) + Z * (H - 1) + (S - 1)
        + SumAll.copies(z)
    )
    small = 2 * z.HS
    count = len(args)
    results_of = [
        sds((W, R), F32),
        sds((Ds, C), F32),
        sds((Ds, C), F32),
        sds((Ds, C), F32),
        sds((3, Ds, C), BF16),
        sds((D, R), BF16),
        sds((S, 8, DG), F32),
        sds((small, C), BF16),
        sds((8, C), F32),
        sds((Ds, z.F2), BF16),
        sds((Ds, z.F2), BF16),
    ]

    def body(*refs):
        far, rest = refs[:count], refs[count:]
        outs, held, rest = rest[:11], rest[11 : 10 + count], rest[10 + count :]
        kept, leave_sem, rest = rest[:11], rest[11], rest[12:]
        leaving = []

        def leave(*indexes):
            for index in indexes:
                copy = pltpu.make_async_copy(kept[index], outs[index], leave_sem.at[index])
                copy.start()
                leaving.append(copy)

        back_kernel(z, far, held, rest[0], leave, *kept, *rest[1:])
        for copy in leaving:
            copy.wait()

    return call(
        body,
        "back",
        2,
        results_of,
        [VM(a.shape, a.dtype) for a in list(args[:-1]) + results_of]
        + [sem(len(results_of))]
        + [sem(count)]
        + [
            VM((R // 2, C), F32),
            *chain_scratch(z, R, C),
            VM((R, C), F32),
            VM((R, C), F32),
            VM((R, C), BF16),
            VM((R, C), BF16),
            VM((S, 8, C), F32),
            VM((8, C), F32),
            VM((H, R, C), BF16),
            VM((H, R, C), BF16),
            VM((R + 8, C), F32),
            VM((TX, C), BF16),
            VM((TX, C), BF16),
            VM((H, Q, TX), BF16),
            VM((H, Q, TX), BF16),
            VM((H, 8, R), F32),
            VM((Z, 8, R), F32),
            VM((Q, TX), BF16),
            VM((DG, TX), F32),
            VM((DG, C), F32),
            VM((H, 8, DG), F32),
            VM((small, C), BF16),
            VM((small // 2, C), BF16),
            VM((Z, small // S, C), BF16),
            VM((S, 8, C), F32),
            VM((3, Ds, C), BF16),
            VM((D, T), BF16),
        ]
        + SumAll.scratch(z, W, R)
        + [sem(copies), sem(copies)],
        args,
        range(count),
        True,
    )


def results_kernel(z, *refs):
    sources, count = 12, 17
    inputs, outs = refs[:sources], refs[sources : sources + count]
    held = refs[sources + count : 2 * sources + count]
    stage = refs[2 * sources + count : 2 * (sources + count)]
    in_sem, out_sem = refs[-2:]
    fetch = {}
    for index in (4, 1, 2, 3, 9, 10, 11, 5, 0, 7, 8, 6):
        copy = pltpu.make_async_copy(inputs[index], held[index], in_sem.at[index])
        copy.start()
        fetch[index] = copy
    mixed, owg, xwg, ywg, twins, full, gains, small, vec, back_g, back_u, back_d = held
    copies = []

    def need(*indexes):
        for index in indexes:
            fetch[index].wait()

    def emit(index, value):
        stage[index][...] = value
        copy = pltpu.make_async_copy(stage[index], outs[index], out_sem.at[index])
        copy.start()
        copies.append(copy)

    need(4, 1, 2, 3)
    for index, slot, src in ((12, 0, owg), (4, 1, ywg), (3, 2, xwg)):
        emit(index, src[...] + twins[slot].astype(F32))
    for index, at_input, src in ((14, 9, back_g), (15, 10, back_u), (16, 11, back_d)):
        need(at_input)
        emit(index, src[...].astype(F32))
    need(5, 0, 7, 8, 6)
    emit(1, full[...].astype(F32).T)
    emit(0, mixed[...].T.astype(BF16))
    emit(7, small[0 : z.HS, :].astype(F32))
    emit(9, small[z.HS : 2 * z.HS, :].astype(F32))
    emit(5, vec[0:CONV, :])
    for index, row in ((6, 4), (8, 5), (10, 6), (11, 7)):
        outs[index][...] = vec[row, :]
    for index, row in ((2, 1), (13, 0)):
        sums = [gains[2 * b, row, :] + gains[2 * b + 1, row, :] for b in range(z.Z)]
        outs[index][...] = jnp.concatenate(sums)
    for copy in copies:
        copy.wait()


def results(z, *args):
    R, D, Ds, C, F2 = z.R, z.D, z.Ds, z.C, z.F2
    row = sds((C,), F32)
    outs = [
        sds((R, D // z.H), BF16),
        sds((R, D), F32),
        sds((D,), F32),
        sds((Ds, C), F32),
        sds((Ds, C), F32),
        sds((CONV, C), F32),
        row,
        sds((z.HS, C), F32),
        row,
        sds((z.HS, C), F32),
        row,
        row,
        sds((Ds, C), F32),
        sds((D,), F32),
        sds((Ds, F2), F32),
        sds((Ds, F2), F32),
        sds((Ds, F2), F32),
    ]
    return pl.pallas_call(
        functools.partial(results_kernel, z),
        out_shape=outs,
        in_specs=[pl.BlockSpec(memory_space=ANY)] * len(args),
        out_specs=[
            pl.BlockSpec(memory_space=VM if len(out.shape) == 1 else ANY) for out in outs
        ],
        scratch_shapes=[VM(a.shape, a.dtype) for a in list(args) + outs]
        + [sem(len(args)), sem(len(outs))],
        compiler_params=pltpu.CompilerParams(vmem_limit_bytes=62 << 20),
        name="results",
    )(*args)


def dealt(
    z,
    tokens,
    norm_gain,
    x_weight,
    y_weight,
    conv_weight,
    conv_bias,
    a_weight,
    a_bias,
    i_weight,
    i_bias,
    decay,
    out_weight,
    mlp_gain,
    gate_weight,
    up_weight,
    down_weight,
    cotangent,
):
    (
        xw2, yw2, ow2, tok2, fn2, rn, yb, pad, conv, a_pre, i_pre, st, entry, mix, res,
        vec, mask, spread, gain_q, hid, dc, uwg, dwg, msum, bg, back_g, up_part,
    ) = front(
        z, tokens, norm_gain, mlp_gain, x_weight, y_weight, out_weight, conv_weight, conv_bias,
        a_bias, i_bias, decay, a_weight, i_weight,
        cotangent, gate_weight, up_weight, down_weight,
    )
    mixed, owg, xwg, ywg, twins, tg, gains, small, vec_sum, back_u, back_d = back(
        z, bg, ow2, hid, dc, res, mix, yb, vec, a_pre, i_pre, st, entry, conv, pad, a_weight,
        i_weight, spread, mask, xw2, yw2, fn2, tok2, rn, gain_q, msum, uwg, dwg, up_part,
    )
    return tuple(
        results(z, mixed, owg, xwg, ywg, twins, tg, gains, small, vec_sum, back_g, back_u, back_d)
    )


def from_behind(x, axis, by):
    size = lax.axis_size(axis)
    pairs = [(i, i + by) for i in range(size) if 0 <= i + by < size]
    return lax.ppermute(x, axis, pairs)


def rms_norm(values, gain):
    return values * lax.rsqrt(jnp.mean(values * values, axis=-1, keepdims=True) + EPSILON) * gain


def linear_pair(earlier, later):
    return (later[0] * earlier[0], later[0] * earlier[1] + later[1])


def gelu_back(values, grad):
    return jax.vjp(jax.nn.gelu, values)[1](grad)[0]


def gathered_weights(
    tokens,
    norm_gain,
    x_weight,
    y_weight,
    conv_weight,
    conv_bias,
    a_weight,
    a_bias,
    i_weight,
    i_bias,
    decay,
    out_weight,
    mlp_gain,
    gate_weight,
    up_weight,
    down_weight,
    cotangent,
):
    row_count = tokens.shape[0]
    model_width = tokens.shape[1]
    lane_count = x_weight.shape[1]
    head_size = a_weight.shape[0]
    head_index = lax.axis_index("head")
    seq_index = lax.axis_index("seq")
    head_devices = lax.axis_size("head")
    float_type = jnp.float32
    half_type = jnp.bfloat16
    gathered = (
        lax.all_gather(x_weight, "seq", axis=0, tiled=True),
        lax.all_gather(y_weight, "seq", axis=0, tiled=True),
        lax.all_gather(out_weight, "seq", axis=0, tiled=True),
        lax.all_gather(gate_weight, "seq", axis=0, tiled=True),
        lax.all_gather(up_weight, "seq", axis=0, tiled=True),
        lax.all_gather(down_weight, "seq", axis=0, tiled=True),
    )
    x_full, y_full, out_full, gate_full, up_full, down_full = gathered
    tokens_wide = tokens.astype(float_type)
    first_gain = norm_gain.astype(float_type)
    first_norm = rms_norm(tokens_wide, first_gain)
    first_low = first_norm.astype(half_type)
    x_branch = jnp.dot(first_low, x_full, preferred_element_type=float_type).astype(half_type)
    y_branch = jnp.dot(first_low, y_full, preferred_element_type=float_type)
    y_gate = jax.nn.gelu(y_branch)
    left_edge = from_behind(x_branch[row_count - (CONV - 1) :], "seq", 1)
    padded = jnp.concatenate([left_edge, x_branch], axis=0).astype(float_type)
    conv_taps = conv_weight.astype(float_type)
    conv_out = conv_bias.astype(float_type) + sum(
        (
            conv_taps[lag_index] * padded[CONV - 1 - lag_index : CONV - 1 - lag_index + row_count]
            for lag_index in range(CONV)
        )
    )
    conv_low = conv_out.astype(half_type)
    conv_value = conv_low.astype(float_type)
    all_channels = lax.all_gather(conv_low, "head", axis=1, tiled=True)
    head_count = all_channels.shape[1] // head_size
    group_count = lane_count // head_count
    heads_view = all_channels.reshape(row_count, head_size, head_count)

    def block_gate(weight, bias):
        product = jnp.einsum(
            "tih,ijh->tjh",
            heads_view,
            weight.reshape(head_size, group_count, head_count),
            preferred_element_type=float_type,
        )
        return product.reshape(row_count, lane_count) + bias.astype(float_type)

    a_pre = block_gate(a_weight, a_bias)
    i_pre = block_gate(i_weight, i_bias)
    recall = jax.nn.sigmoid(a_pre)
    input_gate = jax.nn.sigmoid(i_pre)
    decay_rate = jax.nn.softplus(decay)
    log_decay = -8.0 * recall * decay_rate
    factor = jnp.exp(log_decay)
    double_decay = jnp.exp(2.0 * log_decay)
    one_minus = -jnp.expm1(2.0 * log_decay)
    root_value = jnp.sqrt(jnp.maximum(one_minus, SQUARE_FLOOR))
    position = seq_index * row_count + jnp.arange(row_count)
    anchor = (position == 0)[:, None]
    root_scale = jnp.where(anchor, 1.0, root_value)
    root_live = jnp.logical_and(one_minus > SQUARE_FLOOR, jnp.logical_not(anchor))
    driven = conv_value * input_gate * root_scale
    local_prod, local_state = lax.associative_scan(linear_pair, (factor, driven))

    def relay_step(turn_number, carried):
        return from_behind(local_prod[-1] * carried + local_state[-1], "seq", 1)

    state_entry = lax.fori_loop(
        0, lax.axis_size("seq") - 1, relay_step, jnp.zeros_like(local_state[-1])
    )
    state_all = local_state + local_prod * state_entry
    mixed_in = (state_all * y_gate).astype(half_type)
    branch_part = jnp.einsum("tc,dc->td", mixed_in, out_full, preferred_element_type=float_type)
    branch = lax.psum(branch_part, "head")
    residual = tokens_wide + branch
    second_gain = mlp_gain.astype(float_type)
    second_low = rms_norm(residual, second_gain).astype(half_type)
    gate_pre = jnp.dot(second_low, gate_full, preferred_element_type=float_type)
    up_pre = jnp.dot(second_low, up_full, preferred_element_type=float_type)
    gate_act = jax.nn.gelu(gate_pre)
    hidden = (gate_act * up_pre).astype(half_type)
    mlp_part = jnp.einsum("tf,df->td", hidden, down_full, preferred_element_type=float_type)
    own_columns = lax.psum_scatter(mlp_part, "head", scatter_dimension=1, tiled=True)
    column_count = model_width // head_devices
    mixed = (
        lax.dynamic_slice_in_dim(residual, head_index * column_count, column_count, 1) + own_columns
    ).astype(half_type)
    regathered = (
        lax.all_gather(x_weight, "seq", axis=0, tiled=True),
        lax.all_gather(y_weight, "seq", axis=0, tiled=True),
        lax.all_gather(out_weight, "seq", axis=0, tiled=True),
        lax.all_gather(gate_weight, "seq", axis=0, tiled=True),
        lax.all_gather(up_weight, "seq", axis=0, tiled=True),
        lax.all_gather(down_weight, "seq", axis=0, tiled=True),
    )
    x_full, y_full, out_full, gate_full, up_full, down_full = regathered
    hidden_grad = jnp.dot(cotangent, down_full, preferred_element_type=float_type)
    gate_grad = gelu_back(gate_pre, hidden_grad * up_pre).astype(half_type)
    up_grad = (hidden_grad * gate_act).astype(half_type)
    second_part = jnp.einsum(
        "tf,df->td", gate_grad, gate_full, preferred_element_type=float_type
    ) + jnp.einsum("tf,df->td", up_grad, up_full, preferred_element_type=float_type)
    second_grad = lax.psum(second_part, "head")
    resid_back, mlp_gain_term = jax.vjp(rms_norm, residual, second_gain)[1](second_grad)
    resid_grad = cotangent.astype(float_type) + resid_back
    branch_grad = resid_grad.astype(half_type)
    mixed_grad = jnp.dot(branch_grad, out_full, preferred_element_type=float_type)
    state_grad = mixed_grad * y_gate
    y_grad = gelu_back(y_branch, mixed_grad * state_all).astype(half_type)
    next_factor = jnp.concatenate([factor[1:], jnp.ones_like(factor[:1])], axis=0)
    back_prod, back_adjoint = lax.associative_scan(
        linear_pair, (next_factor[::-1], state_grad[::-1])
    )
    back_prod = back_prod[::-1]
    back_adjoint = back_adjoint[::-1]
    tail_prod = factor[0] * back_prod[0]
    tail_value = factor[0] * back_adjoint[0]

    def relay_back(turn_number, carried):
        return from_behind(tail_value + tail_prod * carried, "seq", -1)

    exit_carry = lax.fori_loop(0, lax.axis_size("seq") - 1, relay_back, jnp.zeros_like(tail_value))
    adjoint = back_adjoint + back_prod * exit_carry
    prev_state = jnp.concatenate([state_entry[None], state_all[:-1]], axis=0)
    scale_grad = adjoint * conv_value * input_gate
    log_grad = adjoint * prev_state * factor + jnp.where(
        root_live, -scale_grad * double_decay / root_value, 0.0
    )
    a_grad = (log_grad * (-8.0 * decay_rate) * recall * (1.0 - recall)).astype(half_type)
    i_grad = (adjoint * conv_value * root_scale * input_gate * (1.0 - input_gate)).astype(half_type)
    decay_term = jnp.sum(log_grad * (-8.0 * recall), axis=0) * jax.nn.sigmoid(decay)
    a_bias_term = jnp.sum(a_grad.astype(float_type), axis=0)
    i_bias_term = jnp.sum(i_grad.astype(float_type), axis=0)

    def gate_back(grad, weight):
        grad_view = grad.reshape(row_count, group_count, head_count)
        weight_term = jnp.einsum(
            "tih,tjh->ijh", heads_view, grad_view, preferred_element_type=float_type
        ).reshape(head_size, lane_count)
        input_term = jnp.einsum(
            "tjh,ijh->tih",
            grad_view,
            weight.reshape(head_size, group_count, head_count),
            preferred_element_type=float_type,
        )
        return (weight_term, input_term)

    a_wgrad, a_input = gate_back(a_grad, a_weight)
    i_wgrad, i_input = gate_back(i_grad, i_weight)
    gate_input_grad = lax.psum_scatter(
        (a_input + i_input).reshape(row_count, head_size * head_count),
        "head",
        scatter_dimension=1,
        tiled=True,
    )
    conv_grad = gate_input_grad + adjoint * input_gate * root_scale
    right_edge = from_behind(conv_grad[: CONV - 1], "seq", -1)
    extended_grad = jnp.concatenate([conv_grad, right_edge], axis=0)
    x_branch_grad = sum(
        (
            conv_taps[lag_index] * extended_grad[lag_index : lag_index + row_count]
            for lag_index in range(CONV)
        )
    ).astype(half_type)
    conv_wgrad = jnp.stack(
        [
            jnp.sum(
                conv_grad * padded[CONV - 1 - lag_index : CONV - 1 - lag_index + row_count], axis=0
            )
            for lag_index in range(CONV)
        ],
        axis=0,
    )
    conv_bgrad = jnp.sum(conv_grad, axis=0)
    first_part = jnp.einsum(
        "tc,dc->td", x_branch_grad, x_full, preferred_element_type=float_type
    ) + jnp.einsum("tc,dc->td", y_grad, y_full, preferred_element_type=float_type)
    first_grad = lax.psum(first_part, "head")
    tokens_back, norm_gain_term = jax.vjp(rms_norm, tokens_wide, first_gain)[1](first_grad)
    tokens_grad = resid_grad + tokens_back
    pairings = (
        (first_low, x_branch_grad),
        (first_low, y_grad),
        (branch_grad, mixed_in),
        (second_low, gate_grad),
        (second_low, up_grad),
        (cotangent, hidden),
    )
    products = tuple(
        (
            jnp.einsum("td,tc->dc", left, right, preferred_element_type=float_type)
            for left, right in pairings
        )
    )
    weight_sums = lax.psum_scatter(products, "seq", scatter_dimension=0, tiled=True)
    small_sums = lax.psum(
        (
            norm_gain_term,
            conv_wgrad,
            conv_bgrad,
            a_wgrad,
            a_bias_term,
            i_wgrad,
            i_bias_term,
            decay_term,
            mlp_gain_term,
        ),
        "seq",
    )
    return (
        mixed,
        tokens_grad,
        small_sums[0],
        weight_sums[0],
        weight_sums[1],
        small_sums[1],
        small_sums[2],
        small_sums[3],
        small_sums[4],
        small_sums[5],
        small_sums[6],
        small_sums[7],
        weight_sums[2],
        small_sums[8],
        weight_sums[3],
        weight_sums[4],
        weight_sums[5],
    )


def solution(mesh):
    sizes = mesh.shape["seq"], mesh.shape["head"]

    def body(*args):
        z = Size(sizes, args[0], args[2], args[6], args[13])
        return dealt(z, *args) if z.fits() else gathered_weights(*args)

    return jax.shard_map(
        body,
        mesh=mesh,
        in_specs=(
            P("seq", None),
            P(),
            P("seq", "head"),
            P("seq", "head"),
            P(None, "head"),
            P("head"),
            P(None, "head"),
            P("head"),
            P(None, "head"),
            P("head"),
            P("head"),
            P("seq", "head"),
            P(),
            P("seq", "head"),
            P("seq", "head"),
            P("seq", "head"),
            P("seq", None),
        ),
        out_specs=(
            P("seq", "head"),
            P("seq", None),
            P(),
            P("seq", "head"),
            P("seq", "head"),
            P(None, "head"),
            P("head"),
            P(None, "head"),
            P("head"),
            P(None, "head"),
            P("head"),
            P("head"),
            P("seq", "head"),
            P(),
            P("seq", "head"),
            P("seq", "head"),
            P("seq", "head"),
        ),
        check_vma=False,
    )
```
